128 devices in a mesh: dp: 16 (over y_lo, x, core), mp: 8 (over z, y_hi).
Axes of the slice: x: 4, y: 4 (y_hi: 2, y_lo: 2; y = y_hi * 2 + y_lo), z: 4, core: 2. Of those that a mesh axis runs over, the one named last changes fastest.
Arguments:
- hidden: bfloat16 [32768, 1536], P(('dp', 'mp')), may hold values from -6 to 6
- grad_out: bfloat16 [32768, 1536], P(('dp', 'mp')), may hold values from -6 to 6
- norm_gain: float32 [1536], replicated, may hold values from 0.5 to 1.5
- w_zx: bfloat16 [1536, 2, 3072], P('dp', None, 'mp'), may hold values from -0.15625 to 0.15625
- w_bc: bfloat16 [1536, 256], P('dp'), may hold values from -0.15625 to 0.15625
- w_dt: bfloat16 [1536, 48], P('dp', 'mp'), may hold values from -0.15625 to 0.15625
- conv_x: float32 [5, 3072], P(None, 'mp'), may hold values from -3 to 3
- conv_bc: float32 [5, 256], replicated, may hold values from -3 to 3
- a_log: float32 [48], P('mp'), may hold values from -5 to 1
- dt_bias: float32 [48], P('mp'), may hold values from -4 to 0
- d_skip: float32 [48], P('mp'), may hold values from 0.5 to 1.5
- gate_gain: float32 [3072], P('mp'), may hold values from 0.5 to 1.5
- w_out: bfloat16 [3072, 1536], P('mp', 'dp'), may hold values from -0.109375 to 0.109375
Outputs:
- result: bfloat16 [32768, 1536], P(('dp', 'mp'))
- grad_hidden: float32 [32768, 1536], P(('dp', 'mp'))
- grad_norm_gain: float32 [1536], replicated
- grad_w_zx: float32 [1536, 2, 3072], P('dp', None, 'mp')
- grad_w_bc: float32 [1536, 256], P('dp')
- grad_w_dt: float32 [1536, 48], P('dp', 'mp')
- grad_conv_x: float32 [5, 3072], P(None, 'mp')
- grad_conv_bc: float32 [5, 256], replicated
- grad_a_log: float32 [48], P('mp')
- grad_dt_bias: float32 [48], P('mp')
- grad_d_skip: float32 [48], P('mp')
- grad_gate_gain: float32 [3072], P('mp')
- grad_w_out: float32 [3072, 1536], P('mp', 'dp')
The draws below stay inside these ranges and needn't reach their ends.
All inputs are finite; a program needn't handle non-finite values.
Results may differ from the reference program's by a relative error of at most 0.03.
Values may be sent and summed in bfloat16 or wider, within the bound.
A program may use at most 192 MiB of HBM per device.

```python
import jax
import jax.numpy as jnp
from jax import lax

D = 1536
HEADS = 48
HEAD_DIM = 64
STATE = 128
CONV = 4
SPAN = 256
LEN = 2048
INNER = 3072
TOKENS = 32768


def block_levels(key, extent, pieces, low, high):
    loudness = 1.0
    for axis_at, blocks in pieces:
        heights = jax.random.uniform(jax.random.fold_in(jax.random.fold_in(key, 6), axis_at), (blocks,), jnp.float32, low / len(pieces), high / len(pieces))
        loudness = loudness * jnp.repeat(jnp.exp(heights), extent[axis_at] // blocks).reshape((-1,) + (1,) * (len(extent) - 1 - axis_at))
    return loudness


def normal_values(key, extent, scale, bound, cuts=(), kind=jnp.bfloat16):
    level = block_levels(key, extent, cuts, -0.22, 0.18) if cuts else 1.0
    values = jax.random.normal(key, extent, jnp.float32) * scale * level
    return jnp.minimum(jnp.maximum(values, -bound), bound).astype(kind)


def setup_inputs(seed: int = 0) -> dict:
    streams_of = jax.random.split(jax.random.key(seed), 14)
    hidden = normal_values(streams_of[0], (TOKENS, D), 1.0, 6.0, ((0, 128),))
    grad_out = normal_values(streams_of[1], (TOKENS, D), 1.0, 6.0, ((0, 128),))
    norm_gain = jnp.clip(1.0 + 0.1 * jax.random.normal(streams_of[2], (D,), jnp.float32), 0.5, 1.5)
    w_zx = normal_values(streams_of[3], (D, 2, INNER), D ** -0.5, 0.15625, ((0, 16), (2, 8)))
    w_bc = normal_values(streams_of[4], (D, 2 * STATE), D ** -0.5, 0.15625, ((0, 16),))
    w_dt = normal_values(streams_of[5], (D, HEADS), D ** -0.5, 0.15625, ((0, 16), (1, 8)))
    conv_x = normal_values(streams_of[6], (CONV + 1, INNER), 0.5, 3.0, ((1, 8),), jnp.float32)
    conv_bc = normal_values(streams_of[7], (CONV + 1, 2 * STATE), 0.5, 3.0, (), jnp.float32)
    a_log = jnp.clip(-5.0 + 6.0 * jax.random.uniform(streams_of[8], (HEADS,), jnp.float32) ** block_levels(streams_of[8], (HEADS,), ((0, 8),), -0.2, 0.2), -5.0, 1.0)
    dt_bias = jnp.clip(-4.0 + 4.0 * jax.random.uniform(streams_of[9], (HEADS,), jnp.float32) ** block_levels(streams_of[9], (HEADS,), ((0, 8),), -0.2, 0.2), -4.0, 0.0)
    d_skip = jnp.clip(0.5 + 1.0 * jax.random.uniform(streams_of[10], (HEADS,), jnp.float32) ** block_levels(streams_of[10], (HEADS,), ((0, 8),), -0.2, 0.2), 0.5, 1.5)
    gate_gain = jnp.clip(1.0 + 0.1 * jax.random.normal(streams_of[11], (INNER,), jnp.float32), 0.5, 1.5)
    w_out = normal_values(streams_of[12], (INNER, D), INNER ** -0.5, 0.109375, ((0, 8), (1, 16)))
    return dict(hidden=hidden, grad_out=grad_out, norm_gain=norm_gain, w_zx=w_zx, w_bc=w_bc, w_dt=w_dt, conv_x=conv_x, conv_bc=conv_bc, a_log=a_log, dt_bias=dt_bias, d_skip=d_skip, gate_gain=gate_gain, w_out=w_out)


EPS = 1e-05
EXACT = lax.Precision.HIGHEST

@jax.custom_vjp
def low(v):
    return lax.optimization_barrier(v.astype(jnp.bfloat16)).astype(jnp.float32)

@jax.custom_vjp
def low_back(v):
    return v

def low_keep(v):
    return (low(v), None)

def low_pass(kept, grad):
    return (grad,)

def back_keep(v):
    return (v, None)

def back_low(kept, grad):
    return (low(grad),)
low.defvjp(low_keep, low_pass)
low_back.defvjp(back_keep, back_low)

def rms_scale(values):
    return lax.rsqrt(lax.optimization_barrier(jnp.mean(values * values, axis=-1, keepdims=True)) + EPS)

def causal_conv(values, taps):
    width = taps.shape[0] - 1
    length = values.shape[0]
    padded = jnp.pad(values, ((width - 1, 0), (0, 0)))
    total = taps[width] + padded[0:length] * taps[0]
    for offset in range(1, width):
        total = total + padded[offset:offset + length] * taps[offset]
    return jax.nn.silu(total)

def span_step(state, block):
    u_blk, rate_blk, b_blk, c_blk = block
    size = rate_blk.shape[0]
    cum = jnp.cumsum(rate_blk, axis=0).T
    where_causal = jnp.arange(size)[:, None] >= jnp.arange(size)[None, :]
    diff = cum[:, :, None] - cum[:, None, :]
    decay = jnp.where(where_causal, jnp.exp(jnp.where(where_causal, diff, 0.0)), 0.0)
    gram = jnp.dot(c_blk, b_blk.T, precision=EXACT)
    mixing = decay * gram
    inside = jnp.einsum('hts,shp->thp', mixing, u_blk, precision=EXACT)
    carried = jnp.einsum('tn,hpn->thp', c_blk, state, precision=EXACT) * jnp.exp(cum).T[:, :, None]
    tail = jnp.exp(cum[:, -1:] - cum)
    weighted = u_blk * tail.T[:, :, None]
    new_state = state * jnp.exp(cum[:, -1])[:, None, None] + jnp.einsum('shp,sn->hpn', weighted, b_blk, precision=EXACT)
    return (new_state, inside + carried)

def ssd_scan(inputs, log_decay, b_vals, c_vals):
    length, heads, channels = inputs.shape
    count = length // SPAN
    blocks = (inputs.reshape(count, SPAN, heads, channels), log_decay.reshape(count, SPAN, heads), b_vals.reshape(count, SPAN, -1), c_vals.reshape(count, SPAN, -1))
    state = jnp.zeros((heads, channels, b_vals.shape[-1]), jnp.float32)
    final, outputs = lax.scan(jax.checkpoint(span_step), state, blocks)
    return outputs.reshape(length, heads, channels)

def forward(hidden, norm_gain, w_zx, w_bc, w_dt, conv_x, conv_bc, a_log, dt_bias, d_skip, gate_gain, w_out):
    normed = low(hidden * rms_scale(hidden) * norm_gain)
    proj_zx = low_back(jnp.einsum('ld,dki->lki', normed, w_zx, precision=EXACT))
    bc_pre = low_back(jnp.dot(normed, w_bc, precision=EXACT))
    dt_raw = low_back(jnp.dot(normed, w_dt, precision=EXACT))
    gate_pre = proj_zx[:, 0]
    x_conv = low(causal_conv(proj_zx[:, 1], conv_x))
    bc_conv = low(causal_conv(bc_pre, conv_bc))
    step = jax.nn.softplus(dt_raw + dt_bias)
    log_decay = step * -jnp.exp(a_log)
    x_heads = x_conv.reshape(LEN, HEADS, HEAD_DIM)
    inputs = step[:, :, None] * x_heads
    scanned = ssd_scan(inputs, log_decay, bc_conv[:, :STATE], bc_conv[:, STATE:])
    y_full = (scanned + d_skip[:, None] * x_heads).reshape(LEN, INNER)
    gated = y_full * jax.nn.silu(gate_pre)
    out_in = low(gated * rms_scale(gated) * gate_gain)
    return hidden + jnp.dot(out_in, w_out, precision=EXACT)

def reference(hidden, grad_out, norm_gain, w_zx, w_bc, w_dt, conv_x, conv_bc, a_log, dt_bias, d_skip, gate_gain, w_out):
    params = (norm_gain.astype(jnp.float32), w_zx.astype(jnp.float32), w_bc.astype(jnp.float32), w_dt.astype(jnp.float32), conv_x.astype(jnp.float32), conv_bc.astype(jnp.float32), a_log.astype(jnp.float32), dt_bias.astype(jnp.float32), d_skip.astype(jnp.float32), gate_gain.astype(jnp.float32), w_out.astype(jnp.float32))
    seq_total = hidden.shape[0] // LEN
    sequences = hidden.astype(jnp.float32).reshape(seq_total, LEN, D)
    cotangents = grad_out.astype(jnp.float32).reshape(seq_total, LEN, D)

    def one_sequence(totals, item):
        values, cotangent = item
        output, back = jax.vjp(forward, values, *params)
        grads = back(cotangent)
        totals = tuple((total + grad for total, grad in zip(totals, grads[1:])))
        return (totals, (output.astype(jnp.bfloat16), grads[0]))
    start = tuple((jnp.zeros_like(param) for param in params))
    totals, (outputs, input_grads) = lax.scan(one_sequence, start, (sequences, cotangents))
    return (outputs.reshape(-1, D), input_grads.reshape(-1, D), totals[0], totals[1], totals[2], totals[3], totals[4], totals[5], totals[6], totals[7], totals[8], totals[9], totals[10])
```

```python
import jax
import jax.numpy as jnp
from jax import lax
from jax.experimental import pallas as pl
from jax.experimental.pallas import tpu as pltpu
from jax.sharding import Mesh
from jax.sharding import PartitionSpec as P

MP = ("z", "yhi")
DP = ("ylo", "x", "core")
DP_MP = DP + MP
BLOCKS = 8
F32 = jnp.float32
BF16 = jnp.bfloat16
ROWS = 256
WIDTH = 1536
GROUPS = 8
COLS = 384
HEADS = 6
HALO = 16
EPS = 1e-05
INNER = GROUPS * COLS
VMEM_LIMIT = 56 * 2**20


def dot(a, b, contract=(1, 0), precision=None):
    return lax.dot_general(
        a, b, (((contract[0],), (contract[1],)), ((), ())),
        preferred_element_type=F32, precision=precision,
    )


def spread(per_head):
    rows = per_head.shape[0]
    low = lax.broadcasted_iota(jnp.int32, (rows, 128), 1) < 64
    tiles = [
        jnp.where(low, per_head[:, 2 * i : 2 * i + 1], per_head[:, 2 * i + 1 : 2 * i + 2])
        for i in range(COLS // 128)
    ]
    return jnp.concatenate(tiles, axis=1)


def gathered_heads(values):
    rows = values.shape[0]
    low = lax.broadcasted_iota(jnp.int32, (rows, 128), 1) < 64
    lane = lax.broadcasted_iota(jnp.int32, (rows, 8), 1)
    out = jnp.zeros((rows, 8), F32)
    for i in range(COLS // 128):
        tile = values[:, 128 * i : 128 * i + 128]
        first = jnp.sum(jnp.where(low, tile, 0.0), axis=1, keepdims=True)
        both = jnp.sum(tile, axis=1, keepdims=True)
        out = jnp.where(lane == 2 * i, first, out)
        out = jnp.where(lane == 2 * i + 1, both - first, out)
    return out


def softplus(v):
    return jnp.maximum(v, 0.0) + jnp.log1p(jnp.exp(-jnp.abs(v)))


def conv_pre(ext, taps):
    total = taps[4:5]
    for j in range(4):
        total = total + ext[HALO - 3 + j : HALO - 3 + j + ROWS] * taps[j : j + 1]
    return total


def conv_transposed(ext, taps, rows=ROWS):
    total = ext[3 : 3 + rows] * taps[0:1]
    for j in range(1, 4):
        total = total + ext[3 - j : 3 - j + rows] * taps[j : j + 1]
    return total


def conv_grads(dpre, ext, sixth, seventh):
    rows = [
        jnp.sum(dpre * ext[HALO - 3 + j : HALO - 3 + j + ROWS], axis=0, keepdims=True)
        for j in range(4)
    ]
    rows.append(jnp.sum(dpre, axis=0, keepdims=True))
    rows += [sixth, seventh, jnp.zeros((1, dpre.shape[1]), F32)]
    return jnp.concatenate(rows, axis=0)


def triangle(upper):
    row = lax.broadcasted_iota(jnp.int32, (ROWS, ROWS), 0)
    col = lax.broadcasted_iota(jnp.int32, (ROWS, ROWS), 1)
    return row <= col if upper else row >= col


def first_kernel(hid, halo, cot, gain, w_small, taps_bc, a_log, dt_bias,
                 normed, normed_t, cot_t, bc_pre, bc_conv, steps, cum_col, step_col, cum_row, step_row):
    for at, part in ((0, halo), (HALO, hid)):
        v = part[...].astype(F32)
        r = lax.rsqrt(jnp.mean(v * v, axis=1, keepdims=True) + EPS)
        normed[at : at + part.shape[0], :] = (v * r * gain[...]).astype(BF16)
    normed_t[...] = normed[HALO:, :].T.reshape(8, 2, 96, ROWS)
    cot_t[...] = cot[...].T.reshape(8, 2, 96, ROWS)
    small = dot(normed[...], w_small[...])
    bc_pre[...] = small[:, :256]
    pre = conv_pre(small[:, :256], taps_bc[...])
    bc_conv[...] = (pre * jax.nn.sigmoid(pre)).astype(BF16)
    shifted = small[HALO:, 256:384] + dt_bias[...]
    steps[...] = shifted
    step = softplus(shifted)
    decay = -step * jnp.exp(a_log[...])
    tri = triangle(False).astype(F32)
    cum = dot(tri, decay, precision=lax.Precision.HIGHEST)
    cum_t = cum.T
    step_t = step.T
    for m in range(GROUPS):
        cum_col[m] = cum[:, HEADS * m : HEADS * m + 8]
        step_col[m] = step[:, HEADS * m : HEADS * m + 8]
        cum_row[m] = cum_t[HEADS * m : HEADS * m + 8]
        step_row[m] = step_t[HEADS * m : HEADS * m + 8]


def sds(*shape, dtype=F32):
    return jax.ShapeDtypeStruct(shape, dtype)


def params():
    return pltpu.CompilerParams(vmem_limit_bytes=VMEM_LIMIT)


def first(hid, halo, cot, gain, w_small, taps_bc, a_log, dt_bias):
    return pl.pallas_call(
        first_kernel,
        out_shape=(
            sds(HALO + ROWS, WIDTH, dtype=BF16), sds(8, 2, 96, ROWS, dtype=BF16), sds(8, 2, 96, ROWS, dtype=BF16),
            sds(HALO + ROWS, 256), sds(ROWS, 256, dtype=BF16),
            sds(ROWS, 128), sds(GROUPS, ROWS, 8), sds(GROUPS, ROWS, 8),
            sds(GROUPS, 8, ROWS), sds(GROUPS, 8, ROWS),
        ),
        compiler_params=params(),
        name="norm_and_small_projections",
    )(hid, halo, cot, gain, w_small, taps_bc, a_log, dt_bias)


def whole(*shape):
    return pl.BlockSpec(shape, lambda m: (0,) * len(shape))


def lead(*shape):
    return pl.BlockSpec((None, *shape), lambda m: (m,) + (0,) * len(shape))


def weight(item):
    return pl.BlockSpec((None, None, WIDTH, COLS), lambda m: (item, m, 0, 0))


def second_kernel(normed, w, taps, bc_conv, cum_col, step_col, x_pre, x_conv, state):
    ext = dot(normed[...], w[...])
    x_pre[...] = ext
    pre = conv_pre(ext, taps[...])
    xc = (pre * jax.nn.sigmoid(pre)).astype(BF16)
    x_conv[...] = xc
    cum = cum_col[...]
    weights = step_col[...] * jnp.exp(cum[ROWS - 1 : ROWS] - cum)
    weighted = (xc.astype(F32) * spread(weights)).astype(BF16)
    state[...] = dot(weighted, bc_conv[:, :128], (0, 0)).astype(BF16)


def second(normed, w_all, taps, bc_conv, cum_col, step_col):
    return pl.pallas_call(
        second_kernel,
        grid=(GROUPS,),
        in_specs=[whole(HALO + ROWS, WIDTH), weight(0), lead(8, COLS), whole(ROWS, 256), lead(ROWS, 8), lead(ROWS, 8)],
        out_specs=(lead(HALO + ROWS, COLS), lead(ROWS, COLS), lead(COLS, 128)),
        out_shape=(sds(GROUPS, HALO + ROWS, COLS), sds(GROUPS, ROWS, COLS, dtype=BF16), sds(GROUPS, COLS, 128, dtype=BF16)),
        compiler_params=params(),
        name="x_projection_and_state",
    )(normed, w_all, taps, bc_conv, cum_col, step_col)


def third_kernel(normed, cot, w_z, w_o, x_conv, bc_conv, cum_col, cum_row, step_row, state, skip, gain,
                 z_out, y_out, d_out, square, inner, gram):
    @pl.when(pl.program_id(0) == 0)
    def _():
        g = dot(bc_conv[:, 128:], bc_conv[:, :128], (1, 1))
        gram[...] = jnp.where(triangle(False), g, 0.0)
        square[...] = jnp.zeros_like(square)
        inner[...] = jnp.zeros_like(inner)

    xc = x_conv[...]
    cum = cum_col[...]
    parts = []
    for h in range(HEADS):
        decay = jnp.exp(jnp.minimum(cum[:, h : h + 1] - cum_row[h : h + 1, :], 0.0))
        mixing = (decay * gram[...] * step_row[h : h + 1, :]).astype(BF16)
        parts.append(dot(mixing, xc[:, 64 * h : 64 * h + 64]))
    inside = jnp.concatenate(parts, axis=1)
    carried = dot(bc_conv[:, 128:], state[...], (1, 1))
    y = inside + spread(jnp.exp(cum)) * carried + skip[...] * xc.astype(F32)
    z = dot(normed[HALO:, :], w_z[...])
    d = dot(cot[...], w_o[...])
    gated = y * (z * jax.nn.sigmoid(z))
    z_out[...] = z
    y_out[...] = y
    d_out[...] = d
    sq = gated * gated
    ip = d * gain[...] * gated
    square[...] += sq[:, :128] + sq[:, 128:256] + sq[:, 256:]
    inner[...] += ip[:, :128] + ip[:, 128:256] + ip[:, 256:]


def third(normed, cot, w_all, x_conv, bc_conv, cum_col, cum_row, step_row, state, skip, gain):
    return pl.pallas_call(
        third_kernel,
        grid=(GROUPS,),
        in_specs=[whole(HALO + ROWS, WIDTH), whole(ROWS, WIDTH), weight(1), weight(2), lead(ROWS, COLS), whole(ROWS, 256),
                  lead(ROWS, 8), lead(8, ROWS), lead(8, ROWS), lead(COLS, 128), lead(1, COLS), lead(1, COLS)],
        out_specs=(lead(ROWS, COLS), lead(ROWS, COLS), lead(ROWS, COLS), whole(ROWS, 128), whole(ROWS, 128)),
        out_shape=(sds(GROUPS, ROWS, COLS), sds(GROUPS, ROWS, COLS), sds(GROUPS, ROWS, COLS), sds(ROWS, 128), sds(ROWS, 128)),
        scratch_shapes=[pltpu.VMEM((ROWS, ROWS), F32)],
        compiler_params=params(),
        name="scan_and_gate",
    )(normed, cot, w_all, w_all, x_conv, bc_conv, cum_col, cum_row, step_row, state, skip, gain)


def fourth_kernel(hid, square, inner, z_in, y_in, d_in, gain, w_o, x_conv, bc_conv, cum_col, step_col, cum_row, step_row,
                  state, skip,
                  result, out_in, d_z, d_x, d_state, d_cum, d_step, d_bc, gain_part, skip_part,
                  gram, d_gram, acc, d_c):
    step_id = pl.program_id(0)

    @pl.when(step_id == 0)
    def _():
        g = dot(bc_conv[:, 128:], bc_conv[:, :128], (1, 1))
        gram[...] = jnp.where(triangle(False), g, 0.0)
        d_gram[...] = jnp.zeros_like(d_gram)
        acc[...] = jnp.zeros_like(acc)
        d_c[...] = jnp.zeros_like(d_c)

    z = z_in[...]
    y = y_in[...]
    d = d_in[...]
    sig = jax.nn.sigmoid(z)
    act = z * sig
    gated = y * act
    r2 = lax.rsqrt(jnp.sum(square[...], axis=1, keepdims=True) / INNER + EPS)
    total = jnp.sum(inner[...], axis=1, keepdims=True)
    unit = gated * r2
    o = (unit * gain[...]).astype(BF16)
    out_in[...] = o
    acc[...] += dot(o, w_o[...], (1, 1))
    gain_part[...] = jnp.sum(d * unit, axis=0, keepdims=True)
    d_gated = r2 * (d * gain[...]) - gated * (r2 * r2 * r2 * (total / INNER))
    dy = d_gated * act
    d_z[...] = (d_gated * y * sig * (1.0 + z * (1.0 - sig))).astype(BF16)

    xc = x_conv[...]
    xf = xc.astype(F32)
    cum = cum_col[...]
    step = step_col[...]
    dyb = dy.astype(BF16)
    c_mat = bc_conv[:, 128:]
    skip_part[...] = jnp.sum(dy * xf, axis=0, keepdims=True)
    grown = spread(jnp.exp(cum))
    dye = (grown * dy).astype(BF16)
    d_c[...] += dot(dye, state[...])
    d_state[...] = dot(dye, c_mat, (0, 0)).astype(BF16)
    carried = grown * dot(c_mat, state[...], (1, 1))
    d_cum_col = gathered_heads(dy * carried)
    lane = lax.broadcasted_iota(jnp.int32, (ROWS, 8), 1)
    parts = []
    cols = []
    for h in range(HEADS):
        xh = xc[:, 64 * h : 64 * h + 64]
        dyh = dyb[:, 64 * h : 64 * h + 64]
        decay = jnp.exp(jnp.minimum(cum[:, h : h + 1] - cum_row[h : h + 1, :], 0.0))
        d_mix = dot(dyh, xh, (1, 1))
        grown_row = step_row[h : h + 1, :]
        plain = decay * gram[...]
        r = plain * d_mix
        cols.append(jnp.sum(r, axis=0, keepdims=True))
        row = jnp.sum(r * grown_row, axis=1, keepdims=True)
        d_cum_col = jnp.where(lane == h, d_cum_col + row, d_cum_col)
        d_gram[...] += decay * d_mix * grown_row
        parts.append(dot((plain * grown_row).astype(BF16), dyh, (0, 0)))
    cols.append(jnp.zeros((2, ROWS), F32))
    cols = jnp.concatenate(cols, axis=0).T
    d_x[...] = jnp.concatenate(parts, axis=1) + skip[...] * dy
    d_step[...] = cols
    d_cum[...] = d_cum_col - cols * step

    @pl.when(step_id == GROUPS - 1)
    def _():
        result[...] = (hid[...].astype(F32) + acc[...]).astype(BF16)
        dg = jnp.where(triangle(False), d_gram[...], 0.0).astype(BF16)
        d_bc[:, :128] = dot(dg, c_mat, (0, 0))
        d_bc[:, 128:] = d_c[...] + dot(dg, bc_conv[:, :128])


def fourth(hid, square, inner, z, y, d, gain, w_all, x_conv, bc_conv, cum_col, step_col, cum_row, step_row, state, skip):
    return pl.pallas_call(
        fourth_kernel,
        grid=(GROUPS,),
        in_specs=[whole(ROWS, WIDTH), whole(ROWS, 128), whole(ROWS, 128), lead(ROWS, COLS), lead(ROWS, COLS), lead(ROWS, COLS),
                  lead(1, COLS), weight(2), lead(ROWS, COLS), whole(ROWS, 256), lead(ROWS, 8), lead(ROWS, 8), lead(8, ROWS),
                  lead(8, ROWS), lead(COLS, 128), lead(1, COLS)],
        out_specs=(whole(ROWS, WIDTH), lead(ROWS, COLS), lead(ROWS, COLS), lead(ROWS, COLS), lead(COLS, 128), lead(ROWS, 8),
                   lead(ROWS, 8), whole(ROWS, 256), lead(1, COLS), lead(1, COLS)),
        out_shape=(sds(ROWS, WIDTH, dtype=BF16), sds(GROUPS, ROWS, COLS, dtype=BF16), sds(GROUPS, ROWS, COLS, dtype=BF16),
                   sds(GROUPS, ROWS, COLS), sds(GROUPS, COLS, 128, dtype=BF16), sds(GROUPS, ROWS, 8), sds(GROUPS, ROWS, 8),
                   sds(ROWS, 256), sds(GROUPS, 1, COLS), sds(GROUPS, 1, COLS)),
        scratch_shapes=[pltpu.VMEM((ROWS, ROWS), F32), pltpu.VMEM((ROWS, ROWS), F32),
                        pltpu.VMEM((ROWS, WIDTH), F32), pltpu.VMEM((ROWS, 128), F32)],
        compiler_params=params(),
        name="gate_backward_and_scan_backward",
    )(hid, square, inner, z, y, d, gain, w_all, x_conv, bc_conv, cum_col, step_col, cum_row, step_row, state, skip)


MESHID = pl.DeviceIdType.MESH
ORDERS = (("x", "y", "z"), ("y", "z", "x"), ("z", "x", "y"))
SUB = 32


def neighbour(axis, s):
    if axis == "core":
        return {"core": 1 - lax.axis_index("core")}
    if axis == "y":
        y = lax.rem(lax.axis_index("yhi") * 2 + lax.axis_index("ylo") + (s + 4), 4)
        return {"ylo": lax.rem(y, 2), "yhi": y // 2}
    return {axis: lax.rem(lax.axis_index(axis) + (s + 4), 4)}

def ag_kernel(w_ref, b_ref, g_ref, gb_ref, tss, trs, css, crs, bss, brs, lsem):
    me = dict(x=lax.axis_index("x"), z=lax.axis_index("z"), y=lax.axis_index("yhi")*2+lax.axis_index("ylo"))
    core = lax.axis_index("core")
    def at(item, r, pos, lo=0, n=SUB):
        z = slice(None) if pos["z"] is None else pos["z"]
        x = slice(None) if pos["x"] is None else pos["x"]
        if pos["y"] is None: yh=yl=slice(None)
        else: yh, yl = pos["y"]//2, lax.rem(pos["y"],2)
        return g_ref.at[item, z, yh, yl, x, core, pl.ds(r*SUB+lo, n)]
    def w(pos, a, d):
        p=dict(pos); p[a]=lax.rem(me[a]+(d+4),4); return p
    bar = pltpu.get_barrier_semaphore()
    for a in "xyz":
        for s in (1,-1):
            pl.semaphore_signal(bar, inc=1, device_id=neighbour(a,s), device_id_type=MESHID)
    pl.semaphore_signal(bar, inc=1, device_id=neighbour("core",1), device_id_type=MESHID)
    own = g_ref.at[:, me["z"], me["y"]//2, lax.rem(me["y"],2), me["x"], core]
    lc = pltpu.make_async_copy(w_ref, own, lsem.at[0]); lc.start()
    lb = pltpu.make_async_copy(b_ref, gb_ref.at[lax.rem(me["y"],2), me["x"], core], lsem.at[1]); lb.start()
    pl.semaphore_wait(bar, 7)
    pend=[]
    def rc(src, dst, ss, rs, dev):
        c=pltpu.make_async_remote_copy(src_ref=src, dst_ref=dst, send_sem=ss, recv_sem=rs, device_id=dev, device_id_type=MESHID)
        c.start(); pend.append(c); return c
    class Chunk:
        def __init__(s, item, r):
            s.item, s.r, s.order, s.k = item, r, ORDERS[r], item*3+r
            s.ncore=0; s.corer=[]
        def pos(s, st):
            p={}
            for i,a in enumerate(s.order): p[a]= None if i<st else me[a]
            return p
        def send(s, st):
            a=s.order[st]; p=s.pos(st); ref=at(s.item,s.r,p); t=s.k*12+st*4
            src = ref if st else w_ref.at[s.item, pl.ds(s.r*SUB,SUB)]
            s.c=[rc(src, ref, tss.at[t+i], trs.at[t+i], neighbour(a,d)) for i,d in enumerate((1,-1))]
            if st==0: s.core_fwd(ref, src)
        def core_fwd(s, ref, src=None):
            k=s.k*10+s.ncore; s.ncore+=1
            s.corer.append(rc(ref if src is None else src, ref, css.at[k], crs.at[k], neighbour("core",1)))
        def fwd(s, st):
            a=s.order[st]; p=s.pos(st); t=s.k*12+st*4+2
            s.f=[]
            for i,d in enumerate((1,-1)):
                s.c[i].wait_recv()
                ps=w(p,a,-d)
                h=at(s.item,s.r,ps,lo=16*i,n=16)
                s.f.append(rc(h,h,tss.at[t+i],trs.at[t+i],neighbour(a,d)))
                s.core_fwd(at(s.item,s.r,ps))
        def fin(s, st):
            for f in s.f: f.wait_recv()
            s.core_fwd(at(s.item,s.r,w(s.pos(st),s.order[st],2)))
    C=[[Chunk(i,r) for r in range(3)] for i in range(3)]
    for it in range(3):
        for c in C[it]: c.send(0)
    def gb(x, yl, lo=0, n=96): return gb_ref.at[yl, x, core, pl.ds(lo,n)]
    yl=lax.rem(me["y"],2); x=me["x"]
    bc=[rc(b_ref, gb(x,yl), bss.at[i], brs.at[i], neighbour("x",d)) for i,d in enumerate((1,-1))]
    bcore=[rc(b_ref, gb(x,yl), bss.at[2], brs.at[2], neighbour("core",1))]
    lc.wait(); lb.wait()
    for c in C[0]: c.fwd(0)
    bf=[]
    for i,d in enumerate((1,-1)):
        bc[i].wait_recv()
        h=gb(lax.rem(x-d+4,4),yl,48*i,48)
        bf.append(rc(h,h,bss.at[3+i],brs.at[3+i],neighbour("x",d)))
    for c in C[0]: c.fin(0); c.send(1)
    for f in bf: f.wait_recv()
    sl=gb_ref.at[yl,:,core]
    by=rc(sl,sl,bss.at[5],brs.at[5],{"ylo":1-yl})
    for dx in (1,2,3):
        h=gb(lax.rem(x+dx,4),yl)
        bcore.append(rc(h,h,bss.at[5+dx],brs.at[5+dx],neighbour("core",1)))
    for it in (1,2):
        for c in C[it]: c.fwd(0)
    for c in C[0]: c.fwd(1)
    for c in C[0]: c.fin(1); c.send(2)
    for it in (1,2):
        for c in C[it]: c.fin(0); c.send(1)
    by.wait_recv()
    sl=gb_ref.at[1-yl,:,core]
    bcore.append(rc(sl,sl,bss.at[9],brs.at[9],neighbour("core",1)))
    for c in C[1]: c.fwd(1)
    for c in C[1]: c.fin(1); c.send(2)
    for c in C[0]: c.fwd(2)
    for c in C[2]: c.fwd(1)
    for c in C[2]: c.fin(1); c.send(2)
    for c in C[0]: c.fin(2)
    for c in C[1]: c.fwd(2)
    for c in C[1]: c.fin(2)
    for c in C[2]: c.fwd(2)
    for c in C[2]: c.fin(2)
    for it in range(3):
        for c in C[it]:
            for q in c.corer: q.wait_recv()
    for q in bcore: q.wait_recv()
    for q in pend: q.wait_send()
def ag(w3, sb):
    A=pl.BlockSpec(memory_space=pl.ANY)
    D=pltpu.SemaphoreType.DMA
    return pl.pallas_call(ag_kernel,
        out_shape=(jax.ShapeDtypeStruct((3,4,2,2,4,2,96,384),jnp.bfloat16), jax.ShapeDtypeStruct((2,4,2,96,384),jnp.bfloat16)),
        in_specs=[A,A], out_specs=(A,A),
        scratch_shapes=[D((108,)),D((108,)),D((90,)),D((90,)),D((10,)),D((10,)),D((2,))],
        compiler_params=pltpu.CompilerParams(collective_id=0, has_side_effects=True))(w3,sb)


def my_place():
    return {"x": lax.axis_index("x"), "z": lax.axis_index("z"), "y": lax.axis_index("yhi") * 2 + lax.axis_index("ylo")}


def block_device(p):
    return {"z": p // 2, "yhi": lax.rem(p, 2)}


def f32(ref):
    return ref[...].astype(F32)


class Sender:
    def __init__(self):
        self.pending = {}

    def __call__(self, src, dst, send, recv, device):
        c = pltpu.make_async_remote_copy(src_ref=src, dst_ref=dst, send_sem=send, recv_sem=recv, device_id=device,
                                         device_id_type=MESHID)
        c.start()
        self.pending[id(c)] = c
        return c

    def sent(self, c):
        c.wait_send()
        del self.pending[id(c)]

    def all_sent(self):
        for c in self.pending.values():
            c.wait_send()


class Total:
    def __init__(self, rc, value, core, xs, yl, yh, zs, send, recv):
        self.rc, self.value, self.core, self.xs, self.yl, self.yh, self.zs = rc, value, core, xs, yl, yh, zs
        self.send, self.recv, self.at = send, recv, 0
        self.me = my_place()

    def push(self, dst, device):
        k = self.at
        self.at += 1
        return self.rc(self.value, dst, self.send.at[k], self.recv.at[k], device)

    def done(self):
        for c in self.flying:
            c.wait_recv()
        for c in self.flying:
            self.rc.sent(c)

    def step(self, j):
        v, me = self.value, self.me
        if j == 0:
            self.flying = [self.push(self.core, neighbour("core", 1))]
        elif j == 1:
            self.done()
            v[...] = v[...] + self.core[...]
            self.xs[me["x"]] = v[...]
            self.flying = [self.push(self.xs.at[me["x"]], neighbour("x", d)) for d in (1, 2, 3)]
        elif j == 2:
            self.done()
            v[...] = (self.xs[0] + self.xs[1]) + (self.xs[2] + self.xs[3])
            self.flying = [self.push(self.yl, {"ylo": 1 - lax.axis_index("ylo")})]
        elif j == 3:
            self.done()
            v[...] = v[...] + self.yl[...]
            self.flying = [self.push(self.yh, {"yhi": 1 - lax.axis_index("yhi")})]
        elif j == 4:
            self.done()
            v[...] = v[...] + self.yh[...]
            self.zs[me["z"]] = v[...]
            self.flying = [self.push(self.zs.at[me["z"]], neighbour("z", d)) for d in (1, 2, 3)]
        elif j == 5:
            self.done()
            v[...] = (self.zs[0] + self.zs[1]) + (self.zs[2] + self.zs[3])


class SmallSum:
    def __init__(self, rc, parts, sib, xs, ys, zs, hs, send, recv):
        self.rc, self.parts, self.sib, self.xs, self.ys, self.zs, self.hs = rc, parts, sib, xs, ys, zs, hs
        self.send, self.recv = send, recv
        self.me = my_place()

    def step(self, j, out=None):
        rc, me, parts, s, r = self.rc, self.me, self.parts, self.send, self.recv
        core, ylo = lax.axis_index("core"), lax.axis_index("ylo")
        if j == 0:
            self.c = [rc(parts.at[:, :, 1 - core], self.sib, s.at[0], r.at[0], neighbour("core", 1))]
        elif j == 1:
            self.c[0].wait_recv()

            def one(x):
                for yl in range(2):
                    m = parts.at[yl, x, core]
                    m[...] = (f32(m) + f32(self.sib.at[yl, x])).astype(BF16)

            pl.loop(0, 4)(one)
            self.c = [rc(parts.at[:, lax.rem(me["x"] + d, 4), core], self.xs.at[d - 1], s.at[d], r.at[d], neighbour("x", d))
                      for d in (1, 2, 3)]
        elif j == 2:
            for c in self.c:
                c.wait_recv()
            for yl in range(2):
                m = parts.at[yl, me["x"], core]
                m[...] = (f32(m) + f32(self.xs.at[0, yl]) + f32(self.xs.at[1, yl]) + f32(self.xs.at[2, yl])).astype(BF16)
            self.c = [rc(parts.at[1 - ylo, me["x"], core], self.ys, s.at[4], r.at[4], {"ylo": 1 - ylo})]
        elif j == 3:
            self.c[0].wait_recv()
            m = parts.at[ylo, me["x"], core]
            m[...] = (f32(m) + f32(self.ys)).astype(BF16)
            self.zs[me["z"]] = m[...]
            self.c = [rc(m, self.zs.at[me["z"]], s.at[4 + d], r.at[4 + d], neighbour("z", d)) for d in (1, 2, 3)]
        elif j == 4:
            for c in self.c:
                c.wait_recv()
            z, hs = self.zs, self.hs
            hs[0] = ((f32(z.at[0]) + f32(z.at[1])) + (f32(z.at[2]) + f32(z.at[3]))).astype(BF16)
            self.c = [rc(hs.at[0], hs.at[1], s.at[8], r.at[8], {"yhi": 1 - lax.axis_index("yhi")})]
        elif j == 5:
            self.c[0].wait_recv()
            out[...] = f32(self.hs.at[0]) + f32(self.hs.at[1])


SLOTS = 4
LAG = 2


def part_of(ref, item, pos, lo, n):
    z = slice(None) if pos["z"] is None else pos["z"]
    x = slice(None) if pos["x"] is None else pos["x"]
    if pos["y"] is None:
        yh = yl = slice(None)
    else:
        yh, yl = pos["y"] // 2, lax.rem(pos["y"], 2)
    return ref.at[item, z, yh, yl, x, pl.ds(lo, n)]


class Chunk:
    def __init__(self, rc, own, out, bufs, sems, item, slot, r):
        self.rc, self.own, self.out, self.item, self.slot, self.r = rc, own, out, item, slot, r
        full1, half1, full2, half2, full3, half3 = bufs
        self.bufs = [(full1[r].at[slot], half1[r].at[slot]), (full2[r].at[slot], half2[r].at[slot]),
                     (full3.at[slot * 3 + r], half3.at[slot * 3 + r])]
        self.send, self.recv = sems
        self.base = (slot * 3 + r) * 12
        self.me = my_place()
        self.sends = []

    def slab(self, st, d, lo=0, n=SUB):
        p = {a: (self.me[a] if i < st else None) for i, a in enumerate(ORDERS[self.r])}
        a = ORDERS[self.r][st]
        p[a] = lax.rem(self.me[a] + (d + 4), 4)
        return part_of(self.own, self.slot, p, self.r * SUB + lo, n)

    def loop(self, st, body):
        sizes = []
        for a, n in (("z", (4,)), ("y", (2, 2)), ("x", (4,))):
            if ORDERS[self.r].index(a) > st:
                sizes += n
        total = 1
        for n in sizes:
            total *= n

        def one(i):
            index = []
            for n in reversed(sizes):
                index.append(lax.rem(i, n))
                i = i // n
            body(tuple(reversed(index)))

        if total == 1:
            body(())
        else:
            pl.loop(0, total)(one)

    def push(self, st, k, src, dst, d):
        t = self.base + st * 4 + k
        c = self.rc(src, dst, self.send.at[t], self.recv.at[t], neighbour(ORDERS[self.r][st], d))
        self.sends.append(c)
        return c

    def far(self, st):
        half = self.bufs[st][1]
        self.far_c = [self.push(st, i, self.slab(st, 2, 16 * i, 16), half.at[i], d) for i, d in enumerate((1, -1))]

    def near(self, st):
        full, half = self.bufs[st]
        self.near_c = []
        for i, d in enumerate((1, -1)):
            self.far_c[i].wait_recv()
            mine = self.slab(st, d, 16 * i, 16)

            def add(index, mine=mine, i=i):
                m = mine.at[index] if index else mine
                m[...] = (f32(m) + f32(half.at[(i, *index)])).astype(BF16)

            self.loop(st, add)
            self.near_c.append(self.push(st, 2 + i, self.slab(st, d), full.at[i], d))

    def finish(self, st):
        full = self.bufs[st][0]
        for c in self.near_c:
            c.wait_recv()
        mine = self.slab(st, 0)
        if st < 2:
            def add(index):
                m = mine.at[index]
                m[...] = (f32(m) + f32(full.at[(0, *index)]) + f32(full.at[(1, *index)])).astype(BF16)

            self.loop(st, add)
            self.far(st + 1)
        else:
            self.out[self.item, pl.ds(self.r * SUB, SUB)] = f32(mine) + f32(full.at[0]) + f32(full.at[1])

    def step(self, j):
        if j == 0:
            self.far(0)
        elif j % 2:
            self.near(j // 2)
        else:
            self.finish(j // 2 - 1)


def backward_kernel(g_ref, x_conv_ref, d_x_ref, x_pre_ref, cum_ref, step_ref, d_cum_ref, d_step_ref,
                    w_small, n_t, c_t, hid, cot, out_in, d_z, d_local, state, dec, taps, d_bc_in, bc_pre, bc_conv, taps_bc,
                    shifted, a_log, gain, gain_part, skip_part,
                    out_ref, sout_ref, vout_ref, nout_ref, grad_hidden, *scr):
    (own, send, sib, rec_a, out_b, rec_b, dxp, tails, halo_src, halo_dst, acc, wbuf, bxc, bdx, bxp, bcum, bstep, bdc, bds,
     d_b, d_cum_all, d_step_all, parts, s_sib, s_xs, s_ys, s_zs, s_hs,
     v_core, v_xs, v_yl, v_yh, v_zs, n_core, n_xs, n_yl, n_yh, n_zs) = scr[:38]
    bufs = [scr[38:41], scr[41:44], scr[44:47], scr[47:50], scr[50], scr[51]]
    (t_s, t_r, c_s, c_r, e_s, e_r, b_s, b_r, h_s, h_r, ss, sr, vs, vr, ns, nr, wsem, lsem, credit, freed) = scr[52:]
    rc = Sender()
    core = lax.axis_index("core")
    block = lax.axis_index("z") * 2 + lax.axis_index("yhi")
    bar = pltpu.get_barrier_semaphore()
    for a in "xyz":
        for s in (1, 2, 3):
            pl.semaphore_signal(bar, inc=1, device_id=neighbour(a, s), device_id_type=MESHID)
    for d in (1, 2, 3):
        diagonal = {"z": lax.rem(lax.axis_index("z") + d, 4), "yhi": 1 - lax.axis_index("yhi")}
        pl.semaphore_signal(bar, inc=1, device_id=diagonal, device_id_type=MESHID)
    pl.semaphore_signal(bar, inc=1, device_id=neighbour("core", 1), device_id_type=MESHID)
    pl.semaphore_wait(bar, 13)

    to_owner = []
    for d in range(1, 8):
        p = lax.rem(block + d, 8)
        to_owner.append(rc(d_local.at[p], rec_a.at[block], e_s.at[d], e_r.at[d], block_device(p)))
    rec_a[block] = d_local[block]

    def core_copy(m):
        k = lax.rem(m, SLOTS)
        return pltpu.make_async_remote_copy(src_ref=send.at[k], dst_ref=sib.at[k], send_sem=c_s.at[k], recv_sem=c_r.at[k],
                                            device_id=neighbour("core", 1), device_id_type=MESHID)

    def gradient(lhs_t, rhs, slot, first_item):
        def one(m):
            @pl.when(m < GROUPS)
            def _():
                k = lax.rem(m, SLOTS)

                def wait_slot():
                    core_copy(m).wait_send()
                    pl.semaphore_wait(credit, 1)

                if first_item:
                    pl.when(m >= SLOTS)(wait_slot)
                else:
                    wait_slot()
                v = dot(lhs_t.at[:, 1 - core][...].reshape(768, ROWS), rhs[m])
                send[k] = v.astype(BF16).reshape(2, 4, 96, COLS)
                core_copy(m).start()

            @pl.when(m >= LAG)
            def _():
                q = m - LAG
                k = lax.rem(q, SLOTS)
                core_copy(q).wait_recv()
                v = dot(lhs_t.at[:, core][...].reshape(768, ROWS), rhs[q])
                own[slot, q // 2, lax.rem(q, 2)] = (v + sib[k].reshape(768, COLS).astype(F32)).astype(BF16).reshape(2, 4, 96, COLS)
                pl.semaphore_signal(credit, inc=1, device_id=neighbour("core", 1), device_id_type=MESHID)

        pl.loop(0, GROUPS + LAG)(one)

    def chunks(item, slot):
        return [Chunk(rc, own, out_ref, bufs, (t_s, t_r), item, slot, r) for r in range(3)]

    def steps(cs, j):
        for c in cs:
            c.step(j)

    oc, zc, xc_ = chunks(2, 0), chunks(1, 1), chunks(0, 0)

    gradient(c_t, out_in, 0, True)
    steps(oc, 0)

    for c in to_owner:
        c.wait_recv()
    for h in range(HEADS):
        rows = pl.ds(64 * h, 64)
        run = jnp.zeros((64, 128), F32)
        for i in range(BLOCKS - 1, -1, -1):
            out_b[i, rows] = run.astype(BF16)
            run = run * dec[i, pl.ds(h, 1)] + rec_a[i, rows].astype(F32)
    back = []
    for d in range(1, 8):
        p = lax.rem(block + d, 8)
        back.append(rc(out_b.at[p], rec_b.at[block], b_s.at[d], b_r.at[d], block_device(p)))
    rec_b[block] = out_b[block]

    gradient(n_t, d_z, 1, False)
    steps(oc, 1)
    steps(zc, 0)
    steps(oc, 2)
    for c in back:
        c.wait_recv()

    streams = ((x_conv_ref, bxc), (d_x_ref, bdx), (x_pre_ref, bxp), (cum_ref, bcum), (step_ref, bstep), (d_cum_ref, bdc),
               (d_step_ref, bds))

    def load(m):
        k = lax.rem(m, 2)
        return [pltpu.make_async_copy(src.at[m], dst.at[k], lsem.at[k, i]) for i, (src, dst) in enumerate(streams)]

    def fifth_group(m):
        k = lax.rem(m, 2)

        @pl.when(m < GROUPS - 1)
        def _():
            for c in load(m + 1):
                c.start()

        for c in load(m):
            c.wait()
        ds = rec_b[m]
        xf = bxc[k].astype(F32)
        cum = bcum[k]
        last = cum[ROWS - 1 : ROWS]
        tail = jnp.exp(last - cum)
        weights = bstep[k] * tail
        wide = spread(weights)
        d_weighted = dot(bc_conv[:, :128], ds, (1, 1))
        d_b[...] += dot((xf * wide).astype(BF16), ds)
        dx = bdx[k] + wide * d_weighted
        d_weights = gathered_heads(d_weighted * xf)
        both = weights * d_weights
        lane = lax.broadcasted_iota(jnp.int32, (1, 8), 1)
        product = jnp.sum(state[m].astype(F32) * ds.astype(F32), axis=1, keepdims=True)
        d_last = jnp.sum(both, axis=0, keepdims=True)
        for h in range(HEADS):
            dots = jnp.sum(product[64 * h : 64 * h + 64], axis=0, keepdims=True)
            d_last = jnp.where(lane == h, d_last + jnp.exp(last) * dots, d_last)
        row = lax.broadcasted_iota(jnp.int32, (ROWS, 8), 0)
        d_cum = bdc[k] - both
        d_cum_all[m] = jnp.where(row == ROWS - 1, d_cum + d_last, d_cum)
        d_step_all[m] = bds[k] + tail * d_weights
        ext = bxp[k]
        tap = taps[m]
        pre = conv_pre(ext, tap)
        sig = jax.nn.sigmoid(pre)
        dp = dx * (sig * (1.0 + pre * (1.0 - sig)))
        v_value[m] = conv_grads(dp, ext, gain_part[m], skip_part[m])
        whole_dx = conv_transposed(jnp.concatenate([dp, jnp.zeros((8, COLS), F32)], axis=0), tap)
        dxp[m] = whole_dx.astype(BF16)
        tails[m] = whole_dx[ROWS - 16 :]
        halo_src[m] = dp[:8]

    v_value = vout_ref
    d_b[...] = jnp.zeros_like(d_b)
    for c in load(0):
        c.start()
    pl.loop(0, 4)(fifth_group)
    steps(zc, 1)
    steps(oc, 3)
    pl.loop(4, GROUPS)(fifth_group)

    d_bc = jnp.concatenate([d_bc_in[:, :128] + d_b[...], d_bc_in[:, 128:]], axis=1)
    ext = bc_pre[...]
    pre = conv_pre(ext, taps_bc[...])
    sig = jax.nn.sigmoid(pre)
    dp_bc = d_bc * (sig * (1.0 + pre * (1.0 - sig)))
    halo_src[GROUPS] = jnp.concatenate([dp_bc[:8], jnp.zeros((8, 128), F32)], axis=1)
    before = lax.rem(block + 7, 8)
    halo = rc(halo_src, halo_dst, h_s, h_r, block_device(before))
    steps(oc, 4)
    steps(zc, 2)
    zero8 = jnp.zeros((1, 256), F32)
    d_cum = jnp.concatenate([d_cum_all[m][:, :HEADS] for m in range(GROUPS)] + [jnp.zeros((ROWS, 80), F32)], axis=1)
    d_step = jnp.concatenate([d_step_all[m][:, :HEADS] for m in range(GROUPS)] + [jnp.zeros((ROWS, 80), F32)], axis=1)
    d_decay = dot(triangle(True).astype(F32), d_cum, precision=lax.Precision.HIGHEST)
    rate = -jnp.exp(a_log[...])
    v = shifted[...]
    d_dt = (d_step + rate * d_decay) * jax.nn.sigmoid(v)
    log_grad = jnp.sum(d_decay * (softplus(v) * rate), axis=0, keepdims=True)
    shift_grad = jnp.sum(d_dt, axis=0, keepdims=True)
    bc_rows = conv_grads(dp_bc, ext, jnp.concatenate([log_grad, shift_grad], axis=1), zero8)
    v_value[GROUPS] = jnp.concatenate([bc_rows, jnp.zeros((8, 128), F32)], axis=1)
    vec = Total(rc, v_value, v_core, v_xs, v_yl, v_yh, v_zs, vs, vr)
    vec.step(0)

    halo.wait_recv()
    inside = block < 7

    def below(k):
        return jnp.where(inside, halo_dst[k], 0.0)

    def fix(m):
        ext = jnp.concatenate([jnp.zeros((16, COLS), F32), below(m)], axis=0)
        dxp[m, pl.ds(ROWS - 16, 16)] = (tails[m] + conv_transposed(ext, taps[m], 16)).astype(BF16)

    pl.loop(0, GROUPS)(fix)
    d_bc = conv_transposed(jnp.concatenate([dp_bc, below(GROUPS)[:, :256]], axis=0), taps_bc[...])
    small = jnp.concatenate([d_bc, d_dt], axis=1).astype(BF16)
    steps(oc, 5)
    steps(oc, 6)
    for c in [c for k in oc for c in k.sends]:
        rc.sent(c)
    for a in "xyz":
        for s in (1, -1):
            pl.semaphore_signal(freed, inc=1, device_id=neighbour(a, s), device_id_type=MESHID)
    vec.step(1)

    def weights(m):
        k = lax.rem(m, 2)
        return [pltpu.make_async_copy(g_ref.at[i, m], wbuf.at[k, i], wsem.at[k, i]) for i in range(2)]

    for c in weights(0):
        c.start()
    gradient(n_t, dxp, 0, False)
    pl.semaphore_wait(freed, 6)
    steps(xc_, 0)
    steps(zc, 3)
    vec.step(2)
    for i in range(2):
        lhs = n_t.at[:, i][...].reshape(768, ROWS)
        parts[:, :, i] = dot(lhs, small).astype(BF16).reshape(2, 4, 96, COLS)
    sums = SmallSum(rc, parts, s_sib, s_xs, s_ys, s_zs, s_hs, ss, sr)
    sums.step(0)
    steps(zc, 4)
    acc[...] = dot(small, w_small[...], (1, 1))
    steps(xc_, 1)

    def input_group(m):
        k = lax.rem(m, 2)

        @pl.when(m < GROUPS - 1)
        def _():
            for c in weights(m + 1):
                c.start()

        for c in weights(m):
            c.wait()
        lhs = jnp.concatenate([dxp[m], d_z[m]], axis=1)
        rhs = jnp.concatenate([wbuf[k, 0], wbuf[k, 1]], axis=1)
        acc[...] += dot(lhs, rhs, (1, 1))

    pl.loop(0, 3)(input_group)
    steps(zc, 5)
    sums.step(1)
    vec.step(3)
    pl.loop(3, 6)(input_group)
    steps(xc_, 2)
    sums.step(2)
    vec.step(4)
    steps(zc, 6)
    pl.loop(6, GROUPS)(input_group)
    steps(xc_, 3)
    v = hid[...].astype(F32)
    r = lax.rsqrt(jnp.mean(v * v, axis=1, keepdims=True) + EPS)
    unit = v * r
    dn = acc[...]
    gain_grad = jnp.sum(dn * unit, axis=0, keepdims=True)
    for i in range(4):
        nout_ref[0, pl.ds(i, 1)] = gain_grad[:, COLS * i : COLS * i + COLS]
    nout_ref[0, pl.ds(4, 4)] = jnp.zeros((4, COLS), F32)
    nvec = Total(rc, nout_ref, n_core, n_xs, n_yl, n_yh, n_zs, ns, nr)
    nvec.step(0)
    sums.step(3)
    d_in = dn * gain[...]
    grad_hidden[...] = r * (d_in - unit * jnp.mean(d_in * unit, axis=1, keepdims=True)) + cot[...].astype(F32)
    vec.step(5)
    steps(xc_, 4)
    nvec.step(1)
    sums.step(4)
    steps(xc_, 5)
    nvec.step(2)
    sums.step(5, sout_ref)
    steps(xc_, 6)
    for j in (3, 4, 5):
        nvec.step(j)
    for k in range(SLOTS):
        core_copy(GROUPS - SLOTS + k).wait_send()
    pl.semaphore_wait(credit, SLOTS)
    rc.all_sent()


def backward(w_all, x_conv, d_x, x_pre, cum_col, step_col, d_cum, d_step, w_small, n_t, c_t, hid, cot, out_in, d_z, d_local,
             state, dec, taps, d_bc, bc_pre, bc_conv, taps_bc, shifted, a_log, gain, gain_part, skip_part):
    hbm = pl.BlockSpec(memory_space=pl.ANY)
    vmem = pl.BlockSpec(memory_space=pltpu.VMEM)
    sem = pltpu.SemaphoreType.DMA

    def buf(*shape, dtype=BF16):
        return pltpu.VMEM((*shape, COLS), dtype)

    def v(*shape, dtype=F32):
        return pltpu.VMEM(shape, dtype)

    scratch = [
        buf(2, 4, 2, 2, 4, 96), buf(SLOTS, 2, 4, 96), buf(SLOTS, 2, 4, 96),
        v(GROUPS, COLS, 128, dtype=BF16), v(GROUPS, COLS, 128, dtype=BF16), v(GROUPS, COLS, 128, dtype=BF16),
        buf(GROUPS, ROWS), buf(GROUPS, 16, dtype=F32), buf(GROUPS + 1, 8, dtype=F32), buf(GROUPS + 1, 8, dtype=F32),
        v(ROWS, WIDTH), buf(2, 2, WIDTH),
        buf(2, ROWS), buf(2, ROWS, dtype=F32), buf(2, HALO + ROWS, dtype=F32),
        v(2, ROWS, 8), v(2, ROWS, 8), v(2, ROWS, 8), v(2, ROWS, 8),
        v(ROWS, 128), v(GROUPS, ROWS, 8), v(GROUPS, ROWS, 8),
        buf(2, 4, 2, 96), buf(2, 4, 96), buf(3, 2, 96), buf(96), buf(4, 96), buf(2, 96),
    ]
    for n in (GROUPS + 1, 1):
        one = buf(n, 8, dtype=F32)
        four = buf(4, n, 8, dtype=F32)
        scratch += [one, four, one, one, four]
    scratch += [buf(2, 2, 4, 2, 2, SUB), buf(2, 2, 4, 4, SUB), buf(2, 2, 2, 2, 4, SUB)]
    scratch += [buf(2, 2, 4, 2, 2, 16), buf(2, 2, 4, 4, 16), buf(2, 2, 2, 2, 4, 16)]
    scratch += [buf(2, 2, 4, SUB), buf(2, 2, 4, SUB), buf(2, 2, 2, 2, SUB)]
    scratch += [buf(2, 2, 4, 16), buf(2, 2, 4, 16), buf(2, 2, 2, 2, 16)]
    scratch += [buf(6, 2, SUB), buf(6, 2, 16)]
    scratch += [sem((72,)), sem((72,)), sem((SLOTS,)), sem((SLOTS,)), sem((8,)), sem((8,)), sem((8,)), sem((8,)),
                sem, sem, sem((9,)), sem((9,)), sem((9,)), sem((9,)), sem((9,)), sem((9,)), sem((2, 2)), sem((2, 7)),
                pltpu.SemaphoreType.REGULAR, pltpu.SemaphoreType.REGULAR]
    return pl.pallas_call(
        backward_kernel,
        out_shape=(sds(3, 96, COLS), sds(96, COLS), sds(GROUPS + 1, 8, COLS), sds(1, 8, COLS), sds(ROWS, WIDTH)),
        in_specs=[hbm] * 8 + [vmem] * 20,
        out_specs=(vmem,) * 5,
        scratch_shapes=scratch,
        compiler_params=pltpu.CompilerParams(collective_id=1, has_side_effects=True, vmem_limit_bytes=62 * 2**20),
        name="backward_between_devices",
    )(w_all, x_conv, d_x, x_pre, cum_col, step_col, d_cum, d_step, w_small, n_t, c_t, hid, cot, out_in, d_z, d_local,
      state, dec, taps, d_bc, bc_pre, bc_conv, taps_bc, shifted, a_log, gain, gain_part, skip_part)
def to_everyone(array):
    copies = jnp.broadcast_to(array, (BLOCKS, *array.shape))
    return lax.all_to_all(copies, MP, split_axis=0, concat_axis=0, tiled=True)


def swapped(array):
    return lax.all_to_all(array, MP, split_axis=0, concat_axis=0, tiled=True)


def carried_states(local, decays, backward):
    blocks = swapped(local).astype(F32)
    state = jnp.zeros(blocks.shape[1:], F32)
    out = [None] * BLOCKS
    for i in range(BLOCKS - 1, -1, -1) if backward else range(BLOCKS):
        out[i] = state.astype(BF16)
        state = state * jnp.repeat(decays[i], 64)[:, None] + blocks[i]
    return swapped(jnp.stack(out))


def shards(hidden, grad_out, norm_gain, w_zx, w_bc, w_dt, conv_x, conv_bc, a_log, dt_bias, d_skip, gate_gain, w_out):
    index = lax.axis_index(MP)
    down = [(i, i + 1) for i in range(BLOCKS - 1)]
    up = [(i + 1, i) for i in range(BLOCKS - 1)]

    halo = lax.ppermute(hidden[-HALO:], MP, down)
    heads = jnp.concatenate([a_log, dt_bias, d_skip, jnp.zeros((COLS - 3 * HEADS,), F32)])[None]
    packed = jnp.concatenate([conv_x, gate_gain[None], heads, jnp.pad(w_dt.astype(F32).reshape(-1), (0, 192)).reshape(2, COLS),
                              jnp.zeros((7, COLS), F32)])
    everyone = to_everyone(packed)
    taps = jnp.pad(everyone[:, :5], ((0, 0), (0, 3), (0, 0)))
    gate = everyone[:, 5:6]
    per_head = [everyone[:, 6, HEADS * i : HEADS * i + HEADS].reshape(1, -1) for i in range(3)]
    log_rate, shift, skip = per_head
    pad = ((0, 0), (0, 128 - BLOCKS * HEADS))
    log_rate, shift = jnp.pad(log_rate, pad), jnp.pad(shift, pad)
    skip = jnp.repeat(skip, 64, axis=1).reshape(GROUPS, 1, COLS)
    w_steps = jnp.moveaxis(everyone[:, 7:9].reshape(BLOCKS, 768)[:, :576].reshape(BLOCKS, 96, HEADS), 0, 1).reshape(96, BLOCKS * HEADS).astype(BF16)
    w_small_own = jnp.concatenate([w_bc, w_steps, jnp.zeros((96, 80), BF16)], axis=1)
    taps_bc = jnp.pad(conv_bc, ((0, 3), (0, 0)))
    gain = norm_gain[None]

    w_all, w_small = ag(jnp.stack([w_zx[:, 1], w_zx[:, 0], w_out.T]), w_small_own)
    w_all = w_all.reshape(3, GROUPS, WIDTH, COLS)
    w_small = w_small.reshape(WIDTH, 384)

    normed, normed_t, cot_t, bc_pre, bc_conv, shifted, cum_col, step_col, cum_row, step_row = first(
        hidden, halo, grad_out, gain, w_small, taps_bc, log_rate, shift)
    x_pre, x_conv, local = second(normed, w_all, taps, bc_conv, cum_col, step_col)
    decays = jnp.exp(swapped(cum_col[:, ROWS - 1, :]))
    state = carried_states(local, decays[:, :HEADS], False)
    z, y, d, square, inner = third(normed, grad_out, w_all, x_conv, bc_conv, cum_col, cum_row, step_row, state, skip, gate)
    result, out_in, d_z, d_x, d_local, d_cum, d_step, d_bc, gain_part, skip_part = fourth(
        hidden, square, inner, z, y, d, gate, w_all, x_conv, bc_conv, cum_col, step_col, cum_row, step_row, state, skip)
    owned, small, vector, norm_sum, grad_hidden = backward(
        w_all, x_conv, d_x, x_pre, cum_col, step_col, d_cum, d_step, w_small, normed_t, cot_t, hidden, grad_out, out_in, d_z,
        d_local, state, jnp.broadcast_to(decays[:, :, None], (BLOCKS, 8, 128)), taps, d_bc, bc_pre, bc_conv, taps_bc, shifted,
        log_rate, gain, gain_part, skip_part)

    def own(flat):
        return lax.dynamic_slice_in_dim(flat, index * HEADS, HEADS, flat.ndim - 1)

    mine = lax.dynamic_index_in_dim(vector, index, 0, keepdims=False)
    return (
        result,
        grad_hidden,
        norm_sum[0, :4].reshape(WIDTH),
        jnp.stack([owned[1], owned[0]], axis=1),
        small[:, :256],
        own(small[:, 256:304]),
        mine[:5],
        vector[GROUPS, :5, :256],
        own(vector[GROUPS, 5, :48]),
        own(vector[GROUPS, 5, 128:176]),
        mine[6].reshape(HEADS, 64).sum(axis=1),
        mine[5],
        owned[2].T,
    )


def solution(mesh):
    finer = Mesh(mesh.devices.reshape(2, 4, 2, 4, 2), DP_MP)
    rows = P(DP_MP, None)
    placed = (rows, rows, P(), P(DP, None, MP), P(DP, None), P(DP, MP), P(None, MP), P(), P(MP), P(MP), P(MP), P(MP),
              P(MP, DP))
    return jax.shard_map(
        shards,
        mesh=finer,
        in_specs=placed,
        out_specs=(rows, rows, P(), P(DP, None, MP), P(DP, None), P(DP, MP), P(None, MP), P(), P(MP), P(MP), P(MP), P(MP),
                   P(MP, DP)),
        check_vma=False,
    )
```

```python
import jax
import jax.numpy as jnp
from jax import lax
from jax.experimental import pallas as pl
from jax.experimental.pallas import tpu as pltpu
from jax.sharding import Mesh
from jax.sharding import PartitionSpec as P

MP = ("z", "yhi")
DP = ("ylo", "x", "core")
DP_MP = DP + MP
BLOCKS = 8
F32 = jnp.float32
BF16 = jnp.bfloat16
ROWS = 256
WIDTH = 1536
GROUPS = 8
COLS = 384
HEADS = 6
HALO = 16
EPS = 1e-05
INNER = GROUPS * COLS
VMEM_LIMIT = 56 * 2**20


def dot(a, b, contract=(1, 0), precision=None):
    return lax.dot_general(
        a, b, (((contract[0],), (contract[1],)), ((), ())),
        preferred_element_type=F32, precision=precision,
    )


def spread(per_head):
    rows = per_head.shape[0]
    low = lax.broadcasted_iota(jnp.int32, (rows, 128), 1) < 64
    tiles = [
        jnp.where(low, per_head[:, 2 * i : 2 * i + 1], per_head[:, 2 * i + 1 : 2 * i + 2])
        for i in range(COLS // 128)
    ]
    return jnp.concatenate(tiles, axis=1)


def gathered_heads(values):
    rows = values.shape[0]
    low = lax.broadcasted_iota(jnp.int32, (rows, 128), 1) < 64
    lane = lax.broadcasted_iota(jnp.int32, (rows, 8), 1)
    out = jnp.zeros((rows, 8), F32)
    for i in range(COLS // 128):
        tile = values[:, 128 * i : 128 * i + 128]
        first = jnp.sum(jnp.where(low, tile, 0.0), axis=1, keepdims=True)
        both = jnp.sum(tile, axis=1, keepdims=True)
        out = jnp.where(lane == 2 * i, first, out)
        out = jnp.where(lane == 2 * i + 1, both - first, out)
    return out


def softplus(v):
    return jnp.maximum(v, 0.0) + jnp.log1p(jnp.exp(-jnp.abs(v)))


def conv_pre(ext, taps):
    total = taps[4:5]
    for j in range(4):
        total = total + ext[HALO - 3 + j : HALO - 3 + j + ROWS] * taps[j : j + 1]
    return total


def conv_transposed(ext, taps, rows=ROWS):
    total = ext[3 : 3 + rows] * taps[0:1]
    for j in range(1, 4):
        total = total + ext[3 - j : 3 - j + rows] * taps[j : j + 1]
    return total


def conv_grads(dpre, ext, sixth, seventh):
    rows = [
        jnp.sum(dpre * ext[HALO - 3 + j : HALO - 3 + j + ROWS], axis=0, keepdims=True)
        for j in range(4)
    ]
    rows.append(jnp.sum(dpre, axis=0, keepdims=True))
    rows += [sixth, seventh, jnp.zeros((1, dpre.shape[1]), F32)]
    return jnp.concatenate(rows, axis=0)


def triangle(upper):
    row = lax.broadcasted_iota(jnp.int32, (ROWS, ROWS), 0)
    col = lax.broadcasted_iota(jnp.int32, (ROWS, ROWS), 1)
    return row <= col if upper else row >= col


def sds(*shape, dtype=F32):
    return jax.ShapeDtypeStruct(shape, dtype)


def params():
    return pltpu.CompilerParams(vmem_limit_bytes=VMEM_LIMIT)


def whole(*shape):
    return pl.BlockSpec(shape, lambda m: (0,) * len(shape))


def lead(*shape):
    return pl.BlockSpec((None, *shape), lambda m: (m,) + (0,) * len(shape))


def weight(item):
    return pl.BlockSpec((None, None, WIDTH, COLS), lambda m: (item, m, 0, 0))


def fourth_kernel(hid, square, inner, z_in, y_in, d_in, taps, w_o, x_conv, bc_conv, cols, cum_row, step_row,
                  state,
                  result, out_in, d_z, d_x, d_state, d_cols, d_bc, gain_part, skip_part,
                  gram, d_gram, acc, d_c):
    step_id = pl.program_id(0)

    @pl.when(step_id == 0)
    def _():
        g = dot(bc_conv[:, 128:], bc_conv[:, :128], (1, 1))
        gram[...] = jnp.where(triangle(False), g, 0.0)
        d_gram[...] = jnp.zeros_like(d_gram)
        acc[...] = jnp.zeros_like(acc)
        d_c[...] = jnp.zeros_like(d_c)

    z = z_in[...]
    y = y_in[...]
    d = d_in[...]
    gain = taps[5:6]
    skip = spread(taps[6:7, 12:20])
    sig = jax.nn.sigmoid(z)
    act = z * sig
    gated = y * act
    r2 = lax.rsqrt(jnp.sum(square[...], axis=1, keepdims=True) / INNER + EPS)
    total = jnp.sum(inner[...], axis=1, keepdims=True)
    unit = gated * r2
    o = (unit * gain).astype(BF16)
    out_in[...] = o
    acc[...] += dot(o, w_o[...], (1, 1))
    gain_part[...] = jnp.sum(d * unit, axis=0, keepdims=True)
    d_gated = r2 * (d * gain) - gated * (r2 * r2 * r2 * (total / INNER))
    dy = d_gated * act
    d_z[...] = (d_gated * y * sig * (1.0 + z * (1.0 - sig))).astype(BF16)

    xc = x_conv[...]
    xf = xc.astype(F32)
    cum, step = cols[:, :8], cols[:, 8:]
    dyb = dy.astype(BF16)
    c_mat = bc_conv[:, 128:]
    skip_part[...] = jnp.sum(dy * xf, axis=0, keepdims=True)
    grown = spread(jnp.exp(cum))
    dye = (grown * dy).astype(BF16)
    d_c[...] += dot(dye, state[...])
    d_state[...] = dot(dye, c_mat, (0, 0)).astype(BF16)
    carried = grown * dot(c_mat, state[...], (1, 1))
    d_cum_col = gathered_heads(dy * carried)
    lane = lax.broadcasted_iota(jnp.int32, (ROWS, 8), 1)
    parts = []
    sums = []
    for h in range(HEADS):
        xh = xc[:, 64 * h : 64 * h + 64]
        dyh = dyb[:, 64 * h : 64 * h + 64]
        decay = jnp.exp(jnp.minimum(cum[:, h : h + 1] - cum_row[h : h + 1, :], 0.0))
        d_mix = dot(dyh, xh, (1, 1))
        grown_row = step_row[h : h + 1, :]
        plain = decay * gram[...]
        r = plain * d_mix
        sums.append(jnp.sum(r, axis=0, keepdims=True))
        row = jnp.sum(r * grown_row, axis=1, keepdims=True)
        d_cum_col = jnp.where(lane == h, d_cum_col + row, d_cum_col)
        d_gram[...] += decay * d_mix * grown_row
        parts.append(dot((plain * grown_row).astype(BF16), dyh, (0, 0)))
    sums.append(jnp.zeros((2, ROWS), F32))
    sums = jnp.concatenate(sums, axis=0).T
    d_x[...] = jnp.concatenate(parts, axis=1) + skip * dy
    d_cols[...] = jnp.concatenate([d_cum_col - sums * step, sums], axis=1)

    @pl.when(step_id == GROUPS - 1)
    def _():
        result[...] = (hid[...].astype(F32) + acc[...]).astype(BF16)
        dg = jnp.where(triangle(False), d_gram[...], 0.0).astype(BF16)
        d_bc[:, :128] = dot(dg, c_mat, (0, 0))
        d_bc[:, 128:] = d_c[...] + dot(dg, bc_conv[:, :128])


def fourth(hid, square, inner, z, y, d, taps, w_all, x_conv, bc_conv, cols, cum_row, step_row, state):
    return pl.pallas_call(
        fourth_kernel,
        grid=(GROUPS,),
        in_specs=[whole(ROWS, WIDTH), whole(ROWS, 128), whole(ROWS, 128), lead(ROWS, COLS), lead(ROWS, COLS), lead(ROWS, COLS),
                  lead(8, COLS), weight(2), lead(ROWS, COLS), whole(ROWS, 256), lead(ROWS, 16), lead(8, ROWS),
                  lead(8, ROWS), lead(COLS, 128)],
        out_specs=(whole(ROWS, WIDTH), lead(ROWS, COLS), lead(ROWS, COLS), lead(ROWS, COLS), lead(COLS, 128), lead(ROWS, 16),
                   whole(ROWS, 256), lead(1, COLS), lead(1, COLS)),
        out_shape=(sds(ROWS, WIDTH, dtype=BF16), sds(GROUPS, ROWS, COLS, dtype=BF16), sds(GROUPS, ROWS, COLS, dtype=BF16),
                   sds(GROUPS, ROWS, COLS), sds(GROUPS, COLS, 128, dtype=BF16), sds(GROUPS, ROWS, 16),
                   sds(ROWS, 256), sds(GROUPS, 1, COLS), sds(GROUPS, 1, COLS)),
        scratch_shapes=[pltpu.VMEM((ROWS, ROWS), F32), pltpu.VMEM((ROWS, ROWS), F32),
                        pltpu.VMEM((ROWS, WIDTH), F32), pltpu.VMEM((ROWS, 128), F32)],
        compiler_params=params(),
        name="gate_backward_and_scan_backward",
    )(hid, square, inner, z, y, d, taps, w_all, x_conv, bc_conv, cols, cum_row, step_row, state)


MESHID = pl.DeviceIdType.MESH
ORDERS = (("x", "y", "z"), ("y", "z", "x"), ("z", "x", "y"))
SUB = 32


def neighbour(axis, s):
    if axis == "core":
        return {"core": 1 - lax.axis_index("core")}
    if axis == "y":
        y = lax.rem(lax.axis_index("yhi") * 2 + lax.axis_index("ylo") + (s + 4), 4)
        return {"ylo": lax.rem(y, 2), "yhi": y // 2}
    return {axis: lax.rem(lax.axis_index(axis) + (s + 4), 4)}


def my_place():
    return {"x": lax.axis_index("x"), "z": lax.axis_index("z"), "y": lax.axis_index("yhi") * 2 + lax.axis_index("ylo")}


def block_device(p):
    return {"z": p // 2, "yhi": lax.rem(p, 2)}


def f32(ref):
    return ref[...].astype(F32)


class Sender:
    def __init__(self):
        self.pending = {}

    def __call__(self, src, dst, send, recv, device):
        c = pltpu.make_async_remote_copy(src_ref=src, dst_ref=dst, send_sem=send, recv_sem=recv, device_id=device,
                                         device_id_type=MESHID)
        c.start()
        self.pending[id(c)] = c
        return c

    def sent(self, c):
        c.wait_send()
        del self.pending[id(c)]

    def all_sent(self):
        for c in self.pending.values():
            c.wait_send()


def greet():
    bar = pltpu.get_barrier_semaphore()
    for a in "xyz":
        for s in (1, 2, 3):
            pl.semaphore_signal(bar, inc=1, device_id=neighbour(a, s), device_id_type=MESHID)
    for d in (1, 2, 3):
        diagonal = {"z": lax.rem(lax.axis_index("z") + d, 4), "yhi": 1 - lax.axis_index("yhi")}
        pl.semaphore_signal(bar, inc=1, device_id=diagonal, device_id_type=MESHID)
    pl.semaphore_signal(bar, inc=1, device_id=neighbour("core", 1), device_id_type=MESHID)
    return lambda: pl.semaphore_wait(bar, 13)


def to_peers(rc, src_of, dst, send, recv, block):
    out = []
    for d in range(1, 8):
        p = lax.rem(block + d, 8)
        out.append(rc(src_of(p), dst.at[block], send.at[d], recv.at[d], block_device(p)))
    return out


class Gather:
    def __init__(self, rc, g, w, sems, item, r):
        self.rc, self.g, self.w, self.item, self.r = rc, g, w, item, r
        self.ts, self.tr, self.cs, self.cr = sems
        self.k = item * 3 + r
        self.me = my_place()
        self.core = lax.axis_index("core")
        self.forwarded = []

    def at(self, pos, lo=0, n=SUB):
        z = slice(None) if pos["z"] is None else pos["z"]
        x = slice(None) if pos["x"] is None else pos["x"]
        if pos["y"] is None:
            yh = yl = slice(None)
        else:
            yh, yl = pos["y"] // 2, lax.rem(pos["y"], 2)
        return self.g.at[self.item, z, yh, yl, x, self.core, pl.ds(self.r * SUB + lo, n)]

    def pos(self, st, d=0):
        p = {a: (None if i < st else self.me[a]) for i, a in enumerate(ORDERS[self.r])}
        a = ORDERS[self.r][st]
        p[a] = lax.rem(self.me[a] + (d + 4), 4)
        return p

    def to_sibling(self, ref, src=None):
        k = self.k * 10 + len(self.forwarded)
        self.forwarded.append(self.rc(ref if src is None else src, ref, self.cs.at[k], self.cr.at[k], neighbour("core", 1)))

    def send(self, st):
        a, t = ORDERS[self.r][st], self.k * 12 + st * 4
        ref = self.at(self.pos(st))
        src = ref if st else self.w.at[self.item, pl.ds(self.r * SUB, SUB)]
        self.c = [self.rc(src, ref, self.ts.at[t + i], self.tr.at[t + i], neighbour(a, d)) for i, d in enumerate((1, -1))]
        if st == 0:
            self.to_sibling(ref, src)

    def pass_on(self, st):
        a, t = ORDERS[self.r][st], self.k * 12 + st * 4 + 2
        self.f = []
        for i, d in enumerate((1, -1)):
            self.c[i].wait_recv()
            p = self.pos(st, -d)
            half = self.at(p, 16 * i, 16)
            self.f.append(self.rc(half, half, self.ts.at[t + i], self.tr.at[t + i], neighbour(a, d)))
            self.to_sibling(self.at(p))

    def last(self, st):
        for f in self.f:
            f.wait_recv()
        self.to_sibling(self.at(self.pos(st, 2)))

    def complete(self):
        for c in self.forwarded:
            c.wait_recv()


def forward_kernel(w_ref, bc_ref, dt_ref, pk_ref, hid, cot, gain, taps_bc,
                   g_ref, gb_ref, x_pre_out, x_conv_out, z_out, y_out, d_out,
                   normed_t, cot_t, pk, bc_pre, bc_conv, steps, cols, cum_row, step_row, state, dec, rates, square,
                   inner,
                   normed, halo, dts, small_own, small_all, x_pre, x_conv, zb, yb, db, wbuf, gram, local, rec_a, out_b, dec_own,
                   ts, tr, cs, cr, bs, br, ps, pr, qs, qr, es, er, fs, fr, ds, dr, hs, hr, lsem, wsem, osem):
    rc = Sender()
    me = my_place()
    core = lax.axis_index("core")
    x, ylo = me["x"], lax.axis_index("ylo")
    block = lax.axis_index("z") * 2 + lax.axis_index("yhi")
    arrived = greet()
    own_w = pltpu.make_async_copy(w_ref, g_ref.at[:, me["z"], me["y"] // 2, ylo, x, core], lsem.at[0])
    own_w.start()
    arrived()

    gx, gz, go = [[Gather(rc, g_ref, w_ref, (ts, tr, cs, cr), i, r) for r in range(3)] for i in range(3)]

    def each(group, name, *args):
        for c in group:
            getattr(c, name)(*args)

    each(gx, "send", 0)
    dt_c = to_peers(rc, lambda p: dt_ref, dts, ps, pr, block)
    pk_c = to_peers(rc, lambda p: pk_ref, pk, qs, qr, block)
    halo_c = rc(hid.at[pl.ds(ROWS - HALO, HALO)], halo, hs, hr, block_device(lax.rem(block + 1, 8)))
    each(gz, "send", 0)
    each(go, "send", 0)
    dts[block] = dt_ref[...]
    pk[block] = pk_ref[...]

    def normalize(part, at):
        v = part[...].astype(F32)
        r = lax.rsqrt(jnp.mean(v * v, axis=1, keepdims=True) + EPS)
        normed[pl.ds(at, part.shape[0])] = (v * r * gain[...]).astype(BF16)

    normalize(hid, HALO)
    own_w.wait()
    each(gx, "pass_on", 0)

    for c in dt_c:
        c.wait_recv()
    total = f32(dts.at[0])
    for i in range(1, 8):
        total = total + f32(dts.at[i])
    small_own[:, :256] = bc_ref[...]
    small_own[:, 256:] = total.astype(BF16)
    mine = gb_ref.at[ylo, x, core]
    own_b = pltpu.make_async_copy(small_own, mine, lsem.at[1])
    own_b.start()
    b_c = [rc(small_own, mine, bs.at[i], br.at[i], neighbour("x", d)) for i, d in enumerate((1, -1))]
    b_core = [rc(small_own, mine, bs.at[2], br.at[2], neighbour("core", 1))]
    normed_t[...] = normed[HALO:, :].T.reshape(8, 2, 96, ROWS)
    each(gx, "last", 0)
    each(gx, "send", 1)
    each(gz, "pass_on", 0)
    each(go, "pass_on", 0)
    b_f = []
    for i, d in enumerate((1, -1)):
        b_c[i].wait_recv()
        from_x = lax.rem(x - d + 4, 4)
        h = gb_ref.at[ylo, from_x, core, pl.ds(48 * i, 48)]
        b_f.append(rc(h, h, bs.at[3 + i], br.at[3 + i], neighbour("x", d)))
    cot_t[...] = cot[...].T.reshape(8, 2, 96, ROWS)
    each(gx, "pass_on", 1)
    for c in b_f:
        c.wait_recv()
    own_b.wait()
    line = gb_ref.at[ylo, :, core]
    b_y = rc(line, line, bs.at[5], br.at[5], {"ylo": 1 - ylo})
    for dx in (1, 2, 3):
        h = gb_ref.at[ylo, lax.rem(x + dx, 4), core]
        b_core.append(rc(h, h, bs.at[5 + dx], br.at[5 + dx], neighbour("core", 1)))
    each(gx, "last", 1)
    each(gx, "send", 2)
    each(gz, "last", 0)
    each(gz, "send", 1)
    each(go, "last", 0)
    each(go, "send", 1)
    halo_c.wait_recv()
    normalize(halo, 0)

    @pl.when(block == 0)
    def _():
        normed[pl.ds(0, HALO)] = jnp.zeros((HALO, WIDTH), BF16)

    b_y.wait_recv()
    line = gb_ref.at[1 - ylo, :, core]
    b_core.append(rc(line, line, bs.at[9], br.at[9], neighbour("core", 1)))
    for c in b_core:
        c.wait_recv()
    small_in = pltpu.make_async_copy(gb_ref, small_all, lsem.at[1])
    small_in.start()
    each(gz, "pass_on", 1)
    for c in pk_c:
        c.wait_recv()
    small_in.wait()

    def row(lo):
        pieces = [pk[m, 6:7, lo : lo + HEADS] for m in range(GROUPS)]
        return jnp.concatenate(pieces + [jnp.zeros((1, 80), F32)], axis=1)

    rates[0:1] = row(0)
    rates[1:2] = row(HEADS)
    rates[2:8] = jnp.zeros((6, 128), F32)
    small = dot(normed[...], small_all[...].reshape(WIDTH, COLS))
    bc_pre[...] = small[:, :256]
    pre = conv_pre(small[:, :256], taps_bc[...])
    bc_conv[...] = (pre * jax.nn.sigmoid(pre)).astype(BF16)
    shifted = small[HALO:, 256:384] + rates[1:2]
    steps[...] = shifted
    step = softplus(shifted)
    decay = -step * jnp.exp(rates[0:1])
    cum = dot(triangle(False).astype(F32), decay, precision=lax.Precision.HIGHEST)
    cum_t = cum.T
    step_t = step.T
    lasts = jnp.broadcast_to(jnp.exp(cum_t[:, ROWS - 1 : ROWS]), (128, 128))
    for m in range(GROUPS):
        at = slice(HEADS * m, HEADS * m + 8)
        cols[m] = jnp.concatenate([cum[:, at], step[:, at]], axis=1)
        cum_row[m] = cum_t[HEADS * m : HEADS * m + 8]
        step_row[m] = step_t[HEADS * m : HEADS * m + 8]
        dec_own[m] = lasts[HEADS * m : HEADS * m + 8]
    dec_c = to_peers(rc, lambda p: dec_own.at[p], dec, ds, dr, block)
    dec[block] = dec_own[block]
    gram[...] = jnp.where(triangle(False), dot(bc_conv[:, 128:], bc_conv[:, :128], (1, 1)), 0.0)
    each(gz, "last", 1)
    each(gz, "send", 2)
    each(gx, "pass_on", 2)
    each(go, "pass_on", 1)
    each(gx, "last", 2)
    each(gx, "complete")

    g_flat = g_ref.reshape(3, GROUPS, WIDTH, COLS)

    def weights(item, m):
        k = lax.rem(m, 2)
        return pltpu.make_async_copy(g_flat.at[item, m], wbuf.at[k], wsem.at[k])

    def over_groups(item, lo, hi, body):
        weights(item, lo).start()

        @pl.loop(lo, hi)
        def _(m):
            @pl.when(m < hi - 1)
            def _():
                weights(item, m + 1).start()

            weights(item, m).wait()
            body(m, wbuf.at[lax.rem(m, 2)])

    def second_group(m, w):
        ext = dot(normed[...], w[...])
        x_pre[m] = ext
        pre = conv_pre(ext, pk[m])
        xc = (pre * jax.nn.sigmoid(pre)).astype(BF16)
        x_conv[m] = xc
        cum, step = cols[m][:, :8], cols[m][:, 8:]
        weighted = (xc.astype(F32) * spread(step * jnp.exp(cum[ROWS - 1 : ROWS] - cum))).astype(BF16)
        local[m] = dot(weighted, bc_conv[:, :128], (0, 0)).astype(BF16)

    over_groups(0, 0, 4, second_group)
    each(go, "last", 1)
    over_groups(0, 4, GROUPS, second_group)
    a_c = to_peers(rc, lambda p: local.at[p], rec_a, es, er, block)
    rec_a[block] = local[block]
    each(gz, "pass_on", 2)
    each(go, "send", 2)
    outs = [pltpu.make_async_copy(x_pre, x_pre_out, osem.at[0]), pltpu.make_async_copy(x_conv, x_conv_out, osem.at[1])]

    def scan_group(m):
        xc = x_conv[m]
        cum = cols[m][:, :8]
        rows = cum_row[m]
        step_rows = step_row[m]
        parts = []
        for h in range(HEADS):
            decay = jnp.exp(jnp.minimum(cum[:, h : h + 1] - rows[h : h + 1, :], 0.0))
            mixing = (decay * gram[...] * step_rows[h : h + 1, :]).astype(BF16)
            parts.append(dot(mixing, xc[:, 64 * h : 64 * h + 64]))
        yb[m] = jnp.concatenate(parts, axis=1) + spread(pk[m, 6:7, 12:20]) * xc.astype(F32)

    for c in outs:
        c.start()
    pl.loop(0, 3)(scan_group)
    for c in dec_c + a_c:
        c.wait_recv()
    for h in range(HEADS):
        rows = pl.ds(64 * h, 64)
        run = jnp.zeros((64, 128), F32)
        for i in range(BLOCKS):
            out_b[i, rows] = run.astype(BF16)
            run = run * dec[i, pl.ds(h, 1)] + rec_a[i, rows].astype(F32)
    f_c = to_peers(rc, lambda p: out_b.at[p], state, fs, fr, block)
    state[block] = out_b[block]
    each(gz, "last", 2)
    pl.loop(3, GROUPS)(scan_group)
    each(go, "pass_on", 2)
    each(gz, "complete")

    def gate_group(m, w):
        zb[m] = dot(normed[HALO:, :], w[...])

    over_groups(1, 0, GROUPS, gate_group)
    z_c = pltpu.make_async_copy(zb, z_out, osem.at[2])
    z_c.start()
    each(go, "last", 2)
    for c in f_c:
        c.wait_recv()
    each(go, "complete")
    square[...] = jnp.zeros_like(square)
    inner[...] = jnp.zeros_like(inner)

    def out_group(m, w):
        carried = dot(bc_conv[:, 128:], state[m], (1, 1))
        y = yb[m] + spread(jnp.exp(cols[m][:, :8])) * carried
        yb[m] = y
        d = dot(cot[...], w[...])
        db[m] = d
        z = zb[m]
        gated = y * (z * jax.nn.sigmoid(z))
        sq = gated * gated
        ip = d * pk[m, 5:6] * gated
        square[...] += sq[:, :128] + sq[:, 128:256] + sq[:, 256:]
        inner[...] += ip[:, :128] + ip[:, 128:256] + ip[:, 256:]

    over_groups(2, 0, GROUPS, out_group)
    more = [pltpu.make_async_copy(yb, y_out, osem.at[3]), pltpu.make_async_copy(db, d_out, osem.at[4])]
    for c in more:
        c.start()
    for c in outs + [z_c] + more:
        c.wait()
    rc.all_sent()


def forward(w3, bc, dt, pk, hid, cot, gain, taps_bc):
    hbm = pl.BlockSpec(memory_space=pl.ANY)
    vmem = pl.BlockSpec(memory_space=pltpu.VMEM)
    sem = pltpu.SemaphoreType.DMA

    def v(*shape, dtype=F32):
        return pltpu.VMEM(shape, dtype)

    def b(*shape):
        return v(*shape, dtype=BF16)

    groups = (GROUPS, ROWS, COLS)
    return pl.pallas_call(
        forward_kernel,
        out_shape=(
            sds(3, 4, 2, 2, 4, 2, 96, COLS, dtype=BF16), sds(2, 4, 2, 96, COLS, dtype=BF16),
            sds(GROUPS, HALO + ROWS, COLS), sds(*groups, dtype=BF16), sds(*groups), sds(*groups), sds(*groups),
            sds(8, 2, 96, ROWS, dtype=BF16), sds(8, 2, 96, ROWS, dtype=BF16), sds(GROUPS, 8, COLS),
            sds(HALO + ROWS, 256), sds(ROWS, 256, dtype=BF16), sds(ROWS, 128), sds(GROUPS, ROWS, 16),
            sds(GROUPS, 8, ROWS), sds(GROUPS, 8, ROWS), sds(GROUPS, COLS, 128, dtype=BF16), sds(BLOCKS, 8, 128), sds(8, 128),
            sds(ROWS, 128), sds(ROWS, 128),
        ),
        in_specs=[hbm] + [vmem] * 7,
        out_specs=(hbm,) * 7 + (vmem,) * 14,
        scratch_shapes=[
            b(HALO + ROWS, WIDTH), b(HALO, WIDTH), b(BLOCKS, 96, 128), b(96, COLS), b(2, 4, 2, 96, COLS),
            v(GROUPS, HALO + ROWS, COLS), b(*groups), v(*groups), v(*groups), v(*groups), b(2, WIDTH, COLS), v(ROWS, ROWS),
            b(GROUPS, COLS, 128), b(GROUPS, COLS, 128), b(GROUPS, COLS, 128), v(GROUPS, 8, 128),
            sem((108,)), sem((108,)), sem((90,)), sem((90,)), sem((10,)), sem((10,)), sem((8,)), sem((8,)), sem((8,)),
            sem((8,)), sem((8,)), sem((8,)), sem((8,)), sem((8,)), sem((8,)), sem((8,)), sem, sem, sem((2,)), sem((2,)),
            sem((5,)),
        ],
        compiler_params=pltpu.CompilerParams(collective_id=0, has_side_effects=True, vmem_limit_bytes=60 * 2**20),
        name="forward_between_devices",
    )(w3, bc, dt, pk, hid, cot, gain, taps_bc)


class Total:
    def __init__(self, rc, value, core, xs, yl, yh, zs, send, recv):
        self.rc, self.value, self.core, self.xs, self.yl, self.yh, self.zs = rc, value, core, xs, yl, yh, zs
        self.send, self.recv, self.at = send, recv, 0
        self.me = my_place()

    def push(self, dst, device):
        k = self.at
        self.at += 1
        return self.rc(self.value, dst, self.send.at[k], self.recv.at[k], device)

    def done(self):
        for c in self.flying:
            c.wait_recv()
        for c in self.flying:
            self.rc.sent(c)

    def step(self, j):
        v, me = self.value, self.me
        if j == 0:
            self.flying = [self.push(self.core, neighbour("core", 1))]
        elif j == 1:
            self.done()
            v[...] = v[...] + self.core[...]
            self.xs[me["x"]] = v[...]
            self.flying = [self.push(self.xs.at[me["x"]], neighbour("x", d)) for d in (1, 2, 3)]
        elif j == 2:
            self.done()
            v[...] = (self.xs[0] + self.xs[1]) + (self.xs[2] + self.xs[3])
            self.flying = [self.push(self.yl, {"ylo": 1 - lax.axis_index("ylo")})]
        elif j == 3:
            self.done()
            v[...] = v[...] + self.yl[...]
            self.flying = [self.push(self.yh, {"yhi": 1 - lax.axis_index("yhi")})]
        elif j == 4:
            self.done()
            v[...] = v[...] + self.yh[...]
            self.zs[me["z"]] = v[...]
            self.flying = [self.push(self.zs.at[me["z"]], neighbour("z", d)) for d in (1, 2, 3)]
        elif j == 5:
            self.done()
            v[...] = (self.zs[0] + self.zs[1]) + (self.zs[2] + self.zs[3])


class SmallSum:
    def __init__(self, rc, parts, sib, xs, ys, zs, hs, send, recv):
        self.rc, self.parts, self.sib, self.xs, self.ys, self.zs, self.hs = rc, parts, sib, xs, ys, zs, hs
        self.send, self.recv = send, recv
        self.me = my_place()

    def step(self, j, out=None):
        rc, me, parts, s, r = self.rc, self.me, self.parts, self.send, self.recv
        core, ylo = lax.axis_index("core"), lax.axis_index("ylo")
        if j == 0:
            self.c = [rc(parts.at[:, :, 1 - core], self.sib, s.at[0], r.at[0], neighbour("core", 1))]
        elif j == 1:
            self.c[0].wait_recv()

            def one(x):
                for yl in range(2):
                    m = parts.at[yl, x, core]
                    m[...] = (f32(m) + f32(self.sib.at[yl, x])).astype(BF16)

            pl.loop(0, 4)(one)
            self.c = [rc(parts.at[:, lax.rem(me["x"] + d, 4), core], self.xs.at[d - 1], s.at[d], r.at[d], neighbour("x", d))
                      for d in (1, 2, 3)]
        elif j == 2:
            for c in self.c:
                c.wait_recv()
            for yl in range(2):
                m = parts.at[yl, me["x"], core]
                m[...] = (f32(m) + f32(self.xs.at[0, yl]) + f32(self.xs.at[1, yl]) + f32(self.xs.at[2, yl])).astype(BF16)
            self.c = [rc(parts.at[1 - ylo, me["x"], core], self.ys, s.at[4], r.at[4], {"ylo": 1 - ylo})]
        elif j == 3:
            self.c[0].wait_recv()
            m = parts.at[ylo, me["x"], core]
            m[...] = (f32(m) + f32(self.ys)).astype(BF16)
            self.zs[me["z"]] = m[...]
            self.c = [rc(m, self.zs.at[me["z"]], s.at[4 + d], r.at[4 + d], neighbour("z", d)) for d in (1, 2, 3)]
        elif j == 4:
            for c in self.c:
                c.wait_recv()
            z, hs = self.zs, self.hs
            hs[0] = ((f32(z.at[0]) + f32(z.at[1])) + (f32(z.at[2]) + f32(z.at[3]))).astype(BF16)
            self.c = [rc(hs.at[0], hs.at[1], s.at[8], r.at[8], {"yhi": 1 - lax.axis_index("yhi")})]
        elif j == 5:
            self.c[0].wait_recv()
            out[...] = f32(self.hs.at[0]) + f32(self.hs.at[1])


SLOTS = 4
LAG = 2


def part_of(ref, item, pos, lo, n):
    z = slice(None) if pos["z"] is None else pos["z"]
    x = slice(None) if pos["x"] is None else pos["x"]
    if pos["y"] is None:
        yh = yl = slice(None)
    else:
        yh, yl = pos["y"] // 2, lax.rem(pos["y"], 2)
    return ref.at[item, z, yh, yl, x, pl.ds(lo, n)]


class Chunk:
    def __init__(self, rc, own, out, bufs, sems, item, slot, wide, r):
        self.rc, self.own, self.out, self.item, self.slot, self.r = rc, own, out, item, slot, r
        full, half, second, third = bufs
        self.full, self.half = full[r].at[wide], half[r].at[wide]
        self.direct = {1: second[r].at[slot], 2: third.at[slot * 3 + r]}
        self.send, self.recv = sems
        self.base = (slot * 3 + r) * 10
        self.me = my_place()

    def slab(self, st, d, lo=0, n=SUB):
        p = {a: (self.me[a] if i < st else None) for i, a in enumerate(ORDERS[self.r])}
        a = ORDERS[self.r][st]
        p[a] = lax.rem(self.me[a] + (d + 4), 4)
        return part_of(self.own, self.slot, p, self.r * SUB + lo, n)

    def loop(self, st, body):
        sizes = []
        for a, n in (("z", (4,)), ("y", (2, 2)), ("x", (4,))):
            if ORDERS[self.r].index(a) > st:
                sizes += n
        if not sizes:
            body(())
        elif len(sizes) == 1 or sizes == [2, 2]:
            for i in range(4):
                body((i,) if len(sizes) == 1 else (i // 2, i % 2))
        else:
            @pl.loop(0, 4)
            def _(i):
                for k in range(4):
                    if sizes == [4, 4]:
                        body((i, k))
                    elif sizes == [4, 2, 2]:
                        body((i, k // 2, k % 2))
                    else:
                        body((i // 2, lax.rem(i, 2), k))

    def push(self, k, src, dst, st, d):
        t = self.base + k
        return self.rc(src, dst, self.send.at[t], self.recv.at[t], neighbour(ORDERS[self.r][st], d))

    def far(self):
        self.far_c = [self.push(i, self.slab(0, 2, 16 * i, 16), self.half.at[i], 0, d) for i, d in enumerate((1, -1))]

    def near(self):
        self.near_c = []
        for i, d in enumerate((1, -1)):
            self.far_c[i].wait_recv()
            mine = self.slab(0, d, 16 * i, 16)

            def add(index, mine=mine, i=i):
                m = mine.at[index]
                m[...] = m[...] + self.half[(i, *index)]

            self.loop(0, add)
            self.near_c.append(self.push(2 + i, self.slab(0, d), self.full.at[i], 0, d))

    def straight(self, st):
        self.straight_c = [self.push(1 + 3 * st + d - 1, self.slab(st, d), self.direct[st].at[d - 1], st, d) for d in (1, 2, 3)]

    def step(self, j):
        if j == 0:
            self.far()
        elif j == 1:
            self.near()
        elif j == 2:
            for c in self.near_c:
                c.wait_recv()
            mine = self.slab(0, 0)

            def add(index):
                m = mine.at[index]
                m[...] = (f32(m) + f32(self.full.at[(0, *index)]) + f32(self.full.at[(1, *index)])).astype(BF16)

            self.loop(0, add)
            self.straight(1)
        else:
            for c in self.straight_c:
                c.wait_recv()
            st = j - 2
            mine = self.slab(st, 0)
            got = self.direct[st]

            def total(index):
                m = mine.at[index] if index else mine
                return (f32(m) + f32(got.at[(0, *index)])) + (f32(got.at[(1, *index)]) + f32(got.at[(2, *index)]))

            if st == 1:
                def add(index):
                    mine[index] = total(index).astype(BF16)

                self.loop(1, add)
                self.straight(2)
            else:
                self.out[self.item, pl.ds(self.r * SUB, SUB)] = total(())


def backward_kernel(g_ref, x_conv_ref, d_x_ref, x_pre_ref, cols_ref, d_cols_ref,
                    w_small, n_t, c_t, hid, cot, out_in, d_z, d_local, state, dec, taps, d_bc_in, bc_pre, bc_conv, taps_bc,
                    shifted, a_log, gain, gain_part, skip_part,
                    out_ref, sout_ref, vout_ref, nout_ref, grad_hidden, *scr):
    (own, send, sib, rec_a, out_b, rec_b, dxp, tails, halo_src, halo_dst, acc, wbuf, bxc, bdx, bxp, bcols, bdc,
     d_b, d_all, parts, s_sib, s_xs, s_ys, s_zs, s_hs,
     v_core, v_xs, v_yl, v_yh, v_zs, n_core, n_xs, n_yl, n_yh, n_zs) = scr[:35]
    bufs = [scr[35:38], scr[38:41], scr[41:44], scr[44]]
    (t_s, t_r, c_s, c_r, e_s, e_r, b_s, b_r, h_s, h_r, ss, sr, vs, vr, ns, nr, wsem, lsem, credit, freed) = scr[45:]
    rc = Sender()
    core = lax.axis_index("core")
    block = lax.axis_index("z") * 2 + lax.axis_index("yhi")
    greet()()

    to_owner = []
    for d in range(1, 8):
        p = lax.rem(block + d, 8)
        to_owner.append(rc(d_local.at[p], rec_a.at[block], e_s.at[d], e_r.at[d], block_device(p)))
    rec_a[block] = d_local[block]

    def core_copy(m):
        k = lax.rem(m, SLOTS)
        return pltpu.make_async_remote_copy(src_ref=send.at[k], dst_ref=sib.at[k], send_sem=c_s.at[k], recv_sem=c_r.at[k],
                                            device_id=neighbour("core", 1), device_id_type=MESHID)

    def gradient(lhs_t, rhs, slot, first_item):
        def one(m):
            @pl.when(m < GROUPS)
            def _():
                k = lax.rem(m, SLOTS)

                def wait_slot():
                    core_copy(m).wait_send()
                    pl.semaphore_wait(credit, 1)

                if first_item:
                    pl.when(m >= SLOTS)(wait_slot)
                else:
                    wait_slot()
                v = dot(lhs_t.at[:, 1 - core][...].reshape(768, ROWS), rhs[m])
                send[k] = v.astype(BF16).reshape(2, 4, 96, COLS)
                core_copy(m).start()

            @pl.when(m >= LAG)
            def _():
                q = m - LAG
                k = lax.rem(q, SLOTS)
                core_copy(q).wait_recv()
                v = dot(lhs_t.at[:, core][...].reshape(768, ROWS), rhs[q])
                own[slot, q // 2, lax.rem(q, 2)] = (v + sib[k].reshape(768, COLS).astype(F32)).astype(BF16).reshape(2, 4, 96, COLS)
                pl.semaphore_signal(credit, inc=1, device_id=neighbour("core", 1), device_id_type=MESHID)

        pl.loop(0, GROUPS + LAG)(one)

    def chunks(item, slot, wide):
        return [Chunk(rc, own, out_ref, bufs, (t_s, t_r), item, slot, wide, r) for r in range(3)]

    def steps(cs, j):
        for c in cs:
            c.step(j)

    oc, zc, xc_ = chunks(2, 0, 0), chunks(1, 1, 1), chunks(0, 2, 0)

    gradient(c_t, out_in, 0, True)
    steps(oc, 0)

    for c in to_owner:
        c.wait_recv()
    for h in range(HEADS):
        rows = pl.ds(64 * h, 64)
        run = jnp.zeros((64, 128), F32)
        for i in range(BLOCKS - 1, -1, -1):
            out_b[i, rows] = run.astype(BF16)
            run = run * dec[i, pl.ds(h, 1)] + rec_a[i, rows].astype(F32)
    back = []
    for d in range(1, 8):
        p = lax.rem(block + d, 8)
        back.append(rc(out_b.at[p], rec_b.at[block], b_s.at[d], b_r.at[d], block_device(p)))
    rec_b[block] = out_b[block]

    gradient(n_t, d_z, 1, False)
    steps(oc, 1)
    steps(zc, 0)
    for c in back:
        c.wait_recv()

    streams = ((x_conv_ref, bxc), (d_x_ref, bdx), (x_pre_ref, bxp), (cols_ref, bcols), (d_cols_ref, bdc))

    def load(m):
        k = lax.rem(m, 2)
        return [pltpu.make_async_copy(src.at[m], dst.at[k], lsem.at[k, i]) for i, (src, dst) in enumerate(streams)]

    def fifth_group(m):
        k = lax.rem(m, 2)

        @pl.when(m < GROUPS - 1)
        def _():
            for c in load(m + 1):
                c.start()

        for c in load(m):
            c.wait()
        ds = rec_b[m]
        xf = bxc[k].astype(F32)
        cum, step = bcols[k][:, :8], bcols[k][:, 8:]
        last = cum[ROWS - 1 : ROWS]
        tail = jnp.exp(last - cum)
        weights = step * tail
        wide = spread(weights)
        d_weighted = dot(bc_conv[:, :128], ds, (1, 1))
        d_b[...] += dot((xf * wide).astype(BF16), ds)
        dx = bdx[k] + wide * d_weighted
        d_weights = gathered_heads(d_weighted * xf)
        both = weights * d_weights
        lane = lax.broadcasted_iota(jnp.int32, (1, 8), 1)
        product = jnp.sum(state[m].astype(F32) * ds.astype(F32), axis=1, keepdims=True)
        d_last = jnp.sum(both, axis=0, keepdims=True)
        for h in range(HEADS):
            dots = jnp.sum(product[64 * h : 64 * h + 64], axis=0, keepdims=True)
            d_last = jnp.where(lane == h, d_last + jnp.exp(last) * dots, d_last)
        row = lax.broadcasted_iota(jnp.int32, (ROWS, 8), 0)
        d_cum = bdc[k][:, :8] - both
        d_cum = jnp.where(row == ROWS - 1, d_cum + d_last, d_cum)
        d_all[m] = jnp.concatenate([d_cum, bdc[k][:, 8:] + tail * d_weights], axis=1)
        ext = bxp[k]
        tap = taps[m]
        pre = conv_pre(ext, tap)
        sig = jax.nn.sigmoid(pre)
        dp = dx * (sig * (1.0 + pre * (1.0 - sig)))
        v_value[m] = conv_grads(dp, ext, gain_part[m], skip_part[m])
        whole_dx = conv_transposed(jnp.concatenate([dp, jnp.zeros((8, COLS), F32)], axis=0), tap)
        dxp[m] = whole_dx.astype(BF16)
        tails[m] = whole_dx[ROWS - 16 :]
        halo_src[m] = dp[:8]

    v_value = vout_ref
    d_b[...] = jnp.zeros_like(d_b)
    for c in load(0):
        c.start()
    pl.loop(0, 4)(fifth_group)
    steps(zc, 1)
    pl.loop(4, GROUPS)(fifth_group)

    d_bc = jnp.concatenate([d_bc_in[:, :128] + d_b[...], d_bc_in[:, 128:]], axis=1)
    ext = bc_pre[...]
    pre = conv_pre(ext, taps_bc[...])
    sig = jax.nn.sigmoid(pre)
    dp_bc = d_bc * (sig * (1.0 + pre * (1.0 - sig)))
    halo_src[GROUPS] = jnp.concatenate([dp_bc[:8], jnp.zeros((8, 128), F32)], axis=1)
    before = lax.rem(block + 7, 8)
    halo = rc(halo_src, halo_dst, h_s, h_r, block_device(before))
    steps(oc, 2)
    for a in "xyz":
        for s in (1, -1):
            pl.semaphore_signal(freed, inc=1, device_id=neighbour(a, s), device_id_type=MESHID)
    zero8 = jnp.zeros((1, 256), F32)
    d_cum = jnp.concatenate([d_all[m][:, :HEADS] for m in range(GROUPS)] + [jnp.zeros((ROWS, 80), F32)], axis=1)
    d_step = jnp.concatenate([d_all[m][:, 8 : 8 + HEADS] for m in range(GROUPS)] + [jnp.zeros((ROWS, 80), F32)], axis=1)
    d_decay = dot(triangle(True).astype(F32), d_cum, precision=lax.Precision.HIGHEST)
    rate = -jnp.exp(a_log[0:1])
    v = shifted[...]
    d_dt = (d_step + rate * d_decay) * jax.nn.sigmoid(v)
    log_grad = jnp.sum(d_decay * (softplus(v) * rate), axis=0, keepdims=True)
    shift_grad = jnp.sum(d_dt, axis=0, keepdims=True)
    bc_rows = conv_grads(dp_bc, ext, jnp.concatenate([log_grad, shift_grad], axis=1), zero8)
    v_value[GROUPS] = jnp.concatenate([bc_rows, jnp.zeros((8, 128), F32)], axis=1)
    vec = Total(rc, v_value, v_core, v_xs, v_yl, v_yh, v_zs, vs, vr)
    vec.step(0)

    halo.wait_recv()
    inside = block < 7

    def below(k):
        return jnp.where(inside, halo_dst[k], 0.0)

    def fix(m):
        ext = jnp.concatenate([jnp.zeros((16, COLS), F32), below(m)], axis=0)
        dxp[m, pl.ds(ROWS - 16, 16)] = (tails[m] + conv_transposed(ext, taps[m], 16)).astype(BF16)

    pl.loop(0, GROUPS)(fix)
    d_bc = conv_transposed(jnp.concatenate([dp_bc, below(GROUPS)[:, :256]], axis=0), taps_bc[...])
    small = jnp.concatenate([d_bc, d_dt], axis=1).astype(BF16)
    def weights(m):
        k = lax.rem(m, 2)
        return [pltpu.make_async_copy(g_ref.at[i, m], wbuf.at[k, i], wsem.at[k, i]) for i in range(2)]

    for c in weights(0):
        c.start()
    gradient(n_t, dxp, 2, False)
    pl.semaphore_wait(freed, 6)
    steps(xc_, 0)
    steps(oc, 3)
    steps(zc, 2)
    for i in range(2):
        lhs = n_t.at[:, i][...].reshape(768, ROWS)
        parts[:, :, i] = dot(lhs, small).astype(BF16).reshape(2, 4, 96, COLS)
    sums = SmallSum(rc, parts, s_sib, s_xs, s_ys, s_zs, s_hs, ss, sr)
    sums.step(0)
    acc[...] = dot(small, w_small[...], (1, 1))

    def input_group(m):
        k = lax.rem(m, 2)

        @pl.when(m < GROUPS - 1)
        def _():
            for c in weights(m + 1):
                c.start()

        for c in weights(m):
            c.wait()
        lhs = jnp.concatenate([dxp[m], d_z[m]], axis=1)
        rhs = jnp.concatenate([wbuf[k, 0], wbuf[k, 1]], axis=1)
        acc[...] += dot(lhs, rhs, (1, 1))

    pl.loop(0, 2)(input_group)
    steps(xc_, 1)
    pl.loop(2, 5)(input_group)
    steps(oc, 4)
    steps(zc, 3)
    sums.step(1)
    vec.step(1)
    pl.loop(5, GROUPS)(input_group)
    sums.step(2)
    vec.step(2)
    v = hid[...].astype(F32)
    r = lax.rsqrt(jnp.mean(v * v, axis=1, keepdims=True) + EPS)
    unit = v * r
    dn = acc[...]
    gain_grad = jnp.sum(dn * unit, axis=0, keepdims=True)
    for i in range(4):
        nout_ref[0, pl.ds(i, 1)] = gain_grad[:, COLS * i : COLS * i + COLS]
    nout_ref[0, pl.ds(4, 4)] = jnp.zeros((4, COLS), F32)
    nvec = Total(rc, nout_ref, n_core, n_xs, n_yl, n_yh, n_zs, ns, nr)
    nvec.step(0)
    steps(xc_, 2)
    nvec.step(1)
    d_in = dn * gain[...]
    grad_hidden[...] = r * (d_in - unit * jnp.mean(d_in * unit, axis=1, keepdims=True)) + cot[...].astype(F32)
    sums.step(3)
    vec.step(3)
    steps(zc, 4)
    nvec.step(2)
    steps(xc_, 3)
    sums.step(4)
    vec.step(4)
    nvec.step(3)
    sums.step(5, sout_ref)
    vec.step(5)
    steps(xc_, 4)
    nvec.step(4)
    nvec.step(5)
    for k in range(SLOTS):
        core_copy(GROUPS - SLOTS + k).wait_send()
    pl.semaphore_wait(credit, SLOTS)
    rc.all_sent()


def backward(w_all, x_conv, d_x, x_pre, cols, d_cols, w_small, n_t, c_t, hid, cot, out_in, d_z, d_local,
             state, dec, taps, d_bc, bc_pre, bc_conv, taps_bc, shifted, a_log, gain, gain_part, skip_part):
    hbm = pl.BlockSpec(memory_space=pl.ANY)
    vmem = pl.BlockSpec(memory_space=pltpu.VMEM)
    sem = pltpu.SemaphoreType.DMA

    def buf(*shape, dtype=BF16):
        return pltpu.VMEM((*shape, COLS), dtype)

    def v(*shape, dtype=F32):
        return pltpu.VMEM(shape, dtype)

    scratch = [
        buf(3, 4, 2, 2, 4, 96), buf(SLOTS, 2, 4, 96), buf(SLOTS, 2, 4, 96),
        v(GROUPS, COLS, 128, dtype=BF16), v(GROUPS, COLS, 128, dtype=BF16), v(GROUPS, COLS, 128, dtype=BF16),
        buf(GROUPS, ROWS), buf(GROUPS, 16, dtype=F32), buf(GROUPS + 1, 8, dtype=F32), buf(GROUPS + 1, 8, dtype=F32),
        v(ROWS, WIDTH), buf(2, 2, WIDTH),
        buf(2, ROWS), buf(2, ROWS, dtype=F32), buf(2, HALO + ROWS, dtype=F32),
        v(2, ROWS, 16), v(2, ROWS, 16),
        v(ROWS, 128), v(GROUPS, ROWS, 16),
        buf(2, 4, 2, 96), buf(2, 4, 96), buf(3, 2, 96), buf(96), buf(4, 96), buf(2, 96),
    ]
    for n in (GROUPS + 1, 1):
        one = buf(n, 8, dtype=F32)
        four = buf(4, n, 8, dtype=F32)
        scratch += [one, four, one, one, four]
    scratch += [buf(2, 2, 4, 2, 2, SUB), buf(2, 2, 4, 4, SUB), buf(2, 2, 2, 2, 4, SUB)]
    scratch += [buf(2, 2, 4, 2, 2, 16), buf(2, 2, 4, 4, 16), buf(2, 2, 2, 2, 4, 16)]
    scratch += [buf(3, 3, 4, SUB), buf(3, 3, 4, SUB), buf(3, 3, 2, 2, SUB), buf(9, 3, SUB)]
    scratch += [sem((90,)), sem((90,)), sem((SLOTS,)), sem((SLOTS,)), sem((8,)), sem((8,)), sem((8,)), sem((8,)),
                sem, sem, sem((9,)), sem((9,)), sem((9,)), sem((9,)), sem((9,)), sem((9,)), sem((2, 2)), sem((2, 5)),
                pltpu.SemaphoreType.REGULAR, pltpu.SemaphoreType.REGULAR]
    return pl.pallas_call(
        backward_kernel,
        out_shape=(sds(3, 96, COLS), sds(96, COLS), sds(GROUPS + 1, 8, COLS), sds(1, 8, COLS), sds(ROWS, WIDTH)),
        in_specs=[hbm] * 6 + [vmem] * 20,
        out_specs=(vmem,) * 5,
        scratch_shapes=scratch,
        compiler_params=pltpu.CompilerParams(collective_id=1, has_side_effects=True, vmem_limit_bytes=63 * 2**20),
        name="backward_between_devices",
    )(w_all, x_conv, d_x, x_pre, cols, d_cols, w_small, n_t, c_t, hid, cot, out_in, d_z, d_local,
      state, dec, taps, d_bc, bc_pre, bc_conv, taps_bc, shifted, a_log, gain, gain_part, skip_part)
def shards(hidden, grad_out, norm_gain, w_zx, w_bc, w_dt, conv_x, conv_bc, a_log, dt_bias, d_skip, gate_gain, w_out):
    index = lax.axis_index(MP)
    heads = jnp.concatenate([a_log, dt_bias, d_skip, jnp.zeros((COLS - 3 * HEADS,), F32)])[None]
    packed = jnp.concatenate([conv_x, gate_gain[None], heads, jnp.zeros((1, COLS), F32)])
    steps_own = lax.dynamic_update_slice(jnp.zeros((96, 128), BF16), w_dt, (0, index * HEADS))
    taps_bc = jnp.pad(conv_bc, ((0, 3), (0, 0)))
    gain = norm_gain[None]
    (w_all, w_small, x_pre, x_conv, z, y, d, normed_t, cot_t, taps, bc_pre, bc_conv, shifted, cols, cum_row,
     step_row, state, decays, rates, square, inner) = forward(
        jnp.stack([w_zx[:, 1], w_zx[:, 0], w_out.T]), w_bc, steps_own, packed, hidden, grad_out, gain, taps_bc)
    w_all = w_all.reshape(3, GROUPS, WIDTH, COLS)
    w_small = w_small.reshape(WIDTH, COLS)
    result, out_in, d_z, d_x, d_local, d_cols, d_bc, gain_part, skip_part = fourth(
        hidden, square, inner, z, y, d, taps, w_all, x_conv, bc_conv, cols, cum_row, step_row, state)
    owned, small, vector, norm_sum, grad_hidden = backward(
        w_all, x_conv, d_x, x_pre, cols, d_cols, w_small, normed_t, cot_t, hidden, grad_out, out_in, d_z,
        d_local, state, decays, taps, d_bc, bc_pre, bc_conv, taps_bc, shifted,
        rates, gain, gain_part, skip_part)

    def own(flat):
        return lax.dynamic_slice_in_dim(flat, index * HEADS, HEADS, flat.ndim - 1)

    mine = lax.dynamic_index_in_dim(vector, index, 0, keepdims=False)
    return (
        result,
        grad_hidden,
        norm_sum[0, :4].reshape(WIDTH),
        jnp.stack([owned[1], owned[0]], axis=1),
        small[:, :256],
        own(small[:, 256:304]),
        mine[:5],
        vector[GROUPS, :5, :256],
        own(vector[GROUPS, 5, :48]),
        own(vector[GROUPS, 5, 128:176]),
        mine[6].reshape(HEADS, 64).sum(axis=1),
        mine[5],
        owned[2].T,
    )


def solution(mesh):
    finer = Mesh(mesh.devices.reshape(2, 4, 2, 4, 2), DP_MP)
    rows = P(DP_MP, None)
    placed = (rows, rows, P(), P(DP, None, MP), P(DP, None), P(DP, MP), P(None, MP), P(), P(MP), P(MP), P(MP), P(MP),
              P(MP, DP))
    return jax.shard_map(
        shards,
        mesh=finer,
        in_specs=placed,
        out_specs=(rows, rows, P(), P(DP, None, MP), P(DP, None), P(DP, MP), P(None, MP), P(), P(MP), P(MP), P(MP), P(MP),
                   P(MP, DP)),
        check_vma=False,
    )
```

```python
import jax
import jax.numpy as jnp
from jax import lax
from jax.experimental import pallas as pl
from jax.experimental.pallas import tpu as pltpu
from jax.sharding import Mesh
from jax.sharding import PartitionSpec as P

MP = ("z", "yhi")
DP = ("ylo", "x", "core")
DP_MP = DP + MP
BLOCKS = 8
F32 = jnp.float32
BF16 = jnp.bfloat16
ROWS = 256
WIDTH = 1536
GROUPS = 8
COLS = 384
HEADS = 6
HALO = 16
EPS = 1e-05
INNER = GROUPS * COLS
VMEM_LIMIT = 56 * 2**20


def dot(a, b, contract=(1, 0), precision=None):
    return lax.dot_general(
        a, b, (((contract[0],), (contract[1],)), ((), ())),
        preferred_element_type=F32, precision=precision,
    )


def spread(per_head):
    rows = per_head.shape[0]
    low = lax.broadcasted_iota(jnp.int32, (rows, 128), 1) < 64
    tiles = [
        jnp.where(low, per_head[:, 2 * i : 2 * i + 1], per_head[:, 2 * i + 1 : 2 * i + 2])
        for i in range(COLS // 128)
    ]
    return jnp.concatenate(tiles, axis=1)


def gathered_heads(values):
    rows = values.shape[0]
    low = lax.broadcasted_iota(jnp.int32, (rows, 128), 1) < 64
    lane = lax.broadcasted_iota(jnp.int32, (rows, 8), 1)
    out = jnp.zeros((rows, 8), F32)
    for i in range(COLS // 128):
        tile = values[:, 128 * i : 128 * i + 128]
        first = jnp.sum(jnp.where(low, tile, 0.0), axis=1, keepdims=True)
        both = jnp.sum(tile, axis=1, keepdims=True)
        out = jnp.where(lane == 2 * i, first, out)
        out = jnp.where(lane == 2 * i + 1, both - first, out)
    return out


def softplus(v):
    return jnp.maximum(v, 0.0) + jnp.log1p(jnp.exp(-jnp.abs(v)))


def conv_pre(ext, taps):
    total = taps[4:5]
    for j in range(4):
        total = total + ext[HALO - 3 + j : HALO - 3 + j + ROWS] * taps[j : j + 1]
    return total


def conv_transposed(ext, taps, rows=ROWS):
    total = ext[3 : 3 + rows] * taps[0:1]
    for j in range(1, 4):
        total = total + ext[3 - j : 3 - j + rows] * taps[j : j + 1]
    return total


def conv_grads(dpre, ext, sixth, seventh):
    rows = [
        jnp.sum(dpre * ext[HALO - 3 + j : HALO - 3 + j + ROWS], axis=0, keepdims=True)
        for j in range(4)
    ]
    rows.append(jnp.sum(dpre, axis=0, keepdims=True))
    rows += [sixth, seventh, jnp.zeros((1, dpre.shape[1]), F32)]
    return jnp.concatenate(rows, axis=0)


def triangle(upper):
    row = lax.broadcasted_iota(jnp.int32, (ROWS, ROWS), 0)
    col = lax.broadcasted_iota(jnp.int32, (ROWS, ROWS), 1)
    return row <= col if upper else row >= col


def sds(*shape, dtype=F32):
    return jax.ShapeDtypeStruct(shape, dtype)


def params():
    return pltpu.CompilerParams(vmem_limit_bytes=VMEM_LIMIT)


MESHID = pl.DeviceIdType.MESH
ORDERS = (("x", "y", "z"), ("y", "z", "x"), ("z", "x", "y"))
SUB = 32


def neighbour(axis, s):
    if axis == "core":
        return {"core": 1 - lax.axis_index("core")}
    if axis == "y":
        y = lax.rem(lax.axis_index("yhi") * 2 + lax.axis_index("ylo") + (s + 4), 4)
        return {"ylo": lax.rem(y, 2), "yhi": y // 2}
    return {axis: lax.rem(lax.axis_index(axis) + (s + 4), 4)}


def my_place():
    return {"x": lax.axis_index("x"), "z": lax.axis_index("z"), "y": lax.axis_index("yhi") * 2 + lax.axis_index("ylo")}


def block_device(p):
    return {"z": p // 2, "yhi": lax.rem(p, 2)}


def f32(ref):
    return ref[...].astype(F32)


class Sender:
    def __init__(self):
        self.pending = {}

    def __call__(self, src, dst, send, recv, device):
        c = pltpu.make_async_remote_copy(src_ref=src, dst_ref=dst, send_sem=send, recv_sem=recv, device_id=device,
                                         device_id_type=MESHID)
        c.start()
        self.pending[id(c)] = c
        return c

    def sent(self, c):
        c.wait_send()
        del self.pending[id(c)]

    def all_sent(self):
        for c in self.pending.values():
            c.wait_send()


def greet():
    bar = pltpu.get_barrier_semaphore()
    for a in "xyz":
        for s in (1, 2, 3):
            pl.semaphore_signal(bar, inc=1, device_id=neighbour(a, s), device_id_type=MESHID)
    for d in (1, 2, 3):
        diagonal = {"z": lax.rem(lax.axis_index("z") + d, 4), "yhi": 1 - lax.axis_index("yhi")}
        pl.semaphore_signal(bar, inc=1, device_id=diagonal, device_id_type=MESHID)
    pl.semaphore_signal(bar, inc=1, device_id=neighbour("core", 1), device_id_type=MESHID)
    return lambda: pl.semaphore_wait(bar, 13)


def to_peers(rc, src_of, dst, send, recv, block):
    out = []
    for d in range(1, 8):
        p = lax.rem(block + d, 8)
        out.append(rc(src_of(p), dst.at[block], send.at[d], recv.at[d], block_device(p)))
    return out


class Gather:
    def __init__(self, rc, g, w, sems, item, r):
        self.rc, self.g, self.w, self.item, self.r = rc, g, w, item, r
        self.ts, self.tr, self.cs, self.cr = sems
        self.k = item * 3 + r
        self.me = my_place()
        self.core = lax.axis_index("core")
        self.forwarded = []

    def at(self, pos, lo=0, n=SUB):
        z = slice(None) if pos["z"] is None else pos["z"]
        x = slice(None) if pos["x"] is None else pos["x"]
        if pos["y"] is None:
            yh = yl = slice(None)
        else:
            yh, yl = pos["y"] // 2, lax.rem(pos["y"], 2)
        return self.g.at[self.item, z, yh, yl, x, self.core, pl.ds(self.r * SUB + lo, n)]

    def pos(self, st, d=0):
        p = {a: (None if i < st else self.me[a]) for i, a in enumerate(ORDERS[self.r])}
        a = ORDERS[self.r][st]
        p[a] = lax.rem(self.me[a] + (d + 4), 4)
        return p

    def to_sibling(self, ref, src=None):
        k = self.k * 10 + len(self.forwarded)
        self.forwarded.append(self.rc(ref if src is None else src, ref, self.cs.at[k], self.cr.at[k], neighbour("core", 1)))

    def straight(self, st):
        ref, t = self.at(self.pos(st)), self.k * 10 + st * 3 - 1
        src = ref if st else self.w.at[self.item, pl.ds(self.r * SUB, SUB)]
        self.c = [self.rc(src, ref, self.ts.at[t + d], self.tr.at[t + d], neighbour(ORDERS[self.r][st], d)) for d in (1, 2, 3)]
        if st == 0:
            self.to_sibling(ref, src)

    def line(self, st):
        for d in (1, 2, 3):
            self.c[d - 1].wait_recv()
            self.to_sibling(self.at(self.pos(st, -d)))

    def near(self):
        a, t = ORDERS[self.r][2], self.k * 10 + 6
        ref = self.at(self.pos(2))
        self.c = [self.rc(ref, ref, self.ts.at[t + i], self.tr.at[t + i], neighbour(a, d)) for i, d in enumerate((1, -1))]

    def pass_on(self):
        a, t = ORDERS[self.r][2], self.k * 10 + 8
        self.f = []
        for i, d in enumerate((1, -1)):
            self.c[i].wait_recv()
            p = self.pos(2, -d)
            half = self.at(p, 16 * i, 16)
            self.f.append(self.rc(half, half, self.ts.at[t + i], self.tr.at[t + i], neighbour(a, d)))
            self.to_sibling(self.at(p))

    def last(self):
        for f in self.f:
            f.wait_recv()
        self.to_sibling(self.at(self.pos(2, 2)))

    def complete(self):
        for c in self.forwarded:
            c.wait_recv()


def forward_kernel(w_ref, bc_ref, dt_ref, pk_ref, hid, cot_ref, gain, taps_bc, g_ref, gb_ref,
                   pk_out, x_pre_out, x_conv_out, d_x_out, normed_t_out, cot_t_out, state_out, bc_pre_out, bc_conv_out,
                   steps_out, rates_out, cols_out, cum_row_out, step_row_out, dec_out, result_out,
                   out_in_out, d_z_out, gain_part_out, skip_part_out, d_cols_out, d_bc_out, d_state_out,
                   normed_t2_out, cot_t2_out, out_in2_out, d_z2_out, *scr):
    (pk, x_pre, x_conv, normed_t, cot_t, state, bc_pre, bc_conv, steps, rates, cols, cum_row, step_row, dec,
     result, out_in, d_z, gain_part, skip_part, d_cols, d_bc, d_state,
     cot, normed, halo, dts, dt_own, small_all, zb, yb, db, wbuf, gram, d_gram, local, rec_a, out_b, dec_own, square, inner,
     scales, acc, d_c,
     ts, tr, cs, cr, bs, br, ps, pr, qs, qr, es, er, fs, fr, gs, gr, ds, dr, hs, hr, lsem, wsem, osem, ysem, xs, xr) = scr
    rc = Sender()
    me = my_place()
    core = lax.axis_index("core")
    x, ylo = me["x"], lax.axis_index("ylo")
    block = lax.axis_index("z") * 2 + lax.axis_index("yhi")
    arrived = greet()
    writes = []

    def out(src, dst):
        c = pltpu.make_async_copy(src, dst, osem.at[len(writes)])
        c.start()
        writes.append(c)

    cot_c = pltpu.make_async_copy(cot_ref, cot, lsem.at[3])
    cot_c.start()
    own_w = pltpu.make_async_copy(w_ref, g_ref.at[:, me["z"], me["y"] // 2, ylo, x, core], lsem.at[0])
    own_w.start()
    arrived()

    gx, gz, go = [[Gather(rc, g_ref, w_ref, (ts, tr, cs, cr), i, r) for r in range(3)] for i in range(3)]

    def each(group, name, *args):
        for c in group:
            getattr(c, name)(*args)

    each(gx, "straight", 0)
    dt_c = to_peers(rc, lambda p: dt_ref, dts, ps, pr, block)

    def small(lo, n):
        cols = pl.ds(lo, n)
        sems = iter(range(9 * (lo // 256), 9 * (lo // 256) + 9))

        def push(src, dst, device):
            k = next(sems)
            return rc(src, dst, bs.at[k], br.at[k], device)

        def at(yl, x_at):
            return gb_ref.at[yl, x_at, core, :, cols]

        def over_y(src):
            own = pltpu.make_async_copy(src, at(ylo, x), lsem.at[1 + lo // 256])
            own.start()
            return [push(src, at(ylo, x), {"ylo": 1 - ylo}), push(src, at(ylo, x), neighbour("core", 1))], own

        def over_x(first, own):
            first[0].wait_recv()
            own.wait()
            line = gb_ref.at[:, x, core, :, cols]
            other = at(1 - ylo, x)
            rest = [push(line, line, neighbour("x", d)) for d in (1, 2, 3)]
            return rest, [first[1], push(other, other, neighbour("core", 1))]

        def to_sibling(rest, cores):
            for d in (1, 2, 3):
                rest[d - 1].wait_recv()
                line = gb_ref.at[:, lax.rem(x + 4 - d, 4), core, :, cols]
                cores.append(push(line, line, neighbour("core", 1)))
            return cores

        return over_y, over_x, to_sibling

    bc_y, bc_x, bc_end = small(0, 256)
    dt_y, dt_x, dt_end = small(256, 128)
    bc_s = bc_y(bc_ref)
    halo_c = rc(hid.at[pl.ds(ROWS - HALO, HALO)], halo, hs, hr, block_device(lax.rem(block + 1, 8)))
    each(gz, "straight", 0)
    each(go, "straight", 0)
    pk_c = to_peers(rc, lambda p: pk_ref, pk, qs, qr, block)
    dts[block] = dt_ref[...]
    pk[block] = pk_ref[...]

    def normalize(part, at):
        v = part[...].astype(F32)
        r = lax.rsqrt(jnp.mean(v * v, axis=1, keepdims=True) + EPS)
        normed[pl.ds(at, part.shape[0])] = (v * r * gain[...]).astype(BF16)

    normalize(hid, HALO)
    own_w.wait()
    bc_s = bc_x(*bc_s)
    each(gx, "line", 0)
    each(gx, "straight", 1)

    for c in dt_c:
        c.wait_recv()
    total = f32(dts.at[0])
    for i in range(1, 8):
        total = total + f32(dts.at[i])
    dt_own[...] = total.astype(BF16)
    dt_s = dt_y(dt_own)
    normed_t[...] = normed[HALO:, :].T.reshape(8, 2, 96, ROWS)
    out(normed_t, normed_t_out)
    dt_s = dt_x(*dt_s)
    each(gx, "line", 1)
    each(gx, "near")
    each(gz, "line", 0)
    each(gz, "straight", 1)
    cot_c.wait()
    cot_t[...] = cot[...].T.reshape(8, 2, 96, ROWS)
    out(cot_t, cot_t_out)
    halo_c.wait_recv()
    normalize(halo, 0)

    @pl.when(block == 0)
    def _():
        normed[pl.ds(0, HALO)] = jnp.zeros((HALO, WIDTH), BF16)

    each(go, "line", 0)
    for c in pk_c:
        c.wait_recv()
    out(pk, pk_out)
    b_core = bc_end(*bc_s) + dt_end(*dt_s)
    for c in b_core:
        c.wait_recv()
    small_in = pltpu.make_async_copy(gb_ref, small_all, lsem.at[1])
    small_in.start()
    each(gx, "pass_on")
    each(go, "straight", 1)
    small_in.wait()

    def row(lo):
        pieces = [pk[m, 6:7, lo : lo + HEADS] for m in range(GROUPS)]
        return jnp.concatenate(pieces + [jnp.zeros((1, 80), F32)], axis=1)

    rates[0:1] = row(0)
    rates[1:2] = row(HEADS)
    rates[2:8] = jnp.zeros((6, 128), F32)
    little = dot(normed[...], small_all[...].reshape(WIDTH, COLS))
    bc_pre[...] = little[:, :256]
    pre = conv_pre(little[:, :256], taps_bc[...])
    bc_conv[...] = (pre * jax.nn.sigmoid(pre)).astype(BF16)
    shifted = little[HALO:, 256:384] + rates[1:2]
    steps[...] = shifted
    step = softplus(shifted)
    decay = -step * jnp.exp(rates[0:1])
    cum = dot(triangle(False).astype(F32), decay, precision=lax.Precision.HIGHEST)
    cum_t = cum.T
    step_t = step.T
    lasts = jnp.broadcast_to(jnp.exp(cum_t[:, ROWS - 1 : ROWS]), (128, 128))
    for m in range(GROUPS):
        at = slice(HEADS * m, HEADS * m + 8)
        cols[m] = jnp.concatenate([cum[:, at], step[:, at]], axis=1)
        cum_row[m] = cum_t[HEADS * m : HEADS * m + 8]
        step_row[m] = step_t[HEADS * m : HEADS * m + 8]
        dec_own[m] = lasts[HEADS * m : HEADS * m + 8]
    dec_c = to_peers(rc, lambda p: dec_own.at[p], dec, ds, dr, block)
    dec[block] = dec_own[block]
    gram[...] = jnp.where(triangle(False), dot(bc_conv[:, 128:], bc_conv[:, :128], (1, 1)), 0.0)
    out(bc_pre, bc_pre_out)
    out(bc_conv, bc_conv_out)
    out(steps, steps_out)
    out(rates, rates_out)
    out(cols, cols_out)
    out(cum_row, cum_row_out)
    out(step_row, step_row_out)
    each(gz, "line", 1)
    each(gz, "near")
    each(gx, "last")
    each(gx, "complete")

    g_flat = g_ref.reshape(3, GROUPS, WIDTH, COLS)

    def weights(item, m, buf):
        return pltpu.make_async_copy(g_flat.at[item, m], wbuf.at[buf, m], wsem.at[buf, m])

    def load(item, buf):
        for m in range(GROUPS):
            weights(item, m, buf).start()

    def pairs(item, buf, lo, hi, body):
        @pl.loop(lo, hi)
        def _(i):
            for k in range(2):
                weights(item, 2 * i + k, buf).wait()
            body(i, jnp.concatenate([wbuf[buf, 2 * i], wbuf[buf, 2 * i + 1]], axis=1))

    load(0, 0)

    def to_owner(m):
        return pltpu.make_async_remote_copy(src_ref=local.at[m], dst_ref=rec_a.at[block], send_sem=es.at[m], recv_sem=er.at[block],
                                            device_id=block_device(m), device_id_type=MESHID)

    def second_pair(i, w):
        both = dot(normed[...], w)
        for k in range(2):
            m = 2 * i + k
            ext = both[:, COLS * k : COLS * k + COLS]
            x_pre[m] = ext
            pre = conv_pre(ext, pk[m])
            xc = (pre * jax.nn.sigmoid(pre)).astype(BF16)
            x_conv[m] = xc
            cum, step = cols[m][:, :8], cols[m][:, 8:]
            weighted = (xc.astype(F32) * spread(step * jnp.exp(cum[ROWS - 1 : ROWS] - cum))).astype(BF16)
            local[m] = dot(weighted, bc_conv[:, :128], (0, 0)).astype(BF16)
            pl.when(m != block)(lambda m=m: to_owner(m).start())

    pairs(0, 0, 0, 4, second_pair)
    rec_a[block] = local[block]
    out(x_pre, x_pre_out)
    out(x_conv, x_conv_out)

    top, low = slice(0, HALF), slice(HALF, ROWS)

    def decays(cum, rows, h):
        col, row = cum[:, h : h + 1], rows[h : h + 1, :]
        return (jnp.exp(jnp.minimum(col[top] - row[:, top], 0.0)), jnp.exp(jnp.minimum(col[low] - row, 0.0)))

    def scan_group(m):
        xc = x_conv[m]
        cum = cols[m][:, :8]
        rows = cum_row[m]
        step_rows = step_row[m]
        parts = []
        for h in range(HEADS):
            xh = xc[:, 64 * h : 64 * h + 64]
            step = step_rows[h : h + 1, :]
            upper, lower = decays(cum, rows, h)
            upper = (upper * gram[top, top] * step[:, top]).astype(BF16)
            lower = (lower * gram[low] * step).astype(BF16)
            parts.append(jnp.concatenate([dot(upper, xh[top]), dot(lower, xh)], axis=0))
        yb[m] = jnp.concatenate(parts, axis=1) + spread(pk[m, 6:7, 12:20]) * xc.astype(F32)

    each(go, "line", 1)
    each(gz, "pass_on")
    each(go, "near")
    pl.loop(0, GROUPS)(scan_group)
    for c in dec_c:
        c.wait_recv()
    out(dec, dec_out)

    def exchanged(src, sends, recvs):
        for d in range(1, 8):
            other = lax.rem(block + d, 8)
            pltpu.make_async_remote_copy(src_ref=src.at[other], dst_ref=rec_a.at[other], send_sem=sends.at[other],
                                         recv_sem=recvs.at[other], device_id=block_device(other), device_id_type=MESHID).wait()

    def carry(order):
        for h in range(HEADS):
            rows = pl.ds(64 * h, 64)
            run = jnp.zeros((64, 128), F32)
            for i in order:
                out_b[i, rows] = run.astype(BF16)
                run = run * dec[i, pl.ds(h, 1)] + rec_a[i, rows].astype(F32)

    exchanged(local, es, er)
    carry(range(BLOCKS))
    f_c = to_peers(rc, lambda p: out_b.at[p], state, fs, fr, block)
    state[block] = out_b[block]
    each(gz, "last")
    each(go, "pass_on")
    each(gz, "complete")
    load(1, 1)

    def gate_pair(i, w):
        z = dot(normed[HALO:, :], w)
        for k in range(2):
            zb[2 * i + k] = z[:, COLS * k : COLS * k + COLS]

    pairs(1, 1, 0, 4, gate_pair)
    each(go, "last")
    each(go, "complete")
    load(2, 0)

    def cot_pair(i, w):
        d = dot(cot[...], w)
        for k in range(2):
            db[2 * i + k] = d[:, COLS * k : COLS * k + COLS]

    pairs(2, 0, 0, 4, cot_pair)
    for c in f_c:
        c.wait_recv()
        rc.sent(c)
    out(state, state_out)
    square[...] = jnp.zeros_like(square)
    inner[...] = jnp.zeros_like(inner)
    c_mat = bc_conv[:, 128:]

    @pl.loop(0, GROUPS)
    def _(m):
        carried = dot(c_mat, state[m], (1, 1))
        y = yb[m] + spread(jnp.exp(cols[m][:, :8])) * carried
        yb[m] = y
        z = zb[m]
        gated = y * (z * jax.nn.sigmoid(z))
        sq = gated * gated
        ip = db[m] * pk[m, 5:6] * gated
        square[...] += sq[:, :128] + sq[:, 128:256] + sq[:, 256:]
        inner[...] += ip[:, :128] + ip[:, 128:256] + ip[:, 256:]

    r2 = lax.rsqrt(jnp.sum(square[...], axis=1, keepdims=True) / INNER + EPS)
    slope = r2 * r2 * r2 * (jnp.sum(inner[...], axis=1, keepdims=True) / INNER)
    scales[...] = jnp.concatenate([r2, slope, jnp.zeros((ROWS, 6), F32)], axis=1)
    acc[...] = jnp.zeros_like(acc)
    d_c[...] = jnp.zeros_like(d_c)
    d_gram[...] = jnp.zeros_like(d_gram)

    def to_owner_back(m):
        return pltpu.make_async_remote_copy(src_ref=local.at[m], dst_ref=rec_a.at[block], send_sem=gs.at[m], recv_sem=gr.at[block],
                                            device_id=block_device(m), device_id_type=MESHID)

    @pl.loop(0, 4)
    def _(i):
        r2, slope = scales[:, 0:1], scales[:, 1:2]
        for k in range(2):
            m = 2 * i + k
            z, y, d = zb[m], yb[m], db[m]
            gain_row = pk[m, 5:6]
            sig = jax.nn.sigmoid(z)
            act = z * sig
            gated = y * act
            unit = gated * r2
            out_in[m] = (unit * gain_row).astype(BF16)
            gain_part[m] = jnp.sum(d * unit, axis=0, keepdims=True)
            d_gated = r2 * (d * gain_row) - gated * slope
            dy = d_gated * act
            d_z[m] = (d_gated * y * sig * (1.0 + z * (1.0 - sig))).astype(BF16)
            yb[m] = dy
            skip_part[m] = jnp.sum(dy * x_conv[m].astype(F32), axis=0, keepdims=True)
            grown = spread(jnp.exp(cols[m][:, :8]))
            dye = (grown * dy).astype(BF16)
            d_c[...] += dot(dye, state[m])
            local[m] = dot(dye, c_mat, (0, 0)).astype(BF16)
            pl.when(m != block)(lambda m=m: to_owner_back(m).start())
            d_cols[m] = jnp.concatenate([gathered_heads(dy * (grown * dot(c_mat, state[m], (1, 1)))), jnp.zeros((ROWS, 8), F32)],
                                        axis=1)
        acc[...] += dot(jnp.concatenate([out_in[2 * i], out_in[2 * i + 1]], axis=1),
                        jnp.concatenate([wbuf[0, 2 * i], wbuf[0, 2 * i + 1]], axis=1), (1, 1))

    rec_a[block] = local[block]
    result[...] = (hid[...].astype(F32) + acc[...]).astype(BF16)
    across = [rc(src, dst, xs.at[i], xr.at[i], neighbour("core", 1)) for i, (src, dst) in enumerate((
        (cot_t.at[:, 1 - core], cot_t2_out), (out_in, out_in2_out), (normed_t.at[:, 1 - core], normed_t2_out),
        (d_z, d_z2_out)))]
    out(result, result_out)
    out(out_in, out_in_out)
    out(d_z, d_z_out)
    out(gain_part, gain_part_out)
    out(skip_part, skip_part_out)

    def d_x_copy(m):
        return pltpu.make_async_copy(zb.at[m], d_x_out.at[m], ysem.at[m])

    def inner_group(m):
        dy = yb[m]
        dyb = dy.astype(BF16)
        xc = x_conv[m]
        cum = cols[m][:, :8]
        rows = cum_row[m]
        step_rows = step_row[m]
        d_cum = d_cols[m][:, :8]
        lane = lax.broadcasted_iota(jnp.int32, (ROWS, 8), 1)
        parts = []
        sums = []
        for h in range(HEADS):
            xh = xc[:, 64 * h : 64 * h + 64]
            dyh = dyb[:, 64 * h : 64 * h + 64]
            step = step_rows[h : h + 1, :]
            upper, lower = decays(cum, rows, h)
            d_upper = dot(dyh[top], xh[top], (1, 1))
            d_lower = dot(dyh[low], xh, (1, 1))
            up, lo = upper * gram[top, top], lower * gram[low]
            ru, rl = up * d_upper, lo * d_lower
            col = jnp.sum(rl, axis=0, keepdims=True)
            sums.append(jnp.concatenate([col[:, top] + jnp.sum(ru, axis=0, keepdims=True), col[:, low]], axis=1))
            row = jnp.concatenate([jnp.sum(ru * step[:, top], axis=1, keepdims=True),
                                   jnp.sum(rl * step, axis=1, keepdims=True)], axis=0)
            d_cum = jnp.where(lane == h, d_cum + row, d_cum)
            d_gram[top, top] += upper * d_upper * step[:, top]
            d_gram[low] += lower * d_lower * step
            below = dot((lo * step).astype(BF16), dyh[low], (0, 0))
            parts.append(jnp.concatenate([below[top] + dot((up * step[:, top]).astype(BF16), dyh[top], (0, 0)), below[low]],
                                         axis=0))
        sums = jnp.concatenate(sums + [jnp.zeros((2, ROWS), F32)], axis=0).T
        zb[m] = jnp.concatenate(parts, axis=1) + spread(pk[m, 6:7, 12:20]) * dy
        d_x_copy(m).start()
        d_cols[m] = jnp.concatenate([d_cum - sums * cols[m][:, 8:], sums], axis=1)

    pl.loop(0, 4)(inner_group)
    exchanged(local, gs, gr)
    carry(range(BLOCKS - 1, -1, -1))
    b_c = to_peers(rc, lambda p: out_b.at[p], d_state, fs, fr, block)
    d_state[block] = out_b[block]
    pl.loop(4, GROUPS)(inner_group)
    out(d_cols, d_cols_out)
    dg = jnp.where(triangle(False), d_gram[...], 0.0).astype(BF16)
    d_bc[:, :128] = dot(dg, c_mat, (0, 0))
    d_bc[:, 128:] = d_c[...] + dot(dg, bc_conv[:, :128])
    out(d_bc, d_bc_out)
    for c in b_c + across:
        c.wait_recv()
    out(d_state, d_state_out)
    for c in writes:
        c.wait()
    for m in range(GROUPS):
        d_x_copy(m).wait()
    rc.all_sent()


HALF = ROWS // 2
RESULTS = (
    ("pk", (GROUPS, 8, COLS), F32), ("x_pre", (GROUPS, HALO + ROWS, COLS), F32), ("x_conv", (GROUPS, ROWS, COLS), BF16),
    ("d_x", (GROUPS, ROWS, COLS), F32), ("normed_t", (8, 2, 96, ROWS), BF16), ("cot_t", (8, 2, 96, ROWS), BF16),
    ("state", (GROUPS, COLS, 128), BF16), ("bc_pre", (HALO + ROWS, 256), F32), ("bc_conv", (ROWS, 256), BF16),
    ("steps", (ROWS, 128), F32), ("rates", (8, 128), F32), ("cols", (GROUPS, ROWS, 16), F32),
    ("cum_row", (GROUPS, 8, ROWS), F32), ("step_row", (GROUPS, 8, ROWS), F32), ("dec", (BLOCKS, 8, 128), F32),
    ("result", (ROWS, WIDTH), BF16), ("out_in", (GROUPS, ROWS, COLS), BF16), ("d_z", (GROUPS, ROWS, COLS), BF16),
    ("gain_part", (GROUPS, 1, COLS), F32), ("skip_part", (GROUPS, 1, COLS), F32), ("d_cols", (GROUPS, ROWS, 16), F32),
    ("d_bc", (ROWS, 256), F32), ("d_state", (GROUPS, COLS, 128), BF16),
)
SIBLING = (
    ("normed_t2", (8, 96, ROWS), BF16), ("cot_t2", (8, 96, ROWS), BF16), ("out_in2", (GROUPS, ROWS, COLS), BF16),
    ("d_z2", (GROUPS, ROWS, COLS), BF16),
)


def forward(w3, bc, dt, pk, hid, cot, gain, taps_bc):
    hbm = pl.BlockSpec(memory_space=pl.ANY)
    vmem = pl.BlockSpec(memory_space=pltpu.VMEM)
    sem = pltpu.SemaphoreType.DMA

    def v(*shape, dtype=F32):
        return pltpu.VMEM(shape, dtype)

    def b(*shape):
        return v(*shape, dtype=BF16)

    groups = (GROUPS, ROWS, COLS)
    outs = pl.pallas_call(
        forward_kernel,
        out_shape=(sds(3, 4, 2, 2, 4, 2, 96, COLS, dtype=BF16), sds(2, 4, 2, 96, COLS, dtype=BF16),
                   *[sds(*shape, dtype=dtype) for _, shape, dtype in RESULTS + SIBLING]),
        in_specs=[hbm, vmem, vmem, vmem, vmem, hbm, vmem, vmem],
        out_specs=(hbm,) * (2 + len(RESULTS) + len(SIBLING)),
        scratch_shapes=[
            *[pltpu.VMEM(shape, dtype) for name, shape, dtype in RESULTS if name != "d_x"],
            b(ROWS, WIDTH), b(HALO + ROWS, WIDTH), b(HALO, WIDTH), b(BLOCKS, 96, 128), b(96, 128), b(2, 4, 2, 96, COLS),
            v(*groups), v(*groups), v(*groups), b(2, GROUPS, WIDTH, COLS), v(ROWS, ROWS), v(ROWS, ROWS),
            b(GROUPS, COLS, 128), b(GROUPS, COLS, 128), b(GROUPS, COLS, 128), v(GROUPS, 8, 128),
            v(ROWS, 128), v(ROWS, 128), v(ROWS, 8), v(ROWS, WIDTH), v(ROWS, 128),
            sem((90,)), sem((90,)), sem((90,)), sem((90,)), sem((18,)), sem((18,)), sem((8,)), sem((8,)), sem((8,)),
            sem((8,)), sem((8,)), sem((8,)), sem((8,)), sem((8,)), sem((8,)), sem((8,)), sem((8,)), sem((8,)), sem, sem,
            sem((4,)), sem((2, GROUPS)), sem((len(RESULTS),)), sem((GROUPS,)), sem((4,)), sem((4,)),
        ],
        compiler_params=pltpu.CompilerParams(collective_id=0, has_side_effects=True, vmem_limit_bytes=62 * 2**20),
        name="forward_between_devices",
    )(w3, bc, dt, pk, hid, cot, gain, taps_bc)
    return outs[0], outs[1], dict(zip([name for name, _, _ in RESULTS + SIBLING], outs[2:]))


class Total:
    def __init__(self, rc, value, core, xs, yl, yh, zs, send, recv):
        self.rc, self.value, self.core, self.xs, self.yl, self.yh, self.zs = rc, value, core, xs, yl, yh, zs
        self.send, self.recv, self.at = send, recv, 0
        self.me = my_place()

    def push(self, dst, device):
        k = self.at
        self.at += 1
        return self.rc(self.value, dst, self.send.at[k], self.recv.at[k], device)

    def done(self):
        for c in self.flying:
            c.wait_recv()
        for c in self.flying:
            self.rc.sent(c)

    def step(self, j):
        v, me = self.value, self.me
        if j == 0:
            self.flying = [self.push(self.core, neighbour("core", 1))]
        elif j == 1:
            self.done()
            v[...] = v[...] + self.core[...]
            self.xs[me["x"]] = v[...]
            self.flying = [self.push(self.xs.at[me["x"]], neighbour("x", d)) for d in (1, 2, 3)]
        elif j == 2:
            self.done()
            v[...] = (self.xs[0] + self.xs[1]) + (self.xs[2] + self.xs[3])
            self.flying = [self.push(self.yl, {"ylo": 1 - lax.axis_index("ylo")})]
        elif j == 3:
            self.done()
            v[...] = v[...] + self.yl[...]
            self.flying = [self.push(self.yh, {"yhi": 1 - lax.axis_index("yhi")})]
        elif j == 4:
            self.done()
            v[...] = v[...] + self.yh[...]
            self.zs[me["z"]] = v[...]
            self.flying = [self.push(self.zs.at[me["z"]], neighbour("z", d)) for d in (1, 2, 3)]
        elif j == 5:
            self.done()
            v[...] = (self.zs[0] + self.zs[1]) + (self.zs[2] + self.zs[3])


class SmallSum:
    def __init__(self, rc, parts, xs, ys, zs, hs, send, recv):
        self.rc, self.parts, self.xs, self.ys, self.zs, self.hs = rc, parts, xs, ys, zs, hs
        self.send, self.recv = send, recv
        self.me = my_place()

    def step(self, j, out=None):
        rc, me, parts, s, r = self.rc, self.me, self.parts, self.send, self.recv
        ylo = lax.axis_index("ylo")
        if j == 0:
            self.c = [rc(parts.at[:, lax.rem(me["x"] + d, 4)], self.xs.at[d - 1], s.at[d], r.at[d], neighbour("x", d))
                      for d in (1, 2, 3)]
        elif j == 1:
            for c in self.c:
                c.wait_recv()
            for yl in range(2):
                m = parts.at[yl, me["x"]]
                m[...] = (f32(m) + f32(self.xs.at[0, yl]) + f32(self.xs.at[1, yl]) + f32(self.xs.at[2, yl])).astype(BF16)
            self.c = [rc(parts.at[1 - ylo, me["x"]], self.ys, s.at[4], r.at[4], {"ylo": 1 - ylo})]
        elif j == 2:
            self.c[0].wait_recv()
            m = parts.at[ylo, me["x"]]
            m[...] = (f32(m) + f32(self.ys)).astype(BF16)
            self.zs[me["z"]] = m[...]
            self.c = [rc(m, self.zs.at[me["z"]], s.at[4 + d], r.at[4 + d], neighbour("z", d)) for d in (1, 2, 3)]
        elif j == 3:
            for c in self.c:
                c.wait_recv()
            z, hs = self.zs, self.hs
            hs[0] = ((f32(z.at[0]) + f32(z.at[1])) + (f32(z.at[2]) + f32(z.at[3]))).astype(BF16)
            self.c = [rc(hs.at[0], hs.at[1], s.at[8], r.at[8], {"yhi": 1 - lax.axis_index("yhi")})]
        elif j == 4:
            self.c[0].wait_recv()
            out[...] = f32(self.hs.at[0]) + f32(self.hs.at[1])


def part_of(ref, item, pos, lo, n):
    z = slice(None) if pos["z"] is None else pos["z"]
    x = slice(None) if pos["x"] is None else pos["x"]
    if pos["y"] is None:
        yh = yl = slice(None)
    else:
        yh, yl = pos["y"] // 2, lax.rem(pos["y"], 2)
    return ref.at[item, z, yh, yl, x, pl.ds(lo, n)]


class Chunk:
    def __init__(self, rc, own, out, bufs, sems, item, slot, wide, r):
        self.rc, self.own, self.out, self.item, self.slot, self.r = rc, own, out, item, slot, r
        full, half, second, third = bufs
        self.full, self.half = full[r].at[wide], half[r].at[wide]
        self.direct = {1: second[r].at[slot], 2: third.at[slot * 3 + r]}
        self.send, self.recv = sems
        self.base = (slot * 3 + r) * 10
        self.me = my_place()

    def slab(self, st, d, lo=0, n=SUB):
        p = {a: (self.me[a] if i < st else None) for i, a in enumerate(ORDERS[self.r])}
        a = ORDERS[self.r][st]
        p[a] = lax.rem(self.me[a] + (d + 4), 4)
        return part_of(self.own, self.slot, p, self.r * SUB + lo, n)

    def loop(self, st, body):
        sizes = []
        for a, n in (("z", (4,)), ("y", (2, 2)), ("x", (4,))):
            if ORDERS[self.r].index(a) > st:
                sizes += n
        if not sizes:
            body(())
        elif len(sizes) == 1 or sizes == [2, 2]:
            for i in range(4):
                body((i,) if len(sizes) == 1 else (i // 2, i % 2))
        else:
            @pl.loop(0, 4)
            def _(i):
                for k in range(4):
                    if sizes == [4, 4]:
                        body((i, k))
                    elif sizes == [4, 2, 2]:
                        body((i, k // 2, k % 2))
                    else:
                        body((i // 2, lax.rem(i, 2), k))

    def push(self, k, src, dst, st, d):
        t = self.base + k
        return self.rc(src, dst, self.send.at[t], self.recv.at[t], neighbour(ORDERS[self.r][st], d))

    def far(self):
        self.far_c = [self.push(i, self.slab(0, 2, 16 * i, 16), self.half.at[i], 0, d) for i, d in enumerate((1, -1))]

    def near(self):
        self.near_c = []
        for i, d in enumerate((1, -1)):
            self.far_c[i].wait_recv()
            mine = self.slab(0, d, 16 * i, 16)

            def add(index, mine=mine, i=i):
                m = mine.at[index]
                m[...] = m[...] + self.half[(i, *index)]

            self.loop(0, add)
            self.near_c.append(self.push(2 + i, self.slab(0, d), self.full.at[i], 0, d))

    def straight(self, st):
        self.straight_c = [self.push(1 + 3 * st + d - 1, self.slab(st, d), self.direct[st].at[d - 1], st, d) for d in (1, 2, 3)]

    def step(self, j):
        if j == 0:
            self.far()
        elif j == 1:
            self.near()
        elif j == 2:
            for c in self.near_c:
                c.wait_recv()
            mine = self.slab(0, 0)

            def add(index):
                m = mine.at[index]
                m[...] = (f32(m) + f32(self.full.at[(0, *index)]) + f32(self.full.at[(1, *index)])).astype(BF16)

            self.loop(0, add)
            self.straight(1)
        else:
            for c in self.straight_c:
                c.wait_recv()
            st = j - 2
            mine = self.slab(st, 0)
            got = self.direct[st]

            def total(index):
                m = mine.at[index] if index else mine
                return (f32(m) + f32(got.at[(0, *index)])) + (f32(got.at[(1, *index)]) + f32(got.at[(2, *index)]))

            if st == 1:
                def add(index):
                    mine[index] = total(index).astype(BF16)

                self.loop(1, add)
                self.straight(2)
            else:
                self.out[self.item, pl.ds(self.r * SUB, SUB)] = total(())


def backward_kernel(g_ref, x_conv_ref, d_x_ref, x_pre_ref, cols_ref, d_cols_ref, cot_t_ref, cot_t2_ref, out_in_ref, out_in2_ref,
                    normed_t_ref, normed_t2_ref, d_z_ref, d_z2_ref, state_ref, d_state_ref, w_small_ref, hid_ref, cot_ref,
                    taps, d_bc_in, bc_pre, bc_conv, taps_bc, shifted, rates, gain, gain_part, skip_part,
                    out_ref, sout_ref, vout_ref, nout_ref, grad_hidden, *scr):
    (own, l_c, l_c2, l_n, l_n2, rhs_o, rhs_z, rhs_x, state, d_state, w_small, hid, cot, tails, halo_src, halo_dst, acc, wbuf,
     bxc, bdx, bxp, bcols, bdc, d_b, d_all, parts, small2, s_xs, s_ys, s_zs, s_hs,
     v_core, v_xs, v_yl, v_yh, v_zs, n_core, n_xs, n_yl, n_yh, n_zs) = scr[:41]
    bufs = [scr[41:44], scr[44:47], scr[47:50], scr[50]]
    (t_s, t_r, x_s, x_r, h_s, h_r, m_s, m_r, ss, sr, vs, vr, ns, nr, wsem, lsem, isem, freed) = scr[51:]
    rc = Sender()
    core = lax.axis_index("core")
    block = lax.axis_index("z") * 2 + lax.axis_index("yhi")
    arrived = greet()

    loads = {}

    def load_in(name, *pairs):
        loads[name] = []
        for src, dst in pairs:
            c = pltpu.make_async_copy(src, dst, isem.at[sum(len(v) for v in loads.values())])
            c.start()
            loads[name].append(c)

    def ready(name):
        for c in loads[name]:
            c.wait()

    load_in("o", (cot_t_ref.at[:, core], l_c), (cot_t2_ref, l_c2), (out_in_ref, rhs_o.at[0]), (out_in2_ref, rhs_o.at[1]))
    load_in("z", (normed_t_ref.at[:, core], l_n), (normed_t2_ref, l_n2), (d_z_ref, rhs_z.at[0]), (d_z2_ref, rhs_z.at[1]))
    load_in("s", (state_ref, state), (d_state_ref, d_state))

    def chunks(item, slot, wide):
        return [Chunk(rc, own, out_ref, bufs, (t_s, t_r), item, slot, wide, r) for r in range(3)]

    def steps(cs, j):
        for c in cs:
            c.step(j)

    def both_tokens(own_t, other_t):
        return jnp.concatenate([own_t[...].reshape(768, ROWS), other_t[...].reshape(768, ROWS)], axis=1)

    def gradient(left, left2, rhs, slot):
        def one(m):
            v = dot(both_tokens(left, left2), jnp.concatenate([rhs[0, m], rhs[1, m]], axis=0))
            own[slot, m // 2, lax.rem(m, 2)] = v.astype(BF16).reshape(2, 4, 96, COLS)

        pl.loop(0, GROUPS)(one)

    oc, zc, xc_ = chunks(2, 0, 0), chunks(1, 1, 1), chunks(0, 2, 0)
    ready("o")
    gradient(l_c, l_c2, rhs_o, 0)
    arrived()
    steps(oc, 0)
    ready("z")

    streams = ((x_conv_ref, bxc), (d_x_ref, bdx), (x_pre_ref, bxp), (cols_ref, bcols), (d_cols_ref, bdc))

    def load(m):
        k = lax.rem(m, 2)
        return [pltpu.make_async_copy(src.at[m], dst.at[k], lsem.at[k, i]) for i, (src, dst) in enumerate(streams)]

    for c in load(0):
        c.start()
    gradient(l_n, l_n2, rhs_z, 1)
    steps(zc, 0)
    ready("s")
    load_in("end", (w_small_ref, w_small), (hid_ref, hid), (cot_ref, cot))

    def fifth_group(m):
        k = lax.rem(m, 2)

        @pl.when(m < GROUPS - 1)
        def _():
            for c in load(m + 1):
                c.start()

        for c in load(m):
            c.wait()
        ds = d_state[m]
        xf = bxc[k].astype(F32)
        cum, step = bcols[k][:, :8], bcols[k][:, 8:]
        last = cum[ROWS - 1 : ROWS]
        tail = jnp.exp(last - cum)
        weights = step * tail
        wide = spread(weights)
        d_weighted = dot(bc_conv[:, :128], ds, (1, 1))
        d_b[...] += dot((xf * wide).astype(BF16), ds)
        dx = bdx[k] + wide * d_weighted
        d_weights = gathered_heads(d_weighted * xf)
        both = weights * d_weights
        lane = lax.broadcasted_iota(jnp.int32, (1, 8), 1)
        product = jnp.sum(state[m].astype(F32) * ds.astype(F32), axis=1, keepdims=True)
        d_last = jnp.sum(both, axis=0, keepdims=True)
        for h in range(HEADS):
            dots = jnp.sum(product[64 * h : 64 * h + 64], axis=0, keepdims=True)
            d_last = jnp.where(lane == h, d_last + jnp.exp(last) * dots, d_last)
        row = lax.broadcasted_iota(jnp.int32, (ROWS, 8), 0)
        d_cum = bdc[k][:, :8] - both
        d_cum = jnp.where(row == ROWS - 1, d_cum + d_last, d_cum)
        d_all[m] = jnp.concatenate([d_cum, bdc[k][:, 8:] + tail * d_weights], axis=1)
        ext = bxp[k]
        tap = taps[m]
        pre = conv_pre(ext, tap)
        sig = jax.nn.sigmoid(pre)
        dp = dx * (sig * (1.0 + pre * (1.0 - sig)))
        vout_ref[m] = conv_grads(dp, ext, gain_part[m], skip_part[m])
        whole_dx = conv_transposed(jnp.concatenate([dp, jnp.zeros((8, COLS), F32)], axis=0), tap)
        rhs_x[0, m] = whole_dx.astype(BF16)
        tails[m] = whole_dx[ROWS - 16 :]
        halo_src[m] = dp[:8]

    d_b[...] = jnp.zeros_like(d_b)
    pl.loop(0, 2)(fifth_group)
    steps(oc, 1)
    pl.loop(2, GROUPS)(fifth_group)

    d_bc = jnp.concatenate([d_bc_in[:, :128] + d_b[...], d_bc_in[:, 128:]], axis=1)
    ext = bc_pre[...]
    pre = conv_pre(ext, taps_bc[...])
    sig = jax.nn.sigmoid(pre)
    dp_bc = d_bc * (sig * (1.0 + pre * (1.0 - sig)))
    halo_src[GROUPS] = jnp.concatenate([dp_bc[:8], jnp.zeros((8, 128), F32)], axis=1)
    halo = rc(halo_src, halo_dst, h_s, h_r, block_device(lax.rem(block + 7, 8)))
    steps(zc, 1)
    steps(oc, 2)
    for a in "xyz":
        for s in (1, -1):
            pl.semaphore_signal(freed, inc=1, device_id=neighbour(a, s), device_id_type=MESHID)
    zero8 = jnp.zeros((1, 256), F32)
    d_cum = jnp.concatenate([d_all[m][:, :HEADS] for m in range(GROUPS)] + [jnp.zeros((ROWS, 80), F32)], axis=1)
    d_step = jnp.concatenate([d_all[m][:, 8 : 8 + HEADS] for m in range(GROUPS)] + [jnp.zeros((ROWS, 80), F32)], axis=1)
    d_decay = dot(triangle(True).astype(F32), d_cum, precision=lax.Precision.HIGHEST)
    rate = -jnp.exp(rates[0:1])
    v = shifted[...]
    d_dt = (d_step + rate * d_decay) * jax.nn.sigmoid(v)
    log_grad = jnp.sum(d_decay * (softplus(v) * rate), axis=0, keepdims=True)
    shift_grad = jnp.sum(d_dt, axis=0, keepdims=True)
    bc_rows = conv_grads(dp_bc, ext, jnp.concatenate([log_grad, shift_grad], axis=1), zero8)
    vout_ref[GROUPS] = jnp.concatenate([bc_rows, jnp.zeros((8, 128), F32)], axis=1)
    vec = Total(rc, vout_ref, v_core, v_xs, v_yl, v_yh, v_zs, vs, vr)
    vec.step(0)

    halo.wait_recv()
    inside = block < 7

    def below(k):
        return jnp.where(inside, halo_dst[k], 0.0)

    def across(m):
        return pltpu.make_async_remote_copy(src_ref=rhs_x.at[0, m], dst_ref=rhs_x.at[1, m], send_sem=x_s.at[m],
                                            recv_sem=x_r.at[m], device_id=neighbour("core", 1), device_id_type=MESHID)

    def fix(m):
        ext = jnp.concatenate([jnp.zeros((16, COLS), F32), below(m)], axis=0)
        rhs_x[0, m, pl.ds(ROWS - 16, 16)] = (tails[m] + conv_transposed(ext, taps[m], 16)).astype(BF16)
        across(m).start()

    pl.loop(0, GROUPS)(fix)
    d_bc = conv_transposed(jnp.concatenate([dp_bc, below(GROUPS)[:, :256]], axis=0), taps_bc[...])
    small2[0] = jnp.concatenate([d_bc, d_dt], axis=1).astype(BF16)
    small_c = rc(small2.at[0], small2.at[1], m_s, m_r, neighbour("core", 1))
    vec.step(1)

    def weights(m):
        k = lax.rem(m, 2)
        return [pltpu.make_async_copy(g_ref.at[i, m], wbuf.at[k, i], wsem.at[k, i]) for i in range(2)]

    for c in weights(0):
        c.start()
    for m in range(GROUPS):
        across(m).wait()
    gradient(l_n, l_n2, rhs_x, 2)
    pl.semaphore_wait(freed, 6)
    steps(xc_, 0)
    small_c.wait_recv()
    parts[...] = dot(both_tokens(l_n, l_n2), small2[...].reshape(2 * ROWS, COLS)).astype(BF16).reshape(2, 4, 96, COLS)
    ready("end")
    acc[...] = dot(small2[0], w_small[...], (1, 1))

    def input_group(m):
        k = lax.rem(m, 2)

        @pl.when(m < GROUPS - 1)
        def _():
            for c in weights(m + 1):
                c.start()

        for c in weights(m):
            c.wait()
        lhs = jnp.concatenate([rhs_x[0, m], rhs_z[0, m]], axis=1)
        rhs = jnp.concatenate([wbuf[k, 0], wbuf[k, 1]], axis=1)
        acc[...] += dot(lhs, rhs, (1, 1))

    pl.loop(0, 4)(input_group)
    vec.step(2)
    steps(xc_, 1)
    sums = SmallSum(rc, parts, s_xs, s_ys, s_zs, s_hs, ss, sr)
    sums.step(0)
    pl.loop(4, GROUPS)(input_group)
    v = hid[...].astype(F32)
    r = lax.rsqrt(jnp.mean(v * v, axis=1, keepdims=True) + EPS)
    unit = v * r
    dn = acc[...]
    gain_grad = jnp.sum(dn * unit, axis=0, keepdims=True)
    for i in range(4):
        nout_ref[0, pl.ds(i, 1)] = gain_grad[:, COLS * i : COLS * i + COLS]
    nout_ref[0, pl.ds(4, 4)] = jnp.zeros((4, COLS), F32)
    nvec = Total(rc, nout_ref, n_core, n_xs, n_yl, n_yh, n_zs, ns, nr)
    nvec.step(0)
    vec.step(3)
    d_in = dn * gain[...]
    grad_hidden[...] = r * (d_in - unit * jnp.mean(d_in * unit, axis=1, keepdims=True)) + cot[...].astype(F32)
    nvec.step(1)
    steps(zc, 2)
    steps(oc, 3)
    vec.step(4)
    nvec.step(2)
    steps(xc_, 2)
    sums.step(1)
    nvec.step(3)
    vec.step(5)
    sums.step(2)
    nvec.step(4)
    steps(oc, 4)
    steps(zc, 3)
    steps(xc_, 3)
    sums.step(3)
    nvec.step(5)
    steps(zc, 4)
    sums.step(4, sout_ref)
    steps(xc_, 4)
    rc.all_sent()


def backward(w_all, r, w_small, hid, cot, taps_bc, gain):
    hbm = pl.BlockSpec(memory_space=pl.ANY)
    vmem = pl.BlockSpec(memory_space=pltpu.VMEM)
    sem = pltpu.SemaphoreType.DMA

    def buf(*shape, dtype=BF16):
        return pltpu.VMEM((*shape, COLS), dtype)

    def v(*shape, dtype=F32):
        return pltpu.VMEM(shape, dtype)

    def b(*shape):
        return v(*shape, dtype=BF16)

    scratch = [
        buf(3, 4, 2, 2, 4, 96), b(8, 96, ROWS), b(8, 96, ROWS), b(8, 96, ROWS), b(8, 96, ROWS),
        buf(2, GROUPS, ROWS), buf(2, GROUPS, ROWS), buf(2, GROUPS, ROWS), b(GROUPS, COLS, 128), b(GROUPS, COLS, 128),
        buf(WIDTH), b(ROWS, WIDTH), b(ROWS, WIDTH),
        buf(GROUPS, 16, dtype=F32), buf(GROUPS + 1, 8, dtype=F32), buf(GROUPS + 1, 8, dtype=F32),
        v(ROWS, WIDTH), buf(2, 2, WIDTH),
        buf(2, ROWS), buf(2, ROWS, dtype=F32), buf(2, HALO + ROWS, dtype=F32), v(2, ROWS, 16), v(2, ROWS, 16),
        v(ROWS, 128), v(GROUPS, ROWS, 16), buf(2, 4, 96), buf(2, ROWS), buf(3, 2, 96), buf(96), buf(4, 96), buf(2, 96),
    ]
    for n in (GROUPS + 1, 1):
        one = buf(n, 8, dtype=F32)
        four = buf(4, n, 8, dtype=F32)
        scratch += [one, four, one, one, four]
    scratch += [buf(2, 2, 4, 2, 2, SUB), buf(2, 2, 4, 4, SUB), buf(2, 2, 2, 2, 4, SUB)]
    scratch += [buf(2, 2, 4, 2, 2, 16), buf(2, 2, 4, 4, 16), buf(2, 2, 2, 2, 4, 16)]
    scratch += [buf(3, 3, 4, SUB), buf(3, 3, 4, SUB), buf(3, 3, 2, 2, SUB), buf(9, 3, SUB)]
    scratch += [sem((90,)), sem((90,)), sem((8,)), sem((8,)), sem, sem, sem, sem, sem((9,)), sem((9,)), sem((9,)), sem((9,)),
                sem((9,)), sem((9,)), sem((2, 2)), sem((2, 5)), sem((13,)), pltpu.SemaphoreType.REGULAR]
    names = ("x_conv", "d_x", "x_pre", "cols", "d_cols", "cot_t", "cot_t2", "out_in", "out_in2", "normed_t", "normed_t2", "d_z",
             "d_z2", "state", "d_state")
    return pl.pallas_call(
        backward_kernel,
        out_shape=(sds(3, 96, COLS), sds(96, COLS), sds(GROUPS + 1, 8, COLS), sds(1, 8, COLS), sds(ROWS, WIDTH)),
        in_specs=[hbm] * 19 + [vmem] * 10,
        out_specs=(vmem,) * 5,
        scratch_shapes=scratch,
        compiler_params=pltpu.CompilerParams(collective_id=1, has_side_effects=True, vmem_limit_bytes=63 * 2**20),
        name="backward_between_devices",
    )(w_all, *[r[name] for name in names], w_small, hid, cot, r["pk"], r["d_bc"], r["bc_pre"], r["bc_conv"], taps_bc,
      r["steps"], r["rates"], gain, r["gain_part"], r["skip_part"])
def shards(hidden, grad_out, norm_gain, w_zx, w_bc, w_dt, conv_x, conv_bc, a_log, dt_bias, d_skip, gate_gain, w_out):
    index = lax.axis_index(MP)
    heads = jnp.concatenate([a_log, dt_bias, d_skip, jnp.zeros((COLS - 3 * HEADS,), F32)])[None]
    packed = jnp.concatenate([conv_x, gate_gain[None], heads, jnp.zeros((1, COLS), F32)])
    steps_own = lax.dynamic_update_slice(jnp.zeros((96, 128), BF16), w_dt, (0, index * HEADS))
    taps_bc = jnp.pad(conv_bc, ((0, 3), (0, 0)))
    gain = norm_gain[None]
    w_all, w_small, r = forward(
        jnp.stack([w_zx[:, 1], w_zx[:, 0], w_out.T]), w_bc, steps_own, packed, hidden, grad_out, gain, taps_bc)
    w_all = w_all.reshape(3, GROUPS, WIDTH, COLS)
    w_small = w_small.reshape(WIDTH, COLS)
    owned, small, vector, norm_sum, grad_hidden = backward(w_all, r, w_small, hidden, grad_out, taps_bc, gain)

    def own(flat):
        return lax.dynamic_slice_in_dim(flat, index * HEADS, HEADS, flat.ndim - 1)

    mine = lax.dynamic_index_in_dim(vector, index, 0, keepdims=False)
    return (
        r["result"],
        grad_hidden,
        norm_sum[0, :4].reshape(WIDTH),
        jnp.stack([owned[1], owned[0]], axis=1),
        small[:, :256],
        own(small[:, 256:304]),
        mine[:5],
        vector[GROUPS, :5, :256],
        own(vector[GROUPS, 5, :48]),
        own(vector[GROUPS, 5, 128:176]),
        mine[6].reshape(HEADS, 64).sum(axis=1),
        mine[5],
        owned[2].T,
    )


def solution(mesh):
    finer = Mesh(mesh.devices.reshape(2, 4, 2, 4, 2), DP_MP)
    rows = P(DP_MP, None)
    placed = (rows, rows, P(), P(DP, None, MP), P(DP, None), P(DP, MP), P(None, MP), P(), P(MP), P(MP), P(MP), P(MP),
              P(MP, DP))
    return jax.shard_map(
        shards,
        mesh=finer,
        in_specs=placed,
        out_specs=(rows, rows, P(), P(DP, None, MP), P(DP, None), P(DP, MP), P(None, MP), P(), P(MP), P(MP), P(MP), P(MP),
                   P(MP, DP)),
        check_vma=False,
    )
```

```python
import jax
import jax.numpy as jnp
from jax import lax
from jax.experimental import pallas as pl
from jax.experimental.pallas import tpu as pltpu
from jax.sharding import Mesh
from jax.sharding import PartitionSpec as P

MP = ("z", "yhi")
DP = ("ylo", "x", "core")
DP_MP = DP + MP
BLOCKS = 8
F32 = jnp.float32
BF16 = jnp.bfloat16
ROWS = 256
WIDTH = 1536
GROUPS = 8
COLS = 384
HEADS = 6
HALO = 16
EPS = 1e-05
INNER = GROUPS * COLS
VMEM_LIMIT = 56 * 2**20


def dot(a, b, contract=(1, 0), precision=None):
    return lax.dot_general(
        a, b, (((contract[0],), (contract[1],)), ((), ())),
        preferred_element_type=F32, precision=precision,
    )


def spread(per_head):
    rows = per_head.shape[0]
    low = lax.broadcasted_iota(jnp.int32, (rows, 128), 1) < 64
    tiles = [
        jnp.where(low, per_head[:, 2 * i : 2 * i + 1], per_head[:, 2 * i + 1 : 2 * i + 2])
        for i in range(COLS // 128)
    ]
    return jnp.concatenate(tiles, axis=1)


def gathered_heads(values):
    rows = values.shape[0]
    low = lax.broadcasted_iota(jnp.int32, (rows, 128), 1) < 64
    lane = lax.broadcasted_iota(jnp.int32, (rows, 8), 1)
    out = jnp.zeros((rows, 8), F32)
    for i in range(COLS // 128):
        tile = values[:, 128 * i : 128 * i + 128]
        first = jnp.sum(jnp.where(low, tile, 0.0), axis=1, keepdims=True)
        both = jnp.sum(tile, axis=1, keepdims=True)
        out = jnp.where(lane == 2 * i, first, out)
        out = jnp.where(lane == 2 * i + 1, both - first, out)
    return out


def softplus(v):
    return jnp.maximum(v, 0.0) + jnp.log1p(jnp.exp(-jnp.abs(v)))


def conv_pre(ext, taps):
    total = taps[4:5]
    for j in range(4):
        total = total + ext[HALO - 3 + j : HALO - 3 + j + ROWS] * taps[j : j + 1]
    return total


def conv_transposed(ext, taps, rows=ROWS):
    total = ext[3 : 3 + rows] * taps[0:1]
    for j in range(1, 4):
        total = total + ext[3 - j : 3 - j + rows] * taps[j : j + 1]
    return total


def conv_grads(dpre, ext, sixth, seventh):
    rows = [
        jnp.sum(dpre * ext[HALO - 3 + j : HALO - 3 + j + ROWS], axis=0, keepdims=True)
        for j in range(4)
    ]
    rows.append(jnp.sum(dpre, axis=0, keepdims=True))
    rows += [sixth, seventh, jnp.zeros((1, dpre.shape[1]), F32)]
    return jnp.concatenate(rows, axis=0)


def triangle(upper):
    row = lax.broadcasted_iota(jnp.int32, (ROWS, ROWS), 0)
    col = lax.broadcasted_iota(jnp.int32, (ROWS, ROWS), 1)
    return row <= col if upper else row >= col


def sds(*shape, dtype=F32):
    return jax.ShapeDtypeStruct(shape, dtype)


def params():
    return pltpu.CompilerParams(vmem_limit_bytes=VMEM_LIMIT)


MESHID = pl.DeviceIdType.MESH
ORDERS = (("x", "y", "z"), ("y", "z", "x"), ("z", "x", "y"))
SUB = 32


def neighbour(axis, s):
    if axis == "core":
        return {"core": 1 - lax.axis_index("core")}
    if axis == "y":
        y = lax.rem(lax.axis_index("yhi") * 2 + lax.axis_index("ylo") + (s + 4), 4)
        return {"ylo": lax.rem(y, 2), "yhi": y // 2}
    return {axis: lax.rem(lax.axis_index(axis) + (s + 4), 4)}


def my_place():
    return {"x": lax.axis_index("x"), "z": lax.axis_index("z"), "y": lax.axis_index("yhi") * 2 + lax.axis_index("ylo")}


def block_device(p):
    return {"z": p // 2, "yhi": lax.rem(p, 2)}


def f32(ref):
    return ref[...].astype(F32)


class Sender:
    def __init__(self):
        self.pending = {}

    def __call__(self, src, dst, send, recv, device):
        c = pltpu.make_async_remote_copy(src_ref=src, dst_ref=dst, send_sem=send, recv_sem=recv, device_id=device,
                                         device_id_type=MESHID)
        c.start()
        self.pending[id(c)] = c
        return c

    def sent(self, c):
        c.wait_send()
        del self.pending[id(c)]

    def all_sent(self):
        for c in self.pending.values():
            c.wait_send()


def greet():
    bar = pltpu.get_barrier_semaphore()
    for a in "xyz":
        for s in (1, 2, 3):
            pl.semaphore_signal(bar, inc=1, device_id=neighbour(a, s), device_id_type=MESHID)
    for d in (1, 2, 3):
        diagonal = {"z": lax.rem(lax.axis_index("z") + d, 4), "yhi": 1 - lax.axis_index("yhi")}
        pl.semaphore_signal(bar, inc=1, device_id=diagonal, device_id_type=MESHID)
    pl.semaphore_signal(bar, inc=1, device_id=neighbour("core", 1), device_id_type=MESHID)
    return lambda: pl.semaphore_wait(bar, 13)


def to_peers(rc, src_of, dst, send, recv, block):
    out = []
    for d in range(1, 8):
        p = lax.rem(block + d, 8)
        out.append(rc(src_of(p), dst.at[block], send.at[d], recv.at[d], block_device(p)))
    return out


PIECES = (((0, 32), (32, 32), (64, 32)),) * 3


class Gather:
    def __init__(self, rc, g, w, sems, item, r):
        self.rc, self.g, self.w, self.item, self.r = rc, g, w, item, r
        self.flying = {}
        self.ts, self.tr, self.cs, self.cr = sems
        self.k = item * 3 + r
        self.lo, self.n = PIECES[item][r]
        self.me = my_place()
        self.core = lax.axis_index("core")
        self.forwarded = []

    def at(self, pos, lo=0, n=None):
        z = slice(None) if pos["z"] is None else pos["z"]
        x = slice(None) if pos["x"] is None else pos["x"]
        if pos["y"] is None:
            yh = yl = slice(None)
        else:
            yh, yl = pos["y"] // 2, lax.rem(pos["y"], 2)
        return self.g.at[z, yh, yl, x, self.core, pl.ds(self.lo + lo, self.n if n is None else n)]

    def pos(self, st, d=0):
        p = {a: (None if i < st else self.me[a]) for i, a in enumerate(ORDERS[self.r])}
        a = ORDERS[self.r][st]
        p[a] = lax.rem(self.me[a] + (d + 4), 4)
        return p

    def to_sibling(self, ref):
        k = self.k * 4 + len(self.forwarded)
        self.forwarded.append(self.rc(ref, ref, self.cs.at[k], self.cr.at[k], neighbour("core", 1)))

    def push(self, k, src, dst, a, d):
        s = k % 3 if k < 6 else k % 2
        if s in self.flying:
            self.rc.sent(self.flying[s])
        c = self.rc(src, dst, self.ts.at[3 * self.k + s], self.tr.at[10 * self.k + k], neighbour(a, d))
        self.flying[s] = c
        return c

    def straight(self, st):
        ref = self.at(self.pos(st))
        src = ref if st else self.w.at[pl.ds(self.lo, self.n)]
        self.c = [self.push(3 * st + d - 1, src, ref, ORDERS[self.r][st], d) for d in (1, 2, 3)]

    def line(self, st):
        for c in self.c:
            c.wait_recv()
        if st == 1:
            self.to_sibling(self.at(self.pos(2)))

    def near(self):
        ref = self.at(self.pos(2))
        self.c = [self.push(6 + i, ref, ref, ORDERS[self.r][2], d) for i, d in enumerate((1, -1))]

    def pass_on(self):
        self.f = []
        for i, d in enumerate((1, -1)):
            self.c[i].wait_recv()
            p = self.pos(2, -d)
            first = 16 * ((self.n + 16) // 32)
            lo, n = ((0, first), (first, self.n - first))[i]
            if n:
                half = self.at(p, lo, n)
                self.f.append(self.push(8 + i, half, half, ORDERS[self.r][2], d))
            self.to_sibling(self.at(p))

    def last(self):
        for f in self.f:
            f.wait_recv()
        self.to_sibling(self.at(self.pos(2, 2)))

    def complete(self):
        for c in self.forwarded:
            c.wait_recv()

    def drained(self):
        for c in [*self.flying.values(), *self.forwarded]:
            self.rc.sent(c)


def forward_kernel(zx_ref, wo_ref, bc_ref, hid, cot_ref, norm_gain, dt_ref, conv_x, taps_bc, log_ref, shift_ref, skip_ref,
                   gate_ref, g_ref, gb_ref,
                   pk_out, x_pre_out, x_conv_out, d_x_out, normed_t_out, cot_t_out, state_out, bc_pre_out, bc_conv_out,
                   steps_out, rates_out, cols_out, cum_row_out, step_row_out, dec_out, result_out,
                   out_in_out, d_z_out, gain_part_out, skip_part_out, d_cols_out, d_bc_out, d_state_out,
                   normed_t2_out, cot_t2_out, out_in2_out, d_z2_out, *scr):
    (pk, x_pre, x_conv, normed_t, cot_t, state, bc_pre, bc_conv, steps, rates, cols, cum_row, step_row, dec,
     result, out_in, d_z, gain_part, skip_part, d_cols, d_bc, d_state,
     cot, normed, halo, dt_own, small_all, zb, yb, uppers, lowers, wx, wo, gram, d_gram, local, rec_a, out_b, dec_own, square,
     scales, acc, d_c, pk_ref, gain,
     ts, tr, cs, cr, bs, br, qs, qr, es, er, fs, fr, ds, dr, hs, hr, lsem, wsem, osem, xs, xr) = scr
    rc = Sender()
    me = my_place()
    core = lax.axis_index("core")
    x, ylo = me["x"], lax.axis_index("ylo")
    block = lax.axis_index("z") * 2 + lax.axis_index("yhi")
    arrived = greet()
    writes, count = [], [0]

    def out(src, dst):
        c = pltpu.make_async_copy(src, dst, osem.at[count[0]])
        c.start()
        count[0] += 1
        writes.append(c)

    cot_c = pltpu.make_async_copy(cot_ref, cot, lsem.at[3])
    cot_c.start()
    def spot(ref):
        return ref.at[me["z"], me["y"] // 2, ylo, x, core]

    own_w = [pltpu.make_async_copy(src, spot(dst), lsem.at[4 + i])
             for i, (src, dst) in enumerate(((zx_ref.at[1], wx), (zx_ref.at[0], g_ref.at[1]), (wo_ref, wo)))]
    for c in own_w:
        c.start()
    pk_ref[...] = jnp.zeros_like(pk_ref)
    pk_ref[0:5] = conv_x[...]
    pk_ref[5] = gate_ref[...]
    for at, ref in ((6, log_ref), (7, shift_ref), (14, skip_ref)):
        pk_ref[at, 0:HEADS] = ref[...]
    pk_ref[8 : 8 + HEADS, 0:96] = dt_ref[...].astype(F32)
    gain[0] = norm_gain[...]
    arrived()

    gx, gz, go = [[Gather(rc, g, w, (ts, tr, cs, cr), i, r) for r in range(3)]
                  for i, (g, w) in enumerate(((wx, zx_ref.at[1]), (g_ref.at[1], zx_ref.at[0]), (wo, wo_ref)))]

    def each(group, name, *args):
        for c in group:
            getattr(c, name)(*args)

    each(gx, "straight", 0)
    pk_c = to_peers(rc, lambda p: pk_ref, pk, qs, qr, block)

    def small(lo, n):
        cols = pl.ds(lo, n)
        sems = iter(range(9 * (lo // 256), 9 * (lo // 256) + 9))

        def push(src, dst, device):
            k = next(sems)
            return rc(src, dst, bs.at[k], br.at[k], device)

        def at(yl, x_at):
            return gb_ref.at[yl, x_at, core, :, cols]

        def over_y(src):
            own = pltpu.make_async_copy(src, at(ylo, x), lsem.at[1 + lo // 256])
            own.start()
            return [push(src, at(ylo, x), {"ylo": 1 - ylo}), push(src, at(ylo, x), neighbour("core", 1))], own

        def over_x(first, own):
            first[0].wait_recv()
            own.wait()
            line = gb_ref.at[:, x, core, :, cols]
            other = at(1 - ylo, x)
            rest = [push(line, line, neighbour("x", d)) for d in (1, 2, 3)]
            return rest, [first[1], push(other, other, neighbour("core", 1))]

        def to_sibling(rest, cores):
            for d in (1, 2, 3):
                rest[d - 1].wait_recv()
                line = gb_ref.at[:, lax.rem(x + 4 - d, 4), core, :, cols]
                cores.append(push(line, line, neighbour("core", 1)))
            return cores

        return over_y, over_x, to_sibling

    bc_y, bc_x, bc_end = small(0, 256)
    dt_y, dt_x, dt_end = small(256, 128)
    bc_s = bc_y(bc_ref)
    pk[block] = pk_ref[...]

    def normalize(part, at):
        v = part[...].astype(F32)
        r = lax.rsqrt(jnp.mean(v * v, axis=1, keepdims=True) + EPS)
        normed[pl.ds(at, part.shape[0])] = (v * r * gain[...]).astype(BF16)

    normalize(hid, HALO)
    each(gx, "line", 0)
    for c in own_w:
        c.wait()
    each(gx, "straight", 1)
    halo_c = rc(hid.at[pl.ds(ROWS - HALO, HALO)], halo, hs, hr, block_device(lax.rem(block + 1, 8)))

    for c in pk_c:
        c.wait_recv()
    out(pk, pk_out)
    columns = jnp.concatenate([pk[m, 8 : 8 + HEADS, 0:128] for m in range(GROUPS)] + [jnp.zeros((80, 128), F32)], axis=0)
    dt_own[...] = columns.T[:96].astype(BF16)
    dt_s = dt_y(dt_own)
    normed_t[...] = normed[HALO:, :].T.reshape(8, 2, 96, ROWS)
    out(normed_t, normed_t_out)
    each(gx, "line", 1)
    each(gx, "near")
    bc_s = bc_x(*bc_s)
    dt_s = dt_x(*dt_s)
    each(gz, "straight", 0)
    each(go, "straight", 0)
    cot_c.wait()
    cot_t[...] = cot[...].T.reshape(8, 2, 96, ROWS)
    out(cot_t, cot_t_out)
    halo_c.wait_recv()
    normalize(halo, 0)

    @pl.when(block == 0)
    def _():
        normed[pl.ds(0, HALO)] = jnp.zeros((HALO, WIDTH), BF16)

    each(gx, "pass_on")
    each(gz, "line", 0)
    each(gz, "straight", 1)
    b_core = bc_end(*bc_s) + dt_end(*dt_s)
    for c in b_core:
        c.wait_recv()
    small_in = pltpu.make_async_copy(gb_ref, small_all, lsem.at[1])
    small_in.start()
    each(go, "line", 0)
    each(go, "straight", 1)
    small_in.wait()

    def row(at):
        pieces = [pk[m, at : at + 1, 0:HEADS] for m in range(GROUPS)]
        return jnp.concatenate(pieces + [jnp.zeros((1, 80), F32)], axis=1)

    rates[0:1] = row(6)
    rates[1:2] = row(7)
    rates[2:8] = jnp.zeros((6, 128), F32)
    little = dot(normed[...], small_all[...].reshape(WIDTH, COLS))
    bc_pre[...] = little[:, :256]
    pre = conv_pre(little[:, :256], taps_bc[...])
    bc_conv[...] = (pre * jax.nn.sigmoid(pre)).astype(BF16)
    shifted = little[HALO:, 256:384] + rates[1:2]
    steps[...] = shifted
    step = softplus(shifted)
    decay = -step * jnp.exp(rates[0:1])
    cum = dot(triangle(False).astype(F32), decay, precision=lax.Precision.HIGHEST)
    cum_t = cum.T
    step_t = step.T
    lasts = jnp.broadcast_to(jnp.exp(cum_t[:, ROWS - 1 : ROWS]), (128, 128))
    for m in range(GROUPS):
        at = slice(HEADS * m, HEADS * m + 8)
        cols[m] = jnp.concatenate([cum[:, at], step[:, at]], axis=1)
        cum_row[m] = cum_t[HEADS * m : HEADS * m + 8]
        step_row[m] = step_t[HEADS * m : HEADS * m + 8]
        dec_own[m] = lasts[HEADS * m : HEADS * m + 8]
    dec_c = to_peers(rc, lambda p: dec_own.at[p], dec, ds, dr, block)
    dec[block] = dec_own[block]
    gram[...] = jnp.where(triangle(False), dot(bc_conv[:, 128:], bc_conv[:, :128], (1, 1)), 0.0)
    out(bc_pre, bc_pre_out)
    out(bc_conv, bc_conv_out)
    out(steps, steps_out)
    out(rates, rates_out)
    out(cols, cols_out)
    out(cum_row, cum_row_out)
    out(step_row, step_row_out)
    each(gx, "last")
    each(gz, "line", 1)
    each(gz, "near")
    each(gx, "complete")

    x_flat, o_flat = wx.reshape(GROUPS, WIDTH, COLS), wo.reshape(GROUPS, WIDTH, COLS)
    g_flat = g_ref.reshape(2, GROUPS, WIDTH, COLS)

    def z_copy(m):
        return pltpu.make_async_copy(g_flat.at[1, m], x_flat.at[m], wsem.at[m])

    def pairs(buf, lo, hi, body, ready=None):
        @pl.loop(lo, hi)
        def _(i):
            if ready is not None:
                for k in range(2):
                    ready(2 * i + k).wait()
            body(i, jnp.concatenate([buf[2 * i], buf[2 * i + 1]], axis=1))

    out(wx, g_ref.at[0])
    x_written = writes.pop()

    def to_owner(m):
        return pltpu.make_async_remote_copy(src_ref=local.at[m], dst_ref=rec_a.at[block], send_sem=es.at[m], recv_sem=er.at[block],
                                            device_id=block_device(m), device_id_type=MESHID)

    def second_pair(i, w):
        both = dot(normed[...], w)
        for k in range(2):
            m = 2 * i + k
            ext = both[:, COLS * k : COLS * k + COLS]
            x_pre[m] = ext
            pre = conv_pre(ext, pk[m])
            xc = (pre * jax.nn.sigmoid(pre)).astype(BF16)
            x_conv[m] = xc
            cum, step = cols[m][:, :8], cols[m][:, 8:]
            weighted = (xc.astype(F32) * spread(step * jnp.exp(cum[ROWS - 1 : ROWS] - cum))).astype(BF16)
            local[m] = dot(weighted, bc_conv[:, :128], (0, 0)).astype(BF16)
            pl.when(m != block)(lambda m=m: to_owner(m).start())

    pairs(x_flat, 0, 4, second_pair)
    each(go, "line", 1)
    rec_a[block] = local[block]
    out(x_pre, x_pre_out)
    out(x_conv, x_conv_out)

    top, low = slice(0, HALF), slice(HALF, ROWS)

    def scan_group(m):
        xc = x_conv[m]
        cum = cols[m][:, :8]
        rows = cum_row[m]
        step_rows = step_row[m]
        parts = []
        for h in range(HEADS):
            xh = xc[:, 64 * h : 64 * h + 64]
            col, row, step = cum[:, h : h + 1], rows[h : h + 1, :], step_rows[h : h + 1, :]
            upper = (jnp.exp(jnp.minimum(col[top] - row[:, top], 0.0)) * step[:, top]).astype(BF16)
            lower = (jnp.exp(jnp.minimum(col[low] - row, 0.0)) * step).astype(BF16)
            uppers[m, h] = upper
            lowers[m, h] = lower
            parts.append(jnp.concatenate([dot((upper.astype(F32) * gram[top, top]).astype(BF16), xh[top]),
                                          dot((lower.astype(F32) * gram[low]).astype(BF16), xh)], axis=0))
        yb[m] = jnp.concatenate(parts, axis=1) + spread(pk[m, 14:15, 0:8]) * xc.astype(F32)

    pl.loop(0, 4)(scan_group)
    each(gz, "pass_on")
    each(go, "near")
    pl.loop(4, GROUPS)(scan_group)
    for c in dec_c:
        c.wait_recv()
    out(dec, dec_out)

    def exchanged(src, sends, recvs):
        for d in range(1, 8):
            other = lax.rem(block + d, 8)
            pltpu.make_async_remote_copy(src_ref=src.at[other], dst_ref=rec_a.at[other], send_sem=sends.at[other],
                                         recv_sem=recvs.at[other], device_id=block_device(other), device_id_type=MESHID).wait()

    def carry(order):
        for h in range(HEADS):
            rows = pl.ds(64 * h, 64)
            run = jnp.zeros((64, 128), F32)
            for i in order:
                out_b[i, rows] = run.astype(BF16)
                run = run * dec[i, pl.ds(h, 1)] + rec_a[i, rows].astype(F32)

    exchanged(local, es, er)
    carry(range(BLOCKS))
    f_c = to_peers(rc, lambda p: out_b.at[p], state, fs, fr, block)
    state[block] = out_b[block]
    each(gz, "last")
    each(gz, "complete")
    x_written.wait()
    each(gx, "drained")
    for m in range(GROUPS):
        z_copy(m).start()

    def gate_pair(i, w):
        z = dot(normed[HALO:, :], w)
        for k in range(2):
            zb[2 * i + k] = z[:, COLS * k : COLS * k + COLS]

    pairs(x_flat, 0, 4, gate_pair, z_copy)
    each(go, "pass_on")
    for c in f_c:
        c.wait_recv()
        rc.sent(c)
    out(state, state_out)
    square[...] = jnp.zeros_like(square)
    c_mat = bc_conv[:, 128:]

    @pl.loop(0, GROUPS)
    def _(m):
        carried = dot(c_mat, state[m], (1, 1))
        y = yb[m] + spread(jnp.exp(cols[m][:, :8])) * carried
        z = zb[m]
        sig = jax.nn.sigmoid(z)
        act = z * sig
        gated = y * act
        yb[m] = gated
        zb[m] = act
        d_z[m] = (y * sig * (1.0 + z * (1.0 - sig))).astype(BF16)
        sq = gated * gated
        square[...] += sq[:, :128] + sq[:, 128:256] + sq[:, 256:]

    r2 = lax.rsqrt(jnp.sum(square[...], axis=1, keepdims=True) / INNER + EPS)

    @pl.loop(0, GROUPS)
    def _(m):
        out_in[m] = (yb[m] * r2 * pk[m, 5:6]).astype(BF16)

    acc[...] = jnp.zeros_like(acc)
    d_c[...] = jnp.zeros_like(d_c)
    d_gram[...] = jnp.zeros_like(d_gram)
    each(go, "last")
    each(go, "complete")

    def result_pair(i, w):
        acc[...] += dot(jnp.concatenate([out_in[2 * i], out_in[2 * i + 1]], axis=1), w, (1, 1))

    pairs(o_flat, 0, 4, result_pair)
    total = jnp.sum(cot[...].astype(F32) * acc[...], axis=1, keepdims=True)
    scales[...] = jnp.concatenate([r2, r2 * r2 * (total / INNER), jnp.zeros((ROWS, 6), F32)], axis=1)
    result[...] = (hid[...].astype(F32) + acc[...]).astype(BF16)
    out(result, result_out)

    def to_owner_back(m):
        return pltpu.make_async_remote_copy(src_ref=local.at[m], dst_ref=rec_a.at[block], send_sem=es.at[m], recv_sem=er.at[block],
                                            device_id=block_device(m), device_id_type=MESHID)

    def gate_back(i, w):
        r2, slope = scales[:, 0:1], scales[:, 1:2]
        both = dot(cot[...], w)
        for k in range(2):
            m = 2 * i + k
            d = both[:, COLS * k : COLS * k + COLS]
            gated = yb[m]
            gain_part[m] = jnp.sum(d * (gated * r2), axis=0, keepdims=True)
            d_gated = r2 * (d * pk[m, 5:6]) - gated * slope
            dy = d_gated * zb[m]
            d_z[m] = (d_gated * d_z[m].astype(F32)).astype(BF16)
            yb[m] = dy
            skip_part[m] = jnp.sum(dy * x_conv[m].astype(F32), axis=0, keepdims=True)
            grown = spread(jnp.exp(cols[m][:, :8]))
            scaled = grown * dy
            dye = scaled.astype(BF16)
            d_c[...] += dot(dye, state[m])
            local[m] = dot(dye, c_mat, (0, 0)).astype(BF16)
            pl.when(m != block)(lambda m=m: to_owner_back(m).start())
            d_cols[m] = jnp.concatenate([gathered_heads(scaled * dot(c_mat, state[m], (1, 1))), jnp.zeros((ROWS, 8), F32)], axis=1)

    pairs(o_flat, 0, 4, gate_back)
    rec_a[block] = local[block]
    across = [rc(src, dst, xs.at[i], xr.at[i], neighbour("core", 1)) for i, (src, dst) in enumerate((
        (cot_t.at[:, 1 - core], cot_t2_out), (out_in, out_in2_out), (normed_t.at[:, 1 - core], normed_t2_out),
        (d_z, d_z2_out)))]
    out(out_in, out_in_out)
    out(d_z, d_z_out)
    out(gain_part, gain_part_out)
    out(skip_part, skip_part_out)

    def d_x_copy(m):
        return pltpu.make_async_copy(zb.at[m], d_x_out.at[m], wsem.at[m])

    def inner_group(m):
        dy = yb[m]
        dyb = dy.astype(BF16)
        xc = x_conv[m]
        d_cum = d_cols[m][:, :8]
        lane = lax.broadcasted_iota(jnp.int32, (ROWS, 8), 1)
        parts = []
        sums = []
        for h in range(HEADS):
            xh = xc[:, 64 * h : 64 * h + 64]
            dyh = dyb[:, 64 * h : 64 * h + 64]
            upper, lower = uppers[m, h].astype(F32), lowers[m, h].astype(F32)
            tu = upper * dot(dyh[top], xh[top], (1, 1))
            tl = lower * dot(dyh[low], xh, (1, 1))
            d_gram[top, top] += tu
            d_gram[low] += tl
            qu, ql = tu * gram[top, top], tl * gram[low]
            col = jnp.sum(ql, axis=0, keepdims=True)
            sums.append(jnp.concatenate([col[:, top] + jnp.sum(qu, axis=0, keepdims=True), col[:, low]], axis=1))
            row = jnp.concatenate([jnp.sum(qu, axis=1, keepdims=True),
                                   jnp.sum(ql[:, top] + ql[:, low], axis=1, keepdims=True)], axis=0)
            d_cum = jnp.where(lane == h, d_cum + row, d_cum)
            below = dot((lower * gram[low]).astype(BF16), dyh[low], (0, 0))
            above = dot((upper * gram[top, top]).astype(BF16), dyh[top], (0, 0))
            parts.append(jnp.concatenate([below[top] + above, below[low]], axis=0))
        sums = jnp.concatenate(sums + [jnp.zeros((2, ROWS), F32)], axis=0).T
        zb[m] = jnp.concatenate(parts, axis=1) + spread(pk[m, 14:15, 0:8]) * dy
        d_x_copy(m).start()
        d_cols[m] = jnp.concatenate([d_cum - sums, sums], axis=1)

    pl.loop(0, 4)(inner_group)
    exchanged(local, es, er)
    carry(range(BLOCKS - 1, -1, -1))
    b_c = to_peers(rc, lambda p: out_b.at[p], d_state, fs, fr, block)
    d_state[block] = out_b[block]
    pl.loop(4, GROUPS)(inner_group)
    out(d_cols, d_cols_out)
    dg = jnp.where(triangle(False), d_gram[...], 0.0).astype(BF16)
    d_bc[:, :128] = dot(dg, c_mat, (0, 0))
    d_bc[:, 128:] = d_c[...] + dot(dg, bc_conv[:, :128])
    out(d_bc, d_bc_out)
    for c in b_c + across:
        c.wait_recv()
    out(d_state, d_state_out)
    for c in writes:
        c.wait()
    for m in range(GROUPS):
        d_x_copy(m).wait()
    rc.all_sent()


HALF = ROWS // 2
RESULTS = (
    ("pk", (GROUPS, 16, COLS), F32), ("x_pre", (GROUPS, HALO + ROWS, COLS), F32), ("x_conv", (GROUPS, ROWS, COLS), BF16),
    ("d_x", (GROUPS, ROWS, COLS), F32), ("normed_t", (8, 2, 96, ROWS), BF16), ("cot_t", (8, 2, 96, ROWS), BF16),
    ("state", (GROUPS, COLS, 128), BF16), ("bc_pre", (HALO + ROWS, 256), F32), ("bc_conv", (ROWS, 256), BF16),
    ("steps", (ROWS, 128), F32), ("rates", (8, 128), F32), ("cols", (GROUPS, ROWS, 16), F32),
    ("cum_row", (GROUPS, 8, ROWS), F32), ("step_row", (GROUPS, 8, ROWS), F32), ("dec", (BLOCKS, 8, 128), F32),
    ("result", (ROWS, WIDTH), BF16), ("out_in", (GROUPS, ROWS, COLS), BF16), ("d_z", (GROUPS, ROWS, COLS), BF16),
    ("gain_part", (GROUPS, 1, COLS), F32), ("skip_part", (GROUPS, 1, COLS), F32), ("d_cols", (GROUPS, ROWS, 16), F32),
    ("d_bc", (ROWS, 256), F32), ("d_state", (GROUPS, COLS, 128), BF16),
)
SIBLING = (
    ("normed_t2", (8, 96, ROWS), BF16), ("cot_t2", (8, 96, ROWS), BF16), ("out_in2", (GROUPS, ROWS, COLS), BF16),
    ("d_z2", (GROUPS, ROWS, COLS), BF16),
)


def forward(zx, wo, bc, hid, cot, *params):
    hbm = pl.BlockSpec(memory_space=pl.ANY)
    vmem = pl.BlockSpec(memory_space=pltpu.VMEM)
    sem = pltpu.SemaphoreType.DMA

    def v(*shape, dtype=F32):
        return pltpu.VMEM(shape, dtype)

    def b(*shape):
        return v(*shape, dtype=BF16)

    groups = (GROUPS, ROWS, COLS)
    outs = pl.pallas_call(
        forward_kernel,
        out_shape=(sds(2, 4, 2, 2, 4, 2, 96, COLS, dtype=BF16), sds(2, 4, 2, 96, COLS, dtype=BF16),
                   *[sds(*shape, dtype=dtype) for _, shape, dtype in RESULTS + SIBLING]),
        in_specs=[hbm, hbm, vmem, vmem, hbm] + [vmem] * 8,
        out_specs=(hbm,) * (2 + len(RESULTS) + len(SIBLING)),
        scratch_shapes=[
            *[pltpu.VMEM(shape, dtype) for name, shape, dtype in RESULTS if name != "d_x"],
            b(ROWS, WIDTH), b(HALO + ROWS, WIDTH), b(HALO, WIDTH), b(96, 128), b(2, 4, 2, 96, COLS),
            v(*groups), v(*groups), b(GROUPS, HEADS, HALF, HALF), b(GROUPS, HEADS, HALF, ROWS),
            b(4, 2, 2, 4, 2, 96, COLS), b(4, 2, 2, 4, 2, 96, COLS),
            v(ROWS, ROWS), v(ROWS, ROWS),
            b(GROUPS, COLS, 128), b(GROUPS, COLS, 128), b(GROUPS, COLS, 128), v(GROUPS, 8, 128),
            v(ROWS, 128), v(ROWS, 8), v(ROWS, WIDTH), v(ROWS, 128), v(16, COLS), v(1, WIDTH),
            sem((27,)), sem((90,)), sem((36,)), sem((36,)), sem((18,)), sem((18,)), sem((8,)), sem((8,)), sem((8,)), sem((8,)),
            sem((8,)), sem((8,)), sem((8,)), sem((8,)), sem, sem, sem((7,)), sem((GROUPS,)), sem((len(RESULTS),)), sem((4,)),
            sem((4,)),
        ],
        compiler_params=pltpu.CompilerParams(collective_id=0, has_side_effects=True, vmem_limit_bytes=62 * 2**20),
        name="forward_between_devices",
    )(zx, wo, bc, hid, cot, *params)
    return outs[0], outs[1], dict(zip([name for name, _, _ in RESULTS + SIBLING], outs[2:]))


class Total:
    def __init__(self, rc, value, lines, axes, send, recv):
        self.rc, self.value, self.lines, self.axes, self.send, self.recv = rc, value, lines, axes, send, recv
        self.me = dict(my_place(), core=lax.axis_index("core"), ylo=lax.axis_index("ylo"))

    def step(self, j):
        if j > 0:
            for c in self.flying:
                c.wait_recv()
                self.rc.sent(c)
            l, i = self.lines, j - 1
            if self.axes[i] in ("core", "ylo"):
                self.value[...] = l[i, 0] + l[i, 1]
            else:
                self.value[...] = (l[i, 0] + l[i, 1]) + (l[i, 2] + l[i, 3])
        if j < len(self.axes):
            a = self.axes[j]
            mine = self.lines.at[j, self.me[a]]
            mine[...] = self.value[...]
            if a in ("core", "ylo"):
                devices = [{a: 1 - self.me[a]}]
            else:
                devices = [neighbour(a, d) for d in (1, 2, 3)]
            self.flying = [self.rc(mine, mine, self.send.at[d], self.recv.at[3 * j + d], device)
                           for d, device in enumerate(devices)]


class SmallSum:
    def __init__(self, rc, parts, xs, ys, zs, send, recv):
        self.rc, self.parts, self.xs, self.ys, self.zs = rc, parts, xs, ys, zs
        self.send, self.recv = send, recv
        self.me = my_place()

    def step(self, j, out=None):
        rc, me, parts, s, r = self.rc, self.me, self.parts, self.send, self.recv
        ylo = lax.rem(me["y"], 2)
        if j == 0:
            self.c = [rc(parts.at[:, lax.rem(me["x"] + d, 4)], self.xs.at[d - 1], s.at[d], r.at[d], neighbour("x", d))
                      for d in (1, 2, 3)]
            return
        for c in self.c:
            c.wait_recv()
        if j == 1:
            for yl in range(2):
                m = parts.at[yl, me["x"]]
                m[...] = (f32(m) + f32(self.xs.at[0, yl]) + f32(self.xs.at[1, yl]) + f32(self.xs.at[2, yl])).astype(BF16)
            self.ys[me["y"]] = parts[ylo, me["x"]]
            self.c = [rc(parts.at[lax.rem(me["y"] + d, 2), me["x"]], self.ys.at[me["y"]], s.at[3 + d], r.at[3 + d],
                         neighbour("y", d)) for d in (1, 2, 3)]
        elif j == 2:
            y = self.ys
            m = self.zs.at[me["z"]]
            m[...] = ((f32(y.at[0]) + f32(y.at[1])) + (f32(y.at[2]) + f32(y.at[3]))).astype(BF16)
            self.c = [rc(m, m, s.at[6 + d], r.at[6 + d], neighbour("z", d)) for d in (1, 2, 3)]
        elif j == 3:
            z = self.zs
            return (f32(z.at[0]) + f32(z.at[1])) + (f32(z.at[2]) + f32(z.at[3]))


def part_of(ref, item, pos, lo, n):
    z = slice(None) if pos["z"] is None else pos["z"]
    x = slice(None) if pos["x"] is None else pos["x"]
    if pos["y"] is None:
        yh = yl = slice(None)
    else:
        yh, yl = pos["y"] // 2, lax.rem(pos["y"], 2)
    return ref.at[item, z, yh, yl, x, pl.ds(lo, n)]


class Chunk:
    def __init__(self, rc, own, out, bufs, sems, item, slot, wide, r):
        self.rc, self.own, self.out, self.item, self.slot, self.r = rc, own, out, item, slot, r
        full, half, second, third = bufs
        self.full, self.half = full[r].at[wide], half[r].at[wide]
        self.direct = {1: second[r].at[slot], 2: third.at[slot * 3 + r]}
        self.send, self.recv = sems
        self.number = slot * 3 + r
        self.base = self.number * 10
        self.me = my_place()
        self.flying = {}

    def slab(self, st, d, lo=0, n=SUB):
        p = {a: (self.me[a] if i < st else None) for i, a in enumerate(ORDERS[self.r])}
        a = ORDERS[self.r][st]
        p[a] = lax.rem(self.me[a] + (d + 4), 4)
        return part_of(self.own, self.slot, p, self.r * SUB + lo, n)

    def loop(self, st, body):
        sizes = []
        for a, n in (("z", (4,)), ("y", (2, 2)), ("x", (4,))):
            if ORDERS[self.r].index(a) > st:
                sizes += n
        if not sizes:
            body(())
        elif len(sizes) == 1 or sizes == [2, 2]:
            for i in range(4):
                body((i,) if len(sizes) == 1 else (i // 2, i % 2))
        else:
            @pl.loop(0, 4)
            def _(i):
                for k in range(4):
                    if sizes == [4, 4]:
                        body((i, k))
                    elif sizes == [4, 2, 2]:
                        body((i, k // 2, k % 2))
                    else:
                        body((i // 2, lax.rem(i, 2), k))

    def push(self, k, src, dst, st, d):
        s = k % 2 if k < 4 else (k - 4) % 3
        if s in self.flying:
            self.rc.sent(self.flying[s])
        c = self.rc(src, dst, self.send.at[3 * self.number + s], self.recv.at[self.base + k], neighbour(ORDERS[self.r][st], d))
        self.flying[s] = c
        return c

    def far(self):
        self.far_c = [self.push(i, self.slab(0, 2, 16 * i, 16), self.half.at[i], 0, d) for i, d in enumerate((1, -1))]

    def near(self):
        self.near_c = []
        for i, d in enumerate((1, -1)):
            self.far_c[i].wait_recv()
            mine = self.slab(0, d, 16 * i, 16)

            def add(index, mine=mine, i=i):
                m = mine.at[index]
                m[...] = m[...] + self.half[(i, *index)]

            self.loop(0, add)
            self.near_c.append(self.push(2 + i, self.slab(0, d), self.full.at[i], 0, d))

    def straight(self, st):
        self.straight_c = [self.push(1 + 3 * st + d - 1, self.slab(st, d), self.direct[st].at[d - 1], st, d) for d in (1, 2, 3)]

    def step(self, j):
        if j == 0:
            self.far()
        elif j == 1:
            self.near()
        elif j == 2:
            for c in self.near_c:
                c.wait_recv()
            mine = self.slab(0, 0)

            def add(index):
                m = mine.at[index]
                m[...] = (f32(m) + f32(self.full.at[(0, *index)]) + f32(self.full.at[(1, *index)])).astype(BF16)

            self.loop(0, add)
            self.straight(1)
        else:
            for c in self.straight_c:
                c.wait_recv()
            st = j - 2
            mine = self.slab(st, 0)
            got = self.direct[st]

            def total(index):
                m = mine.at[index] if index else mine
                return (f32(m) + f32(got.at[(0, *index)])) + (f32(got.at[(1, *index)]) + f32(got.at[(2, *index)]))

            if st == 1:
                def add(index):
                    mine[index] = total(index).astype(BF16)

                self.loop(1, add)
                self.straight(2)
            else:
                self.out(pl.ds(self.r * SUB, SUB))[...] = total(())


def backward_kernel(g_ref, x_conv_ref, d_x_ref, x_pre_ref, cols_ref, d_cols_ref, cot_t_ref, cot_t2_ref, out_in_ref, out_in2_ref,
                    normed_t_ref, normed_t2_ref, d_z_ref, d_z2_ref, state_ref, d_state_ref, w_small_ref, hid_ref, cot_ref,
                    taps, d_bc_in, bc_pre, bc_conv, taps_bc, norm_gain, shifted, rates, gain_part, skip_part,
                    zx_out, wo_out, wbc_out, wdt_out, taps_out, taps_bc_out, log_out, shift_out, skip_out, gate_out, norm_out,
                    grad_hidden, *scr):
    (own, l_c, l_c2, l_n, l_n2, rhs_o, rhs_z, rhs_x, state, d_state, w_small, hid, cot, tails, halo_src, halo_dst, acc, wbuf,
     bxc, bdx, bxp, bcols, bdc, d_b, d_all, parts, small2, s_xs, s_ys, s_zs,
     v_all, v_in, v_sum, v_lines, n_all, n_lines, gain) = scr[:37]
    bufs = [scr[37:40], scr[40:43], scr[43:46], scr[46]]
    (t_s, t_r, x_s, x_r, h_s, h_r, m_s, m_r, ss, sr, vms, vmr, vs, vr, ns, nr, wsem, lsem, isem, freed) = scr[47:]
    rc = Sender()
    gain[0] = norm_gain[...]
    core = lax.axis_index("core")
    block = lax.axis_index("z") * 2 + lax.axis_index("yhi")
    arrived = greet()

    loads = {}

    def load_in(name, *pairs):
        loads[name] = []
        for src, dst in pairs:
            c = pltpu.make_async_copy(src, dst, isem.at[sum(len(v) for v in loads.values())])
            c.start()
            loads[name].append(c)

    def ready(name):
        for c in loads[name]:
            c.wait()

    load_in("o", (cot_t_ref.at[:, core], l_c), (cot_t2_ref, l_c2), (out_in_ref, rhs_o.at[0]), (out_in2_ref, rhs_o.at[1]))
    load_in("z", (normed_t_ref.at[:, core], l_n), (normed_t2_ref, l_n2), (d_z_ref, rhs_z.at[0]), (d_z2_ref, rhs_z.at[1]))
    load_in("s", (state_ref, state), (d_state_ref, d_state))

    outs = (lambda at: zx_out.at[at, 1], lambda at: zx_out.at[at, 0], lambda at: wo_out.at[at])

    def chunks(item, slot, wide):
        return [Chunk(rc, own, outs[item], bufs, (t_s, t_r), item, slot, wide, r) for r in range(3)]

    def steps(cs, j):
        for c in cs:
            c.step(j)

    def both_tokens(own_t, other_t):
        return jnp.concatenate([own_t[...].reshape(768, ROWS), other_t[...].reshape(768, ROWS)], axis=1)

    def gradient(left, left2, rhs, slot, ready=None):
        def one(m):
            if ready is not None:
                ready(m)
            v = dot(both_tokens(left, left2), jnp.concatenate([rhs[0, m], rhs[1, m]], axis=0))
            own[slot, m // 2, lax.rem(m, 2)] = v.astype(BF16).reshape(2, 4, 96, COLS)

        pl.loop(0, GROUPS)(one)

    oc, zc, xc_ = chunks(2, 0, 0), chunks(1, 1, 1), chunks(0, 2, 0)
    ready("o")
    gradient(l_c, l_c2, rhs_o, 0)
    arrived()
    steps(oc, 0)
    ready("z")

    streams = ((x_conv_ref, bxc), (d_x_ref, bdx), (x_pre_ref, bxp), (cols_ref, bcols), (d_cols_ref, bdc))

    def load(m):
        k = lax.rem(m, 2)
        return [pltpu.make_async_copy(src.at[m], dst.at[k], lsem.at[k, i]) for i, (src, dst) in enumerate(streams)]

    for c in load(0):
        c.start()
    gradient(l_n, l_n2, rhs_z, 1)
    steps(zc, 0)
    ready("s")
    load_in("end", (w_small_ref, w_small), (hid_ref, hid), (cot_ref, cot))

    def fifth_group(m):
        k = lax.rem(m, 2)

        @pl.when(m < GROUPS - 1)
        def _():
            for c in load(m + 1):
                c.start()

        for c in load(m):
            c.wait()
        ds = d_state[m]
        xf = bxc[k].astype(F32)
        cum, step = bcols[k][:, :8], bcols[k][:, 8:]
        last = cum[ROWS - 1 : ROWS]
        tail = jnp.exp(last - cum)
        weights = step * tail
        wide = spread(weights)
        d_weighted = dot(bc_conv[:, :128], ds, (1, 1))
        d_b[...] += dot((xf * wide).astype(BF16), ds)
        dx = bdx[k] + wide * d_weighted
        d_weights = gathered_heads(d_weighted * xf)
        both = weights * d_weights
        lane = lax.broadcasted_iota(jnp.int32, (1, 8), 1)
        product = jnp.sum(state[m].astype(F32) * ds.astype(F32), axis=1, keepdims=True)
        d_last = jnp.sum(both, axis=0, keepdims=True)
        for h in range(HEADS):
            dots = jnp.sum(product[64 * h : 64 * h + 64], axis=0, keepdims=True)
            d_last = jnp.where(lane == h, d_last + jnp.exp(last) * dots, d_last)
        row = lax.broadcasted_iota(jnp.int32, (ROWS, 8), 0)
        d_cum = bdc[k][:, :8] - both
        d_cum = jnp.where(row == ROWS - 1, d_cum + d_last, d_cum)
        d_all[m] = jnp.concatenate([d_cum, bdc[k][:, 8:] + both], axis=1)
        ext = bxp[k]
        tap = taps[m]
        pre = conv_pre(ext, tap)
        sig = jax.nn.sigmoid(pre)
        dp = dx * (sig * (1.0 + pre * (1.0 - sig)))
        v_all[m, 0:8] = conv_grads(dp, ext, gain_part[m], skip_part[m])
        whole_dx = conv_transposed(jnp.concatenate([dp, jnp.zeros((8, COLS), F32)], axis=0), tap)
        rhs_x[0, m] = whole_dx.astype(BF16)
        tails[m] = whole_dx[ROWS - 16 :]
        halo_src[m] = dp[:8]

    d_b[...] = jnp.zeros_like(d_b)
    pl.loop(0, 2)(fifth_group)
    steps(oc, 1)
    pl.loop(2, GROUPS)(fifth_group)

    d_bc = jnp.concatenate([d_bc_in[:, :128] + d_b[...], d_bc_in[:, 128:]], axis=1)
    ext = bc_pre[...]
    pre = conv_pre(ext, taps_bc[...])
    sig = jax.nn.sigmoid(pre)
    dp_bc = d_bc * (sig * (1.0 + pre * (1.0 - sig)))
    halo_src[GROUPS] = jnp.concatenate([dp_bc[:8], jnp.zeros((8, 128), F32)], axis=1)
    halo = rc(halo_src, halo_dst, h_s, h_r, block_device(lax.rem(block + 7, 8)))
    steps(zc, 1)
    steps(oc, 2)
    for a in "xyz":
        for s in (1, -1):
            pl.semaphore_signal(freed, inc=1, device_id=neighbour(a, s), device_id_type=MESHID)
    zero8 = jnp.zeros((1, 256), F32)
    d_cum = jnp.concatenate([d_all[m][:, :HEADS] for m in range(GROUPS)] + [jnp.zeros((ROWS, 80), F32)], axis=1)
    d_step = jnp.concatenate([d_all[m][:, 8 : 8 + HEADS] for m in range(GROUPS)] + [jnp.zeros((ROWS, 80), F32)], axis=1)
    d_decay = dot(triangle(True).astype(F32), d_cum, precision=lax.Precision.HIGHEST)
    rate = -jnp.exp(rates[0:1])
    v = shifted[...]
    sig = jax.nn.sigmoid(v)
    far = v < -16.0
    ratio = jnp.where(far, 1.0, sig / jnp.where(far, 1.0, softplus(v)))
    d_dt = d_step * ratio + rate * d_decay * sig
    log_grad = jnp.sum(d_decay * (softplus(v) * rate), axis=0, keepdims=True)
    shift_grad = jnp.sum(d_dt, axis=0, keepdims=True)
    bc_rows = conv_grads(dp_bc, ext, jnp.concatenate([log_grad, shift_grad], axis=1), zero8)
    bc_rows = jnp.concatenate([bc_rows, jnp.zeros((8, 128), F32)], axis=1)
    for m in range(GROUPS):
        v_all[m, 8:16] = bc_rows
    vec_c = to_peers(rc, lambda p: v_all.at[p], v_in, vms, vmr, block)
    v_in[block] = v_all[block]

    halo.wait_recv()
    inside = block < 7

    def below(k):
        return jnp.where(inside, halo_dst[k], 0.0)

    def across(m):
        return pltpu.make_async_remote_copy(src_ref=rhs_x.at[0, m], dst_ref=rhs_x.at[1, m], send_sem=x_s.at[m],
                                            recv_sem=x_r.at[m], device_id=neighbour("core", 1), device_id_type=MESHID)

    def fix(m):
        ext = jnp.concatenate([jnp.zeros((16, COLS), F32), below(m)], axis=0)
        rhs_x[0, m, pl.ds(ROWS - 16, 16)] = (tails[m] + conv_transposed(ext, taps[m], 16)).astype(BF16)
        across(m).start()

    pl.loop(0, GROUPS)(fix)
    d_bc = conv_transposed(jnp.concatenate([dp_bc, below(GROUPS)[:, :256]], axis=0), taps_bc[...])
    small2[0] = jnp.concatenate([d_bc, d_dt], axis=1).astype(BF16)
    small_c = rc(small2.at[0], small2.at[1], m_s, m_r, neighbour("core", 1))

    def weights(m):
        k = lax.rem(m, 2)
        return [pltpu.make_async_copy(g_ref.at[i, m], wbuf.at[k, i], wsem.at[k, i]) for i in range(2)]

    for c in weights(0):
        c.start()
    small_c.wait_recv()
    parts[...] = dot(both_tokens(l_n, l_n2), small2[...].reshape(2 * ROWS, COLS)).astype(BF16).reshape(2, 4, 96, COLS)
    sums = SmallSum(rc, parts, s_xs, s_ys, s_zs, ss, sr)
    sums.step(0)
    gradient(l_n, l_n2, rhs_x, 2, lambda m: across(m).wait())
    pl.semaphore_wait(freed, 6)
    steps(xc_, 0)
    ready("end")
    acc[...] = dot(small2[0], w_small[...], (1, 1))
    def input_group(m):
        k = lax.rem(m, 2)

        @pl.when(m < GROUPS - 1)
        def _():
            for c in weights(m + 1):
                c.start()

        for c in weights(m):
            c.wait()
        lhs = jnp.concatenate([rhs_x[0, m], rhs_z[0, m]], axis=1)
        rhs = jnp.concatenate([wbuf[k, 0], wbuf[k, 1]], axis=1)
        acc[...] += dot(lhs, rhs, (1, 1))

    pl.loop(0, 4)(input_group)
    steps(xc_, 1)
    for c in vec_c:
        c.wait_recv()
    t = v_in[0]
    for i in range(1, BLOCKS):
        t = t + v_in[i]
    v_sum[...] = t
    vec = Total(rc, v_sum, v_lines, ("core", "x", "ylo"), vs, vr)
    vec.step(0)
    pl.loop(4, GROUPS)(input_group)
    v = hid[...].astype(F32)
    r = lax.rsqrt(jnp.mean(v * v, axis=1, keepdims=True) + EPS)
    unit = v * r
    dn = acc[...]
    gain_grad = jnp.sum(dn * unit, axis=0, keepdims=True)
    for i in range(4):
        n_all[pl.ds(i, 1)] = gain_grad[:, COLS * i : COLS * i + COLS]
    n_all[pl.ds(4, 4)] = jnp.zeros((4, COLS), F32)
    nvec = Total(rc, n_all, n_lines, ("core", "x", "y", "z"), ns, nr)
    nvec.step(0)
    sums.step(1)
    vec.step(1)
    d_in = dn * gain[...]
    grad_hidden[...] = r * (d_in - unit * jnp.mean(d_in * unit, axis=1, keepdims=True)) + cot[...].astype(F32)
    nvec.step(1)
    steps(xc_, 2)
    steps(zc, 2)
    steps(oc, 3)
    sums.step(2)
    nvec.step(2)
    vec.step(2)
    steps(xc_, 3)
    nvec.step(3)
    vec.step(3)
    steps(zc, 3)
    steps(oc, 4)

    pick = lax.broadcasted_iota(jnp.int32, (8, 128), 0) + block * HEADS
    pick = (pick == lax.broadcasted_iota(jnp.int32, (8, 128), 1)).astype(F32)

    def own_heads(row):
        return dot(row, pick, (1, 1), precision=lax.Precision.HIGHEST)

    mine = v_sum[...]
    taps_out[...] = mine[:5]
    gate_out[...] = mine[5]
    skip_out[...] = gathered_heads(mine[6:7])[0, :HEADS]
    taps_bc_out[...] = mine[8:13, :256]
    log_out[...] = own_heads(mine[13:14, :128])[0, :HEADS]
    shift_out[...] = own_heads(mine[13:14, 128:256])[0, :HEADS]
    steps(xc_, 4)
    steps(zc, 4)
    little = sums.step(3)
    wbc_out[...] = little[:, :256]
    wdt_out[...] = dot(pick, little[:, 256:], (1, 1), precision=lax.Precision.HIGHEST)[:HEADS]
    nvec.step(4)
    for i in range(4):
        norm_out[pl.ds(COLS * i, COLS)] = n_all[i]
    rc.all_sent()


def backward(w_all, r, w_small, hid, cot, norm_gain, conv_bc):
    hbm = pl.BlockSpec(memory_space=pl.ANY)
    vmem = pl.BlockSpec(memory_space=pltpu.VMEM)
    sem = pltpu.SemaphoreType.DMA

    def buf(*shape, dtype=BF16):
        return pltpu.VMEM((*shape, COLS), dtype)

    def v(*shape, dtype=F32):
        return pltpu.VMEM(shape, dtype)

    def b(*shape):
        return v(*shape, dtype=BF16)

    scratch = [
        buf(3, 4, 2, 2, 4, 96), b(8, 96, ROWS), b(8, 96, ROWS), b(8, 96, ROWS), b(8, 96, ROWS),
        buf(2, GROUPS, ROWS), buf(2, GROUPS, ROWS), buf(2, GROUPS, ROWS), b(GROUPS, COLS, 128), b(GROUPS, COLS, 128),
        buf(WIDTH), b(ROWS, WIDTH), b(ROWS, WIDTH),
        buf(GROUPS, 16, dtype=F32), buf(GROUPS + 1, 8, dtype=F32), buf(GROUPS + 1, 8, dtype=F32),
        v(ROWS, WIDTH), buf(2, 2, WIDTH),
        buf(2, ROWS), buf(2, ROWS, dtype=F32), buf(2, HALO + ROWS, dtype=F32), v(2, ROWS, 16), v(2, ROWS, 16),
        v(ROWS, 128), v(GROUPS, ROWS, 16), buf(2, 4, 96), buf(2, ROWS), buf(3, 2, 96), buf(4, 96), buf(4, 96),
    ]
    scratch += [buf(GROUPS, 16, dtype=F32), buf(GROUPS, 16, dtype=F32), buf(16, dtype=F32), buf(3, 4, 16, dtype=F32)]
    scratch += [buf(8, dtype=F32), buf(4, 4, 8, dtype=F32), v(1, WIDTH)]
    scratch += [buf(2, 2, 4, 2, 2, SUB), buf(2, 2, 4, 4, SUB), buf(2, 2, 2, 2, 4, SUB)]
    scratch += [buf(2, 2, 4, 2, 2, 16), buf(2, 2, 4, 4, 16), buf(2, 2, 2, 2, 4, 16)]
    scratch += [buf(3, 3, 4, SUB), buf(3, 3, 4, SUB), buf(3, 3, 2, 2, SUB), buf(9, 3, SUB)]
    scratch += [sem((27,)), sem((90,)), sem((8,)), sem((8,)), sem, sem, sem, sem, sem((10,)), sem((10,)), sem((8,)), sem((8,)),
                sem((3,)), sem((9,)), sem((3,)), sem((12,)), sem((2, 2)), sem((2, 5)), sem((13,)), pltpu.SemaphoreType.REGULAR]
    names = ("x_conv", "d_x", "x_pre", "cols", "d_cols", "cot_t", "cot_t2", "out_in", "out_in2", "normed_t", "normed_t2", "d_z",
             "d_z2", "state", "d_state")
    return pl.pallas_call(
        backward_kernel,
        out_shape=(sds(96, 2, COLS), sds(96, COLS), sds(96, 256), sds(HEADS, 96), sds(5, COLS), sds(5, 256), sds(HEADS), sds(HEADS),
                   sds(HEADS), sds(COLS), sds(WIDTH), sds(ROWS, WIDTH)),
        in_specs=[hbm] * 19 + [vmem] * 10,
        out_specs=(vmem,) * 12,
        scratch_shapes=scratch,
        compiler_params=pltpu.CompilerParams(collective_id=1, has_side_effects=True, vmem_limit_bytes=63 * 2**20),
        name="backward_between_devices",
    )(w_all, *[r[name] for name in names], w_small, hid, cot, r["pk"], r["d_bc"], r["bc_pre"], r["bc_conv"], conv_bc, norm_gain,
      r["steps"], r["rates"], r["gain_part"], r["skip_part"])
def shards(hidden, grad_out, norm_gain, w_zx, w_bc, w_dt, conv_x, conv_bc, a_log, dt_bias, d_skip, gate_gain, w_out):
    w_all, w_small, r = forward(jnp.moveaxis(w_zx, 1, 0), w_out.T, w_bc, hidden, grad_out, norm_gain, w_dt.T, conv_x, conv_bc,
                                a_log, dt_bias, d_skip, gate_gain)
    w_all = w_all.reshape(2, GROUPS, WIDTH, COLS)
    w_small = w_small.reshape(WIDTH, COLS)
    zx, wo, wbc, wdt, grad_taps, grad_taps_bc, log_rate, shift, skip, gate, norm, grad_hidden = backward(
        w_all, r, w_small, hidden, grad_out, norm_gain, conv_bc)
    return (r["result"], grad_hidden, norm, zx, wbc, wdt.T, grad_taps, grad_taps_bc, log_rate, shift, skip, gate, wo.T)


def solution(mesh):
    finer = Mesh(mesh.devices.reshape(2, 4, 2, 4, 2), DP_MP)
    rows = P(DP_MP, None)
    placed = (rows, rows, P(), P(DP, None, MP), P(DP, None), P(DP, MP), P(None, MP), P(), P(MP), P(MP), P(MP), P(MP),
              P(MP, DP))
    return jax.shard_map(
        shards,
        mesh=finer,
        in_specs=placed,
        out_specs=(rows, rows, P(), P(DP, None, MP), P(DP, None), P(DP, MP), P(None, MP), P(), P(MP), P(MP), P(MP), P(MP),
                   P(MP, DP)),
        check_vma=False,
    )
```

```python
import jax
import jax.numpy as jnp
from jax import lax
from jax.experimental import pallas as pl
from jax.experimental.pallas import tpu as pltpu
from jax.sharding import Mesh
from jax.sharding import PartitionSpec as P

MP = ("z", "yhi")
DP = ("ylo", "x", "core")
DP_MP = DP + MP
BLOCKS = 8
F32 = jnp.float32
BF16 = jnp.bfloat16
ROWS = 256
WIDTH = 1536
GROUPS = 8
COLS = 384
HEADS = 6
HALO = 16
EPS = 1e-05
INNER = GROUPS * COLS
VMEM_LIMIT = 56 * 2**20


def dot(a, b, contract=(1, 0), precision=None):
    return lax.dot_general(
        a, b, (((contract[0],), (contract[1],)), ((), ())),
        preferred_element_type=F32, precision=precision,
    )


def spread(per_head):
    rows = per_head.shape[0]
    low = lax.broadcasted_iota(jnp.int32, (rows, 128), 1) < 64
    tiles = [
        jnp.where(low, per_head[:, 2 * i : 2 * i + 1], per_head[:, 2 * i + 1 : 2 * i + 2])
        for i in range(COLS // 128)
    ]
    return jnp.concatenate(tiles, axis=1)


def gathered_heads(values):
    rows = values.shape[0]
    low = lax.broadcasted_iota(jnp.int32, (rows, 128), 1) < 64
    lane = lax.broadcasted_iota(jnp.int32, (rows, 8), 1)
    out = jnp.zeros((rows, 8), F32)
    for i in range(COLS // 128):
        tile = values[:, 128 * i : 128 * i + 128]
        first = jnp.sum(jnp.where(low, tile, 0.0), axis=1, keepdims=True)
        both = jnp.sum(tile, axis=1, keepdims=True)
        out = jnp.where(lane == 2 * i, first, out)
        out = jnp.where(lane == 2 * i + 1, both - first, out)
    return out


def softplus(v):
    return jnp.maximum(v, 0.0) + jnp.log1p(jnp.exp(-jnp.abs(v)))


def conv_pre(ext, taps):
    total = taps[4:5]
    for j in range(4):
        total = total + ext[HALO - 3 + j : HALO - 3 + j + ROWS] * taps[j : j + 1]
    return total


def conv_transposed(ext, taps, rows=ROWS):
    total = ext[3 : 3 + rows] * taps[0:1]
    for j in range(1, 4):
        total = total + ext[3 - j : 3 - j + rows] * taps[j : j + 1]
    return total


def conv_grads(dpre, ext, sixth, seventh):
    rows = [
        jnp.sum(dpre * ext[HALO - 3 + j : HALO - 3 + j + ROWS], axis=0, keepdims=True)
        for j in range(4)
    ]
    rows.append(jnp.sum(dpre, axis=0, keepdims=True))
    rows += [sixth, seventh, jnp.zeros((1, dpre.shape[1]), F32)]
    return jnp.concatenate(rows, axis=0)


def triangle(upper):
    row = lax.broadcasted_iota(jnp.int32, (ROWS, ROWS), 0)
    col = lax.broadcasted_iota(jnp.int32, (ROWS, ROWS), 1)
    return row <= col if upper else row >= col


def sds(*shape, dtype=F32):
    return jax.ShapeDtypeStruct(shape, dtype)


def params():
    return pltpu.CompilerParams(vmem_limit_bytes=VMEM_LIMIT)


MESHID = pl.DeviceIdType.MESH
ORDERS = (("x", "y", "z"), ("y", "z", "x"), ("z", "x", "y"))
SUB = 32


def neighbour(axis, s):
    if axis == "core":
        return {"core": 1 - lax.axis_index("core")}
    if axis == "y":
        y = lax.rem(lax.axis_index("yhi") * 2 + lax.axis_index("ylo") + (s + 4), 4)
        return {"ylo": lax.rem(y, 2), "yhi": y // 2}
    return {axis: lax.rem(lax.axis_index(axis) + (s + 4), 4)}


def my_place():
    return {"x": lax.axis_index("x"), "z": lax.axis_index("z"), "y": lax.axis_index("yhi") * 2 + lax.axis_index("ylo")}


def block_device(p):
    return {"z": p // 2, "yhi": lax.rem(p, 2)}


def f32(ref):
    return ref[...].astype(F32)


class Sender:
    def __init__(self):
        self.pending = {}

    def __call__(self, src, dst, send, recv, device):
        c = pltpu.make_async_remote_copy(src_ref=src, dst_ref=dst, send_sem=send, recv_sem=recv, device_id=device,
                                         device_id_type=MESHID)
        c.start()
        self.pending[id(c)] = c
        return c

    def sent(self, c):
        c.wait_send()
        del self.pending[id(c)]

    def all_sent(self):
        for c in self.pending.values():
            c.wait_send()


def greet():
    bar = pltpu.get_barrier_semaphore()
    for a in "xyz":
        for s in (1, 2, 3):
            pl.semaphore_signal(bar, inc=1, device_id=neighbour(a, s), device_id_type=MESHID)
    for d in (1, 2, 3):
        diagonal = {"z": lax.rem(lax.axis_index("z") + d, 4), "yhi": 1 - lax.axis_index("yhi")}
        pl.semaphore_signal(bar, inc=1, device_id=diagonal, device_id_type=MESHID)
    pl.semaphore_signal(bar, inc=1, device_id=neighbour("core", 1), device_id_type=MESHID)
    return lambda: pl.semaphore_wait(bar, 13)


def to_peers(rc, src_of, dst, send, recv, block):
    out = []
    for d in range(1, 8):
        p = lax.rem(block + d, 8)
        out.append(rc(src_of(p), dst.at[block], send.at[d], recv.at[d], block_device(p)))
    return out


PIECES = (((0, 32), (32, 32), (64, 32)),) * 3


class Gather:
    def __init__(self, rc, g, w, sems, item, r):
        self.rc, self.g, self.w, self.item, self.r = rc, g, w, item, r
        self.flying = {}
        self.ts, self.tr, self.cs, self.cr = sems
        self.k = item * 3 + r
        self.lo, self.n = PIECES[item][r]
        self.me = my_place()
        self.core = lax.axis_index("core")
        self.forwarded = []

    def at(self, pos, lo=0, n=None):
        z = slice(None) if pos["z"] is None else pos["z"]
        x = slice(None) if pos["x"] is None else pos["x"]
        if pos["y"] is None:
            yh = yl = slice(None)
        else:
            yh, yl = pos["y"] // 2, lax.rem(pos["y"], 2)
        return self.g.at[z, yh, yl, x, self.core, pl.ds(self.lo + lo, self.n if n is None else n)]

    def pos(self, st, d=0):
        p = {a: (None if i < st else self.me[a]) for i, a in enumerate(ORDERS[self.r])}
        a = ORDERS[self.r][st]
        p[a] = lax.rem(self.me[a] + (d + 4), 4)
        return p

    def to_sibling(self, ref):
        k = self.k * 4 + len(self.forwarded)
        self.forwarded.append(self.rc(ref, ref, self.cs.at[k], self.cr.at[k], neighbour("core", 1)))

    def push(self, k, src, dst, a, d):
        s = k % 3 if k < 6 else k % 2
        if s in self.flying:
            self.rc.sent(self.flying[s])
        c = self.rc(src, dst, self.ts.at[3 * self.k + s], self.tr.at[10 * self.k + k], neighbour(a, d))
        self.flying[s] = c
        return c

    def straight(self, st):
        ref = self.at(self.pos(st))
        src = ref if st else self.w.at[pl.ds(self.lo, self.n)]
        self.c = [self.push(3 * st + d - 1, src, ref, ORDERS[self.r][st], d) for d in (1, 2, 3)]

    def line(self, st):
        for c in self.c:
            c.wait_recv()
        if st == 1:
            self.to_sibling(self.at(self.pos(2)))

    def near(self):
        ref = self.at(self.pos(2))
        self.c = [self.push(6 + i, ref, ref, ORDERS[self.r][2], d) for i, d in enumerate((1, -1))]

    def pass_on(self):
        self.f = []
        for i, d in enumerate((1, -1)):
            self.c[i].wait_recv()
            p = self.pos(2, -d)
            first = 16 * ((self.n + 16) // 32)
            lo, n = ((0, first), (first, self.n - first))[i]
            if n:
                half = self.at(p, lo, n)
                self.f.append(self.push(8 + i, half, half, ORDERS[self.r][2], d))
            self.to_sibling(self.at(p))

    def last(self):
        for f in self.f:
            f.wait_recv()
        self.to_sibling(self.at(self.pos(2, 2)))

    def complete(self):
        for c in self.forwarded:
            c.wait_recv()

    def drained(self):
        for c in [*self.flying.values(), *self.forwarded]:
            self.rc.sent(c)


def forward_kernel(zx_ref, wo_ref, bc_ref, hid, cot_ref, norm_gain, dt_ref, conv_x, taps_bc, log_ref, shift_ref, skip_ref,
                   gate_ref, g_ref, gb_ref,
                   pk_out, x_pre_out, x_conv_out, d_x_out, normed_t_out, cot_t_out, state_out, bc_pre_out, bc_conv_out,
                   steps_out, rates_out, cols_out, cum_row_out, step_row_out, dec_out, result_out,
                   out_in_out, d_z_out, gain_part_out, skip_part_out, d_cols_out, d_bc_out, d_state_out,
                   normed_t2_out, cot_t2_out, out_in2_out, d_z2_out, *scr):
    (pk, x_pre, x_conv, normed_t, cot_t, state, bc_pre, bc_conv, steps, rates, cols, cum_row, step_row, dec,
     result, out_in, d_z, gain_part, skip_part, d_cols, d_bc,
     cot, normed, halo, dt_own, small_all, zb, yb, uppers, lowers, wx, wo, gram, d_gram, local, rec_a, out_b, dec_own, square,
     scales, acc, d_c, pk_ref, gain,
     ts, tr, cs, cr, bs, br, qs, qr, es, er, fs, fr, ds, dr, hs, hr, lsem, wsem, osem, xs, xr) = scr
    rc = Sender()
    me = my_place()
    core = lax.axis_index("core")
    x, ylo = me["x"], lax.axis_index("ylo")
    block = lax.axis_index("z") * 2 + lax.axis_index("yhi")
    arrived = greet()
    writes, count = [], [0]

    def out(src, dst):
        c = pltpu.make_async_copy(src, dst, osem.at[count[0]])
        c.start()
        count[0] += 1
        writes.append(c)

    cot_c = pltpu.make_async_copy(cot_ref, cot, lsem.at[3])
    cot_c.start()
    def spot(ref):
        return ref.at[me["z"], me["y"] // 2, ylo, x, core]

    own_w = [pltpu.make_async_copy(src, spot(dst), lsem.at[4 + i])
             for i, (src, dst) in enumerate(((zx_ref.at[1], wx), (zx_ref.at[0], g_ref.at[1]), (wo_ref, wo)))]
    for c in own_w:
        c.start()
    pk_ref[...] = jnp.zeros_like(pk_ref)
    pk_ref[0:5] = conv_x[...]
    pk_ref[5] = gate_ref[...]
    for at, ref in ((6, log_ref), (7, shift_ref), (14, skip_ref)):
        pk_ref[at, 0:HEADS] = ref[...]
    pk_ref[8 : 8 + HEADS, 0:96] = dt_ref[...].astype(F32)
    gain[0] = norm_gain[...]
    arrived()

    gx, gz, go = [[Gather(rc, g, w, (ts, tr, cs, cr), i, r) for r in range(3)]
                  for i, (g, w) in enumerate(((wx, zx_ref.at[1]), (g_ref.at[1], zx_ref.at[0]), (wo, wo_ref)))]

    def each(group, name, *args):
        for c in group:
            getattr(c, name)(*args)

    each(gx, "straight", 0)
    pk_c = to_peers(rc, lambda p: pk_ref, pk, qs, qr, block)

    def small(lo, n):
        cols = pl.ds(lo, n)
        sems = iter(range(9 * (lo // 256), 9 * (lo // 256) + 9))

        def push(src, dst, device):
            k = next(sems)
            return rc(src, dst, bs.at[k], br.at[k], device)

        def at(yl, x_at):
            return gb_ref.at[yl, x_at, core, :, cols]

        def over_y(src):
            own = pltpu.make_async_copy(src, at(ylo, x), lsem.at[1 + lo // 256])
            own.start()
            return [push(src, at(ylo, x), {"ylo": 1 - ylo}), push(src, at(ylo, x), neighbour("core", 1))], own

        def over_x(first, own):
            first[0].wait_recv()
            own.wait()
            line = gb_ref.at[:, x, core, :, cols]
            other = at(1 - ylo, x)
            rest = [push(line, line, neighbour("x", d)) for d in (1, 2, 3)]
            return rest, [first[1], push(other, other, neighbour("core", 1))]

        def to_sibling(rest, cores):
            for d in (1, 2, 3):
                rest[d - 1].wait_recv()
                line = gb_ref.at[:, lax.rem(x + 4 - d, 4), core, :, cols]
                cores.append(push(line, line, neighbour("core", 1)))
            return cores

        return over_y, over_x, to_sibling

    bc_y, bc_x, bc_end = small(0, 256)
    dt_y, dt_x, dt_end = small(256, 128)
    bc_s = bc_y(bc_ref)
    pk[block] = pk_ref[...]

    def normalize(part, at):
        v = part[...].astype(F32)
        r = lax.rsqrt(jnp.mean(v * v, axis=1, keepdims=True) + EPS)
        normed[pl.ds(at, part.shape[0])] = (v * r * gain[...]).astype(BF16)

    normalize(hid, HALO)
    each(gx, "line", 0)
    for c in own_w:
        c.wait()
    each(gx, "straight", 1)
    halo_c = rc(hid.at[pl.ds(ROWS - HALO, HALO)], halo, hs, hr, block_device(lax.rem(block + 1, 8)))

    for c in pk_c:
        c.wait_recv()
    out(pk, pk_out)
    columns = jnp.concatenate([pk[m, 8 : 8 + HEADS, 0:128] for m in range(GROUPS)] + [jnp.zeros((80, 128), F32)], axis=0)
    dt_own[...] = columns.T[:96].astype(BF16)
    dt_s = dt_y(dt_own)
    normed_t[...] = normed[HALO:, :].T.reshape(8, 2, 96, ROWS)
    out(normed_t, normed_t_out)
    each(gx, "line", 1)
    each(gx, "near")
    bc_s = bc_x(*bc_s)
    dt_s = dt_x(*dt_s)
    each(gz, "straight", 0)
    each(go, "straight", 0)
    cot_c.wait()
    cot_t[...] = cot[...].T.reshape(8, 2, 96, ROWS)
    out(cot_t, cot_t_out)
    halo_c.wait_recv()
    normalize(halo, 0)

    @pl.when(block == 0)
    def _():
        normed[pl.ds(0, HALO)] = jnp.zeros((HALO, WIDTH), BF16)

    each(gx, "pass_on")
    each(gz, "line", 0)
    each(gz, "straight", 1)
    b_core = bc_end(*bc_s) + dt_end(*dt_s)
    for c in b_core:
        c.wait_recv()
    small_in = pltpu.make_async_copy(gb_ref, small_all, lsem.at[1])
    small_in.start()
    each(go, "line", 0)
    each(go, "straight", 1)
    small_in.wait()

    def row(at):
        pieces = [pk[m, at : at + 1, 0:HEADS] for m in range(GROUPS)]
        return jnp.concatenate(pieces + [jnp.zeros((1, 80), F32)], axis=1)

    rates[0:1] = row(6)
    rates[1:2] = row(7)
    rates[2:8] = jnp.zeros((6, 128), F32)
    little = dot(normed[...], small_all[...].reshape(WIDTH, COLS))
    bc_pre[...] = little[:, :256]
    pre = conv_pre(little[:, :256], taps_bc[...])
    bc_conv[...] = (pre * jax.nn.sigmoid(pre)).astype(BF16)
    shifted = little[HALO:, 256:384] + rates[1:2]
    steps[...] = shifted
    step = softplus(shifted)
    decay = -step * jnp.exp(rates[0:1])
    cum = dot(triangle(False).astype(F32), decay, precision=lax.Precision.HIGHEST)
    cum_t = cum.T
    step_t = step.T
    lasts = jnp.broadcast_to(jnp.exp(cum_t[:, ROWS - 1 : ROWS]), (128, 128))
    for m in range(GROUPS):
        at = slice(HEADS * m, HEADS * m + 8)
        cols[m] = jnp.concatenate([cum[:, at], step[:, at]], axis=1)
        cum_row[m] = cum_t[HEADS * m : HEADS * m + 8]
        step_row[m] = step_t[HEADS * m : HEADS * m + 8]
        dec_own[m] = lasts[HEADS * m : HEADS * m + 8]
    dec_c = to_peers(rc, lambda p: dec_own.at[p], dec, ds, dr, block)
    dec[block] = dec_own[block]
    gram[...] = jnp.where(triangle(False), dot(bc_conv[:, 128:], bc_conv[:, :128], (1, 1)), 0.0)
    out(bc_pre, bc_pre_out)
    out(bc_conv, bc_conv_out)
    out(steps, steps_out)
    out(rates, rates_out)
    out(cols, cols_out)
    out(cum_row, cum_row_out)
    out(step_row, step_row_out)
    each(gx, "last")
    each(gz, "line", 1)
    each(gz, "near")
    each(gx, "complete")

    x_flat, o_flat = wx.reshape(GROUPS, WIDTH, COLS), wo.reshape(GROUPS, WIDTH, COLS)
    g_flat = g_ref.reshape(2, GROUPS, WIDTH, COLS)

    def z_copy(m):
        return pltpu.make_async_copy(g_flat.at[1, m], x_flat.at[m], wsem.at[m])

    def pairs(buf, lo, hi, body, ready=None):
        @pl.loop(lo, hi)
        def _(i):
            if ready is not None:
                for k in range(2):
                    ready(2 * i + k).wait()
            body(i, jnp.concatenate([buf[2 * i], buf[2 * i + 1]], axis=1))

    out(wx, g_ref.at[0])
    x_written = writes.pop()

    def to_owner(m):
        return pltpu.make_async_remote_copy(src_ref=local.at[m], dst_ref=rec_a.at[block], send_sem=es.at[m], recv_sem=er.at[block],
                                            device_id=block_device(m), device_id_type=MESHID)

    def second_pair(i, w):
        both = dot(normed[...], w)
        for k in range(2):
            m = 2 * i + k
            ext = both[:, COLS * k : COLS * k + COLS]
            x_pre[m] = ext
            pre = conv_pre(ext, pk[m])
            xc = (pre * jax.nn.sigmoid(pre)).astype(BF16)
            x_conv[m] = xc
            cum, step = cols[m][:, :8], cols[m][:, 8:]
            weighted = (xc.astype(F32) * spread(step * jnp.exp(cum[ROWS - 1 : ROWS] - cum))).astype(BF16)
            local[m] = dot(weighted, bc_conv[:, :128], (0, 0)).astype(BF16)
            pl.when(m != block)(lambda m=m: to_owner(m).start())

    pairs(x_flat, 0, 4, second_pair)
    each(go, "line", 1)
    rec_a[block] = local[block]
    out(x_pre, x_pre_out)
    out(x_conv, x_conv_out)

    top, low = slice(0, HALF), slice(HALF, ROWS)

    def scan_group(m):
        xc = x_conv[m]
        cum = cols[m][:, :8]
        rows = cum_row[m]
        step_rows = step_row[m]
        parts = []
        for h in range(HEADS):
            xh = xc[:, 64 * h : 64 * h + 64]
            col, row, step = cum[:, h : h + 1], rows[h : h + 1, :], step_rows[h : h + 1, :]
            upper = (jnp.exp(jnp.minimum(col[top] - row[:, top], 0.0)) * step[:, top]).astype(BF16)
            lower = (jnp.exp(jnp.minimum(col[low] - row, 0.0)) * step).astype(BF16)
            uppers[m, h] = upper
            lowers[m, h] = lower
            parts.append(jnp.concatenate([dot((upper.astype(F32) * gram[top, top]).astype(BF16), xh[top]),
                                          dot((lower.astype(F32) * gram[low]).astype(BF16), xh)], axis=0))
        yb[m] = jnp.concatenate(parts, axis=1) + spread(pk[m, 14:15, 0:8]) * xc.astype(F32)

    pl.loop(0, 4)(scan_group)
    each(gz, "pass_on")
    each(go, "near")
    pl.loop(4, GROUPS)(scan_group)
    for c in dec_c:
        c.wait_recv()
    out(dec, dec_out)

    def exchanged(src, sends, recvs):
        for d in range(1, 8):
            other = lax.rem(block + d, 8)
            pltpu.make_async_remote_copy(src_ref=src.at[other], dst_ref=rec_a.at[other], send_sem=sends.at[other],
                                         recv_sem=recvs.at[other], device_id=block_device(other), device_id_type=MESHID).wait()

    def carry(order):
        for h in range(HEADS):
            rows = pl.ds(64 * h, 64)
            run = jnp.zeros((64, 128), F32)
            for i in order:
                out_b[i, rows] = run.astype(BF16)
                run = run * dec[i, pl.ds(h, 1)] + rec_a[i, rows].astype(F32)

    exchanged(local, es, er)
    carry(range(BLOCKS))
    f_c = to_peers(rc, lambda p: out_b.at[p], state, fs, fr, block)
    state[block] = out_b[block]
    each(gz, "last")
    each(gz, "complete")
    x_written.wait()
    each(gx, "drained")
    for m in range(GROUPS):
        z_copy(m).start()

    def gate_pair(i, w):
        z = dot(normed[HALO:, :], w)
        for k in range(2):
            zb[2 * i + k] = z[:, COLS * k : COLS * k + COLS]

    pairs(x_flat, 0, 4, gate_pair, z_copy)
    each(go, "pass_on")
    for c in f_c:
        c.wait_recv()
        rc.sent(c)
    out(state, state_out)
    square[...] = jnp.zeros_like(square)
    c_mat = bc_conv[:, 128:]

    @pl.loop(0, GROUPS)
    def _(m):
        carried = dot(c_mat, state[m], (1, 1))
        y = yb[m] + spread(jnp.exp(cols[m][:, :8])) * carried
        z = zb[m]
        sig = jax.nn.sigmoid(z)
        act = z * sig
        gated = y * act
        yb[m] = gated
        zb[m] = act
        d_z[m] = (y * sig * (1.0 + z * (1.0 - sig))).astype(BF16)
        sq = gated * gated
        square[...] += sq[:, :128] + sq[:, 128:256] + sq[:, 256:]

    r2 = lax.rsqrt(jnp.sum(square[...], axis=1, keepdims=True) / INNER + EPS)

    @pl.loop(0, GROUPS)
    def _(m):
        out_in[m] = (yb[m] * r2 * pk[m, 5:6]).astype(BF16)

    acc[...] = jnp.zeros_like(acc)
    d_c[...] = jnp.zeros_like(d_c)
    d_gram[...] = jnp.zeros_like(d_gram)
    each(go, "last")
    each(go, "complete")

    def result_pair(i, w):
        acc[...] += dot(jnp.concatenate([out_in[2 * i], out_in[2 * i + 1]], axis=1), w, (1, 1))

    pairs(o_flat, 0, 4, result_pair)
    total = jnp.sum(cot[...].astype(F32) * acc[...], axis=1, keepdims=True)
    scales[...] = jnp.concatenate([r2, r2 * r2 * (total / INNER), jnp.zeros((ROWS, 6), F32)], axis=1)
    result[...] = (hid[...].astype(F32) + acc[...]).astype(BF16)
    out(result, result_out)

    def to_owner_back(m):
        return pltpu.make_async_remote_copy(src_ref=local.at[m], dst_ref=rec_a.at[block], send_sem=es.at[m], recv_sem=er.at[block],
                                            device_id=block_device(m), device_id_type=MESHID)

    def gate_back(i, w):
        r2, slope = scales[:, 0:1], scales[:, 1:2]
        both = dot(cot[...], w)
        for k in range(2):
            m = 2 * i + k
            d = both[:, COLS * k : COLS * k + COLS]
            gated = yb[m]
            gain_part[m] = jnp.sum(d * (gated * r2), axis=0, keepdims=True)
            d_gated = r2 * (d * pk[m, 5:6]) - gated * slope
            dy = d_gated * zb[m]
            d_z[m] = (d_gated * d_z[m].astype(F32)).astype(BF16)
            yb[m] = dy
            skip_part[m] = jnp.sum(dy * x_conv[m].astype(F32), axis=0, keepdims=True)
            scaled = spread(jnp.exp(cols[m][:, :8])) * dy
            dye = scaled.astype(BF16)
            local[m] = dot(dye, c_mat, (0, 0)).astype(BF16)
            pl.when(m != block)(lambda m=m: to_owner_back(m).start())
            d_c[...] += dot(dye, state[m])
            d_cols[m] = jnp.concatenate([gathered_heads(scaled * dot(c_mat, state[m], (1, 1))), jnp.zeros((ROWS, 8), F32)], axis=1)

    pairs(o_flat, 0, 4, gate_back)
    rec_a[block] = local[block]
    across = [rc(src, dst, xs.at[i], xr.at[i], neighbour("core", 1)) for i, (src, dst) in enumerate((
        (cot_t.at[:, 1 - core], cot_t2_out), (out_in, out_in2_out), (normed_t.at[:, 1 - core], normed_t2_out),
        (d_z, d_z2_out)))]
    out(out_in, out_in_out)
    out(d_z, d_z_out)
    out(gain_part, gain_part_out)

    def d_x_copy(m):
        return pltpu.make_async_copy(zb.at[m], d_x_out.at[m], wsem.at[m])

    def inner_group(m):
        dy = yb[m]
        dyb = dy.astype(BF16)
        dy_t = dyb.T
        xc = x_conv[m]
        d_cum = d_cols[m][:, :8]
        lane = lax.broadcasted_iota(jnp.int32, (ROWS, 8), 1)
        parts = []
        sums = []
        for h in range(HEADS):
            xh = xc[:, 64 * h : 64 * h + 64]
            dyh = dyb[:, 64 * h : 64 * h + 64]
            upper, lower = uppers[m, h].astype(F32), lowers[m, h].astype(F32)
            tu = upper * dot(dyh[top], xh[top], (1, 1))
            tl = lower * dot(dyh[low], xh, (1, 1))
            d_gram[top, top] += tu
            d_gram[low] += tl
            qu, ql = tu * gram[top, top], tl * gram[low]
            col = jnp.sum(ql, axis=0, keepdims=True)
            sums.append(jnp.concatenate([col[:, top] + jnp.sum(qu, axis=0, keepdims=True), col[:, low]], axis=1))
            row = jnp.concatenate([jnp.sum(qu, axis=1, keepdims=True),
                                   jnp.sum(ql[:, top] + ql[:, low], axis=1, keepdims=True)], axis=0)
            d_cum = jnp.where(lane == h, d_cum + row, d_cum)
            dyt = dy_t[64 * h : 64 * h + 64]
            below = dot(dyt[:, low], (lower * gram[low]).astype(BF16))
            above = dot(dyt[:, top], (upper * gram[top, top]).astype(BF16))
            parts.append(jnp.concatenate([below[:, top] + above, below[:, low]], axis=1))
        sums = jnp.concatenate(sums + [jnp.zeros((2, ROWS), F32)], axis=0).T
        zb[m] = jnp.concatenate(parts, axis=0).T + spread(pk[m, 14:15, 0:8]) * dy
        d_x_copy(m).start()
        d_cols[m] = jnp.concatenate([d_cum - sums, sums], axis=1)

    pl.loop(0, GROUPS)(inner_group)
    out(skip_part, skip_part_out)
    out(d_cols, d_cols_out)
    dg = jnp.where(triangle(False), d_gram[...], 0.0).astype(BF16)
    d_bc[:, :128] = dot(dg, c_mat, (0, 0))
    d_bc[:, 128:] = d_c[...] + dot(dg, bc_conv[:, :128])
    out(d_bc, d_bc_out)
    exchanged(local, es, er)
    carry(range(BLOCKS - 1, -1, -1))
    out(out_b, d_state_out)
    for c in across:
        c.wait_recv()
    for c in writes:
        c.wait()
    for m in range(GROUPS):
        d_x_copy(m).wait()
    rc.all_sent()


HALF = ROWS // 2
RESULTS = (
    ("pk", (GROUPS, 16, COLS), F32), ("x_pre", (GROUPS, HALO + ROWS, COLS), F32), ("x_conv", (GROUPS, ROWS, COLS), BF16),
    ("d_x", (GROUPS, ROWS, COLS), F32), ("normed_t", (8, 2, 96, ROWS), BF16), ("cot_t", (8, 2, 96, ROWS), BF16),
    ("state", (GROUPS, COLS, 128), BF16), ("bc_pre", (HALO + ROWS, 256), F32), ("bc_conv", (ROWS, 256), BF16),
    ("steps", (ROWS, 128), F32), ("rates", (8, 128), F32), ("cols", (GROUPS, ROWS, 16), F32),
    ("cum_row", (GROUPS, 8, ROWS), F32), ("step_row", (GROUPS, 8, ROWS), F32), ("dec", (BLOCKS, 8, 128), F32),
    ("result", (ROWS, WIDTH), BF16), ("out_in", (GROUPS, ROWS, COLS), BF16), ("d_z", (GROUPS, ROWS, COLS), BF16),
    ("gain_part", (GROUPS, 1, COLS), F32), ("skip_part", (GROUPS, 1, COLS), F32), ("d_cols", (GROUPS, ROWS, 16), F32),
    ("d_bc", (ROWS, 256), F32), ("d_state", (GROUPS, COLS, 128), BF16),
)
SIBLING = (
    ("normed_t2", (8, 96, ROWS), BF16), ("cot_t2", (8, 96, ROWS), BF16), ("out_in2", (GROUPS, ROWS, COLS), BF16),
    ("d_z2", (GROUPS, ROWS, COLS), BF16),
)


def forward(zx, wo, bc, hid, cot, *params):
    hbm = pl.BlockSpec(memory_space=pl.ANY)
    vmem = pl.BlockSpec(memory_space=pltpu.VMEM)
    sem = pltpu.SemaphoreType.DMA

    def v(*shape, dtype=F32):
        return pltpu.VMEM(shape, dtype)

    def b(*shape):
        return v(*shape, dtype=BF16)

    groups = (GROUPS, ROWS, COLS)
    outs = pl.pallas_call(
        forward_kernel,
        out_shape=(sds(2, 4, 2, 2, 4, 2, 96, COLS, dtype=BF16), sds(2, 4, 2, 96, COLS, dtype=BF16),
                   *[sds(*shape, dtype=dtype) for _, shape, dtype in RESULTS + SIBLING]),
        in_specs=[hbm, hbm, vmem, vmem, hbm] + [vmem] * 8,
        out_specs=(hbm,) * (2 + len(RESULTS) + len(SIBLING)),
        scratch_shapes=[
            *[pltpu.VMEM(shape, dtype) for name, shape, dtype in RESULTS if name not in ("d_x", "d_state")],
            b(ROWS, WIDTH), b(HALO + ROWS, WIDTH), b(HALO, WIDTH), b(96, 128), b(2, 4, 2, 96, COLS),
            v(*groups), v(*groups), b(GROUPS, HEADS, HALF, HALF), b(GROUPS, HEADS, HALF, ROWS),
            b(4, 2, 2, 4, 2, 96, COLS), b(4, 2, 2, 4, 2, 96, COLS),
            v(ROWS, ROWS), v(ROWS, ROWS),
            b(GROUPS, COLS, 128), b(GROUPS, COLS, 128), b(GROUPS, COLS, 128), v(GROUPS, 8, 128),
            v(ROWS, 128), v(ROWS, 8), v(ROWS, WIDTH), v(ROWS, 128), v(16, COLS), v(1, WIDTH),
            sem((27,)), sem((90,)), sem((36,)), sem((36,)), sem((18,)), sem((18,)), sem((8,)), sem((8,)), sem((8,)), sem((8,)),
            sem((8,)), sem((8,)), sem((8,)), sem((8,)), sem, sem, sem((7,)), sem((GROUPS,)), sem((len(RESULTS),)), sem((4,)),
            sem((4,)),
        ],
        compiler_params=pltpu.CompilerParams(collective_id=0, has_side_effects=True, vmem_limit_bytes=62 * 2**20),
        name="forward_between_devices",
    )(zx, wo, bc, hid, cot, *params)
    return outs[0], outs[1], dict(zip([name for name, _, _ in RESULTS + SIBLING], outs[2:]))


class Total:
    def __init__(self, rc, value, lines, axes, send, recv):
        self.rc, self.value, self.lines, self.axes, self.send, self.recv = rc, value, lines, axes, send, recv
        self.me = dict(my_place(), core=lax.axis_index("core"), ylo=lax.axis_index("ylo"))

    def step(self, j):
        if j > 0:
            for c in self.flying:
                c.wait_recv()
                self.rc.sent(c)
            l, i = self.lines, j - 1
            if self.axes[i] in ("core", "ylo"):
                self.value[...] = l[i, 0] + l[i, 1]
            else:
                self.value[...] = (l[i, 0] + l[i, 1]) + (l[i, 2] + l[i, 3])
        if j < len(self.axes):
            a = self.axes[j]
            mine = self.lines.at[j, self.me[a]]
            mine[...] = self.value[...]
            if a in ("core", "ylo"):
                devices = [{a: 1 - self.me[a]}]
            else:
                devices = [neighbour(a, d) for d in (1, 2, 3)]
            self.flying = [self.rc(mine, mine, self.send.at[d], self.recv.at[3 * j + d], device)
                           for d, device in enumerate(devices)]


class SmallSum:
    def __init__(self, rc, parts, xs, ys, zs, send, recv):
        self.rc, self.parts, self.xs, self.ys, self.zs = rc, parts, xs, ys, zs
        self.send, self.recv = send, recv
        self.me = my_place()

    def step(self, j, out=None):
        rc, me, parts, s, r = self.rc, self.me, self.parts, self.send, self.recv
        ylo = lax.rem(me["y"], 2)
        if j == 0:
            self.c = [rc(parts.at[:, lax.rem(me["x"] + d, 4)], self.xs.at[d - 1], s.at[d], r.at[d], neighbour("x", d))
                      for d in (1, 2, 3)]
            return
        for c in self.c:
            c.wait_recv()
        if j == 1:
            for yl in range(2):
                m = parts.at[yl, me["x"]]
                m[...] = (f32(m) + f32(self.xs.at[0, yl]) + f32(self.xs.at[1, yl]) + f32(self.xs.at[2, yl])).astype(BF16)
            self.ys[me["y"]] = parts[ylo, me["x"]]
            self.c = [rc(parts.at[lax.rem(me["y"] + d, 2), me["x"]], self.ys.at[me["y"]], s.at[3 + d], r.at[3 + d],
                         neighbour("y", d)) for d in (1, 2, 3)]
        elif j == 2:
            y = self.ys
            m = self.zs.at[me["z"]]
            m[...] = ((f32(y.at[0]) + f32(y.at[1])) + (f32(y.at[2]) + f32(y.at[3]))).astype(BF16)
            self.c = [rc(m, m, s.at[6 + d], r.at[6 + d], neighbour("z", d)) for d in (1, 2, 3)]
        elif j == 3:
            z = self.zs
            return (f32(z.at[0]) + f32(z.at[1])) + (f32(z.at[2]) + f32(z.at[3]))


def part_of(ref, item, pos, lo, n):
    z = slice(None) if pos["z"] is None else pos["z"]
    x = slice(None) if pos["x"] is None else pos["x"]
    if pos["y"] is None:
        yh = yl = slice(None)
    else:
        yh, yl = pos["y"] // 2, lax.rem(pos["y"], 2)
    return ref.at[item, z, yh, yl, x, pl.ds(lo, n)]


class Chunk:
    def __init__(self, rc, own, out, bufs, sems, item, slot, wide, r):
        self.rc, self.own, self.out, self.item, self.slot, self.r = rc, own, out, item, slot, r
        full, half, second, third = bufs
        self.full, self.half = full[r].at[wide], half[r].at[wide]
        self.direct = {1: second[r].at[slot], 2: third.at[slot * 3 + r]}
        self.send, self.recv = sems
        self.number = slot * 3 + r
        self.base = self.number * 10
        self.me = my_place()
        self.flying = {}

    def slab(self, st, d, lo=0, n=SUB):
        p = {a: (self.me[a] if i < st else None) for i, a in enumerate(ORDERS[self.r])}
        a = ORDERS[self.r][st]
        p[a] = lax.rem(self.me[a] + (d + 4), 4)
        return part_of(self.own, self.slot, p, self.r * SUB + lo, n)

    def loop(self, st, body):
        sizes = []
        for a, n in (("z", (4,)), ("y", (2, 2)), ("x", (4,))):
            if ORDERS[self.r].index(a) > st:
                sizes += n
        if not sizes:
            body(())
        elif len(sizes) == 1 or sizes == [2, 2]:
            for i in range(4):
                body((i,) if len(sizes) == 1 else (i // 2, i % 2))
        else:
            @pl.loop(0, 4)
            def _(i):
                for k in range(4):
                    if sizes == [4, 4]:
                        body((i, k))
                    elif sizes == [4, 2, 2]:
                        body((i, k // 2, k % 2))
                    else:
                        body((i // 2, lax.rem(i, 2), k))

    def push(self, k, src, dst, st, d):
        s = k % 2 if k < 4 else (k - 4) % 3
        if s in self.flying:
            self.rc.sent(self.flying[s])
        c = self.rc(src, dst, self.send.at[3 * self.number + s], self.recv.at[self.base + k], neighbour(ORDERS[self.r][st], d))
        self.flying[s] = c
        return c

    def far(self):
        self.far_c = [self.push(i, self.slab(0, 2, 16 * i, 16), self.half.at[i], 0, d) for i, d in enumerate((1, -1))]

    def near(self):
        self.near_c = []
        for i, d in enumerate((1, -1)):
            self.far_c[i].wait_recv()
            mine = self.slab(0, d, 16 * i, 16)

            def add(index, mine=mine, i=i):
                m = mine.at[index]
                m[...] = m[...] + self.half[(i, *index)]

            self.loop(0, add)
            self.near_c.append(self.push(2 + i, self.slab(0, d), self.full.at[i], 0, d))

    def straight(self, st):
        self.straight_c = [self.push(1 + 3 * st + d - 1, self.slab(st, d), self.direct[st].at[d - 1], st, d) for d in (1, 2, 3)]

    def step(self, j):
        if j == 0:
            self.far()
        elif j == 1:
            self.near()
        elif j == 2:
            for c in self.near_c:
                c.wait_recv()
            mine = self.slab(0, 0)

            def add(index):
                m = mine.at[index]
                m[...] = (f32(m) + f32(self.full.at[(0, *index)]) + f32(self.full.at[(1, *index)])).astype(BF16)

            self.loop(0, add)
            self.straight(1)
        else:
            for c in self.straight_c:
                c.wait_recv()
            st = j - 2
            mine = self.slab(st, 0)
            got = self.direct[st]

            def total(index):
                m = mine.at[index] if index else mine
                return (f32(m) + f32(got.at[(0, *index)])) + (f32(got.at[(1, *index)]) + f32(got.at[(2, *index)]))

            if st == 1:
                def add(index):
                    mine[index] = total(index).astype(BF16)

                self.loop(1, add)
                self.straight(2)
            else:
                self.out(pl.ds(self.r * SUB, SUB))[...] = total(())


def backward_kernel(g_ref, x_conv_ref, d_x_ref, x_pre_ref, cols_ref, d_cols_ref, cot_t_ref, cot_t2_ref, out_in_ref, out_in2_ref,
                    normed_t_ref, normed_t2_ref, d_z_ref, d_z2_ref, state_ref, d_state_ref, w_small_ref, hid_ref, cot_ref,
                    taps, d_bc_in, bc_pre, bc_conv, taps_bc, norm_gain, shifted, rates, gain_part, skip_part,
                    zx_out, wo_out, wbc_out, wdt_out, taps_out, taps_bc_out, log_out, shift_out, skip_out, gate_out, norm_out,
                    grad_hidden, *scr):
    (own, l_c, l_c2, l_n, l_n2, rhs_o, rhs_z, rhs_x, state, d_state, w_small, hid, cot, tails, halo_src, halo_dst, acc, wbuf,
     bxc, bdx, bxp, bcols, bdc, d_b, d_all, parts, small2, s_xs, s_ys, s_zs,
     v_all, v_in, v_sum, v_lines, n_all, n_lines, gain) = scr[:37]
    bufs = [scr[37:40], scr[40:43], scr[43:46], scr[46]]
    (t_s, t_r, e_s, e_r, x_s, x_r, h_s, h_r, m_s, m_r, ss, sr, vms, vmr, vs, vr, ns, nr, wsem, lsem, isem, freed) = scr[47:]
    rc = Sender()
    gain[0] = norm_gain[...]
    core = lax.axis_index("core")
    block = lax.axis_index("z") * 2 + lax.axis_index("yhi")
    arrived = greet()

    loads = {}

    def load_in(name, *pairs):
        loads[name] = []
        for src, dst in pairs:
            c = pltpu.make_async_copy(src, dst, isem.at[sum(len(v) for v in loads.values())])
            c.start()
            loads[name].append(c)

    def ready(name):
        for c in loads[name]:
            c.wait()

    load_in("o", (cot_t_ref.at[:, core], l_c), (cot_t2_ref, l_c2), (out_in_ref, rhs_o.at[0]), (out_in2_ref, rhs_o.at[1]))
    load_in("z", (normed_t_ref.at[:, core], l_n), (normed_t2_ref, l_n2), (d_z_ref, rhs_z.at[0]), (d_z2_ref, rhs_z.at[1]))
    load_in("s", (state_ref, state), (d_state_ref.at[block], d_state.at[block]))

    outs = (lambda at: zx_out.at[at, 1], lambda at: zx_out.at[at, 0], lambda at: wo_out.at[at])

    def chunks(item, slot, wide):
        return [Chunk(rc, own, outs[item], bufs, (t_s, t_r), item, slot, wide, r) for r in range(3)]

    def steps(cs, j):
        for c in cs:
            c.step(j)

    def both_tokens(own_t, other_t):
        return jnp.concatenate([own_t[...].reshape(768, ROWS), other_t[...].reshape(768, ROWS)], axis=1)

    def gradient(left, left2, rhs, slot, ready=None):
        def one(i):
            if ready is not None:
                ready(2 * i)
                ready(2 * i + 1)
            right = jnp.concatenate([jnp.concatenate([rhs[0, 2 * i + k], rhs[1, 2 * i + k]], axis=0) for k in range(2)], axis=1)
            v = dot(both_tokens(left, left2), right).astype(BF16)
            for k in range(2):
                own[slot, i, k] = v[:, COLS * k : COLS * k + COLS].reshape(2, 4, 96, COLS)

        pl.loop(0, GROUPS // 2)(one)

    oc, zc, xc_ = chunks(2, 0, 0), chunks(1, 1, 1), chunks(0, 2, 0)
    arrived()
    back = to_peers(rc, lambda p: d_state_ref.at[p], d_state, e_s, e_r, block)
    ready("o")
    gradient(l_c, l_c2, rhs_o, 0)
    steps(oc, 0)
    ready("z")

    streams = ((x_conv_ref, bxc), (d_x_ref, bdx), (x_pre_ref, bxp), (cols_ref, bcols), (d_cols_ref, bdc))

    def load(m):
        k = lax.rem(m, 2)
        return [pltpu.make_async_copy(src.at[m], dst.at[k], lsem.at[k, i]) for i, (src, dst) in enumerate(streams)]

    for c in load(0):
        c.start()
    gradient(l_n, l_n2, rhs_z, 1)
    steps(zc, 0)
    ready("s")
    for c in back:
        c.wait_recv()
    load_in("end", (w_small_ref, w_small), (hid_ref, hid), (cot_ref, cot))

    def fifth_group(m):
        k = lax.rem(m, 2)

        @pl.when(m < GROUPS - 1)
        def _():
            for c in load(m + 1):
                c.start()

        for c in load(m):
            c.wait()
        ds = d_state[m]
        xf = bxc[k].astype(F32)
        cum, step = bcols[k][:, :8], bcols[k][:, 8:]
        last = cum[ROWS - 1 : ROWS]
        tail = jnp.exp(last - cum)
        weights = step * tail
        wide = spread(weights)
        d_weighted = dot(bc_conv[:, :128], ds, (1, 1))
        d_b[...] += dot((xf * wide).astype(BF16), ds)
        dx = bdx[k] + wide * d_weighted
        d_weights = gathered_heads(d_weighted * xf)
        both = weights * d_weights
        lane = lax.broadcasted_iota(jnp.int32, (1, 8), 1)
        product = jnp.sum(state[m].astype(F32) * ds.astype(F32), axis=1, keepdims=True)
        d_last = jnp.sum(both, axis=0, keepdims=True)
        for h in range(HEADS):
            dots = jnp.sum(product[64 * h : 64 * h + 64], axis=0, keepdims=True)
            d_last = jnp.where(lane == h, d_last + jnp.exp(last) * dots, d_last)
        row = lax.broadcasted_iota(jnp.int32, (ROWS, 8), 0)
        d_cum = bdc[k][:, :8] - both
        d_cum = jnp.where(row == ROWS - 1, d_cum + d_last, d_cum)
        d_all[m] = jnp.concatenate([d_cum, bdc[k][:, 8:] + both], axis=1)
        ext = bxp[k]
        tap = taps[m]
        pre = conv_pre(ext, tap)
        sig = jax.nn.sigmoid(pre)
        dp = dx * (sig * (1.0 + pre * (1.0 - sig)))
        v_all[m, 0:8] = conv_grads(dp, ext, gain_part[m], skip_part[m])
        whole_dx = conv_transposed(jnp.concatenate([dp, jnp.zeros((8, COLS), F32)], axis=0), tap)
        rhs_x[0, m] = whole_dx.astype(BF16)
        tails[m] = whole_dx[ROWS - 16 :]
        halo_src[m] = dp[:8]

    d_b[...] = jnp.zeros_like(d_b)
    pl.loop(0, 1)(fifth_group)
    steps(oc, 1)
    pl.loop(1, GROUPS)(fifth_group)

    d_bc = jnp.concatenate([d_bc_in[:, :128] + d_b[...], d_bc_in[:, 128:]], axis=1)
    ext = bc_pre[...]
    pre = conv_pre(ext, taps_bc[...])
    sig = jax.nn.sigmoid(pre)
    dp_bc = d_bc * (sig * (1.0 + pre * (1.0 - sig)))
    halo_src[GROUPS] = jnp.concatenate([dp_bc[:8], jnp.zeros((8, 128), F32)], axis=1)
    halo = rc(halo_src, halo_dst, h_s, h_r, block_device(lax.rem(block + 7, 8)))
    steps(oc, 2)
    steps(zc, 1)
    for a in "xyz":
        for s in (1, -1):
            pl.semaphore_signal(freed, inc=1, device_id=neighbour(a, s), device_id_type=MESHID)
    zero8 = jnp.zeros((1, 256), F32)
    d_cum = jnp.concatenate([d_all[m][:, :HEADS] for m in range(GROUPS)] + [jnp.zeros((ROWS, 80), F32)], axis=1)
    d_step = jnp.concatenate([d_all[m][:, 8 : 8 + HEADS] for m in range(GROUPS)] + [jnp.zeros((ROWS, 80), F32)], axis=1)
    d_decay = dot(triangle(True).astype(F32), d_cum, precision=lax.Precision.HIGHEST)
    rate = -jnp.exp(rates[0:1])
    v = shifted[...]
    sig = jax.nn.sigmoid(v)
    far = v < -16.0
    ratio = jnp.where(far, 1.0, sig / jnp.where(far, 1.0, softplus(v)))
    d_dt = d_step * ratio + rate * d_decay * sig
    log_grad = jnp.sum(d_decay * (softplus(v) * rate), axis=0, keepdims=True)
    shift_grad = jnp.sum(d_dt, axis=0, keepdims=True)
    bc_rows = conv_grads(dp_bc, ext, jnp.concatenate([log_grad, shift_grad], axis=1), zero8)
    bc_rows = jnp.concatenate([bc_rows, jnp.zeros((8, 128), F32)], axis=1)
    for m in range(GROUPS):
        v_all[m, 8:16] = bc_rows
    vec_c = to_peers(rc, lambda p: v_all.at[p], v_in, vms, vmr, block)
    v_in[block] = v_all[block]

    halo.wait_recv()
    inside = block < 7

    def below(k):
        return jnp.where(inside, halo_dst[k], 0.0)

    def across(m):
        return pltpu.make_async_remote_copy(src_ref=rhs_x.at[0, m], dst_ref=rhs_x.at[1, m], send_sem=x_s.at[m],
                                            recv_sem=x_r.at[m], device_id=neighbour("core", 1), device_id_type=MESHID)

    def fix(m):
        ext = jnp.concatenate([jnp.zeros((16, COLS), F32), below(m)], axis=0)
        rhs_x[0, m, pl.ds(ROWS - 16, 16)] = (tails[m] + conv_transposed(ext, taps[m], 16)).astype(BF16)
        across(m).start()

    d_bc = conv_transposed(jnp.concatenate([dp_bc, below(GROUPS)[:, :256]], axis=0), taps_bc[...])
    small2[0] = jnp.concatenate([d_bc, d_dt], axis=1).astype(BF16)
    small_c = rc(small2.at[0], small2.at[1], m_s, m_r, neighbour("core", 1))
    pl.loop(0, GROUPS)(fix)

    def weights(m):
        k = lax.rem(m, 2)
        return [pltpu.make_async_copy(g_ref.at[i, m], wbuf.at[k, i], wsem.at[k, i]) for i in range(2)]

    for c in weights(0):
        c.start()
    gradient(l_n, l_n2, rhs_x, 2, lambda m: across(m).wait())
    pl.semaphore_wait(freed, 6)
    steps(xc_, 0)
    small_c.wait_recv()
    parts[...] = dot(both_tokens(l_n, l_n2), small2[...].reshape(2 * ROWS, COLS)).astype(BF16).reshape(2, 4, 96, COLS)
    sums = SmallSum(rc, parts, s_xs, s_ys, s_zs, ss, sr)
    ready("end")
    acc[...] = dot(small2[0], w_small[...], (1, 1))
    def input_group(m):
        k = lax.rem(m, 2)

        @pl.when(m < GROUPS - 1)
        def _():
            for c in weights(m + 1):
                c.start()

        for c in weights(m):
            c.wait()
        lhs = jnp.concatenate([rhs_x[0, m], rhs_z[0, m]], axis=1)
        rhs = jnp.concatenate([wbuf[k, 0], wbuf[k, 1]], axis=1)
        acc[...] += dot(lhs, rhs, (1, 1))

    pl.loop(0, 2)(input_group)
    sums.step(0)
    steps(oc, 3)
    steps(zc, 2)
    pl.loop(2, 4)(input_group)
    for c in vec_c:
        c.wait_recv()
    t = v_in[0]
    for i in range(1, BLOCKS):
        t = t + v_in[i]
    v_sum[...] = t
    vec = Total(rc, v_sum, v_lines, ("core", "x", "ylo"), vs, vr)
    vec.step(0)
    steps(xc_, 1)
    pl.loop(4, GROUPS)(input_group)
    v = hid[...].astype(F32)
    r = lax.rsqrt(jnp.mean(v * v, axis=1, keepdims=True) + EPS)
    unit = v * r
    dn = acc[...]
    gain_grad = jnp.sum(dn * unit, axis=0, keepdims=True)
    for i in range(4):
        n_all[pl.ds(i, 1)] = gain_grad[:, COLS * i : COLS * i + COLS]
    n_all[pl.ds(4, 4)] = jnp.zeros((4, COLS), F32)
    nvec = Total(rc, n_all, n_lines, ("core", "x", "y", "z"), ns, nr)
    nvec.step(0)
    sums.step(1)
    vec.step(1)
    steps(oc, 4)
    steps(zc, 3)
    d_in = dn * gain[...]
    grad_hidden[...] = r * (d_in - unit * jnp.mean(d_in * unit, axis=1, keepdims=True)) + cot[...].astype(F32)
    nvec.step(1)
    steps(xc_, 2)
    sums.step(2)
    vec.step(2)
    nvec.step(2)
    steps(zc, 4)
    steps(xc_, 3)
    vec.step(3)
    nvec.step(3)

    pick = lax.broadcasted_iota(jnp.int32, (8, 128), 0) + block * HEADS
    pick = (pick == lax.broadcasted_iota(jnp.int32, (8, 128), 1)).astype(F32)

    def own_heads(row):
        return dot(row, pick, (1, 1), precision=lax.Precision.HIGHEST)

    mine = v_sum[...]
    taps_out[...] = mine[:5]
    gate_out[...] = mine[5]
    skip_out[...] = gathered_heads(mine[6:7])[0, :HEADS]
    taps_bc_out[...] = mine[8:13, :256]
    log_out[...] = own_heads(mine[13:14, :128])[0, :HEADS]
    shift_out[...] = own_heads(mine[13:14, 128:256])[0, :HEADS]
    steps(xc_, 4)
    little = sums.step(3)
    wbc_out[...] = little[:, :256]
    wdt_out[...] = dot(pick, little[:, 256:], (1, 1), precision=lax.Precision.HIGHEST)[:HEADS]
    nvec.step(4)
    for i in range(4):
        norm_out[pl.ds(COLS * i, COLS)] = n_all[i]
    rc.all_sent()


def backward(w_all, r, w_small, hid, cot, norm_gain, conv_bc):
    hbm = pl.BlockSpec(memory_space=pl.ANY)
    vmem = pl.BlockSpec(memory_space=pltpu.VMEM)
    sem = pltpu.SemaphoreType.DMA

    def buf(*shape, dtype=BF16):
        return pltpu.VMEM((*shape, COLS), dtype)

    def v(*shape, dtype=F32):
        return pltpu.VMEM(shape, dtype)

    def b(*shape):
        return v(*shape, dtype=BF16)

    scratch = [
        buf(3, 4, 2, 2, 4, 96), b(8, 96, ROWS), b(8, 96, ROWS), b(8, 96, ROWS), b(8, 96, ROWS),
        buf(2, GROUPS, ROWS), buf(2, GROUPS, ROWS), buf(2, GROUPS, ROWS), b(GROUPS, COLS, 128), b(GROUPS, COLS, 128),
        buf(WIDTH), b(ROWS, WIDTH), b(ROWS, WIDTH),
        buf(GROUPS, 16, dtype=F32), buf(GROUPS + 1, 8, dtype=F32), buf(GROUPS + 1, 8, dtype=F32),
        v(ROWS, WIDTH), buf(2, 2, WIDTH),
        buf(2, ROWS), buf(2, ROWS, dtype=F32), buf(2, HALO + ROWS, dtype=F32), v(2, ROWS, 16), v(2, ROWS, 16),
        v(ROWS, 128), v(GROUPS, ROWS, 16), buf(2, 4, 96), buf(2, ROWS), buf(3, 2, 96), buf(4, 96), buf(4, 96),
    ]
    scratch += [buf(GROUPS, 16, dtype=F32), buf(GROUPS, 16, dtype=F32), buf(16, dtype=F32), buf(3, 4, 16, dtype=F32)]
    scratch += [buf(8, dtype=F32), buf(4, 4, 8, dtype=F32), v(1, WIDTH)]
    scratch += [buf(2, 2, 4, 2, 2, SUB), buf(2, 2, 4, 4, SUB), buf(2, 2, 2, 2, 4, SUB)]
    scratch += [buf(2, 2, 4, 2, 2, 16), buf(2, 2, 4, 4, 16), buf(2, 2, 2, 2, 4, 16)]
    scratch += [buf(3, 3, 4, SUB), buf(3, 3, 4, SUB), buf(3, 3, 2, 2, SUB), buf(9, 3, SUB)]
    scratch += [sem((27,)), sem((90,)), sem((8,)), sem((8,)), sem((8,)), sem((8,)), sem, sem, sem, sem, sem((10,)), sem((10,)), sem((8,)), sem((8,)),
                sem((3,)), sem((9,)), sem((3,)), sem((12,)), sem((2, 2)), sem((2, 5)), sem((13,)), pltpu.SemaphoreType.REGULAR]
    names = ("x_conv", "d_x", "x_pre", "cols", "d_cols", "cot_t", "cot_t2", "out_in", "out_in2", "normed_t", "normed_t2", "d_z",
             "d_z2", "state", "d_state")
    return pl.pallas_call(
        backward_kernel,
        out_shape=(sds(96, 2, COLS), sds(96, COLS), sds(96, 256), sds(HEADS, 96), sds(5, COLS), sds(5, 256), sds(HEADS), sds(HEADS),
                   sds(HEADS), sds(COLS), sds(WIDTH), sds(ROWS, WIDTH)),
        in_specs=[hbm] * 19 + [vmem] * 10,
        out_specs=(vmem,) * 12,
        scratch_shapes=scratch,
        compiler_params=pltpu.CompilerParams(collective_id=1, has_side_effects=True, vmem_limit_bytes=63 * 2**20),
        name="backward_between_devices",
    )(w_all, *[r[name] for name in names], w_small, hid, cot, r["pk"], r["d_bc"], r["bc_pre"], r["bc_conv"], conv_bc, norm_gain,
      r["steps"], r["rates"], r["gain_part"], r["skip_part"])
def results_kernel(*refs):
    n = (len(refs) - 2) // 3
    sems = refs[-2:]
    into = [pltpu.make_async_copy(refs[i], refs[2 * n + i], sems[0].at[i]) for i in range(n)]
    back = [pltpu.make_async_copy(refs[2 * n + i], refs[n + i], sems[1].at[i]) for i in range(n)]
    for c in into:
        c.start()
    for c, d in zip(into, back):
        c.wait()
        d.start()
    for d in back:
        d.wait()


def as_results(*arrays):
    hbm = pl.BlockSpec(memory_space=pl.ANY)
    return pl.pallas_call(
        results_kernel,
        out_shape=tuple(jax.ShapeDtypeStruct(a.shape, a.dtype) for a in arrays),
        in_specs=[hbm] * len(arrays),
        out_specs=(hbm,) * len(arrays),
        scratch_shapes=[*[pltpu.VMEM(a.shape, a.dtype) for a in arrays], *[pltpu.SemaphoreType.DMA((len(arrays),))] * 2],
        name="results",
    )(*arrays)


def shards(hidden, grad_out, norm_gain, w_zx, w_bc, w_dt, conv_x, conv_bc, a_log, dt_bias, d_skip, gate_gain, w_out):
    w_all, w_small, r = forward(jnp.moveaxis(w_zx, 1, 0), w_out.T, w_bc, hidden, grad_out, norm_gain, w_dt.T, conv_x, conv_bc,
                                a_log, dt_bias, d_skip, gate_gain)
    w_all = w_all.reshape(2, GROUPS, WIDTH, COLS)
    w_small = w_small.reshape(WIDTH, COLS)
    zx, wo, wbc, wdt, grad_taps, grad_taps_bc, log_rate, shift, skip, gate, norm, grad_hidden = backward(
        w_all, r, w_small, hidden, grad_out, norm_gain, conv_bc)
    result, grad_hidden, norm, zx, wbc, wdt, grad_taps, grad_taps_bc, log_rate, shift, skip, gate, wo = as_results(
        r["result"], grad_hidden, norm, zx, wbc, wdt, grad_taps, grad_taps_bc, log_rate, shift, skip, gate, wo)
    return (result, grad_hidden, norm, zx, wbc, wdt.T, grad_taps, grad_taps_bc, log_rate, shift, skip, gate, wo.T)


def solution(mesh):
    finer = Mesh(mesh.devices.reshape(2, 4, 2, 4, 2), DP_MP)
    rows = P(DP_MP, None)
    placed = (rows, rows, P(), P(DP, None, MP), P(DP, None), P(DP, MP), P(None, MP), P(), P(MP), P(MP), P(MP), P(MP),
              P(MP, DP))
    return jax.shard_map(
        shards,
        mesh=finer,
        in_specs=placed,
        out_specs=(rows, rows, P(), P(DP, None, MP), P(DP, None), P(DP, MP), P(None, MP), P(), P(MP), P(MP), P(MP), P(MP),
                   P(MP, DP)),
        check_vma=False,
    )
```

```python
import jax
import jax.numpy as jnp
from jax import lax
from jax.experimental import pallas as pl
from jax.experimental.pallas import tpu as pltpu
from jax.sharding import Mesh
from jax.sharding import PartitionSpec as P

MP = ("z", "yhi")
DP = ("ylo", "x", "core")
DP_MP = DP + MP
BLOCKS = 8
F32 = jnp.float32
BF16 = jnp.bfloat16
ROWS = 256
WIDTH = 1536
GROUPS = 8
COLS = 384
HEADS = 6
HALO = 16
EPS = 1e-05
INNER = GROUPS * COLS
VMEM_LIMIT = 56 * 2**20


def dot(a, b, contract=(1, 0), precision=None):
    return lax.dot_general(
        a, b, (((contract[0],), (contract[1],)), ((), ())),
        preferred_element_type=F32, precision=precision,
    )


def spread(per_head):
    rows = per_head.shape[0]
    low = lax.broadcasted_iota(jnp.int32, (rows, 128), 1) < 64
    tiles = [
        jnp.where(low, per_head[:, 2 * i : 2 * i + 1], per_head[:, 2 * i + 1 : 2 * i + 2])
        for i in range(COLS // 128)
    ]
    return jnp.concatenate(tiles, axis=1)


def gathered_heads(values):
    rows = values.shape[0]
    low = lax.broadcasted_iota(jnp.int32, (rows, 128), 1) < 64
    lane = lax.broadcasted_iota(jnp.int32, (rows, 8), 1)
    out = jnp.zeros((rows, 8), F32)
    for i in range(COLS // 128):
        tile = values[:, 128 * i : 128 * i + 128]
        first = jnp.sum(jnp.where(low, tile, 0.0), axis=1, keepdims=True)
        both = jnp.sum(tile, axis=1, keepdims=True)
        out = jnp.where(lane == 2 * i, first, out)
        out = jnp.where(lane == 2 * i + 1, both - first, out)
    return out


def softplus(v):
    return jnp.maximum(v, 0.0) + jnp.log1p(jnp.exp(-jnp.abs(v)))


def conv_pre(ext, taps):
    total = taps[4:5]
    for j in range(4):
        total = total + ext[HALO - 3 + j : HALO - 3 + j + ROWS] * taps[j : j + 1]
    return total


def conv_transposed(ext, taps, rows=ROWS):
    total = ext[3 : 3 + rows] * taps[0:1]
    for j in range(1, 4):
        total = total + ext[3 - j : 3 - j + rows] * taps[j : j + 1]
    return total


def conv_grads(dpre, ext, sixth, seventh):
    rows = [
        jnp.sum(dpre * ext[HALO - 3 + j : HALO - 3 + j + ROWS], axis=0, keepdims=True)
        for j in range(4)
    ]
    rows.append(jnp.sum(dpre, axis=0, keepdims=True))
    rows += [sixth, seventh, jnp.zeros((1, dpre.shape[1]), F32)]
    return jnp.concatenate(rows, axis=0)


def triangle(upper):
    row = lax.broadcasted_iota(jnp.int32, (ROWS, ROWS), 0)
    col = lax.broadcasted_iota(jnp.int32, (ROWS, ROWS), 1)
    return row <= col if upper else row >= col


def sds(*shape, dtype=F32):
    return jax.ShapeDtypeStruct(shape, dtype)


def params():
    return pltpu.CompilerParams(vmem_limit_bytes=VMEM_LIMIT)


MESHID = pl.DeviceIdType.MESH
ORDERS = (("x", "y", "z"), ("y", "z", "x"), ("z", "x", "y"))
SUB = 32


def neighbour(axis, s):
    if axis == "core":
        return {"core": 1 - lax.axis_index("core")}
    if axis == "y":
        y = lax.rem(lax.axis_index("yhi") * 2 + lax.axis_index("ylo") + (s + 4), 4)
        return {"ylo": lax.rem(y, 2), "yhi": y // 2}
    return {axis: lax.rem(lax.axis_index(axis) + (s + 4), 4)}


def my_place():
    return {"x": lax.axis_index("x"), "z": lax.axis_index("z"), "y": lax.axis_index("yhi") * 2 + lax.axis_index("ylo")}


def block_device(p):
    return {"z": p // 2, "yhi": lax.rem(p, 2)}


def f32(ref):
    return ref[...].astype(F32)


class Sender:
    def __init__(self):
        self.pending = {}

    def __call__(self, src, dst, send, recv, device):
        c = pltpu.make_async_remote_copy(src_ref=src, dst_ref=dst, send_sem=send, recv_sem=recv, device_id=device,
                                         device_id_type=MESHID)
        c.start()
        self.pending[id(c)] = c
        return c

    def sent(self, c):
        c.wait_send()
        del self.pending[id(c)]

    def all_sent(self):
        for c in self.pending.values():
            c.wait_send()


def greet():
    bar = pltpu.get_barrier_semaphore()
    for a in "xyz":
        for s in (1, 2, 3):
            pl.semaphore_signal(bar, inc=1, device_id=neighbour(a, s), device_id_type=MESHID)
    for d in (1, 2, 3):
        diagonal = {"z": lax.rem(lax.axis_index("z") + d, 4), "yhi": 1 - lax.axis_index("yhi")}
        pl.semaphore_signal(bar, inc=1, device_id=diagonal, device_id_type=MESHID)
    pl.semaphore_signal(bar, inc=1, device_id=neighbour("core", 1), device_id_type=MESHID)
    return lambda: pl.semaphore_wait(bar, 13)


def to_peers(rc, src_of, dst, send, recv, block):
    out = []
    for d in range(1, 8):
        p = lax.rem(block + d, 8)
        out.append(rc(src_of(p), dst.at[block], send.at[d], recv.at[d], block_device(p)))
    return out


PIECES = (((0, 32), (32, 32), (64, 32)), ((0, 16), (16, 48), (64, 32)), ((0, 32), (32, 32), (64, 32)))


class Gather:
    def __init__(self, rc, g, w, sems, item, r):
        self.rc, self.g, self.w, self.item, self.r = rc, g, w, item, r
        self.flying = {}
        self.ts, self.tr, self.cs, self.cr = sems
        self.k = item * 3 + r
        self.lo, self.n = PIECES[item][r]
        self.me = my_place()
        self.core = lax.axis_index("core")
        self.forwarded = []

    def at(self, pos, lo=0, n=None):
        z = slice(None) if pos["z"] is None else pos["z"]
        x = slice(None) if pos["x"] is None else pos["x"]
        if pos["y"] is None:
            yh = yl = slice(None)
        else:
            yh, yl = pos["y"] // 2, lax.rem(pos["y"], 2)
        return self.g.at[z, yh, yl, x, self.core, pl.ds(self.lo + lo, self.n if n is None else n)]

    def pos(self, st, d=0):
        p = {a: (None if i < st else self.me[a]) for i, a in enumerate(ORDERS[self.r])}
        a = ORDERS[self.r][st]
        p[a] = lax.rem(self.me[a] + (d + 4), 4)
        return p

    def to_sibling(self, ref):
        k = self.k * 4 + len(self.forwarded)
        self.forwarded.append(self.rc(ref, ref, self.cs.at[k], self.cr.at[k], neighbour("core", 1)))

    def push(self, k, src, dst, a, d):
        s = k % 3 if k < 6 else k % 2
        if s in self.flying:
            self.rc.sent(self.flying[s])
        c = self.rc(src, dst, self.ts.at[3 * self.k + s], self.tr.at[10 * self.k + k], neighbour(a, d))
        self.flying[s] = c
        return c

    def straight(self, st):
        ref = self.at(self.pos(st))
        src = ref if st else self.w.at[pl.ds(self.lo, self.n)]
        self.c = [self.push(3 * st + d - 1, src, ref, ORDERS[self.r][st], d) for d in (1, 2, 3)]

    def line(self, st):
        for c in self.c:
            c.wait_recv()
        if st == 1:
            self.to_sibling(self.at(self.pos(2)))

    def near(self):
        ref = self.at(self.pos(2))
        self.c = [self.push(6 + i, ref, ref, ORDERS[self.r][2], d) for i, d in enumerate((1, -1))]

    def pass_on(self):
        self.f = []
        for i, d in enumerate((1, -1)):
            self.c[i].wait_recv()
            p = self.pos(2, -d)
            first = 16 * ((self.n + 16) // 32)
            lo, n = ((0, first), (first, self.n - first))[i]
            if n:
                half = self.at(p, lo, n)
                self.f.append(self.push(8 + i, half, half, ORDERS[self.r][2], d))
            self.to_sibling(self.at(p))

    def last(self):
        for f in self.f:
            f.wait_recv()
        self.to_sibling(self.at(self.pos(2, 2)))

    def complete(self):
        for c in self.forwarded:
            c.wait_recv()

    def drained(self):
        for c in [*self.flying.values(), *self.forwarded]:
            self.rc.sent(c)


def forward_kernel(zx_ref, wo_ref, bc_ref, hid, cot_ref, norm_gain, dt_ref, conv_x, taps_bc, log_ref, shift_ref, skip_ref,
                   gate_ref, g_ref, gb_ref,
                   pk_out, x_pre_out, x_conv_out, d_x_out, normed_t_out, cot_t_out, state_out, bc_pre_out, bc_conv_out,
                   steps_out, rates_out, cols_out, cum_row_out, step_row_out, dec_out, result_out,
                   out_in_out, d_z_out, gain_part_out, skip_part_out, d_cols_out, d_bc_out, conv_slope_out, d_state_out,
                   normed_t2_out, cot_t2_out, out_in2_out, d_z2_out, *scr):
    (pk, x_pre, x_conv, normed_t, cot_t, state, bc_pre, bc_conv, steps, rates, cols, cum_row, step_row, dec,
     result, out_in, d_z, gain_part, skip_part, d_cols, d_bc, conv_slope,
     cot, normed, halo, dt_own, small_all, zb, yb, uppers, lowers, wx, wo, gram, d_gram, local, rec_a, out_b, dec_own, square,
     scales, acc, d_c, pk_ref, gain, zx,
     ts, tr, cs, cr, bs, br, qs, qr, es, er, fs, fr, ds, dr, hs, hr, lsem, wsem, osem, xs, xr) = scr
    rc = Sender()
    me = my_place()
    core = lax.axis_index("core")
    x, ylo = me["x"], lax.axis_index("ylo")
    block = lax.axis_index("z") * 2 + lax.axis_index("yhi")
    arrived = greet()
    writes, count = [], [0]

    def out(src, dst):
        c = pltpu.make_async_copy(src, dst, osem.at[count[0]])
        c.start()
        count[0] += 1
        writes.append(c)

    cot_c = pltpu.make_async_copy(cot_ref, cot, lsem.at[3])
    cot_c.start()
    def spot(ref):
        return ref.at[me["z"], me["y"] // 2, ylo, x, core]

    split = zx_ref[...].astype(F32)
    for i in range(2):
        zx[i] = split[:, i, :].astype(BF16)
    own_w = [pltpu.make_async_copy(src, spot(dst), lsem.at[4 + i])
             for i, (src, dst) in enumerate(((zx.at[1], wx), (zx.at[0], g_ref.at[1]), (wo_ref, wo)))]
    for c in own_w:
        c.start()
    pk_ref[...] = jnp.zeros_like(pk_ref)
    pk_ref[0:5] = conv_x[...]
    pk_ref[5] = gate_ref[...]
    for at, ref in ((6, log_ref), (7, shift_ref), (14, skip_ref)):
        pk_ref[at, 0:HEADS] = ref[...]
    pk_ref[8 : 8 + HEADS, 0:96] = dt_ref[...].astype(F32)
    gain[0] = norm_gain[...]
    arrived()

    gx, gz, go = [[Gather(rc, g, w, (ts, tr, cs, cr), i, r) for r in range(3)]
                  for i, (g, w) in enumerate(((wx, zx.at[1]), (g_ref.at[1], zx.at[0]), (wo, wo_ref)))]

    def each(group, name, *args):
        for c in group:
            getattr(c, name)(*args)

    each(gx, "straight", 0)
    pk_c = to_peers(rc, lambda p: pk_ref, pk, qs, qr, block)

    def small(lo, n):
        cols = pl.ds(lo, n)
        sems = iter(range(9 * (lo // 256), 9 * (lo // 256) + 9))

        def push(src, dst, device):
            k = next(sems)
            return rc(src, dst, bs.at[k], br.at[k], device)

        def at(yl, x_at):
            return gb_ref.at[yl, x_at, core, :, cols]

        def over_y(src):
            own = pltpu.make_async_copy(src, at(ylo, x), lsem.at[1 + lo // 256])
            own.start()
            return [push(src, at(ylo, x), {"ylo": 1 - ylo}), push(src, at(ylo, x), neighbour("core", 1))], own

        def over_x(first, own):
            first[0].wait_recv()
            own.wait()
            line = gb_ref.at[:, x, core, :, cols]
            other = at(1 - ylo, x)
            rest = [push(line, line, neighbour("x", d)) for d in (1, 2, 3)]
            return rest, [first[1], push(other, other, neighbour("core", 1))]

        def to_sibling(rest, cores):
            for d in (1, 2, 3):
                rest[d - 1].wait_recv()
                line = gb_ref.at[:, lax.rem(x + 4 - d, 4), core, :, cols]
                cores.append(push(line, line, neighbour("core", 1)))
            return cores

        return over_y, over_x, to_sibling

    bc_y, bc_x, bc_end = small(0, 256)
    dt_y, dt_x, dt_end = small(256, 128)
    bc_s = bc_y(bc_ref)
    pk[block] = pk_ref[...]

    def normalize(part, at):
        v = part[...].astype(F32)
        r = lax.rsqrt(jnp.mean(v * v, axis=1, keepdims=True) + EPS)
        normed[pl.ds(at, part.shape[0])] = (v * r * gain[...]).astype(BF16)

    normalize(hid, HALO)
    each(gx, "line", 0)
    for c in own_w:
        c.wait()
    each(gx, "straight", 1)
    each(gz, "straight", 0)
    halo_c = rc(hid.at[pl.ds(ROWS - HALO, HALO)], halo, hs, hr, block_device(lax.rem(block + 1, 8)))
    each(go, "straight", 0)

    for c in pk_c:
        c.wait_recv()
    out(pk, pk_out)
    columns = jnp.concatenate([pk[m, 8 : 8 + HEADS, 0:128] for m in range(GROUPS)] + [jnp.zeros((80, 128), F32)], axis=0)
    dt_own[...] = columns.T[:96].astype(BF16)
    dt_s = dt_y(dt_own)
    normed_t[...] = normed[HALO:, :].T.reshape(8, 2, 96, ROWS)
    out(normed_t, normed_t_out)
    each(gx, "line", 1)
    each(gx, "near")
    bc_s = bc_x(*bc_s)
    dt_s = dt_x(*dt_s)
    cot_c.wait()
    cot_t[...] = cot[...].T.reshape(8, 2, 96, ROWS)
    out(cot_t, cot_t_out)
    halo_c.wait_recv()
    normalize(halo, 0)

    @pl.when(block == 0)
    def _():
        normed[pl.ds(0, HALO)] = jnp.zeros((HALO, WIDTH), BF16)

    each(gx, "pass_on")
    each(gz, "line", 0)
    each(gz, "straight", 1)
    b_core = bc_end(*bc_s) + dt_end(*dt_s)
    for c in b_core:
        c.wait_recv()
    small_in = pltpu.make_async_copy(gb_ref, small_all, lsem.at[1])
    small_in.start()
    each(go, "line", 0)
    each(go, "straight", 1)
    small_in.wait()

    def row(at):
        pieces = [pk[m, at : at + 1, 0:HEADS] for m in range(GROUPS)]
        return jnp.concatenate(pieces + [jnp.zeros((1, 80), F32)], axis=1)

    rates[0:1] = row(6)
    rates[1:2] = row(7)
    rates[2:8] = jnp.zeros((6, 128), F32)
    little = dot(normed[...], small_all[...].reshape(WIDTH, COLS))
    bc_pre[...] = little[:, :256]
    pre = conv_pre(little[:, :256], taps_bc[...])
    bc_conv[...] = (pre * jax.nn.sigmoid(pre)).astype(BF16)
    shifted = little[HALO:, 256:384] + rates[1:2]
    steps[...] = shifted
    step = softplus(shifted)
    decay = -step * jnp.exp(rates[0:1])
    cum = dot(triangle(False).astype(F32), decay, precision=lax.Precision.HIGHEST)
    cum_t = cum.T
    step_t = step.T
    each(gz, "line", 1)
    each(gz, "near")
    lasts = jnp.broadcast_to(jnp.exp(cum_t[:, ROWS - 1 : ROWS]), (128, 128))
    for m in range(GROUPS):
        at = slice(HEADS * m, HEADS * m + 8)
        cols[m] = jnp.concatenate([cum[:, at], step[:, at]], axis=1)
        cum_row[m] = cum_t[HEADS * m : HEADS * m + 8]
        step_row[m] = step_t[HEADS * m : HEADS * m + 8]
        dec_own[m] = lasts[HEADS * m : HEADS * m + 8]
    dec_c = to_peers(rc, lambda p: dec_own.at[p], dec, ds, dr, block)
    dec[block] = dec_own[block]
    gram[...] = jnp.where(triangle(False), dot(bc_conv[:, 128:], bc_conv[:, :128], (1, 1)), 0.0)
    out(bc_pre, bc_pre_out)
    out(bc_conv, bc_conv_out)
    out(steps, steps_out)
    out(rates, rates_out)
    out(cols, cols_out)
    out(cum_row, cum_row_out)
    out(step_row, step_row_out)
    each(gx, "last")
    each(gx, "complete")

    x_flat, o_flat = wx.reshape(GROUPS, WIDTH, COLS), wo.reshape(GROUPS, WIDTH, COLS)
    g_flat = g_ref.reshape(2, GROUPS, WIDTH, COLS)

    def z_copy(m):
        return pltpu.make_async_copy(g_flat.at[1, m], x_flat.at[m], wsem.at[m])

    def pairs(buf, lo, hi, body, ready=None):
        @pl.loop(lo, hi)
        def _(i):
            if ready is not None:
                for k in range(2):
                    ready(2 * i + k).wait()
            body(i, jnp.concatenate([buf[2 * i], buf[2 * i + 1]], axis=1))

    out(wx, g_ref.at[0])
    x_written = writes.pop()

    def to_owner(m):
        return pltpu.make_async_remote_copy(src_ref=local.at[m], dst_ref=rec_a.at[block], send_sem=es.at[m], recv_sem=er.at[block],
                                            device_id=block_device(m), device_id_type=MESHID)

    def second_pair(i, w):
        both = dot(normed[...], w)
        for k in range(2):
            m = 2 * i + k
            ext = both[:, COLS * k : COLS * k + COLS]
            x_pre[m] = ext
            pre = conv_pre(ext, pk[m])
            xc = (pre * jax.nn.sigmoid(pre)).astype(BF16)
            x_conv[m] = xc
            cum, step = cols[m][:, :8], cols[m][:, 8:]
            weighted = (xc.astype(F32) * spread(step * jnp.exp(cum[ROWS - 1 : ROWS] - cum))).astype(BF16)
            local[m] = dot(weighted, bc_conv[:, :128], (0, 0)).astype(BF16)
            pl.when(m != block)(lambda m=m: to_owner(m).start())

    pairs(x_flat, 0, 4, second_pair)
    each(go, "line", 1)
    rec_a[block] = local[block]
    out(x_pre, x_pre_out)
    out(x_conv, x_conv_out)

    top, low = slice(0, HALF), slice(HALF, ROWS)

    def scan_group(m):
        xc = x_conv[m]
        cum = cols[m][:, :8]
        rows = cum_row[m]
        step_rows = step_row[m]
        parts = []
        for h in range(HEADS):
            xh = xc[:, 64 * h : 64 * h + 64]
            col, row, step = cum[:, h : h + 1], rows[h : h + 1, :], step_rows[h : h + 1, :]
            upper = (jnp.exp(jnp.minimum(col[top] - row[:, top], 0.0)) * step[:, top]).astype(BF16)
            lower = (jnp.exp(jnp.minimum(col[low] - row, 0.0)) * step).astype(BF16)
            uppers[m, h] = upper
            lowers[m, h] = lower
            parts.append(jnp.concatenate([dot((upper.astype(F32) * gram[top, top]).astype(BF16), xh[top]),
                                          dot((lower.astype(F32) * gram[low]).astype(BF16), xh)], axis=0))
        yb[m] = jnp.concatenate(parts, axis=1) + spread(pk[m, 14:15, 0:8]) * xc.astype(F32)

    pl.loop(0, 4)(scan_group)
    each(gz, "pass_on")
    each(go, "near")
    pl.loop(4, GROUPS)(scan_group)
    for c in dec_c:
        c.wait_recv()
    out(dec, dec_out)

    def exchanged(src, sends, recvs):
        for d in range(1, 8):
            other = lax.rem(block + d, 8)
            pltpu.make_async_remote_copy(src_ref=src.at[other], dst_ref=rec_a.at[other], send_sem=sends.at[other],
                                         recv_sem=recvs.at[other], device_id=block_device(other), device_id_type=MESHID).wait()

    def carry(order):
        for h in range(HEADS):
            rows = pl.ds(64 * h, 64)
            run = jnp.zeros((64, 128), F32)
            for i in order:
                out_b[i, rows] = run.astype(BF16)
                run = run * dec[i, pl.ds(h, 1)] + rec_a[i, rows].astype(F32)

    exchanged(local, es, er)
    carry(range(BLOCKS))
    f_c = to_peers(rc, lambda p: out_b.at[p], state, fs, fr, block)
    state[block] = out_b[block]

    @pl.loop(0, GROUPS)
    def _(m):
        pre = conv_pre(x_pre[m], pk[m])
        sig = jax.nn.sigmoid(pre)
        conv_slope[m] = (sig * (1.0 + pre * (1.0 - sig))).astype(BF16)

    out(conv_slope, conv_slope_out)
    each(gz, "last")
    each(gz, "complete")
    x_written.wait()
    each(gx, "drained")
    for m in range(GROUPS):
        z_copy(m).start()

    def gate_pair(i, w):
        z = dot(normed[HALO:, :], w)
        for k in range(2):
            zb[2 * i + k] = z[:, COLS * k : COLS * k + COLS]

    pairs(x_flat, 0, 4, gate_pair, z_copy)
    each(go, "pass_on")
    for c in f_c:
        c.wait_recv()
        rc.sent(c)
    out(state, state_out)
    square[...] = jnp.zeros_like(square)
    c_mat = bc_conv[:, 128:]

    @pl.loop(0, GROUPS)
    def _(m):
        carried = dot(c_mat, state[m], (1, 1))
        y = yb[m] + spread(jnp.exp(cols[m][:, :8])) * carried
        z = zb[m]
        sig = jax.nn.sigmoid(z)
        act = z * sig
        gated = y * act
        yb[m] = gated
        zb[m] = act
        d_z[m] = (y * sig * (1.0 + z * (1.0 - sig))).astype(BF16)
        sq = gated * gated
        square[...] += sq[:, :128] + sq[:, 128:256] + sq[:, 256:]

    r2 = lax.rsqrt(jnp.sum(square[...], axis=1, keepdims=True) / INNER + EPS)

    @pl.loop(0, GROUPS)
    def _(m):
        out_in[m] = (yb[m] * r2 * pk[m, 5:6]).astype(BF16)

    acc[...] = jnp.zeros_like(acc)
    d_c[...] = jnp.zeros_like(d_c)
    d_gram[...] = jnp.zeros_like(d_gram)
    each(go, "last")
    each(go, "complete")

    def result_pair(i, w):
        acc[...] += dot(jnp.concatenate([out_in[2 * i], out_in[2 * i + 1]], axis=1), w, (1, 1))

    pairs(o_flat, 0, 4, result_pair)
    total = jnp.sum(cot[...].astype(F32) * acc[...], axis=1, keepdims=True)
    scales[...] = jnp.concatenate([r2, r2 * r2 * (total / INNER), jnp.zeros((ROWS, 6), F32)], axis=1)
    result[...] = (hid[...].astype(F32) + acc[...]).astype(BF16)
    out(result, result_out)

    def to_owner_back(m):
        return pltpu.make_async_remote_copy(src_ref=local.at[m], dst_ref=rec_a.at[block], send_sem=es.at[m], recv_sem=er.at[block],
                                            device_id=block_device(m), device_id_type=MESHID)

    def gate_back(i, w):
        r2, slope = scales[:, 0:1], scales[:, 1:2]
        both = dot(cot[...], w)
        for k in range(2):
            m = 2 * i + k
            d = both[:, COLS * k : COLS * k + COLS]
            gated = yb[m]
            gain_part[m] = jnp.sum(d * (gated * r2), axis=0, keepdims=True)
            d_gated = r2 * (d * pk[m, 5:6]) - gated * slope
            dy = d_gated * zb[m]
            d_z[m] = (d_gated * d_z[m].astype(F32)).astype(BF16)
            yb[m] = dy
            skip_part[m] = jnp.sum(dy * x_conv[m].astype(F32), axis=0, keepdims=True)
            scaled = spread(jnp.exp(cols[m][:, :8])) * dy
            dye = scaled.astype(BF16)
            local[m] = dot(dye, c_mat, (0, 0)).astype(BF16)
            pl.when(m != block)(lambda m=m: to_owner_back(m).start())
            d_c[...] += dot(dye, state[m])
            d_cols[m] = jnp.concatenate([gathered_heads(scaled * dot(c_mat, state[m], (1, 1))), jnp.zeros((ROWS, 8), F32)], axis=1)

    pairs(o_flat, 0, 4, gate_back)
    rec_a[block] = local[block]
    across = [rc(src, dst, xs.at[i], xr.at[i], neighbour("core", 1)) for i, (src, dst) in enumerate((
        (cot_t.at[:, 1 - core], cot_t2_out), (out_in, out_in2_out), (normed_t.at[:, 1 - core], normed_t2_out),
        (d_z, d_z2_out)))]
    out(out_in, out_in_out)
    out(d_z, d_z_out)
    out(gain_part, gain_part_out)

    def d_x_copy(m):
        return pltpu.make_async_copy(zb.at[m], d_x_out.at[m], wsem.at[m])

    def inner_group(m):
        dy = yb[m]
        dyb = dy.astype(BF16)
        dy_t = dyb.T
        xc = x_conv[m]
        d_cum = d_cols[m][:, :8]
        lane = lax.broadcasted_iota(jnp.int32, (ROWS, 8), 1)
        parts = []
        sums = []
        for h in range(HEADS):
            xh = xc[:, 64 * h : 64 * h + 64]
            dyh = dyb[:, 64 * h : 64 * h + 64]
            upper, lower = uppers[m, h].astype(F32), lowers[m, h].astype(F32)
            tu = upper * dot(dyh[top], xh[top], (1, 1))
            tl = lower * dot(dyh[low], xh, (1, 1))
            d_gram[top, top] += tu
            d_gram[low] += tl
            qu, ql = tu * gram[top, top], tl * gram[low]
            col = jnp.sum(ql, axis=0, keepdims=True)
            sums.append(jnp.concatenate([col[:, top] + jnp.sum(qu, axis=0, keepdims=True), col[:, low]], axis=1))
            row = jnp.concatenate([jnp.sum(qu, axis=1, keepdims=True),
                                   jnp.sum(ql[:, top] + ql[:, low], axis=1, keepdims=True)], axis=0)
            d_cum = jnp.where(lane == h, d_cum + row, d_cum)
            dyt = dy_t[64 * h : 64 * h + 64]
            below = dot(dyt[:, low], (lower * gram[low]).astype(BF16))
            above = dot(dyt[:, top], (upper * gram[top, top]).astype(BF16))
            parts.append(jnp.concatenate([below[:, top] + above, below[:, low]], axis=1))
        sums = jnp.concatenate(sums + [jnp.zeros((2, ROWS), F32)], axis=0).T
        zb[m] = jnp.concatenate(parts, axis=0).T + spread(pk[m, 14:15, 0:8]) * dy
        d_x_copy(m).start()
        d_cols[m] = jnp.concatenate([d_cum - sums, sums], axis=1)

    pl.loop(0, GROUPS)(inner_group)
    out(skip_part, skip_part_out)
    out(d_cols, d_cols_out)
    dg = jnp.where(triangle(False), d_gram[...], 0.0).astype(BF16)
    d_bc[:, :128] = dot(dg, c_mat, (0, 0))
    d_bc[:, 128:] = d_c[...] + dot(dg, bc_conv[:, :128])
    out(d_bc, d_bc_out)
    exchanged(local, es, er)
    carry(range(BLOCKS - 1, -1, -1))
    out(out_b, d_state_out)
    for c in across:
        c.wait_recv()
    for c in writes:
        c.wait()
    for m in range(GROUPS):
        d_x_copy(m).wait()
    rc.all_sent()


HALF = ROWS // 2
RESULTS = (
    ("pk", (GROUPS, 16, COLS), F32), ("x_pre", (GROUPS, HALO + ROWS, COLS), F32), ("x_conv", (GROUPS, ROWS, COLS), BF16),
    ("d_x", (GROUPS, ROWS, COLS), F32), ("normed_t", (8, 2, 96, ROWS), BF16), ("cot_t", (8, 2, 96, ROWS), BF16),
    ("state", (GROUPS, COLS, 128), BF16), ("bc_pre", (HALO + ROWS, 256), F32), ("bc_conv", (ROWS, 256), BF16),
    ("steps", (ROWS, 128), F32), ("rates", (8, 128), F32), ("cols", (GROUPS, ROWS, 16), F32),
    ("cum_row", (GROUPS, 8, ROWS), F32), ("step_row", (GROUPS, 8, ROWS), F32), ("dec", (BLOCKS, 8, 128), F32),
    ("result", (ROWS, WIDTH), BF16), ("out_in", (GROUPS, ROWS, COLS), BF16), ("d_z", (GROUPS, ROWS, COLS), BF16),
    ("gain_part", (GROUPS, 1, COLS), F32), ("skip_part", (GROUPS, 1, COLS), F32), ("d_cols", (GROUPS, ROWS, 16), F32),
    ("d_bc", (ROWS, 256), F32), ("conv_slope", (GROUPS, ROWS, COLS), BF16), ("d_state", (GROUPS, COLS, 128), BF16),
)
SIBLING = (
    ("normed_t2", (8, 96, ROWS), BF16), ("cot_t2", (8, 96, ROWS), BF16), ("out_in2", (GROUPS, ROWS, COLS), BF16),
    ("d_z2", (GROUPS, ROWS, COLS), BF16),
)


def forward(zx, wo, bc, hid, cot, *params):
    hbm = pl.BlockSpec(memory_space=pl.ANY)
    vmem = pl.BlockSpec(memory_space=pltpu.VMEM)
    sem = pltpu.SemaphoreType.DMA

    def v(*shape, dtype=F32):
        return pltpu.VMEM(shape, dtype)

    def b(*shape):
        return v(*shape, dtype=BF16)

    groups = (GROUPS, ROWS, COLS)
    outs = pl.pallas_call(
        forward_kernel,
        out_shape=(sds(2, 4, 2, 2, 4, 2, 96, COLS, dtype=BF16), sds(2, 4, 2, 96, COLS, dtype=BF16),
                   *[sds(*shape, dtype=dtype) for _, shape, dtype in RESULTS + SIBLING]),
        in_specs=[vmem, hbm, vmem, vmem, hbm] + [vmem] * 8,
        out_specs=(hbm,) * (2 + len(RESULTS) + len(SIBLING)),
        scratch_shapes=[
            *[pltpu.VMEM(shape, dtype) for name, shape, dtype in RESULTS if name not in ("d_x", "d_state")],
            b(ROWS, WIDTH), b(HALO + ROWS, WIDTH), b(HALO, WIDTH), b(96, 128), b(2, 4, 2, 96, COLS),
            v(*groups), v(*groups), b(GROUPS, HEADS, HALF, HALF), b(GROUPS, HEADS, HALF, ROWS),
            b(4, 2, 2, 4, 2, 96, COLS), b(4, 2, 2, 4, 2, 96, COLS),
            v(ROWS, ROWS), v(ROWS, ROWS),
            b(GROUPS, COLS, 128), b(GROUPS, COLS, 128), b(GROUPS, COLS, 128), v(GROUPS, 8, 128),
            v(ROWS, 128), v(ROWS, 8), v(ROWS, WIDTH), v(ROWS, 128), v(16, COLS), v(1, WIDTH), b(2, 96, COLS),
            sem((27,)), sem((90,)), sem((36,)), sem((36,)), sem((18,)), sem((18,)), sem((8,)), sem((8,)), sem((8,)), sem((8,)),
            sem((8,)), sem((8,)), sem((8,)), sem((8,)), sem, sem, sem((7,)), sem((GROUPS,)), sem((len(RESULTS),)), sem((4,)),
            sem((4,)),
        ],
        compiler_params=pltpu.CompilerParams(collective_id=0, has_side_effects=True, vmem_limit_bytes=62 * 2**20),
        name="forward_between_devices",
    )(zx, wo, bc, hid, cot, *params)
    return outs[0], outs[1], dict(zip([name for name, _, _ in RESULTS + SIBLING], outs[2:]))


class Total:
    def __init__(self, rc, value, lines, axes, send, recv):
        self.rc, self.value, self.lines, self.axes, self.send, self.recv = rc, value, lines, axes, send, recv
        self.me = dict(my_place(), core=lax.axis_index("core"), ylo=lax.axis_index("ylo"))

    def step(self, j):
        if j > 0:
            for c in self.flying:
                c.wait_recv()
                self.rc.sent(c)
            l, i = self.lines, j - 1
            if self.axes[i] in ("core", "ylo"):
                self.value[...] = l[i, 0] + l[i, 1]
            else:
                self.value[...] = (l[i, 0] + l[i, 1]) + (l[i, 2] + l[i, 3])
        if j < len(self.axes):
            a = self.axes[j]
            mine = self.lines.at[j, self.me[a]]
            mine[...] = self.value[...]
            if a in ("core", "ylo"):
                devices = [{a: 1 - self.me[a]}]
            else:
                devices = [neighbour(a, d) for d in (1, 2, 3)]
            self.flying = [self.rc(mine, mine, self.send.at[d], self.recv.at[3 * j + d], device)
                           for d, device in enumerate(devices)]


class SmallSum:
    def __init__(self, rc, parts, xs, ys, zs, send, recv):
        self.rc, self.parts, self.xs, self.ys, self.zs = rc, parts, xs, ys, zs
        self.send, self.recv = send, recv
        self.me = my_place()

    def step(self, j, out=None):
        rc, me, parts, s, r = self.rc, self.me, self.parts, self.send, self.recv
        ylo = lax.rem(me["y"], 2)
        if j == 0:
            self.c = [rc(parts.at[:, lax.rem(me["x"] + d, 4)], self.xs.at[d - 1], s.at[d], r.at[d], neighbour("x", d))
                      for d in (1, 2, 3)]
            return
        for c in self.c:
            c.wait_recv()
        if j == 1:
            for yl in range(2):
                m = parts.at[yl, me["x"]]
                m[...] = (f32(m) + f32(self.xs.at[0, yl]) + f32(self.xs.at[1, yl]) + f32(self.xs.at[2, yl])).astype(BF16)
            self.ys[me["y"]] = parts[ylo, me["x"]]
            self.c = [rc(parts.at[lax.rem(me["y"] + d, 2), me["x"]], self.ys.at[me["y"]], s.at[3 + d], r.at[3 + d],
                         neighbour("y", d)) for d in (1, 2, 3)]
        elif j == 2:
            y = self.ys
            m = self.zs.at[me["z"]]
            m[...] = ((f32(y.at[0]) + f32(y.at[1])) + (f32(y.at[2]) + f32(y.at[3]))).astype(BF16)
            self.c = [rc(m, m, s.at[6 + d], r.at[6 + d], neighbour("z", d)) for d in (1, 2, 3)]
        elif j == 3:
            z = self.zs
            return (f32(z.at[0]) + f32(z.at[1])) + (f32(z.at[2]) + f32(z.at[3]))


def part_of(ref, item, pos, lo, n):
    z = slice(None) if pos["z"] is None else pos["z"]
    x = slice(None) if pos["x"] is None else pos["x"]
    if pos["y"] is None:
        yh = yl = slice(None)
    else:
        yh, yl = pos["y"] // 2, lax.rem(pos["y"], 2)
    return ref.at[item, z, yh, yl, x, pl.ds(lo, n)]


class Chunk:
    def __init__(self, rc, own, out, bufs, sems, item, slot, wide, r):
        self.rc, self.own, self.out, self.item, self.slot, self.r = rc, own, out, item, slot, r
        full, half, second, third = bufs
        self.full, self.half = full[r].at[wide], half[r].at[wide]
        self.direct = {1: second[r].at[slot], 2: third.at[slot * 3 + r]}
        self.send, self.recv = sems
        self.number = slot * 3 + r
        self.base = self.number * 10
        self.me = my_place()
        self.flying = {}

    def slab(self, st, d, lo=0, n=SUB):
        p = {a: (self.me[a] if i < st else None) for i, a in enumerate(ORDERS[self.r])}
        a = ORDERS[self.r][st]
        p[a] = lax.rem(self.me[a] + (d + 4), 4)
        return part_of(self.own, self.slot, p, self.r * SUB + lo, n)

    def loop(self, st, body):
        sizes = []
        for a, n in (("z", (4,)), ("y", (2, 2)), ("x", (4,))):
            if ORDERS[self.r].index(a) > st:
                sizes += n
        if not sizes:
            body(())
        elif len(sizes) == 1 or sizes == [2, 2]:
            for i in range(4):
                body((i,) if len(sizes) == 1 else (i // 2, i % 2))
        else:
            @pl.loop(0, 4)
            def _(i):
                for k in range(4):
                    if sizes == [4, 4]:
                        body((i, k))
                    elif sizes == [4, 2, 2]:
                        body((i, k // 2, k % 2))
                    else:
                        body((i // 2, lax.rem(i, 2), k))

    def push(self, k, src, dst, st, d):
        s = k % 2 if k < 4 else (k - 4) % 3
        if s in self.flying:
            self.rc.sent(self.flying[s])
        c = self.rc(src, dst, self.send.at[3 * self.number + s], self.recv.at[self.base + k], neighbour(ORDERS[self.r][st], d))
        self.flying[s] = c
        return c

    def far(self):
        self.far_c = [self.push(i, self.slab(0, 2, 16 * i, 16), self.half.at[i], 0, d) for i, d in enumerate((1, -1))]

    def near(self):
        self.near_c = []
        for i, d in enumerate((1, -1)):
            self.far_c[i].wait_recv()
            mine = self.slab(0, d, 16 * i, 16)

            def add(index, mine=mine, i=i):
                m = mine.at[index]
                m[...] = m[...] + self.half[(i, *index)]

            self.loop(0, add)
            self.near_c.append(self.push(2 + i, self.slab(0, d), self.full.at[i], 0, d))

    def straight(self, st):
        self.straight_c = [self.push(1 + 3 * st + d - 1, self.slab(st, d), self.direct[st].at[d - 1], st, d) for d in (1, 2, 3)]

    def step(self, j):
        if j == 0:
            self.far()
        elif j == 1:
            self.near()
        elif j == 2:
            for c in self.near_c:
                c.wait_recv()
            mine = self.slab(0, 0)

            def add(index):
                m = mine.at[index]
                m[...] = (f32(m) + f32(self.full.at[(0, *index)]) + f32(self.full.at[(1, *index)])).astype(BF16)

            self.loop(0, add)
            self.straight(1)
        else:
            for c in self.straight_c:
                c.wait_recv()
            st = j - 2
            mine = self.slab(st, 0)
            got = self.direct[st]

            def total(index):
                m = mine.at[index] if index else mine
                return (f32(m) + f32(got.at[(0, *index)])) + (f32(got.at[(1, *index)]) + f32(got.at[(2, *index)]))

            if st == 1:
                def add(index):
                    mine[index] = total(index).astype(BF16)

                self.loop(1, add)
                self.straight(2)
            else:
                self.out(pl.ds(self.r * SUB, SUB))[...] = total(())


def backward_kernel(g_ref, x_conv_ref, d_x_ref, x_pre_ref, cols_ref, d_cols_ref, slope_ref, cot_t_ref, cot_t2_ref, out_in_ref, out_in2_ref,
                    normed_t_ref, normed_t2_ref, d_z_ref, d_z2_ref, state_ref, d_state_ref, w_small_ref, hid_ref, cot_ref,
                    taps, d_bc_in, bc_pre, bc_conv, taps_bc, norm_gain, shifted, rates, gain_part, skip_part,
                    zx_out, wo_out, wbc_out, wdt_out, taps_out, taps_bc_out, log_out, shift_out, skip_out, gate_out, norm_out,
                    grad_hidden, *scr):
    (own, l_c, l_c2, l_n, l_n2, rhs_o, rhs_z, rhs_x, state, d_state, w_small, hid, cot, tails, halo_src, halo_dst, acc, wbuf,
     bxc, bdx, bxp, bcols, bdc, bslope, d_b, d_all, parts, small2, s_xs, s_ys, s_zs,
     v_all, v_in, v_sum, v_lines, n_all, n_lines, gain) = scr[:38]
    bufs = [scr[38:41], scr[41:44], scr[44:47], scr[47]]
    (t_s, t_r, e_s, e_r, x_s, x_r, h_s, h_r, m_s, m_r, ss, sr, vms, vmr, vs, vr, ns, nr, wsem, lsem, isem, freed) = scr[48:]
    rc = Sender()
    gain[0] = norm_gain[...]
    core = lax.axis_index("core")
    block = lax.axis_index("z") * 2 + lax.axis_index("yhi")
    arrived = greet()

    loads = {}

    def load_in(name, *pairs):
        loads[name] = []
        for src, dst in pairs:
            c = pltpu.make_async_copy(src, dst, isem.at[sum(len(v) for v in loads.values())])
            c.start()
            loads[name].append(c)

    def ready(name):
        for c in loads[name]:
            c.wait()

    load_in("o", (cot_t_ref.at[:, core], l_c), (cot_t2_ref, l_c2), (out_in_ref, rhs_o.at[0]), (out_in2_ref, rhs_o.at[1]))
    load_in("z", (normed_t_ref.at[:, core], l_n), (normed_t2_ref, l_n2), (d_z_ref, rhs_z.at[0]), (d_z2_ref, rhs_z.at[1]))
    load_in("s", (state_ref, state), (d_state_ref.at[block], d_state.at[block]))

    outs = (lambda at: zx_out.at[at, 1], lambda at: zx_out.at[at, 0], lambda at: wo_out.at[at])

    def chunks(item, slot, wide):
        return [Chunk(rc, own, outs[item], bufs, (t_s, t_r), item, slot, wide, r) for r in range(3)]

    def steps(cs, j):
        for c in cs:
            c.step(j)

    def both_tokens(own_t, other_t):
        return jnp.concatenate([own_t[...].reshape(768, ROWS), other_t[...].reshape(768, ROWS)], axis=1)

    def gradient(left, left2, rhs, slot, ready=None):
        def one(i):
            if ready is not None:
                ready(2 * i)
                ready(2 * i + 1)
            right = jnp.concatenate([jnp.concatenate([rhs[0, 2 * i + k], rhs[1, 2 * i + k]], axis=0) for k in range(2)], axis=1)
            v = dot(both_tokens(left, left2), right).astype(BF16)
            for k in range(2):
                own[slot, i, k] = v[:, COLS * k : COLS * k + COLS].reshape(2, 4, 96, COLS)

        pl.loop(0, GROUPS // 2)(one)

    oc, zc, xc_ = chunks(2, 0, 0), chunks(1, 1, 1), chunks(0, 2, 0)
    arrived()
    back = to_peers(rc, lambda p: d_state_ref.at[p], d_state, e_s, e_r, block)
    ready("o")
    gradient(l_c, l_c2, rhs_o, 0)
    steps(oc, 0)
    ready("z")

    streams = ((x_conv_ref, bxc), (d_x_ref, bdx), (x_pre_ref, bxp), (cols_ref, bcols), (d_cols_ref, bdc), (slope_ref, bslope))

    def load(m):
        k = lax.rem(m, 2)
        return [pltpu.make_async_copy(src.at[m], dst.at[k], lsem.at[k, i]) for i, (src, dst) in enumerate(streams)]

    for c in load(0):
        c.start()
    gradient(l_n, l_n2, rhs_z, 1)
    steps(zc, 0)
    ready("s")
    for c in back:
        c.wait_recv()
    load_in("end", (w_small_ref, w_small), (hid_ref, hid), (cot_ref, cot))

    def fifth_group(m):
        k = lax.rem(m, 2)

        @pl.when(m < GROUPS - 1)
        def _():
            for c in load(m + 1):
                c.start()

        for c in load(m):
            c.wait()
        ds = d_state[m]
        xf = bxc[k].astype(F32)
        cum, step = bcols[k][:, :8], bcols[k][:, 8:]
        last = cum[ROWS - 1 : ROWS]
        tail = jnp.exp(last - cum)
        weights = step * tail
        wide = spread(weights)
        d_weighted = dot(bc_conv[:, :128], ds, (1, 1))
        d_b[...] += dot((xf * wide).astype(BF16), ds)
        dx = bdx[k] + wide * d_weighted
        d_weights = gathered_heads(d_weighted * xf)
        both = weights * d_weights
        lane = lax.broadcasted_iota(jnp.int32, (1, 8), 1)
        product = jnp.sum(state[m].astype(F32) * ds.astype(F32), axis=1, keepdims=True)
        d_last = jnp.sum(both, axis=0, keepdims=True)
        for h in range(HEADS):
            dots = jnp.sum(product[64 * h : 64 * h + 64], axis=0, keepdims=True)
            d_last = jnp.where(lane == h, d_last + jnp.exp(last) * dots, d_last)
        row = lax.broadcasted_iota(jnp.int32, (ROWS, 8), 0)
        d_cum = bdc[k][:, :8] - both
        d_cum = jnp.where(row == ROWS - 1, d_cum + d_last, d_cum)
        d_all[m] = jnp.concatenate([d_cum, bdc[k][:, 8:] + both], axis=1)
        ext = bxp[k]
        tap = taps[m]
        dp = dx * bslope[k].astype(F32)
        v_all[m, 0:8] = conv_grads(dp, ext, gain_part[m], skip_part[m])
        whole_dx = conv_transposed(jnp.concatenate([dp, jnp.zeros((8, COLS), F32)], axis=0), tap)
        rhs_x[0, m] = whole_dx.astype(BF16)
        tails[m] = whole_dx[ROWS - 16 :]
        halo_src[m] = dp[:8]

    d_b[...] = jnp.zeros_like(d_b)
    pl.loop(0, 3)(fifth_group)
    steps(oc, 1)
    pl.loop(3, GROUPS)(fifth_group)

    d_bc = jnp.concatenate([d_bc_in[:, :128] + d_b[...], d_bc_in[:, 128:]], axis=1)
    ext = bc_pre[...]
    pre = conv_pre(ext, taps_bc[...])
    sig = jax.nn.sigmoid(pre)
    dp_bc = d_bc * (sig * (1.0 + pre * (1.0 - sig)))
    halo_src[GROUPS] = jnp.concatenate([dp_bc[:8], jnp.zeros((8, 128), F32)], axis=1)
    halo = rc(halo_src, halo_dst, h_s, h_r, block_device(lax.rem(block + 7, 8)))
    steps(zc, 1)
    zero8 = jnp.zeros((1, 256), F32)
    d_cum = jnp.concatenate([d_all[m][:, :HEADS] for m in range(GROUPS)] + [jnp.zeros((ROWS, 80), F32)], axis=1)
    d_step = jnp.concatenate([d_all[m][:, 8 : 8 + HEADS] for m in range(GROUPS)] + [jnp.zeros((ROWS, 80), F32)], axis=1)
    d_decay = dot(triangle(True).astype(F32), d_cum, precision=lax.Precision.HIGHEST)
    rate = -jnp.exp(rates[0:1])
    v = shifted[...]
    sig = jax.nn.sigmoid(v)
    far = v < -16.0
    ratio = jnp.where(far, 1.0, sig / jnp.where(far, 1.0, softplus(v)))
    d_dt = d_step * ratio + rate * d_decay * sig
    log_grad = jnp.sum(d_decay * (softplus(v) * rate), axis=0, keepdims=True)
    shift_grad = jnp.sum(d_dt, axis=0, keepdims=True)
    bc_rows = conv_grads(dp_bc, ext, jnp.concatenate([log_grad, shift_grad], axis=1), zero8)
    bc_rows = jnp.concatenate([bc_rows, jnp.zeros((8, 128), F32)], axis=1)
    for m in range(GROUPS):
        v_all[m, 8:16] = bc_rows
    vec_c = to_peers(rc, lambda p: v_all.at[p], v_in, vms, vmr, block)
    v_in[block] = v_all[block]

    halo.wait_recv()
    inside = block < 7

    def below(k):
        return jnp.where(inside, halo_dst[k], 0.0)

    def across(m):
        return pltpu.make_async_remote_copy(src_ref=rhs_x.at[0, m], dst_ref=rhs_x.at[1, m], send_sem=x_s.at[m],
                                            recv_sem=x_r.at[m], device_id=neighbour("core", 1), device_id_type=MESHID)

    def fix(m):
        ext = jnp.concatenate([jnp.zeros((16, COLS), F32), below(m)], axis=0)
        rhs_x[0, m, pl.ds(ROWS - 16, 16)] = (tails[m] + conv_transposed(ext, taps[m], 16)).astype(BF16)
        across(m).start()

    d_bc = conv_transposed(jnp.concatenate([dp_bc, below(GROUPS)[:, :256]], axis=0), taps_bc[...])
    small2[0] = jnp.concatenate([d_bc, d_dt], axis=1).astype(BF16)
    small_c = rc(small2.at[0], small2.at[1], m_s, m_r, neighbour("core", 1))
    pl.loop(0, GROUPS)(fix)

    def weights(m):
        k = lax.rem(m, 2)
        return [pltpu.make_async_copy(g_ref.at[i, m], wbuf.at[k, i], wsem.at[k, i]) for i in range(2)]

    for c in weights(0):
        c.start()
    steps(oc, 2)
    for a in "xyz":
        for s in (1, -1):
            pl.semaphore_signal(freed, inc=1, device_id=neighbour(a, s), device_id_type=MESHID)
    gradient(l_n, l_n2, rhs_x, 2, lambda m: across(m).wait())
    pl.semaphore_wait(freed, 6)
    steps(xc_, 0)
    small_c.wait_recv()
    parts[...] = dot(both_tokens(l_n, l_n2), small2[...].reshape(2 * ROWS, COLS)).astype(BF16).reshape(2, 4, 96, COLS)
    sums = SmallSum(rc, parts, s_xs, s_ys, s_zs, ss, sr)
    ready("end")
    acc[...] = dot(small2[0], w_small[...], (1, 1))
    def input_group(m):
        k = lax.rem(m, 2)

        @pl.when(m < GROUPS - 1)
        def _():
            for c in weights(m + 1):
                c.start()

        for c in weights(m):
            c.wait()
        lhs = jnp.concatenate([rhs_x[0, m], rhs_z[0, m]], axis=1)
        rhs = jnp.concatenate([wbuf[k, 0], wbuf[k, 1]], axis=1)
        acc[...] += dot(lhs, rhs, (1, 1))

    pl.loop(0, 2)(input_group)
    sums.step(0)
    pl.loop(2, 4)(input_group)
    steps(zc, 2)
    for c in vec_c:
        c.wait_recv()
    t = v_in[0]
    for i in range(1, BLOCKS):
        t = t + v_in[i]
    v_sum[...] = t
    vec = Total(rc, v_sum, v_lines, ("core", "x", "ylo"), vs, vr)
    vec.step(0)
    steps(xc_, 1)
    pl.loop(4, GROUPS)(input_group)
    steps(oc, 3)
    v = hid[...].astype(F32)
    r = lax.rsqrt(jnp.mean(v * v, axis=1, keepdims=True) + EPS)
    unit = v * r
    dn = acc[...]
    gain_grad = jnp.sum(dn * unit, axis=0, keepdims=True)
    for i in range(4):
        n_all[pl.ds(i, 1)] = gain_grad[:, COLS * i : COLS * i + COLS]
    n_all[pl.ds(4, 4)] = jnp.zeros((4, COLS), F32)
    nvec = Total(rc, n_all, n_lines, ("core", "x", "y", "z"), ns, nr)
    nvec.step(0)
    sums.step(1)
    vec.step(1)
    steps(zc, 3)
    d_in = dn * gain[...]
    grad_hidden[...] = r * (d_in - unit * jnp.mean(d_in * unit, axis=1, keepdims=True)) + cot[...].astype(F32)
    nvec.step(1)
    steps(xc_, 2)
    sums.step(2)
    vec.step(2)
    nvec.step(2)
    steps(oc, 4)
    steps(zc, 4)
    steps(xc_, 3)
    vec.step(3)
    nvec.step(3)

    pick = lax.broadcasted_iota(jnp.int32, (8, 128), 0) + block * HEADS
    pick = (pick == lax.broadcasted_iota(jnp.int32, (8, 128), 1)).astype(F32)

    def own_heads(row):
        return dot(row, pick, (1, 1), precision=lax.Precision.HIGHEST)

    mine = v_sum[...]
    taps_out[...] = mine[:5]
    gate_out[...] = mine[5]
    skip_out[...] = gathered_heads(mine[6:7])[0, :HEADS]
    taps_bc_out[...] = mine[8:13, :256]
    log_out[...] = own_heads(mine[13:14, :128])[0, :HEADS]
    shift_out[...] = own_heads(mine[13:14, 128:256])[0, :HEADS]
    steps(xc_, 4)
    little = sums.step(3)
    wbc_out[...] = little[:, :256]
    wdt_out[...] = dot(pick, little[:, 256:], (1, 1), precision=lax.Precision.HIGHEST)[:HEADS]
    nvec.step(4)
    for i in range(4):
        norm_out[pl.ds(COLS * i, COLS)] = n_all[i]
    rc.all_sent()


def backward(w_all, r, w_small, hid, cot, norm_gain, conv_bc):
    hbm = pl.BlockSpec(memory_space=pl.ANY)
    vmem = pl.BlockSpec(memory_space=pltpu.VMEM)
    sem = pltpu.SemaphoreType.DMA

    def buf(*shape, dtype=BF16):
        return pltpu.VMEM((*shape, COLS), dtype)

    def v(*shape, dtype=F32):
        return pltpu.VMEM(shape, dtype)

    def b(*shape):
        return v(*shape, dtype=BF16)

    scratch = [
        buf(3, 4, 2, 2, 4, 96), b(8, 96, ROWS), b(8, 96, ROWS), b(8, 96, ROWS), b(8, 96, ROWS),
        buf(2, GROUPS, ROWS), buf(2, GROUPS, ROWS), buf(2, GROUPS, ROWS), b(GROUPS, COLS, 128), b(GROUPS, COLS, 128),
        buf(WIDTH), b(ROWS, WIDTH), b(ROWS, WIDTH),
        buf(GROUPS, 16, dtype=F32), buf(GROUPS + 1, 8, dtype=F32), buf(GROUPS + 1, 8, dtype=F32),
        v(ROWS, WIDTH), buf(2, 2, WIDTH),
        buf(2, ROWS), buf(2, ROWS, dtype=F32), buf(2, HALO + ROWS, dtype=F32), v(2, ROWS, 16), v(2, ROWS, 16),
        buf(2, ROWS),
        v(ROWS, 128), v(GROUPS, ROWS, 16), buf(2, 4, 96), buf(2, ROWS), buf(3, 2, 96), buf(4, 96), buf(4, 96),
    ]
    scratch += [buf(GROUPS, 16, dtype=F32), buf(GROUPS, 16, dtype=F32), buf(16, dtype=F32), buf(3, 4, 16, dtype=F32)]
    scratch += [buf(8, dtype=F32), buf(4, 4, 8, dtype=F32), v(1, WIDTH)]
    scratch += [buf(2, 2, 4, 2, 2, SUB), buf(2, 2, 4, 4, SUB), buf(2, 2, 2, 2, 4, SUB)]
    scratch += [buf(2, 2, 4, 2, 2, 16), buf(2, 2, 4, 4, 16), buf(2, 2, 2, 2, 4, 16)]
    scratch += [buf(3, 3, 4, SUB), buf(3, 3, 4, SUB), buf(3, 3, 2, 2, SUB), buf(9, 3, SUB)]
    scratch += [sem((27,)), sem((90,)), sem((8,)), sem((8,)), sem((8,)), sem((8,)), sem, sem, sem, sem, sem((10,)), sem((10,)), sem((8,)), sem((8,)),
                sem((3,)), sem((9,)), sem((3,)), sem((12,)), sem((2, 2)), sem((2, 6)), sem((13,)), pltpu.SemaphoreType.REGULAR]
    names = ("x_conv", "d_x", "x_pre", "cols", "d_cols", "conv_slope", "cot_t", "cot_t2", "out_in", "out_in2", "normed_t", "normed_t2", "d_z",
             "d_z2", "state", "d_state")
    return pl.pallas_call(
        backward_kernel,
        out_shape=(sds(96, 2, COLS), sds(96, COLS), sds(96, 256), sds(HEADS, 96), sds(5, COLS), sds(5, 256), sds(HEADS), sds(HEADS),
                   sds(HEADS), sds(COLS), sds(WIDTH), sds(ROWS, WIDTH)),
        in_specs=[hbm] * 20 + [vmem] * 10,
        out_specs=(vmem,) * 12,
        scratch_shapes=scratch,
        compiler_params=pltpu.CompilerParams(collective_id=1, has_side_effects=True, vmem_limit_bytes=63 * 2**20),
        name="backward_between_devices",
    )(w_all, *[r[name] for name in names], w_small, hid, cot, r["pk"], r["d_bc"], r["bc_pre"], r["bc_conv"], conv_bc, norm_gain,
      r["steps"], r["rates"], r["gain_part"], r["skip_part"])
def results_kernel(*refs):
    n = (len(refs) - 2) // 3
    sems = refs[-2:]
    into = [pltpu.make_async_copy(refs[i], refs[2 * n + i], sems[0].at[i]) for i in range(n)]
    back = [pltpu.make_async_copy(refs[2 * n + i], refs[n + i], sems[1].at[i]) for i in range(n)]
    for c in into:
        c.start()
    for c, d in zip(into, back):
        c.wait()
        d.start()
    for d in back:
        d.wait()


def as_results(*arrays):
    hbm = pl.BlockSpec(memory_space=pl.ANY)
    return pl.pallas_call(
        results_kernel,
        out_shape=tuple(jax.ShapeDtypeStruct(a.shape, a.dtype) for a in arrays),
        in_specs=[hbm] * len(arrays),
        out_specs=(hbm,) * len(arrays),
        scratch_shapes=[*[pltpu.VMEM(a.shape, a.dtype) for a in arrays], *[pltpu.SemaphoreType.DMA((len(arrays),))] * 2],
        name="results",
    )(*arrays)


def shards(hidden, grad_out, norm_gain, w_zx, w_bc, w_dt, conv_x, conv_bc, a_log, dt_bias, d_skip, gate_gain, w_out):
    w_all, w_small, r = forward(w_zx, w_out.T, w_bc, hidden, grad_out, norm_gain, w_dt.T, conv_x, conv_bc,
                                a_log, dt_bias, d_skip, gate_gain)
    w_all = w_all.reshape(2, GROUPS, WIDTH, COLS)
    w_small = w_small.reshape(WIDTH, COLS)
    zx, wo, wbc, wdt, grad_taps, grad_taps_bc, log_rate, shift, skip, gate, norm, grad_hidden = backward(
        w_all, r, w_small, hidden, grad_out, norm_gain, conv_bc)
    result, grad_hidden, norm, zx, wbc, wdt, grad_taps, grad_taps_bc, log_rate, shift, skip, gate, wo = as_results(
        r["result"], grad_hidden, norm, zx, wbc, wdt, grad_taps, grad_taps_bc, log_rate, shift, skip, gate, wo)
    return (result, grad_hidden, norm, zx, wbc, wdt.T, grad_taps, grad_taps_bc, log_rate, shift, skip, gate, wo.T)


def solution(mesh):
    finer = Mesh(mesh.devices.reshape(2, 4, 2, 4, 2), DP_MP)
    rows = P(DP_MP, None)
    placed = (rows, rows, P(), P(DP, None, MP), P(DP, None), P(DP, MP), P(None, MP), P(), P(MP), P(MP), P(MP), P(MP),
              P(MP, DP))
    return jax.shard_map(
        shards,
        mesh=finer,
        in_specs=placed,
        out_specs=(rows, rows, P(), P(DP, None, MP), P(DP, None), P(DP, MP), P(None, MP), P(), P(MP), P(MP), P(MP), P(MP),
                   P(MP, DP)),
        check_vma=False,
    )
```

```python
import jax
import jax.numpy as jnp
from jax import lax
from jax.experimental import pallas as pl
from jax.experimental.pallas import tpu as pltpu
from jax.sharding import Mesh
from jax.sharding import PartitionSpec as P

MP = ("z", "yhi")
DP = ("ylo", "x", "core")
DP_MP = DP + MP
BLOCKS = 8
F32 = jnp.float32
BF16 = jnp.bfloat16
ROWS = 256
WIDTH = 1536
GROUPS = 8
COLS = 384
HEADS = 6
HALO = 16
EPS = 1e-05
INNER = GROUPS * COLS
VMEM_LIMIT = 56 * 2**20


def dot(a, b, contract=(1, 0), precision=None):
    return lax.dot_general(
        a, b, (((contract[0],), (contract[1],)), ((), ())),
        preferred_element_type=F32, precision=precision,
    )


def spread(per_head):
    rows = per_head.shape[0]
    low = lax.broadcasted_iota(jnp.int32, (rows, 128), 1) < 64
    tiles = [
        jnp.where(low, per_head[:, 2 * i : 2 * i + 1], per_head[:, 2 * i + 1 : 2 * i + 2])
        for i in range(COLS // 128)
    ]
    return jnp.concatenate(tiles, axis=1)


def gathered_heads(values):
    rows = values.shape[0]
    low = lax.broadcasted_iota(jnp.int32, (rows, 128), 1) < 64
    lane = lax.broadcasted_iota(jnp.int32, (rows, 8), 1)
    out = jnp.zeros((rows, 8), F32)
    for i in range(COLS // 128):
        tile = values[:, 128 * i : 128 * i + 128]
        first = jnp.sum(jnp.where(low, tile, 0.0), axis=1, keepdims=True)
        both = jnp.sum(tile, axis=1, keepdims=True)
        out = jnp.where(lane == 2 * i, first, out)
        out = jnp.where(lane == 2 * i + 1, both - first, out)
    return out


def softplus(v):
    return jnp.maximum(v, 0.0) + jnp.log1p(jnp.exp(-jnp.abs(v)))


def conv_pre(ext, taps):
    total = taps[4:5]
    for j in range(4):
        total = total + ext[HALO - 3 + j : HALO - 3 + j + ROWS] * taps[j : j + 1]
    return total


def conv_transposed(ext, taps, rows=ROWS):
    total = ext[3 : 3 + rows] * taps[0:1]
    for j in range(1, 4):
        total = total + ext[3 - j : 3 - j + rows] * taps[j : j + 1]
    return total


def conv_grads(dpre, ext, sixth, seventh):
    rows = [
        jnp.sum(dpre * ext[HALO - 3 + j : HALO - 3 + j + ROWS], axis=0, keepdims=True)
        for j in range(4)
    ]
    rows.append(jnp.sum(dpre, axis=0, keepdims=True))
    rows += [sixth, seventh, jnp.zeros((1, dpre.shape[1]), F32)]
    return jnp.concatenate(rows, axis=0)


def triangle(upper):
    row = lax.broadcasted_iota(jnp.int32, (ROWS, ROWS), 0)
    col = lax.broadcasted_iota(jnp.int32, (ROWS, ROWS), 1)
    return row <= col if upper else row >= col


def sds(*shape, dtype=F32):
    return jax.ShapeDtypeStruct(shape, dtype)


def params():
    return pltpu.CompilerParams(vmem_limit_bytes=VMEM_LIMIT)


MESHID = pl.DeviceIdType.MESH
ORDERS = (("x", "y", "z"), ("y", "z", "x"), ("z", "x", "y"))
SUB = 32


def neighbour(axis, s):
    if axis == "core":
        return {"core": 1 - lax.axis_index("core")}
    if axis == "y":
        y = lax.rem(lax.axis_index("yhi") * 2 + lax.axis_index("ylo") + (s + 4), 4)
        return {"ylo": lax.rem(y, 2), "yhi": y // 2}
    return {axis: lax.rem(lax.axis_index(axis) + (s + 4), 4)}


def my_place():
    return {"x": lax.axis_index("x"), "z": lax.axis_index("z"), "y": lax.axis_index("yhi") * 2 + lax.axis_index("ylo")}


def block_device(p):
    return {"z": p // 2, "yhi": lax.rem(p, 2)}


def f32(ref):
    return ref[...].astype(F32)


class Sender:
    def __init__(self):
        self.pending = {}

    def __call__(self, src, dst, send, recv, device):
        c = pltpu.make_async_remote_copy(src_ref=src, dst_ref=dst, send_sem=send, recv_sem=recv, device_id=device,
                                         device_id_type=MESHID)
        c.start()
        self.pending[id(c)] = c
        return c

    def sent(self, c):
        c.wait_send()
        del self.pending[id(c)]

    def all_sent(self):
        for c in self.pending.values():
            c.wait_send()


def greet():
    bar = pltpu.get_barrier_semaphore()
    for a in "xyz":
        for s in (1, 2, 3):
            pl.semaphore_signal(bar, inc=1, device_id=neighbour(a, s), device_id_type=MESHID)
    for d in (1, 2, 3):
        diagonal = {"z": lax.rem(lax.axis_index("z") + d, 4), "yhi": 1 - lax.axis_index("yhi")}
        pl.semaphore_signal(bar, inc=1, device_id=diagonal, device_id_type=MESHID)
    pl.semaphore_signal(bar, inc=1, device_id=neighbour("core", 1), device_id_type=MESHID)
    return lambda: pl.semaphore_wait(bar, 13)


def to_peers(rc, src_of, dst, send, recv, block):
    out = []
    for d in range(1, 8):
        p = lax.rem(block + d, 8)
        out.append(rc(src_of(p), dst.at[block], send.at[d], recv.at[d], block_device(p)))
    return out


PIECES = (((0, 32), (32, 32), (64, 32)), ((0, 16), (16, 48), (64, 32)), ((0, 32), (32, 32), (64, 32)))


class Gather:
    def __init__(self, rc, g, w, sems, item, r):
        self.rc, self.g, self.w, self.item, self.r = rc, g, w, item, r
        self.flying = {}
        self.ts, self.tr, self.cs, self.cr = sems
        self.k = item * 3 + r
        self.lo, self.n = PIECES[item][r]
        self.me = my_place()
        self.core = lax.axis_index("core")
        self.forwarded = []

    def at(self, pos, lo=0, n=None):
        z = slice(None) if pos["z"] is None else pos["z"]
        x = slice(None) if pos["x"] is None else pos["x"]
        if pos["y"] is None:
            yh = yl = slice(None)
        else:
            yh, yl = pos["y"] // 2, lax.rem(pos["y"], 2)
        return self.g.at[z, yh, yl, x, self.core, pl.ds(self.lo + lo, self.n if n is None else n)]

    def pos(self, st, d=0):
        p = {a: (None if i < st else self.me[a]) for i, a in enumerate(ORDERS[self.r])}
        a = ORDERS[self.r][st]
        p[a] = lax.rem(self.me[a] + (d + 4), 4)
        return p

    def to_sibling(self, ref):
        k = self.k * 4 + len(self.forwarded)
        self.forwarded.append(self.rc(ref, ref, self.cs.at[k], self.cr.at[k], neighbour("core", 1)))

    def push(self, k, src, dst, a, d):
        s = k % 3 if k < 6 else k % 2
        if s in self.flying:
            self.rc.sent(self.flying[s])
        c = self.rc(src, dst, self.ts.at[3 * self.k + s], self.tr.at[10 * self.k + k], neighbour(a, d))
        self.flying[s] = c
        return c

    def straight(self, st):
        ref = self.at(self.pos(st))
        src = ref if st else self.w.at[pl.ds(self.lo, self.n)]
        self.c = [self.push(3 * st + d - 1, src, ref, ORDERS[self.r][st], d) for d in (1, 2, 3)]

    def line(self, st):
        for c in self.c:
            c.wait_recv()
        if st == 1:
            self.to_sibling(self.at(self.pos(2)))

    def near(self):
        ref = self.at(self.pos(2))
        self.c = [self.push(6 + i, ref, ref, ORDERS[self.r][2], d) for i, d in enumerate((1, -1))]

    def pass_on(self):
        self.f = []
        for i, d in enumerate((1, -1)):
            self.c[i].wait_recv()
            p = self.pos(2, -d)
            first = 16 * ((self.n + 16) // 32)
            lo, n = ((0, first), (first, self.n - first))[i]
            if n:
                half = self.at(p, lo, n)
                self.f.append(self.push(8 + i, half, half, ORDERS[self.r][2], d))
            self.to_sibling(self.at(p))

    def last(self):
        for f in self.f:
            f.wait_recv()
        self.to_sibling(self.at(self.pos(2, 2)))

    def complete(self):
        for c in self.forwarded:
            c.wait_recv()

    def drained(self):
        for c in [*self.flying.values(), *self.forwarded]:
            self.rc.sent(c)


def forward_kernel(zx_ref, wo_ref, bc_ref, hid, cot_ref, norm_gain, dt_ref, conv_x, taps_bc, log_ref, shift_ref, skip_ref,
                   gate_ref, g_ref, gb_ref,
                   pk_out, x_pre_out, x_conv_out, d_x_out, normed_t_out, cot_t_out, state_out, bc_pre_out, bc_conv_out,
                   steps_out, rates_out, cols_out, cum_row_out, step_row_out, dec_out, result_out,
                   out_in_out, d_z_out, gain_part_out, skip_part_out, d_cols_out, d_bc_out, conv_slope_out, leaving_out, d_state_out,
                   normed_t2_out, cot_t2_out, out_in2_out, d_z2_out, *scr):
    (pk, x_pre, x_conv, normed_t, cot_t, state, bc_pre, bc_conv, steps, rates, cols, cum_row, step_row, dec,
     result, out_in, d_z, gain_part, skip_part, d_cols, d_bc, conv_slope, leaving,
     cot, normed, halo, dt_own, small_all, zb, yb, uppers, lowers, wx, wo, gram, d_gram, local, rec_a, out_b, dec_own, square,
     scales, acc, d_c, pk_ref, gain, zx, grown, entered,
     ts, tr, cs, cr, bs, br, qs, qr, es, er, fs, fr, ds, dr, hs, hr, lsem, wsem, osem, xs, xr) = scr
    rc = Sender()
    me = my_place()
    core = lax.axis_index("core")
    x, ylo = me["x"], lax.axis_index("ylo")
    block = lax.axis_index("z") * 2 + lax.axis_index("yhi")
    arrived = greet()
    writes, count = [], [0]

    def out(src, dst):
        c = pltpu.make_async_copy(src, dst, osem.at[count[0]])
        c.start()
        count[0] += 1
        writes.append(c)

    cot_c = pltpu.make_async_copy(cot_ref, cot, lsem.at[3])
    cot_c.start()
    def spot(ref):
        return ref.at[me["z"], me["y"] // 2, ylo, x, core]

    split = zx_ref[...].astype(F32)
    for i in range(2):
        zx[i] = split[:, i, :].astype(BF16)
    own_w = [pltpu.make_async_copy(src, spot(dst), lsem.at[4 + i])
             for i, (src, dst) in enumerate(((zx.at[1], wx), (zx.at[0], g_ref.at[1]), (wo_ref, wo)))]
    for c in own_w:
        c.start()
    pk_ref[...] = jnp.zeros_like(pk_ref)
    pk_ref[0:5] = conv_x[...]
    pk_ref[5] = gate_ref[...]
    for at, ref in ((6, log_ref), (7, shift_ref), (14, skip_ref)):
        pk_ref[at, 0:HEADS] = ref[...]
    pk_ref[8 : 8 + HEADS, 0:96] = dt_ref[...].astype(F32)
    gain[0] = norm_gain[...]
    arrived()

    gx, gz, go = [[Gather(rc, g, w, (ts, tr, cs, cr), i, r) for r in range(3)]
                  for i, (g, w) in enumerate(((wx, zx.at[1]), (g_ref.at[1], zx.at[0]), (wo, wo_ref)))]

    def each(group, name, *args):
        for c in group:
            getattr(c, name)(*args)

    each(gx, "straight", 0)
    pk_c = to_peers(rc, lambda p: pk_ref, pk, qs, qr, block)

    def small(lo, n):
        cols = pl.ds(lo, n)
        sems = iter(range(9 * (lo // 256), 9 * (lo // 256) + 9))

        def push(src, dst, device):
            k = next(sems)
            return rc(src, dst, bs.at[k], br.at[k], device)

        def at(yl, x_at):
            return gb_ref.at[yl, x_at, core, :, cols]

        def over_y(src):
            own = pltpu.make_async_copy(src, at(ylo, x), lsem.at[1 + lo // 256])
            own.start()
            return [push(src, at(ylo, x), {"ylo": 1 - ylo}), push(src, at(ylo, x), neighbour("core", 1))], own

        def over_x(first, own):
            first[0].wait_recv()
            own.wait()
            line = gb_ref.at[:, x, core, :, cols]
            other = at(1 - ylo, x)
            rest = [push(line, line, neighbour("x", d)) for d in (1, 2, 3)]
            return rest, [first[1], push(other, other, neighbour("core", 1))]

        def to_sibling(rest, cores):
            for d in (1, 2, 3):
                rest[d - 1].wait_recv()
                line = gb_ref.at[:, lax.rem(x + 4 - d, 4), core, :, cols]
                cores.append(push(line, line, neighbour("core", 1)))
            return cores

        return over_y, over_x, to_sibling

    bc_y, bc_x, bc_end = small(0, 256)
    dt_y, dt_x, dt_end = small(256, 128)
    bc_s = bc_y(bc_ref)
    pk[block] = pk_ref[...]

    def normalize(part, at):
        v = part[...].astype(F32)
        r = lax.rsqrt(jnp.mean(v * v, axis=1, keepdims=True) + EPS)
        normed[pl.ds(at, part.shape[0])] = (v * r * gain[...]).astype(BF16)

    normalize(hid, HALO)
    each(gx, "line", 0)
    for c in own_w:
        c.wait()
    each(gx, "straight", 1)
    each(gz, "straight", 0)
    halo_c = rc(hid.at[pl.ds(ROWS - HALO, HALO)], halo, hs, hr, block_device(lax.rem(block + 1, 8)))
    each(go, "straight", 0)

    for c in pk_c:
        c.wait_recv()
    out(pk, pk_out)
    columns = jnp.concatenate([pk[m, 8 : 8 + HEADS, 0:128] for m in range(GROUPS)] + [jnp.zeros((80, 128), F32)], axis=0)
    dt_own[...] = columns.T[:96].astype(BF16)
    dt_s = dt_y(dt_own)
    normed_t[...] = normed[HALO:, :].T.reshape(8, 2, 96, ROWS)
    out(normed_t, normed_t_out)
    each(gx, "line", 1)
    each(gx, "near")
    bc_s = bc_x(*bc_s)
    dt_s = dt_x(*dt_s)
    cot_c.wait()
    cot_t[...] = cot[...].T.reshape(8, 2, 96, ROWS)
    out(cot_t, cot_t_out)
    halo_c.wait_recv()
    normalize(halo, 0)

    @pl.when(block == 0)
    def _():
        normed[pl.ds(0, HALO)] = jnp.zeros((HALO, WIDTH), BF16)

    each(gx, "pass_on")
    each(gz, "line", 0)
    each(gz, "straight", 1)
    b_core = bc_end(*bc_s) + dt_end(*dt_s)
    for c in b_core:
        c.wait_recv()
    small_in = pltpu.make_async_copy(gb_ref, small_all, lsem.at[1])
    small_in.start()
    each(go, "line", 0)
    each(go, "straight", 1)
    small_in.wait()

    def row(at):
        pieces = [pk[m, at : at + 1, 0:HEADS] for m in range(GROUPS)]
        return jnp.concatenate(pieces + [jnp.zeros((1, 80), F32)], axis=1)

    rates[0:1] = row(6)
    rates[1:2] = row(7)
    rates[2:8] = jnp.zeros((6, 128), F32)
    little = dot(normed[...], small_all[...].reshape(WIDTH, COLS))
    bc_pre[...] = little[:, :256]
    pre = conv_pre(little[:, :256], taps_bc[...])
    bc_conv[...] = (pre * jax.nn.sigmoid(pre)).astype(BF16)
    shifted = little[HALO:, 256:384] + rates[1:2]
    steps[...] = shifted
    step = softplus(shifted)
    decay = -step * jnp.exp(rates[0:1])
    cum = dot(triangle(False).astype(F32), decay, precision=lax.Precision.HIGHEST)
    cum_t = cum.T
    step_t = step.T
    each(gx, "last")
    each(gz, "line", 1)
    each(gz, "near")
    lasts = jnp.broadcast_to(jnp.exp(cum_t[:, ROWS - 1 : ROWS]), (128, 128))
    for m in range(GROUPS):
        at = slice(HEADS * m, HEADS * m + 8)
        cols[m] = jnp.concatenate([cum[:, at], step[:, at]], axis=1)
        cum_row[m] = cum_t[HEADS * m : HEADS * m + 8]
        step_row[m] = step_t[HEADS * m : HEADS * m + 8]
        dec_own[m] = lasts[HEADS * m : HEADS * m + 8]
    dec_c = to_peers(rc, lambda p: dec_own.at[p], dec, ds, dr, block)
    dec[block] = dec_own[block]
    gram[...] = jnp.where(triangle(False), dot(bc_conv[:, 128:], bc_conv[:, :128], (1, 1)), 0.0)
    out(bc_pre, bc_pre_out)
    out(bc_conv, bc_conv_out)
    out(steps, steps_out)
    out(rates, rates_out)
    out(cols, cols_out)
    out(cum_row, cum_row_out)
    out(step_row, step_row_out)
    each(gx, "complete")

    x_flat, o_flat = wx.reshape(GROUPS, WIDTH, COLS), wo.reshape(GROUPS, WIDTH, COLS)
    g_flat = g_ref.reshape(2, GROUPS, WIDTH, COLS)

    def z_copy(m):
        return pltpu.make_async_copy(g_flat.at[1, m], x_flat.at[m], wsem.at[m])

    def pairs(buf, lo, hi, body, ready=None):
        @pl.loop(lo, hi)
        def _(i):
            if ready is not None:
                for k in range(2):
                    ready(2 * i + k).wait()
            body(i, jnp.concatenate([buf[2 * i], buf[2 * i + 1]], axis=1))

    out(wx, g_ref.at[0])
    x_written = writes.pop()

    def to_owner(m):
        return pltpu.make_async_remote_copy(src_ref=local.at[m], dst_ref=rec_a.at[block], send_sem=es.at[m], recv_sem=er.at[block],
                                            device_id=block_device(m), device_id_type=MESHID)

    def second_pair(i, w):
        both = dot(normed[...], w)
        for k in range(2):
            m = 2 * i + k
            ext = both[:, COLS * k : COLS * k + COLS]
            x_pre[m] = ext
            pre = conv_pre(ext, pk[m])
            xc = (pre * jax.nn.sigmoid(pre)).astype(BF16)
            x_conv[m] = xc
            cum, step = cols[m][:, :8], cols[m][:, 8:]
            wide = spread(step * jnp.exp(cum[ROWS - 1 : ROWS] - cum))
            leaving[m] = wide.astype(BF16)
            weighted = (xc.astype(F32) * wide).astype(BF16)
            local[m] = dot(weighted, bc_conv[:, :128], (0, 0)).astype(BF16)
            pl.when(m != block)(lambda m=m: to_owner(m).start())

    pairs(x_flat, 0, 4, second_pair)
    each(go, "line", 1)
    rec_a[block] = local[block]
    out(x_pre, x_pre_out)
    out(x_conv, x_conv_out)
    out(leaving, leaving_out)

    top, low = slice(0, HALF), slice(HALF, ROWS)

    def scan_group(m):
        xc = x_conv[m]
        cum = cols[m][:, :8]
        rows = cum_row[m]
        step_rows = step_row[m]
        parts = []
        for h in range(HEADS):
            xh = xc[:, 64 * h : 64 * h + 64]
            col, row, step = cum[:, h : h + 1], rows[h : h + 1, :], step_rows[h : h + 1, :]
            upper = (jnp.exp(jnp.minimum(col[top] - row[:, top], 0.0)) * step[:, top]).astype(BF16)
            lower = (jnp.exp(jnp.minimum(col[low] - row, 0.0)) * step).astype(BF16)
            uppers[m, h] = upper
            lowers[m, h] = lower
            parts.append(jnp.concatenate([dot((upper.astype(F32) * gram[top, top]).astype(BF16), xh[top]),
                                          dot((lower.astype(F32) * gram[low]).astype(BF16), xh)], axis=0))
        yb[m] = jnp.concatenate(parts, axis=1) + spread(pk[m, 14:15, 0:8]) * xc.astype(F32)

    pl.loop(0, 4)(scan_group)
    each(gz, "pass_on")
    each(go, "near")
    pl.loop(4, GROUPS)(scan_group)
    for c in dec_c:
        c.wait_recv()
    out(dec, dec_out)

    def exchanged(src, sends, recvs):
        for d in range(1, 8):
            other = lax.rem(block + d, 8)
            pltpu.make_async_remote_copy(src_ref=src.at[other], dst_ref=rec_a.at[other], send_sem=sends.at[other],
                                         recv_sem=recvs.at[other], device_id=block_device(other), device_id_type=MESHID).wait()

    def carry(order):
        for h in range(HEADS):
            rows = pl.ds(64 * h, 64)
            run = jnp.zeros((64, 128), F32)
            for i in order:
                out_b[i, rows] = run.astype(BF16)
                run = run * dec[i, pl.ds(h, 1)] + rec_a[i, rows].astype(F32)

    exchanged(local, es, er)
    carry(range(BLOCKS))
    f_c = to_peers(rc, lambda p: out_b.at[p], state, fs, fr, block)
    state[block] = out_b[block]

    @pl.loop(0, GROUPS)
    def _(m):
        pre = conv_pre(x_pre[m], pk[m])
        sig = jax.nn.sigmoid(pre)
        conv_slope[m] = (sig * (1.0 + pre * (1.0 - sig))).astype(BF16)

    out(conv_slope, conv_slope_out)
    each(gz, "last")
    each(gz, "complete")
    x_written.wait()
    each(gx, "drained")
    for m in range(GROUPS):
        z_copy(m).start()

    def gate_pair(i, w):
        z = dot(normed[HALO:, :], w)
        for k in range(2):
            part = z[:, COLS * k : COLS * k + COLS]
            sig = jax.nn.sigmoid(part)
            zb[2 * i + k] = part * sig
            d_z[2 * i + k] = (sig * (1.0 + part * (1.0 - sig))).astype(BF16)

    pairs(x_flat, 0, 4, gate_pair, z_copy)
    each(go, "pass_on")
    for c in f_c:
        c.wait_recv()
        rc.sent(c)
    out(state, state_out)
    square[...] = jnp.zeros_like(square)
    c_mat = bc_conv[:, 128:]

    @pl.loop(0, GROUPS)
    def _(m):
        wide = spread(jnp.exp(cols[m][:, :8]))
        carried = wide * dot(c_mat, state[m], (1, 1))
        grown[m] = wide
        entered[m] = carried
        y = yb[m] + carried
        gated = y * zb[m]
        yb[m] = gated
        d_z[m] = (y * d_z[m].astype(F32)).astype(BF16)
        sq = gated * gated
        square[...] += sq[:, :128] + sq[:, 128:256] + sq[:, 256:]

    each(go, "last")
    r2 = lax.rsqrt(jnp.sum(square[...], axis=1, keepdims=True) / INNER + EPS)

    @pl.loop(0, GROUPS)
    def _(m):
        out_in[m] = (yb[m] * r2 * pk[m, 5:6]).astype(BF16)

    acc[...] = jnp.zeros_like(acc)
    d_c[...] = jnp.zeros_like(d_c)
    d_gram[...] = jnp.zeros_like(d_gram)
    each(go, "complete")

    def result_pair(i, w):
        acc[...] += dot(jnp.concatenate([out_in[2 * i], out_in[2 * i + 1]], axis=1), w, (1, 1))

    pairs(o_flat, 0, 4, result_pair)
    total = jnp.sum(cot[...].astype(F32) * acc[...], axis=1, keepdims=True)
    scales[...] = jnp.concatenate([r2, r2 * r2 * (total / INNER), jnp.zeros((ROWS, 6), F32)], axis=1)
    result[...] = (hid[...].astype(F32) + acc[...]).astype(BF16)
    out(result, result_out)

    def to_owner_back(m):
        return pltpu.make_async_remote_copy(src_ref=local.at[m], dst_ref=rec_a.at[block], send_sem=es.at[m], recv_sem=er.at[block],
                                            device_id=block_device(m), device_id_type=MESHID)

    def gate_back(i, w):
        r2, slope = scales[:, 0:1], scales[:, 1:2]
        both = dot(cot[...], w)
        for k in range(2):
            m = 2 * i + k
            d = both[:, COLS * k : COLS * k + COLS]
            gated = yb[m]
            gain_part[m] = jnp.sum(d * (gated * r2), axis=0, keepdims=True)
            d_gated = r2 * (d * pk[m, 5:6]) - gated * slope
            dy = d_gated * zb[m]
            d_z[m] = (d_gated * d_z[m].astype(F32)).astype(BF16)
            yb[m] = dy
            skip_part[m] = jnp.sum(dy * x_conv[m].astype(F32), axis=0, keepdims=True)
            dye = (grown[m] * dy).astype(BF16)
            local[m] = dot(dye, c_mat, (0, 0)).astype(BF16)
            pl.when(m != block)(lambda m=m: to_owner_back(m).start())
            d_c[...] += dot(dye, state[m])
            d_cols[m] = jnp.concatenate([gathered_heads(dy * entered[m]), jnp.zeros((ROWS, 8), F32)], axis=1)

    pairs(o_flat, 0, 4, gate_back)
    rec_a[block] = local[block]
    across = [rc(src, dst, xs.at[i], xr.at[i], neighbour("core", 1)) for i, (src, dst) in enumerate((
        (cot_t.at[:, 1 - core], cot_t2_out), (out_in, out_in2_out), (normed_t.at[:, 1 - core], normed_t2_out),
        (d_z, d_z2_out)))]
    out(out_in, out_in_out)
    out(d_z, d_z_out)
    out(gain_part, gain_part_out)

    def d_x_copy(m):
        return pltpu.make_async_copy(zb.at[m], d_x_out.at[m], wsem.at[m])

    def inner_group(m):
        dy = yb[m]
        dyb = dy.astype(BF16)
        dy_t = dyb.T
        xc = x_conv[m]
        d_cum = d_cols[m][:, :8]
        lane = lax.broadcasted_iota(jnp.int32, (ROWS, 8), 1)
        parts = []
        sums = []
        for h in range(HEADS):
            xh = xc[:, 64 * h : 64 * h + 64]
            dyh = dyb[:, 64 * h : 64 * h + 64]
            upper, lower = uppers[m, h].astype(F32), lowers[m, h].astype(F32)
            tu = upper * dot(dyh[top], xh[top], (1, 1))
            tl = lower * dot(dyh[low], xh, (1, 1))
            d_gram[top, top] += tu
            d_gram[low] += tl
            qu, ql = tu * gram[top, top], tl * gram[low]
            col = jnp.sum(ql, axis=0, keepdims=True)
            sums.append(jnp.concatenate([col[:, top] + jnp.sum(qu, axis=0, keepdims=True), col[:, low]], axis=1))
            row = jnp.concatenate([jnp.sum(qu, axis=1, keepdims=True),
                                   jnp.sum(ql[:, top] + ql[:, low], axis=1, keepdims=True)], axis=0)
            d_cum = jnp.where(lane == h, d_cum + row, d_cum)
            dyt = dy_t[64 * h : 64 * h + 64]
            below = dot(dyt[:, low], (lower * gram[low]).astype(BF16))
            above = dot(dyt[:, top], (upper * gram[top, top]).astype(BF16))
            parts.append(jnp.concatenate([below[:, top] + above, below[:, low]], axis=1))
        sums = jnp.concatenate(sums + [jnp.zeros((2, ROWS), F32)], axis=0).T
        zb[m] = jnp.concatenate(parts, axis=0).T + spread(pk[m, 14:15, 0:8]) * dy
        d_x_copy(m).start()
        d_cols[m] = jnp.concatenate([d_cum - sums, sums], axis=1)

    pl.loop(0, GROUPS)(inner_group)
    out(skip_part, skip_part_out)
    out(d_cols, d_cols_out)
    dg = jnp.where(triangle(False), d_gram[...], 0.0).astype(BF16)
    d_bc[:, :128] = dot(dg, c_mat, (0, 0))
    d_bc[:, 128:] = d_c[...] + dot(dg, bc_conv[:, :128])
    out(d_bc, d_bc_out)
    exchanged(local, es, er)
    carry(range(BLOCKS - 1, -1, -1))
    out(out_b, d_state_out)
    for c in across:
        c.wait_recv()
    for c in writes:
        c.wait()
    for m in range(GROUPS):
        d_x_copy(m).wait()
    rc.all_sent()


HALF = ROWS // 2
RESULTS = (
    ("pk", (GROUPS, 16, COLS), F32), ("x_pre", (GROUPS, HALO + ROWS, COLS), F32), ("x_conv", (GROUPS, ROWS, COLS), BF16),
    ("d_x", (GROUPS, ROWS, COLS), F32), ("normed_t", (8, 2, 96, ROWS), BF16), ("cot_t", (8, 2, 96, ROWS), BF16),
    ("state", (GROUPS, COLS, 128), BF16), ("bc_pre", (HALO + ROWS, 256), F32), ("bc_conv", (ROWS, 256), BF16),
    ("steps", (ROWS, 128), F32), ("rates", (8, 128), F32), ("cols", (GROUPS, ROWS, 16), F32),
    ("cum_row", (GROUPS, 8, ROWS), F32), ("step_row", (GROUPS, 8, ROWS), F32), ("dec", (BLOCKS, 8, 128), F32),
    ("result", (ROWS, WIDTH), BF16), ("out_in", (GROUPS, ROWS, COLS), BF16), ("d_z", (GROUPS, ROWS, COLS), BF16),
    ("gain_part", (GROUPS, 1, COLS), F32), ("skip_part", (GROUPS, 1, COLS), F32), ("d_cols", (GROUPS, ROWS, 16), F32),
    ("d_bc", (ROWS, 256), F32), ("conv_slope", (GROUPS, ROWS, COLS), BF16), ("leaving", (GROUPS, ROWS, COLS), BF16),
    ("d_state", (GROUPS, COLS, 128), BF16),
)
SIBLING = (
    ("normed_t2", (8, 96, ROWS), BF16), ("cot_t2", (8, 96, ROWS), BF16), ("out_in2", (GROUPS, ROWS, COLS), BF16),
    ("d_z2", (GROUPS, ROWS, COLS), BF16),
)


def forward(zx, wo, bc, hid, cot, *params):
    hbm = pl.BlockSpec(memory_space=pl.ANY)
    vmem = pl.BlockSpec(memory_space=pltpu.VMEM)
    sem = pltpu.SemaphoreType.DMA

    def v(*shape, dtype=F32):
        return pltpu.VMEM(shape, dtype)

    def b(*shape):
        return v(*shape, dtype=BF16)

    groups = (GROUPS, ROWS, COLS)
    outs = pl.pallas_call(
        forward_kernel,
        out_shape=(sds(2, 4, 2, 2, 4, 2, 96, COLS, dtype=BF16), sds(2, 4, 2, 96, COLS, dtype=BF16),
                   *[sds(*shape, dtype=dtype) for _, shape, dtype in RESULTS + SIBLING]),
        in_specs=[vmem, hbm, vmem, vmem, hbm] + [vmem] * 8,
        out_specs=(hbm,) * (2 + len(RESULTS) + len(SIBLING)),
        scratch_shapes=[
            *[pltpu.VMEM(shape, dtype) for name, shape, dtype in RESULTS if name not in ("d_x", "d_state")],
            b(ROWS, WIDTH), b(HALO + ROWS, WIDTH), b(HALO, WIDTH), b(96, 128), b(2, 4, 2, 96, COLS),
            v(*groups), v(*groups), b(GROUPS, HEADS, HALF, HALF), b(GROUPS, HEADS, HALF, ROWS),
            b(4, 2, 2, 4, 2, 96, COLS), b(4, 2, 2, 4, 2, 96, COLS),
            v(ROWS, ROWS), v(ROWS, ROWS),
            b(GROUPS, COLS, 128), b(GROUPS, COLS, 128), b(GROUPS, COLS, 128), v(GROUPS, 8, 128),
            v(ROWS, 128), v(ROWS, 8), v(ROWS, WIDTH), v(ROWS, 128), v(16, COLS), v(1, WIDTH), b(2, 96, COLS), v(*groups), v(*groups),
            sem((27,)), sem((90,)), sem((36,)), sem((36,)), sem((18,)), sem((18,)), sem((8,)), sem((8,)), sem((8,)), sem((8,)),
            sem((8,)), sem((8,)), sem((8,)), sem((8,)), sem, sem, sem((7,)), sem((GROUPS,)), sem((len(RESULTS),)), sem((4,)),
            sem((4,)),
        ],
        compiler_params=pltpu.CompilerParams(collective_id=0, has_side_effects=True, vmem_limit_bytes=63 * 2**20),
        name="forward_between_devices",
    )(zx, wo, bc, hid, cot, *params)
    return outs[0], outs[1], dict(zip([name for name, _, _ in RESULTS + SIBLING], outs[2:]))


class Total:
    def __init__(self, rc, value, lines, axes, send, recv):
        self.rc, self.value, self.lines, self.axes, self.send, self.recv = rc, value, lines, axes, send, recv
        self.me = dict(my_place(), core=lax.axis_index("core"), ylo=lax.axis_index("ylo"))

    def step(self, j):
        if j > 0:
            for c in self.flying:
                c.wait_recv()
                self.rc.sent(c)
            l, i = self.lines, j - 1
            if self.axes[i] in ("core", "ylo"):
                self.value[...] = l[i, 0] + l[i, 1]
            else:
                self.value[...] = (l[i, 0] + l[i, 1]) + (l[i, 2] + l[i, 3])
        if j < len(self.axes):
            a = self.axes[j]
            mine = self.lines.at[j, self.me[a]]
            mine[...] = self.value[...]
            if a in ("core", "ylo"):
                devices = [{a: 1 - self.me[a]}]
            else:
                devices = [neighbour(a, d) for d in (1, 2, 3)]
            self.flying = [self.rc(mine, mine, self.send.at[d], self.recv.at[3 * j + d], device)
                           for d, device in enumerate(devices)]


class SmallSum:
    def __init__(self, rc, parts, xs, ys, zs, send, recv):
        self.rc, self.parts, self.xs, self.ys, self.zs = rc, parts, xs, ys, zs
        self.send, self.recv = send, recv
        self.me = my_place()

    def step(self, j, out=None):
        rc, me, parts, s, r = self.rc, self.me, self.parts, self.send, self.recv
        ylo = lax.rem(me["y"], 2)
        if j == 0:
            self.c = [rc(parts.at[:, lax.rem(me["x"] + d, 4)], self.xs.at[d - 1], s.at[d], r.at[d], neighbour("x", d))
                      for d in (1, 2, 3)]
            return
        for c in self.c:
            c.wait_recv()
        if j == 1:
            for yl in range(2):
                m = parts.at[yl, me["x"]]
                m[...] = (f32(m) + f32(self.xs.at[0, yl]) + f32(self.xs.at[1, yl]) + f32(self.xs.at[2, yl])).astype(BF16)
            self.ys[me["y"]] = parts[ylo, me["x"]]
            self.c = [rc(parts.at[lax.rem(me["y"] + d, 2), me["x"]], self.ys.at[me["y"]], s.at[3 + d], r.at[3 + d],
                         neighbour("y", d)) for d in (1, 2, 3)]
        elif j == 2:
            y = self.ys
            m = self.zs.at[me["z"]]
            m[...] = ((f32(y.at[0]) + f32(y.at[1])) + (f32(y.at[2]) + f32(y.at[3]))).astype(BF16)
            self.c = [rc(m, m, s.at[6 + d], r.at[6 + d], neighbour("z", d)) for d in (1, 2, 3)]
        elif j == 3:
            z = self.zs
            return (f32(z.at[0]) + f32(z.at[1])) + (f32(z.at[2]) + f32(z.at[3]))


def part_of(ref, item, pos, lo, n):
    z = slice(None) if pos["z"] is None else pos["z"]
    x = slice(None) if pos["x"] is None else pos["x"]
    if pos["y"] is None:
        yh = yl = slice(None)
    else:
        yh, yl = pos["y"] // 2, lax.rem(pos["y"], 2)
    return ref.at[item, z, yh, yl, x, pl.ds(lo, n)]


class Chunk:
    def __init__(self, rc, own, out, bufs, sems, item, slot, wide, r):
        self.rc, self.own, self.out, self.item, self.slot, self.r = rc, own, out, item, slot, r
        full, half, second, third = bufs
        self.full, self.half = full[r].at[wide], half[r].at[wide]
        self.direct = {1: second[r].at[slot], 2: third.at[slot * 3 + r]}
        self.send, self.recv = sems
        self.number = slot * 3 + r
        self.base = self.number * 10
        self.me = my_place()
        self.flying = {}

    def slab(self, st, d, lo=0, n=SUB):
        p = {a: (self.me[a] if i < st else None) for i, a in enumerate(ORDERS[self.r])}
        a = ORDERS[self.r][st]
        p[a] = lax.rem(self.me[a] + (d + 4), 4)
        return part_of(self.own, self.slot, p, self.r * SUB + lo, n)

    def loop(self, st, body):
        sizes = []
        for a, n in (("z", (4,)), ("y", (2, 2)), ("x", (4,))):
            if ORDERS[self.r].index(a) > st:
                sizes += n
        if not sizes:
            body(())
        elif len(sizes) == 1 or sizes == [2, 2]:
            for i in range(4):
                body((i,) if len(sizes) == 1 else (i // 2, i % 2))
        else:
            @pl.loop(0, 4)
            def _(i):
                for k in range(4):
                    if sizes == [4, 4]:
                        body((i, k))
                    elif sizes == [4, 2, 2]:
                        body((i, k // 2, k % 2))
                    else:
                        body((i // 2, lax.rem(i, 2), k))

    def push(self, k, src, dst, st, d):
        s = k % 2 if k < 4 else (k - 4) % 3
        if s in self.flying:
            self.rc.sent(self.flying[s])
        c = self.rc(src, dst, self.send.at[3 * self.number + s], self.recv.at[self.base + k], neighbour(ORDERS[self.r][st], d))
        self.flying[s] = c
        return c

    def far(self):
        self.far_c = [self.push(i, self.slab(0, 2, 16 * i, 16), self.half.at[i], 0, d) for i, d in enumerate((1, -1))]

    def near(self):
        self.near_c = []
        for i, d in enumerate((1, -1)):
            self.far_c[i].wait_recv()
            mine = self.slab(0, d, 16 * i, 16)

            def add(index, mine=mine, i=i):
                m = mine.at[index]
                m[...] = m[...] + self.half[(i, *index)]

            self.loop(0, add)
            self.near_c.append(self.push(2 + i, self.slab(0, d), self.full.at[i], 0, d))

    def straight(self, st):
        self.straight_c = [self.push(1 + 3 * st + d - 1, self.slab(st, d), self.direct[st].at[d - 1], st, d) for d in (1, 2, 3)]

    def step(self, j):
        if j == 0:
            self.far()
        elif j == 1:
            self.near()
        elif j == 2:
            for c in self.near_c:
                c.wait_recv()
            mine = self.slab(0, 0)

            def add(index):
                m = mine.at[index]
                m[...] = (f32(m) + f32(self.full.at[(0, *index)]) + f32(self.full.at[(1, *index)])).astype(BF16)

            self.loop(0, add)
            self.straight(1)
        else:
            for c in self.straight_c:
                c.wait_recv()
            st = j - 2
            mine = self.slab(st, 0)
            got = self.direct[st]

            def total(index):
                m = mine.at[index] if index else mine
                return (f32(m) + f32(got.at[(0, *index)])) + (f32(got.at[(1, *index)]) + f32(got.at[(2, *index)]))

            if st == 1:
                def add(index):
                    mine[index] = total(index).astype(BF16)

                self.loop(1, add)
                self.straight(2)
            else:
                self.out(pl.ds(self.r * SUB, SUB))[...] = total(())


def backward_kernel(g_ref, x_conv_ref, d_x_ref, x_pre_ref, cols_ref, d_cols_ref, slope_ref, leaving_ref, cot_t_ref, cot_t2_ref, out_in_ref, out_in2_ref,
                    normed_t_ref, normed_t2_ref, d_z_ref, d_z2_ref, state_ref, d_state_ref, w_small_ref, hid_ref, cot_ref,
                    taps, d_bc_in, bc_pre, bc_conv, taps_bc, norm_gain, shifted, rates, gain_part, skip_part,
                    zx_out, wo_out, wbc_out, wdt_out, taps_out, taps_bc_out, log_out, shift_out, skip_out, gate_out, norm_out,
                    grad_hidden, *scr):
    (own, l_c, l_c2, l_n, l_n2, rhs_o, rhs_z, rhs_x, state, d_state, w_small, hid, cot, tails, halo_src, halo_dst, halo_x, halo_x_in, halo_bc, halo_bc_in, acc, wbuf,
     bxc, bdx, bxp, bcols, bdc, bslope, bleave, d_b, d_all, parts, small2, s_xs, s_ys, s_zs,
     v_all, v_in, v_sum, v_lines, n_all, n_lines, gain) = scr[:43]
    bufs = [scr[43:46], scr[46:49], scr[49:52], scr[52]]
    (t_s, t_r, e_s, e_r, x_s, x_r, h_s, h_r, m_s, m_r, ss, sr, vms, vmr, vs, vr, ns, nr, wsem, lsem, isem, freed) = scr[53:]
    rc = Sender()
    gain[0] = norm_gain[...]
    core = lax.axis_index("core")
    block = lax.axis_index("z") * 2 + lax.axis_index("yhi")
    arrived = greet()

    loads = {}

    def load_in(name, *pairs):
        loads[name] = []
        for src, dst in pairs:
            c = pltpu.make_async_copy(src, dst, isem.at[sum(len(v) for v in loads.values())])
            c.start()
            loads[name].append(c)

    def ready(name):
        for c in loads[name]:
            c.wait()

    load_in("o", (cot_t_ref.at[:, core], l_c), (cot_t2_ref, l_c2), (out_in_ref, rhs_o.at[0]), (out_in2_ref, rhs_o.at[1]))
    load_in("z", (normed_t_ref.at[:, core], l_n), (normed_t2_ref, l_n2), (d_z_ref, rhs_z.at[0]), (d_z2_ref, rhs_z.at[1]))
    load_in("s", (state_ref, state), (d_state_ref.at[block], d_state.at[block]))

    outs = (lambda at: zx_out.at[at, 1], lambda at: zx_out.at[at, 0], lambda at: wo_out.at[at])

    def chunks(item, slot, wide):
        return [Chunk(rc, own, outs[item], bufs, (t_s, t_r), item, slot, wide, r) for r in range(3)]

    def steps(cs, j):
        for c in cs:
            c.step(j)

    def both_tokens(own_t, other_t):
        return jnp.concatenate([own_t[...].reshape(768, ROWS), other_t[...].reshape(768, ROWS)], axis=1)

    def gradient(left, left2, rhs, slot, ready=None):
        def one(i):
            if ready is not None:
                ready(2 * i)
                ready(2 * i + 1)
            right = jnp.concatenate([jnp.concatenate([rhs[0, 2 * i + k], rhs[1, 2 * i + k]], axis=0) for k in range(2)], axis=1)
            v = dot(both_tokens(left, left2), right).astype(BF16)
            for k in range(2):
                own[slot, i, k] = v[:, COLS * k : COLS * k + COLS].reshape(2, 4, 96, COLS)

        pl.loop(0, GROUPS // 2)(one)

    oc, zc, xc_ = chunks(2, 0, 0), chunks(1, 1, 1), chunks(0, 2, 0)
    arrived()
    back = to_peers(rc, lambda p: d_state_ref.at[p], d_state, e_s, e_r, block)
    ready("o")
    gradient(l_c, l_c2, rhs_o, 0)
    steps(oc, 0)
    ready("z")

    streams = ((x_conv_ref, bxc), (d_x_ref, bdx), (x_pre_ref, bxp), (cols_ref, bcols), (d_cols_ref, bdc), (slope_ref, bslope), (leaving_ref, bleave))

    def load(m):
        k = lax.rem(m, 3)
        return [pltpu.make_async_copy(src.at[m], dst.at[k], lsem.at[k, i]) for i, (src, dst) in enumerate(streams)]

    for c in load(0) + load(1):
        c.start()
    gradient(l_n, l_n2, rhs_z, 1)
    steps(zc, 0)
    ready("s")
    for c in back:
        c.wait_recv()

    def fifth_group(m):
        k = lax.rem(m, 3)

        @pl.when(m < GROUPS - 2)
        def _():
            for c in load(m + 2):
                c.start()

        for c in load(m):
            c.wait()
        ds = d_state[m]
        xf = bxc[k].astype(F32)
        cum, step = bcols[k][:, :8], bcols[k][:, 8:]
        last = cum[ROWS - 1 : ROWS]
        tail = jnp.exp(last - cum)
        weights = step * tail
        wide = bleave[k].astype(F32)
        d_weighted = dot(bc_conv[:, :128], ds, (1, 1))
        d_b[...] += dot((xf * wide).astype(BF16), ds)
        dx = bdx[k] + wide * d_weighted
        d_weights = gathered_heads(d_weighted * xf)
        both = weights * d_weights
        lane = lax.broadcasted_iota(jnp.int32, (1, 8), 1)
        product = jnp.sum(state[m].astype(F32) * ds.astype(F32), axis=1, keepdims=True)
        d_last = jnp.sum(both, axis=0, keepdims=True)
        for h in range(HEADS):
            dots = jnp.sum(product[64 * h : 64 * h + 64], axis=0, keepdims=True)
            d_last = jnp.where(lane == h, d_last + jnp.exp(last) * dots, d_last)
        row = lax.broadcasted_iota(jnp.int32, (ROWS, 8), 0)
        d_cum = bdc[k][:, :8] - both
        d_cum = jnp.where(row == ROWS - 1, d_cum + d_last, d_cum)
        d_all[m] = jnp.concatenate([d_cum, bdc[k][:, 8:] + both], axis=1)
        ext = bxp[k]
        tap = taps[m]
        dp = dx * bslope[k].astype(F32)
        v_all[m, 0:8] = conv_grads(dp, ext, gain_part[m], skip_part[m])
        whole_dx = conv_transposed(jnp.concatenate([dp, jnp.zeros((8, COLS), F32)], axis=0), tap)
        rhs_x[0, m] = whole_dx.astype(BF16)
        tails[m] = whole_dx[ROWS - 16 :]
        halo_src[m] = dp[:8]

    d_b[...] = jnp.zeros_like(d_b)
    pl.loop(0, 3)(fifth_group)
    steps(oc, 1)
    pl.loop(3, GROUPS)(fifth_group)

    load_in("end", (w_small_ref, w_small), (hid_ref, hid), (cot_ref, cot))
    for m in range(GROUPS):
        halo_x[3 * m : 3 * m + 3] = halo_src[m, 0:3]
    before = block_device(lax.rem(block + 7, 8))
    halo = [rc(halo_x, halo_x_in, h_s.at[0], h_r.at[0], before)]

    d_bc = jnp.concatenate([d_bc_in[:, :128] + d_b[...], d_bc_in[:, 128:]], axis=1)
    ext = bc_pre[...]
    pre = conv_pre(ext, taps_bc[...])
    sig = jax.nn.sigmoid(pre)
    dp_bc = d_bc * (sig * (1.0 + pre * (1.0 - sig)))
    halo_bc[...] = dp_bc[:8]
    halo.append(rc(halo_bc, halo_bc_in, h_s.at[1], h_r.at[1], before))
    steps(zc, 1)
    zero8 = jnp.zeros((1, 256), F32)
    d_cum = jnp.concatenate([d_all[m][:, :HEADS] for m in range(GROUPS)] + [jnp.zeros((ROWS, 80), F32)], axis=1)
    d_step = jnp.concatenate([d_all[m][:, 8 : 8 + HEADS] for m in range(GROUPS)] + [jnp.zeros((ROWS, 80), F32)], axis=1)
    d_decay = dot(triangle(True).astype(F32), d_cum, precision=lax.Precision.HIGHEST)
    rate = -jnp.exp(rates[0:1])
    v = shifted[...]
    sig = jax.nn.sigmoid(v)
    far = v < -16.0
    ratio = jnp.where(far, 1.0, sig / jnp.where(far, 1.0, softplus(v)))
    d_dt = d_step * ratio + rate * d_decay * sig
    log_grad = jnp.sum(d_decay * (softplus(v) * rate), axis=0, keepdims=True)
    shift_grad = jnp.sum(d_dt, axis=0, keepdims=True)
    bc_rows = conv_grads(dp_bc, ext, jnp.concatenate([log_grad, shift_grad], axis=1), zero8)
    bc_rows = jnp.concatenate([bc_rows, jnp.zeros((8, 128), F32)], axis=1)
    for m in range(GROUPS):
        v_all[m, 8:16] = bc_rows
    vec_c = to_peers(rc, lambda p: v_all.at[p], v_in, vms, vmr, block)
    v_in[block] = v_all[block]

    for c in halo:
        c.wait_recv()
    inside = block < 7
    halo_dst[...] = jnp.zeros_like(halo_dst)
    for m in range(GROUPS):
        halo_dst[m, 0:3] = jnp.where(inside, halo_x_in[3 * m : 3 * m + 3], 0.0)

    def below(k):
        return halo_dst[k]

    def across(m):
        return pltpu.make_async_remote_copy(src_ref=rhs_x.at[0, m], dst_ref=rhs_x.at[1, m], send_sem=x_s.at[m],
                                            recv_sem=x_r.at[m], device_id=neighbour("core", 1), device_id_type=MESHID)

    def fix(m):
        ext = jnp.concatenate([jnp.zeros((16, COLS), F32), below(m)], axis=0)
        rhs_x[0, m, pl.ds(ROWS - 16, 16)] = (tails[m] + conv_transposed(ext, taps[m], 16)).astype(BF16)
        across(m).start()

    d_bc = conv_transposed(jnp.concatenate([dp_bc, jnp.where(inside, halo_bc_in[...], 0.0)], axis=0), taps_bc[...])
    small2[0] = jnp.concatenate([d_bc, d_dt], axis=1).astype(BF16)
    small_c = rc(small2.at[0], small2.at[1], m_s, m_r, neighbour("core", 1))
    pl.loop(0, GROUPS)(fix)

    def weights(m):
        k = lax.rem(m, 2)
        return [pltpu.make_async_copy(g_ref.at[i, m], wbuf.at[k, i], wsem.at[k, i]) for i in range(2)]

    for c in weights(0):
        c.start()
    steps(oc, 2)
    for a in "xyz":
        for s in (1, -1):
            pl.semaphore_signal(freed, inc=1, device_id=neighbour(a, s), device_id_type=MESHID)
    gradient(l_n, l_n2, rhs_x, 2, lambda m: across(m).wait())
    pl.semaphore_wait(freed, 6)
    steps(xc_, 0)
    small_c.wait_recv()
    parts[...] = dot(both_tokens(l_n, l_n2), small2[...].reshape(2 * ROWS, COLS)).astype(BF16).reshape(2, 4, 96, COLS)
    sums = SmallSum(rc, parts, s_xs, s_ys, s_zs, ss, sr)
    ready("end")
    acc[...] = dot(small2[0], w_small[...], (1, 1))
    def input_group(m):
        k = lax.rem(m, 2)

        @pl.when(m < GROUPS - 1)
        def _():
            for c in weights(m + 1):
                c.start()

        for c in weights(m):
            c.wait()
        lhs = jnp.concatenate([rhs_x[0, m], rhs_z[0, m]], axis=1)
        rhs = jnp.concatenate([wbuf[k, 0], wbuf[k, 1]], axis=1)
        acc[...] += dot(lhs, rhs, (1, 1))

    pl.loop(0, 2)(input_group)
    sums.step(0)
    pl.loop(2, 4)(input_group)
    steps(zc, 2)
    for c in vec_c:
        c.wait_recv()
    t = v_in[0]
    for i in range(1, BLOCKS):
        t = t + v_in[i]
    v_sum[...] = t
    vec = Total(rc, v_sum, v_lines, ("core", "x", "ylo"), vs, vr)
    vec.step(0)
    steps(xc_, 1)
    pl.loop(4, GROUPS)(input_group)
    steps(oc, 3)
    v = hid[...].astype(F32)
    r = lax.rsqrt(jnp.mean(v * v, axis=1, keepdims=True) + EPS)
    unit = v * r
    dn = acc[...]
    gain_grad = jnp.sum(dn * unit, axis=0, keepdims=True)
    for i in range(4):
        n_all[pl.ds(i, 1)] = gain_grad[:, COLS * i : COLS * i + COLS]
    n_all[pl.ds(4, 4)] = jnp.zeros((4, COLS), F32)
    nvec = Total(rc, n_all, n_lines, ("core", "x", "y", "z"), ns, nr)
    nvec.step(0)
    sums.step(1)
    vec.step(1)
    steps(zc, 3)
    d_in = dn * gain[...]
    grad_hidden[...] = r * (d_in - unit * jnp.mean(d_in * unit, axis=1, keepdims=True)) + cot[...].astype(F32)
    nvec.step(1)
    steps(xc_, 2)
    sums.step(2)
    vec.step(2)
    nvec.step(2)
    steps(oc, 4)
    steps(zc, 4)
    steps(xc_, 3)
    vec.step(3)
    nvec.step(3)

    pick = lax.broadcasted_iota(jnp.int32, (8, 128), 0) + block * HEADS
    pick = (pick == lax.broadcasted_iota(jnp.int32, (8, 128), 1)).astype(F32)

    def own_heads(row):
        return dot(row, pick, (1, 1), precision=lax.Precision.HIGHEST)

    mine = v_sum[...]
    taps_out[...] = mine[:5]
    gate_out[...] = mine[5]
    skip_out[...] = gathered_heads(mine[6:7])[0, :HEADS]
    taps_bc_out[...] = mine[8:13, :256]
    log_out[...] = own_heads(mine[13:14, :128])[0, :HEADS]
    shift_out[...] = own_heads(mine[13:14, 128:256])[0, :HEADS]
    steps(xc_, 4)
    little = sums.step(3)
    wbc_out[...] = little[:, :256]
    wdt_out[...] = dot(pick, little[:, 256:], (1, 1), precision=lax.Precision.HIGHEST)[:HEADS]
    nvec.step(4)
    for i in range(4):
        norm_out[pl.ds(COLS * i, COLS)] = n_all[i]
    rc.all_sent()


def backward(w_all, r, w_small, hid, cot, norm_gain, conv_bc):
    hbm = pl.BlockSpec(memory_space=pl.ANY)
    vmem = pl.BlockSpec(memory_space=pltpu.VMEM)
    sem = pltpu.SemaphoreType.DMA

    def buf(*shape, dtype=BF16):
        return pltpu.VMEM((*shape, COLS), dtype)

    def v(*shape, dtype=F32):
        return pltpu.VMEM(shape, dtype)

    def b(*shape):
        return v(*shape, dtype=BF16)

    scratch = [
        buf(3, 4, 2, 2, 4, 96), b(8, 96, ROWS), b(8, 96, ROWS), b(8, 96, ROWS), b(8, 96, ROWS),
        buf(2, GROUPS, ROWS), buf(2, GROUPS, ROWS), buf(2, GROUPS, ROWS), b(GROUPS, COLS, 128), b(GROUPS, COLS, 128),
        buf(WIDTH), b(ROWS, WIDTH), b(ROWS, WIDTH),
        buf(GROUPS, 16, dtype=F32), buf(GROUPS, 8, dtype=F32), buf(GROUPS, 8, dtype=F32),
        buf(24, dtype=F32), buf(24, dtype=F32), v(8, 256), v(8, 256),
        v(ROWS, WIDTH), buf(2, 2, WIDTH),
        buf(3, ROWS), buf(3, ROWS, dtype=F32), buf(3, HALO + ROWS, dtype=F32), v(3, ROWS, 16), v(3, ROWS, 16),
        buf(3, ROWS), buf(3, ROWS),
        v(ROWS, 128), v(GROUPS, ROWS, 16), buf(2, 4, 96), buf(2, ROWS), buf(3, 2, 96), buf(4, 96), buf(4, 96),
    ]
    scratch += [buf(GROUPS, 16, dtype=F32), buf(GROUPS, 16, dtype=F32), buf(16, dtype=F32), buf(3, 4, 16, dtype=F32)]
    scratch += [buf(8, dtype=F32), buf(4, 4, 8, dtype=F32), v(1, WIDTH)]
    scratch += [buf(2, 2, 4, 2, 2, SUB), buf(2, 2, 4, 4, SUB), buf(2, 2, 2, 2, 4, SUB)]
    scratch += [buf(2, 2, 4, 2, 2, 16), buf(2, 2, 4, 4, 16), buf(2, 2, 2, 2, 4, 16)]
    scratch += [buf(3, 3, 4, SUB), buf(3, 3, 4, SUB), buf(3, 3, 2, 2, SUB), buf(9, 3, SUB)]
    scratch += [sem((27,)), sem((90,)), sem((8,)), sem((8,)), sem((8,)), sem((8,)), sem((2,)), sem((2,)), sem, sem, sem((10,)), sem((10,)), sem((8,)), sem((8,)),
                sem((3,)), sem((9,)), sem((3,)), sem((12,)), sem((2, 2)), sem((3, 7)), sem((13,)), pltpu.SemaphoreType.REGULAR]
    names = ("x_conv", "d_x", "x_pre", "cols", "d_cols", "conv_slope", "leaving", "cot_t", "cot_t2", "out_in", "out_in2", "normed_t", "normed_t2", "d_z",
             "d_z2", "state", "d_state")
    return pl.pallas_call(
        backward_kernel,
        out_shape=(sds(96, 2, COLS), sds(96, COLS), sds(96, 256), sds(HEADS, 96), sds(5, COLS), sds(5, 256), sds(HEADS), sds(HEADS),
                   sds(HEADS), sds(COLS), sds(WIDTH), sds(ROWS, WIDTH)),
        in_specs=[hbm] * 21 + [vmem] * 10,
        out_specs=(vmem,) * 12,
        scratch_shapes=scratch,
        compiler_params=pltpu.CompilerParams(collective_id=1, has_side_effects=True, vmem_limit_bytes=63 * 2**20),
        name="backward_between_devices",
    )(w_all, *[r[name] for name in names], w_small, hid, cot, r["pk"], r["d_bc"], r["bc_pre"], r["bc_conv"], conv_bc, norm_gain,
      r["steps"], r["rates"], r["gain_part"], r["skip_part"])
def results_kernel(*refs):
    n = (len(refs) - 2) // 3
    sems = refs[-2:]
    into = [pltpu.make_async_copy(refs[i], refs[2 * n + i], sems[0].at[i]) for i in range(n)]
    back = [pltpu.make_async_copy(refs[2 * n + i], refs[n + i], sems[1].at[i]) for i in range(n)]
    for c in into:
        c.start()
    for c, d in zip(into, back):
        c.wait()
        d.start()
    for d in back:
        d.wait()


def as_results(*arrays):
    hbm = pl.BlockSpec(memory_space=pl.ANY)
    return pl.pallas_call(
        results_kernel,
        out_shape=tuple(jax.ShapeDtypeStruct(a.shape, a.dtype) for a in arrays),
        in_specs=[hbm] * len(arrays),
        out_specs=(hbm,) * len(arrays),
        scratch_shapes=[*[pltpu.VMEM(a.shape, a.dtype) for a in arrays], *[pltpu.SemaphoreType.DMA((len(arrays),))] * 2],
        name="results",
    )(*arrays)


def shards(hidden, grad_out, norm_gain, w_zx, w_bc, w_dt, conv_x, conv_bc, a_log, dt_bias, d_skip, gate_gain, w_out):
    w_all, w_small, r = forward(w_zx, w_out.T, w_bc, hidden, grad_out, norm_gain, w_dt.T, conv_x, conv_bc,
                                a_log, dt_bias, d_skip, gate_gain)
    w_all = w_all.reshape(2, GROUPS, WIDTH, COLS)
    w_small = w_small.reshape(WIDTH, COLS)
    zx, wo, wbc, wdt, grad_taps, grad_taps_bc, log_rate, shift, skip, gate, norm, grad_hidden = backward(
        w_all, r, w_small, hidden, grad_out, norm_gain, conv_bc)
    result, grad_hidden, norm, zx, wbc, wdt, grad_taps, grad_taps_bc, log_rate, shift, skip, gate, wo = as_results(
        r["result"], grad_hidden, norm, zx, wbc, wdt, grad_taps, grad_taps_bc, log_rate, shift, skip, gate, wo)
    return (result, grad_hidden, norm, zx, wbc, wdt.T, grad_taps, grad_taps_bc, log_rate, shift, skip, gate, wo.T)


def solution(mesh):
    finer = Mesh(mesh.devices.reshape(2, 4, 2, 4, 2), DP_MP)
    rows = P(DP_MP, None)
    placed = (rows, rows, P(), P(DP, None, MP), P(DP, None), P(DP, MP), P(None, MP), P(), P(MP), P(MP), P(MP), P(MP),
              P(MP, DP))
    return jax.shard_map(
        shards,
        mesh=finer,
        in_specs=placed,
        out_specs=(rows, rows, P(), P(DP, None, MP), P(DP, None), P(DP, MP), P(None, MP), P(), P(MP), P(MP), P(MP), P(MP),
                   P(MP, DP)),
        check_vma=False,
    )
```

```python
import jax
import jax.numpy as jnp
from jax import lax
from jax.experimental import pallas as pl
from jax.experimental.pallas import tpu as pltpu
from jax.sharding import Mesh
from jax.sharding import PartitionSpec as P

MP = ("z", "yhi")
DP = ("ylo", "x", "core")
DP_MP = DP + MP
BLOCKS = 8
F32 = jnp.float32
BF16 = jnp.bfloat16
ROWS = 256
WIDTH = 1536
GROUPS = 8
COLS = 384
HEADS = 6
HALO = 16
EPS = 1e-05
INNER = GROUPS * COLS
VMEM_LIMIT = 56 * 2**20


def dot(a, b, contract=(1, 0), precision=None):
    return lax.dot_general(
        a, b, (((contract[0],), (contract[1],)), ((), ())),
        preferred_element_type=F32, precision=precision,
    )


def spread(per_head):
    rows = per_head.shape[0]
    low = lax.broadcasted_iota(jnp.int32, (rows, 128), 1) < 64
    tiles = [
        jnp.where(low, per_head[:, 2 * i : 2 * i + 1], per_head[:, 2 * i + 1 : 2 * i + 2])
        for i in range(COLS // 128)
    ]
    return jnp.concatenate(tiles, axis=1)


def gathered_heads(values):
    rows = values.shape[0]
    low = lax.broadcasted_iota(jnp.int32, (rows, 128), 1) < 64
    lane = lax.broadcasted_iota(jnp.int32, (rows, 8), 1)
    out = jnp.zeros((rows, 8), F32)
    for i in range(COLS // 128):
        tile = values[:, 128 * i : 128 * i + 128]
        first = jnp.sum(jnp.where(low, tile, 0.0), axis=1, keepdims=True)
        both = jnp.sum(tile, axis=1, keepdims=True)
        out = jnp.where(lane == 2 * i, first, out)
        out = jnp.where(lane == 2 * i + 1, both - first, out)
    return out


def softplus(v):
    return jnp.maximum(v, 0.0) + jnp.log1p(jnp.exp(-jnp.abs(v)))


def conv_pre(ext, taps):
    total = taps[4:5]
    for j in range(4):
        total = total + ext[HALO - 3 + j : HALO - 3 + j + ROWS] * taps[j : j + 1]
    return total


def conv_transposed(ext, taps, rows=ROWS):
    total = ext[3 : 3 + rows] * taps[0:1]
    for j in range(1, 4):
        total = total + ext[3 - j : 3 - j + rows] * taps[j : j + 1]
    return total


def conv_grads(dpre, ext, sixth, seventh):
    rows = [
        jnp.sum(dpre * ext[HALO - 3 + j : HALO - 3 + j + ROWS], axis=0, keepdims=True)
        for j in range(4)
    ]
    rows.append(jnp.sum(dpre, axis=0, keepdims=True))
    rows += [sixth, seventh, jnp.zeros((1, dpre.shape[1]), F32)]
    return jnp.concatenate(rows, axis=0)


def triangle(upper):
    row = lax.broadcasted_iota(jnp.int32, (ROWS, ROWS), 0)
    col = lax.broadcasted_iota(jnp.int32, (ROWS, ROWS), 1)
    return row <= col if upper else row >= col


def sds(*shape, dtype=F32):
    return jax.ShapeDtypeStruct(shape, dtype)


def params():
    return pltpu.CompilerParams(vmem_limit_bytes=VMEM_LIMIT)


MESHID = pl.DeviceIdType.MESH
ORDERS = (("x", "y", "z"), ("y", "z", "x"), ("z", "x", "y"))
SUB = 32


def neighbour(axis, s):
    if axis == "core":
        return {"core": 1 - lax.axis_index("core")}
    if axis == "y":
        y = lax.rem(lax.axis_index("yhi") * 2 + lax.axis_index("ylo") + (s + 4), 4)
        return {"ylo": lax.rem(y, 2), "yhi": y // 2}
    return {axis: lax.rem(lax.axis_index(axis) + (s + 4), 4)}


def my_place():
    return {"x": lax.axis_index("x"), "z": lax.axis_index("z"), "y": lax.axis_index("yhi") * 2 + lax.axis_index("ylo")}


def block_device(p):
    return {"z": p // 2, "yhi": lax.rem(p, 2)}


def f32(ref):
    return ref[...].astype(F32)


class Sender:
    def __init__(self):
        self.pending = {}

    def __call__(self, src, dst, send, recv, device):
        c = pltpu.make_async_remote_copy(src_ref=src, dst_ref=dst, send_sem=send, recv_sem=recv, device_id=device,
                                         device_id_type=MESHID)
        c.start()
        self.pending[id(c)] = c
        return c

    def sent(self, c):
        c.wait_send()
        del self.pending[id(c)]

    def all_sent(self):
        for c in self.pending.values():
            c.wait_send()


def greet():
    bar = pltpu.get_barrier_semaphore()
    for a in "xyz":
        for s in (1, 2, 3):
            pl.semaphore_signal(bar, inc=1, device_id=neighbour(a, s), device_id_type=MESHID)
    for d in (1, 2, 3):
        diagonal = {"z": lax.rem(lax.axis_index("z") + d, 4), "yhi": 1 - lax.axis_index("yhi")}
        pl.semaphore_signal(bar, inc=1, device_id=diagonal, device_id_type=MESHID)
    pl.semaphore_signal(bar, inc=1, device_id=neighbour("core", 1), device_id_type=MESHID)
    return lambda: pl.semaphore_wait(bar, 13)


def to_peers(rc, src_of, dst, send, recv, block):
    out = []
    for d in range(1, 8):
        p = lax.rem(block + d, 8)
        out.append(rc(src_of(p), dst.at[block], send.at[d], recv.at[d], block_device(p)))
    return out


PIECES = (((0, 32), (32, 32), (64, 32)), ((0, 16), (16, 48), (64, 32)), ((0, 32), (32, 32), (64, 32)))


class Gather:
    def __init__(self, rc, g, w, sems, item, r):
        self.rc, self.g, self.w, self.item, self.r = rc, g, w, item, r
        self.flying = {}
        self.ts, self.tr, self.cs, self.cr = sems
        self.k = item * 3 + r
        self.lo, self.n = PIECES[item][r]
        self.me = my_place()
        self.core = lax.axis_index("core")
        self.forwarded = []

    def at(self, pos, lo=0, n=None):
        z = slice(None) if pos["z"] is None else pos["z"]
        x = slice(None) if pos["x"] is None else pos["x"]
        if pos["y"] is None:
            yh = yl = slice(None)
        else:
            yh, yl = pos["y"] // 2, lax.rem(pos["y"], 2)
        return self.g.at[z, yh, yl, x, self.core, pl.ds(self.lo + lo, self.n if n is None else n)]

    def pos(self, st, d=0):
        p = {a: (None if i < st else self.me[a]) for i, a in enumerate(ORDERS[self.r])}
        a = ORDERS[self.r][st]
        p[a] = lax.rem(self.me[a] + (d + 4), 4)
        return p

    def to_sibling(self, ref):
        k = self.k * 4 + len(self.forwarded)
        self.forwarded.append(self.rc(ref, ref, self.cs.at[k], self.cr.at[k], neighbour("core", 1)))

    def push(self, k, src, dst, a, d):
        s = k % 3 if k < 6 else k % 2
        if s in self.flying:
            self.rc.sent(self.flying[s])
        c = self.rc(src, dst, self.ts.at[3 * self.k + s], self.tr.at[10 * self.k + k], neighbour(a, d))
        self.flying[s] = c
        return c

    def straight(self, st):
        ref = self.at(self.pos(st))
        src = ref if st else self.w.at[pl.ds(self.lo, self.n)]
        self.c = [self.push(3 * st + d - 1, src, ref, ORDERS[self.r][st], d) for d in (1, 2, 3)]

    def line(self, st):
        for c in self.c:
            c.wait_recv()
        if st == 1:
            self.to_sibling(self.at(self.pos(2)))

    def near(self):
        ref = self.at(self.pos(2))
        self.c = [self.push(6 + i, ref, ref, ORDERS[self.r][2], d) for i, d in enumerate((1, -1))]

    def pass_on(self):
        self.f = []
        for i, d in enumerate((1, -1)):
            self.c[i].wait_recv()
            p = self.pos(2, -d)
            first = 16 * ((self.n + 16) // 32)
            lo, n = ((0, first), (first, self.n - first))[i]
            if n:
                half = self.at(p, lo, n)
                self.f.append(self.push(8 + i, half, half, ORDERS[self.r][2], d))
            self.to_sibling(self.at(p))

    def last(self):
        for f in self.f:
            f.wait_recv()
        self.to_sibling(self.at(self.pos(2, 2)))

    def complete(self):
        for c in self.forwarded:
            c.wait_recv()

    def drained(self):
        for c in [*self.flying.values(), *self.forwarded]:
            self.rc.sent(c)


def forward_kernel(zx_ref, wo_ref, bc_ref, hid, cot_ref, norm_gain, dt_ref, conv_x, taps_bc, log_ref, shift_ref, skip_ref,
                   gate_ref, g_ref, gb_ref,
                   pk_out, x_pre_out, x_conv_out, d_x_out, normed_t_out, cot_t_out, state_out, bc_pre_out, bc_conv_out,
                   steps_out, rates_out, cols_out, cum_row_out, step_row_out, dec_out, result_out,
                   out_in_out, d_z_out, gain_part_out, skip_part_out, d_cols_out, d_bc_out, conv_slope_out, leaving_out, d_state_out,
                   normed_t2_out, cot_t2_out, out_in2_out, d_z2_out, *scr):
    (pk, x_pre, x_conv, normed_t, cot_t, state, bc_pre, bc_conv, steps, rates, cols, cum_row, step_row, dec,
     result, out_in, d_z, gain_part, skip_part, d_cols, d_bc, conv_slope, leaving,
     cot, normed, halo, dt_own, small_all, zb, yb, uppers, lowers, wx, wo, gram, d_gram, local, rec_a, out_b, dec_own, square,
     scales, acc, d_c, pk_ref, gain, zx, grown, entered,
     ts, tr, cs, cr, bs, br, qs, qr, es, er, fs, fr, ds, dr, hs, hr, lsem, wsem, osem, dsem, xs, xr) = scr
    rc = Sender()
    me = my_place()
    core = lax.axis_index("core")
    x, ylo = me["x"], lax.axis_index("ylo")
    block = lax.axis_index("z") * 2 + lax.axis_index("yhi")
    arrived = greet()
    writes, count = [], [0]

    def out(src, dst):
        c = pltpu.make_async_copy(src, dst, osem.at[count[0]])
        c.start()
        count[0] += 1
        writes.append(c)

    cot_c = pltpu.make_async_copy(cot_ref, cot, lsem.at[3])
    cot_c.start()
    def spot(ref):
        return ref.at[me["z"], me["y"] // 2, ylo, x, core]

    split = zx_ref[...].astype(F32)
    for i in range(2):
        zx[i] = split[:, i, :].astype(BF16)
    own_w = [pltpu.make_async_copy(src, spot(dst), lsem.at[4 + i])
             for i, (src, dst) in enumerate(((zx.at[1], wx), (zx.at[0], g_ref.at[1]), (wo_ref, wo)))]
    for c in own_w:
        c.start()
    pk_ref[...] = jnp.zeros_like(pk_ref)
    pk_ref[0:5] = conv_x[...]
    pk_ref[5] = gate_ref[...]
    for at, ref in ((6, log_ref), (7, shift_ref), (14, skip_ref)):
        pk_ref[at, 0:HEADS] = ref[...]
    pk_ref[8 : 8 + HEADS, 0:96] = dt_ref[...].astype(F32)
    gain[0] = norm_gain[...]
    arrived()

    gx, gz, go = [[Gather(rc, g, w, (ts, tr, cs, cr), i, r) for r in range(3)]
                  for i, (g, w) in enumerate(((wx, zx.at[1]), (g_ref.at[1], zx.at[0]), (wo, wo_ref)))]

    def each(group, name, *args):
        for c in group:
            getattr(c, name)(*args)

    each(gx, "straight", 0)
    pk_c = to_peers(rc, lambda p: pk_ref, pk, qs, qr, block)

    def small(lo, n):
        cols = pl.ds(lo, n)
        sems = iter(range(9 * (lo // 256), 9 * (lo // 256) + 9))

        def push(src, dst, device):
            k = next(sems)
            return rc(src, dst, bs.at[k], br.at[k], device)

        def at(yl, x_at):
            return gb_ref.at[yl, x_at, core, :, cols]

        def over_y(src):
            own = pltpu.make_async_copy(src, at(ylo, x), lsem.at[1 + lo // 256])
            own.start()
            return [push(src, at(ylo, x), {"ylo": 1 - ylo}), push(src, at(ylo, x), neighbour("core", 1))], own

        def over_x(first, own):
            first[0].wait_recv()
            own.wait()
            line = gb_ref.at[:, x, core, :, cols]
            other = at(1 - ylo, x)
            rest = [push(line, line, neighbour("x", d)) for d in (1, 2, 3)]
            return rest, [first[1], push(other, other, neighbour("core", 1))]

        def to_sibling(rest, cores):
            for d in (1, 2, 3):
                rest[d - 1].wait_recv()
                line = gb_ref.at[:, lax.rem(x + 4 - d, 4), core, :, cols]
                cores.append(push(line, line, neighbour("core", 1)))
            return cores

        return over_y, over_x, to_sibling

    bc_y, bc_x, bc_end = small(0, 256)
    dt_y, dt_x, dt_end = small(256, 128)
    bc_s = bc_y(bc_ref)
    pk[block] = pk_ref[...]

    def normalize(part, at):
        v = part[...].astype(F32)
        r = lax.rsqrt(jnp.mean(v * v, axis=1, keepdims=True) + EPS)
        normed[pl.ds(at, part.shape[0])] = (v * r * gain[...]).astype(BF16)

    normalize(hid, HALO)
    each(gx, "line", 0)
    for c in own_w:
        c.wait()
    each(gx, "straight", 1)
    each(gz, "straight", 0)
    halo_c = rc(hid.at[pl.ds(ROWS - HALO, HALO)], halo, hs, hr, block_device(lax.rem(block + 1, 8)))
    each(go, "straight", 0)

    for c in pk_c:
        c.wait_recv()
    out(pk, pk_out)
    columns = jnp.concatenate([pk[m, 8 : 8 + HEADS, 0:128] for m in range(GROUPS)] + [jnp.zeros((80, 128), F32)], axis=0)
    dt_own[...] = columns.T[:96].astype(BF16)
    dt_s = dt_y(dt_own)
    normed_t[...] = normed[HALO:, :].T.reshape(8, 2, 96, ROWS)
    out(normed_t, normed_t_out)
    each(gx, "line", 1)
    each(gx, "near")
    bc_s = bc_x(*bc_s)
    dt_s = dt_x(*dt_s)
    cot_c.wait()
    cot_t[...] = cot[...].T.reshape(8, 2, 96, ROWS)
    out(cot_t, cot_t_out)
    halo_c.wait_recv()
    normalize(halo, 0)

    @pl.when(block == 0)
    def _():
        normed[pl.ds(0, HALO)] = jnp.zeros((HALO, WIDTH), BF16)

    each(gx, "pass_on")
    each(gz, "line", 0)
    each(gz, "straight", 1)
    b_core = bc_end(*bc_s) + dt_end(*dt_s)
    for c in b_core:
        c.wait_recv()
    small_in = pltpu.make_async_copy(gb_ref, small_all, lsem.at[1])
    small_in.start()
    each(go, "line", 0)
    each(go, "straight", 1)
    small_in.wait()

    def row(at):
        pieces = [pk[m, at : at + 1, 0:HEADS] for m in range(GROUPS)]
        return jnp.concatenate(pieces + [jnp.zeros((1, 80), F32)], axis=1)

    rates[0:1] = row(6)
    rates[1:2] = row(7)
    rates[2:8] = jnp.zeros((6, 128), F32)
    little = dot(normed[...], small_all[...].reshape(WIDTH, COLS))
    bc_pre[...] = little[:, :256]
    pre = conv_pre(little[:, :256], taps_bc[...])
    bc_conv[...] = (pre * jax.nn.sigmoid(pre)).astype(BF16)
    shifted = little[HALO:, 256:384] + rates[1:2]
    steps[...] = shifted
    step = softplus(shifted)
    decay = -step * jnp.exp(rates[0:1])
    cum = dot(triangle(False).astype(F32), decay, precision=lax.Precision.HIGHEST)
    cum_t = cum.T
    step_t = step.T
    each(gx, "last")
    each(gz, "line", 1)
    each(gz, "near")
    lasts = jnp.broadcast_to(jnp.exp(cum_t[:, ROWS - 1 : ROWS]), (128, 128))
    for m in range(GROUPS):
        at = slice(HEADS * m, HEADS * m + 8)
        cols[m] = jnp.concatenate([cum[:, at], step[:, at]], axis=1)
        cum_row[m] = cum_t[HEADS * m : HEADS * m + 8]
        step_row[m] = step_t[HEADS * m : HEADS * m + 8]
        dec_own[m] = lasts[HEADS * m : HEADS * m + 8]
    dec_c = to_peers(rc, lambda p: dec_own.at[p], dec, ds, dr, block)
    dec[block] = dec_own[block]
    gram[...] = jnp.where(triangle(False), dot(bc_conv[:, 128:], bc_conv[:, :128], (1, 1)), 0.0)
    out(bc_pre, bc_pre_out)
    out(bc_conv, bc_conv_out)
    out(steps, steps_out)
    out(rates, rates_out)
    out(cols, cols_out)
    out(cum_row, cum_row_out)
    out(step_row, step_row_out)
    each(gx, "complete")

    x_flat, o_flat = wx.reshape(GROUPS, WIDTH, COLS), wo.reshape(GROUPS, WIDTH, COLS)
    g_flat = g_ref.reshape(2, GROUPS, WIDTH, COLS)

    def z_copy(m):
        return pltpu.make_async_copy(g_flat.at[1, m], x_flat.at[m], wsem.at[m])

    def pairs(buf, lo, hi, body, ready=None):
        @pl.loop(lo, hi)
        def _(i):
            if ready is not None:
                for k in range(2):
                    ready(2 * i + k).wait()
            body(i, jnp.concatenate([buf[2 * i], buf[2 * i + 1]], axis=1))

    out(wx, g_ref.at[0])
    x_written = writes.pop()

    def to_owner(m):
        return pltpu.make_async_remote_copy(src_ref=local.at[m], dst_ref=rec_a.at[block], send_sem=es.at[m], recv_sem=er.at[block],
                                            device_id=block_device(m), device_id_type=MESHID)

    def second_pair(i, w):
        both = dot(normed[...], w)
        for k in range(2):
            m = 2 * i + k
            ext = both[:, COLS * k : COLS * k + COLS]
            x_pre[m] = ext
            pre = conv_pre(ext, pk[m])
            xc = (pre * jax.nn.sigmoid(pre)).astype(BF16)
            x_conv[m] = xc
            cum, step = cols[m][:, :8], cols[m][:, 8:]
            wide = spread(step * jnp.exp(cum[ROWS - 1 : ROWS] - cum))
            leaving[m] = wide.astype(BF16)
            weighted = (xc.astype(F32) * wide).astype(BF16)
            local[m] = dot(weighted, bc_conv[:, :128], (0, 0)).astype(BF16)
            pl.when(m != block)(lambda m=m: to_owner(m).start())

    pairs(x_flat, 0, 4, second_pair)
    each(go, "line", 1)
    rec_a[block] = local[block]
    out(x_pre, x_pre_out)
    out(x_conv, x_conv_out)
    out(leaving, leaving_out)

    top, low = slice(0, HALF), slice(HALF, ROWS)

    def scan_group(m):
        xc = x_conv[m]
        cum = cols[m][:, :8]
        rows = cum_row[m]
        step_rows = step_row[m]
        parts = []
        for h in range(HEADS):
            xh = xc[:, 64 * h : 64 * h + 64]
            col, row, step = cum[:, h : h + 1], rows[h : h + 1, :], step_rows[h : h + 1, :]
            upper = (jnp.exp(jnp.minimum(col[top] - row[:, top], 0.0)) * step[:, top]).astype(BF16)
            lower = (jnp.exp(jnp.minimum(col[low] - row, 0.0)) * step).astype(BF16)
            uppers[m, h] = upper
            lowers[m, h] = lower
            parts.append(jnp.concatenate([dot((upper.astype(F32) * gram[top, top]).astype(BF16), xh[top]),
                                          dot((lower.astype(F32) * gram[low]).astype(BF16), xh)], axis=0))
        yb[m] = jnp.concatenate(parts, axis=1) + spread(pk[m, 14:15, 0:8]) * xc.astype(F32)

    pl.loop(0, 4)(scan_group)
    each(gz, "pass_on")
    each(go, "near")
    pl.loop(4, GROUPS)(scan_group)
    for c in dec_c:
        c.wait_recv()
    out(dec, dec_out)

    def exchanged(src, sends, recvs):
        for d in range(1, 8):
            other = lax.rem(block + d, 8)
            pltpu.make_async_remote_copy(src_ref=src.at[other], dst_ref=rec_a.at[other], send_sem=sends.at[other],
                                         recv_sem=recvs.at[other], device_id=block_device(other), device_id_type=MESHID).wait()

    def carry(order):
        for h in range(HEADS):
            rows = pl.ds(64 * h, 64)
            run = jnp.zeros((64, 128), F32)
            for i in order:
                out_b[i, rows] = run.astype(BF16)
                run = run * dec[i, pl.ds(h, 1)] + rec_a[i, rows].astype(F32)

    exchanged(local, es, er)
    carry(range(BLOCKS))
    f_c = to_peers(rc, lambda p: out_b.at[p], state, fs, fr, block)
    state[block] = out_b[block]

    @pl.loop(0, GROUPS)
    def _(m):
        pre = conv_pre(x_pre[m], pk[m])
        sig = jax.nn.sigmoid(pre)
        conv_slope[m] = (sig * (1.0 + pre * (1.0 - sig))).astype(BF16)

    out(conv_slope, conv_slope_out)
    each(gz, "last")
    each(gz, "complete")
    x_written.wait()
    each(gx, "drained")
    for m in range(GROUPS):
        z_copy(m).start()

    def gate_pair(i, w):
        z = dot(normed[HALO:, :], w)
        for k in range(2):
            part = z[:, COLS * k : COLS * k + COLS]
            sig = jax.nn.sigmoid(part)
            zb[2 * i + k] = part * sig
            d_z[2 * i + k] = (sig * (1.0 + part * (1.0 - sig))).astype(BF16)

    pairs(x_flat, 0, 4, gate_pair, z_copy)
    each(go, "pass_on")
    for c in f_c:
        c.wait_recv()
        rc.sent(c)
    out(state, state_out)
    square[...] = jnp.zeros_like(square)
    c_mat = bc_conv[:, 128:]

    @pl.loop(0, GROUPS)
    def _(m):
        wide = spread(jnp.exp(cols[m][:, :8]))
        carried = wide * dot(c_mat, state[m], (1, 1))
        grown[m] = wide
        entered[m] = carried
        y = yb[m] + carried
        gated = y * zb[m]
        yb[m] = gated
        d_z[m] = (y * d_z[m].astype(F32)).astype(BF16)
        sq = gated * gated
        square[...] += sq[:, :128] + sq[:, 128:256] + sq[:, 256:]

    each(go, "last")
    r2 = lax.rsqrt(jnp.sum(square[...], axis=1, keepdims=True) / INNER + EPS)

    @pl.loop(0, GROUPS)
    def _(m):
        out_in[m] = (yb[m] * r2 * pk[m, 5:6]).astype(BF16)

    acc[...] = jnp.zeros_like(acc)
    d_c[...] = jnp.zeros_like(d_c)
    d_gram[...] = jnp.zeros_like(d_gram)
    each(go, "complete")

    def result_pair(i, w):
        acc[...] += dot(jnp.concatenate([out_in[2 * i], out_in[2 * i + 1]], axis=1), w, (1, 1))

    pairs(o_flat, 0, 4, result_pair)
    total = jnp.sum(cot[...].astype(F32) * acc[...], axis=1, keepdims=True)
    scales[...] = jnp.concatenate([r2, r2 * r2 * (total / INNER), jnp.zeros((ROWS, 6), F32)], axis=1)
    result[...] = (hid[...].astype(F32) + acc[...]).astype(BF16)
    out(result, result_out)

    def to_owner_back(m):
        return pltpu.make_async_remote_copy(src_ref=local.at[m], dst_ref=rec_a.at[block], send_sem=es.at[m], recv_sem=er.at[block],
                                            device_id=block_device(m), device_id_type=MESHID)

    def gate_back(i, w):
        r2, slope = scales[:, 0:1], scales[:, 1:2]
        both = dot(cot[...], w)
        for k in range(2):
            m = 2 * i + k
            d = both[:, COLS * k : COLS * k + COLS]
            gated = yb[m]
            gain_part[m] = jnp.sum(d * (gated * r2), axis=0, keepdims=True)
            d_gated = r2 * (d * pk[m, 5:6]) - gated * slope
            dy = d_gated * zb[m]
            d_z[m] = (d_gated * d_z[m].astype(F32)).astype(BF16)
            yb[m] = dy
            skip_part[m] = jnp.sum(dy * x_conv[m].astype(F32), axis=0, keepdims=True)
            dye = (grown[m] * dy).astype(BF16)
            local[m] = dot(dye, c_mat, (0, 0)).astype(BF16)
            pl.when(m != block)(lambda m=m: to_owner_back(m).start())
            d_c[...] += dot(dye, state[m])
            d_cols[m] = jnp.concatenate([gathered_heads(dy * entered[m]), jnp.zeros((ROWS, 8), F32)], axis=1)

    pairs(o_flat, 0, 4, gate_back)
    rec_a[block] = local[block]
    across = [rc(src, dst, xs.at[i], xr.at[i], neighbour("core", 1)) for i, (src, dst) in enumerate((
        (cot_t.at[:, 1 - core], cot_t2_out), (out_in, out_in2_out), (normed_t.at[:, 1 - core], normed_t2_out),
        (d_z, d_z2_out)))]
    out(out_in, out_in_out)
    out(d_z, d_z_out)
    out(gain_part, gain_part_out)

    def d_cols_copy(m):
        return pltpu.make_async_copy(d_cols.at[m], d_cols_out.at[m], dsem.at[m])

    def d_x_copy(m):
        return pltpu.make_async_copy(zb.at[m], d_x_out.at[m], wsem.at[m])

    def inner_group(m):
        dy = yb[m]
        dyb = dy.astype(BF16)
        dy_t = dyb.T
        xc = x_conv[m]
        d_cum = d_cols[m][:, :8]
        lane = lax.broadcasted_iota(jnp.int32, (ROWS, 8), 1)
        parts = []
        sums = []
        for h in range(HEADS):
            xh = xc[:, 64 * h : 64 * h + 64]
            dyh = dyb[:, 64 * h : 64 * h + 64]
            upper, lower = uppers[m, h].astype(F32), lowers[m, h].astype(F32)
            tu = upper * dot(dyh[top], xh[top], (1, 1))
            tl = lower * dot(dyh[low], xh, (1, 1))
            d_gram[top, top] += tu
            d_gram[low] += tl
            qu, ql = tu * gram[top, top], tl * gram[low]
            col = jnp.sum(ql, axis=0, keepdims=True)
            sums.append(jnp.concatenate([col[:, top] + jnp.sum(qu, axis=0, keepdims=True), col[:, low]], axis=1))
            row = jnp.concatenate([jnp.sum(qu, axis=1, keepdims=True),
                                   jnp.sum(ql[:, top] + ql[:, low], axis=1, keepdims=True)], axis=0)
            d_cum = jnp.where(lane == h, d_cum + row, d_cum)
            dyt = dy_t[64 * h : 64 * h + 64]
            below = dot(dyt[:, low], (lower * gram[low]).astype(BF16))
            above = dot(dyt[:, top], (upper * gram[top, top]).astype(BF16))
            parts.append(jnp.concatenate([below[:, top] + above, below[:, low]], axis=1))
        sums = jnp.concatenate(sums + [jnp.zeros((2, ROWS), F32)], axis=0).T
        zb[m] = jnp.concatenate(parts, axis=0).T + spread(pk[m, 14:15, 0:8]) * dy
        d_x_copy(m).start()
        d_cols[m] = jnp.concatenate([d_cum - sums, sums], axis=1)
        d_cols_copy(m).start()

    out(skip_part, skip_part_out)
    pl.loop(0, GROUPS - 1)(inner_group)
    exchanged(local, es, er)
    carry(range(BLOCKS - 1, -1, -1))
    out(out_b, d_state_out)
    pl.loop(GROUPS - 1, GROUPS)(inner_group)
    dg = jnp.where(triangle(False), d_gram[...], 0.0).astype(BF16)
    d_bc[:, :128] = dot(dg, c_mat, (0, 0))
    d_bc[:, 128:] = d_c[...] + dot(dg, bc_conv[:, :128])
    out(d_bc, d_bc_out)
    for c in across:
        c.wait_recv()
    for c in writes:
        c.wait()
    for m in range(GROUPS):
        d_x_copy(m).wait()
        d_cols_copy(m).wait()
    rc.all_sent()


HALF = ROWS // 2
RESULTS = (
    ("pk", (GROUPS, 16, COLS), F32), ("x_pre", (GROUPS, HALO + ROWS, COLS), F32), ("x_conv", (GROUPS, ROWS, COLS), BF16),
    ("d_x", (GROUPS, ROWS, COLS), F32), ("normed_t", (8, 2, 96, ROWS), BF16), ("cot_t", (8, 2, 96, ROWS), BF16),
    ("state", (GROUPS, COLS, 128), BF16), ("bc_pre", (HALO + ROWS, 256), F32), ("bc_conv", (ROWS, 256), BF16),
    ("steps", (ROWS, 128), F32), ("rates", (8, 128), F32), ("cols", (GROUPS, ROWS, 16), F32),
    ("cum_row", (GROUPS, 8, ROWS), F32), ("step_row", (GROUPS, 8, ROWS), F32), ("dec", (BLOCKS, 8, 128), F32),
    ("result", (ROWS, WIDTH), BF16), ("out_in", (GROUPS, ROWS, COLS), BF16), ("d_z", (GROUPS, ROWS, COLS), BF16),
    ("gain_part", (GROUPS, 1, COLS), F32), ("skip_part", (GROUPS, 1, COLS), F32), ("d_cols", (GROUPS, ROWS, 16), F32),
    ("d_bc", (ROWS, 256), F32), ("conv_slope", (GROUPS, ROWS, COLS), BF16), ("leaving", (GROUPS, ROWS, COLS), BF16),
    ("d_state", (GROUPS, COLS, 128), BF16),
)
SIBLING = (
    ("normed_t2", (8, 96, ROWS), BF16), ("cot_t2", (8, 96, ROWS), BF16), ("out_in2", (GROUPS, ROWS, COLS), BF16),
    ("d_z2", (GROUPS, ROWS, COLS), BF16),
)


def forward(zx, wo, bc, hid, cot, *params):
    hbm = pl.BlockSpec(memory_space=pl.ANY)
    vmem = pl.BlockSpec(memory_space=pltpu.VMEM)
    sem = pltpu.SemaphoreType.DMA

    def v(*shape, dtype=F32):
        return pltpu.VMEM(shape, dtype)

    def b(*shape):
        return v(*shape, dtype=BF16)

    groups = (GROUPS, ROWS, COLS)
    outs = pl.pallas_call(
        forward_kernel,
        out_shape=(sds(2, 4, 2, 2, 4, 2, 96, COLS, dtype=BF16), sds(2, 4, 2, 96, COLS, dtype=BF16),
                   *[sds(*shape, dtype=dtype) for _, shape, dtype in RESULTS + SIBLING]),
        in_specs=[vmem, hbm, vmem, vmem, hbm] + [vmem] * 8,
        out_specs=(hbm,) * (2 + len(RESULTS) + len(SIBLING)),
        scratch_shapes=[
            *[pltpu.VMEM(shape, dtype) for name, shape, dtype in RESULTS if name not in ("d_x", "d_state")],
            b(ROWS, WIDTH), b(HALO + ROWS, WIDTH), b(HALO, WIDTH), b(96, 128), b(2, 4, 2, 96, COLS),
            v(*groups), v(*groups), b(GROUPS, HEADS, HALF, HALF), b(GROUPS, HEADS, HALF, ROWS),
            b(4, 2, 2, 4, 2, 96, COLS), b(4, 2, 2, 4, 2, 96, COLS),
            v(ROWS, ROWS), v(ROWS, ROWS),
            b(GROUPS, COLS, 128), b(GROUPS, COLS, 128), b(GROUPS, COLS, 128), v(GROUPS, 8, 128),
            v(ROWS, 128), v(ROWS, 8), v(ROWS, WIDTH), v(ROWS, 128), v(16, COLS), v(1, WIDTH), b(2, 96, COLS), v(*groups), v(*groups),
            sem((27,)), sem((90,)), sem((36,)), sem((36,)), sem((18,)), sem((18,)), sem((8,)), sem((8,)), sem((8,)), sem((8,)),
            sem((8,)), sem((8,)), sem((8,)), sem((8,)), sem, sem, sem((7,)), sem((GROUPS,)), sem((len(RESULTS),)), sem((GROUPS,)), sem((4,)),
            sem((4,)),
        ],
        compiler_params=pltpu.CompilerParams(collective_id=0, has_side_effects=True, vmem_limit_bytes=63 * 2**20),
        name="forward_between_devices",
    )(zx, wo, bc, hid, cot, *params)
    return outs[0], outs[1], dict(zip([name for name, _, _ in RESULTS + SIBLING], outs[2:]))


class Total:
    def __init__(self, rc, value, lines, axes, send, recv):
        self.rc, self.value, self.lines, self.axes, self.send, self.recv = rc, value, lines, axes, send, recv
        self.me = dict(my_place(), core=lax.axis_index("core"), ylo=lax.axis_index("ylo"))

    def step(self, j):
        if j > 0:
            for c in self.flying:
                c.wait_recv()
                self.rc.sent(c)
            l, i = self.lines, j - 1
            if self.axes[i] in ("core", "ylo"):
                self.value[...] = l[i, 0] + l[i, 1]
            else:
                self.value[...] = (l[i, 0] + l[i, 1]) + (l[i, 2] + l[i, 3])
        if j < len(self.axes):
            a = self.axes[j]
            mine = self.lines.at[j, self.me[a]]
            mine[...] = self.value[...]
            if a in ("core", "ylo"):
                devices = [{a: 1 - self.me[a]}]
            else:
                devices = [neighbour(a, d) for d in (1, 2, 3)]
            self.flying = [self.rc(mine, mine, self.send.at[d], self.recv.at[3 * j + d], device)
                           for d, device in enumerate(devices)]


class SmallSum:
    def __init__(self, rc, parts, xs, ys, zs, send, recv):
        self.rc, self.parts, self.xs, self.ys, self.zs = rc, parts, xs, ys, zs
        self.send, self.recv = send, recv
        self.me = my_place()

    def step(self, j, out=None):
        rc, me, parts, s, r = self.rc, self.me, self.parts, self.send, self.recv
        ylo = lax.rem(me["y"], 2)
        if j == 0:
            self.c = [rc(parts.at[:, lax.rem(me["x"] + d, 4)], self.xs.at[d - 1], s.at[d], r.at[d], neighbour("x", d))
                      for d in (1, 2, 3)]
            return
        for c in self.c:
            c.wait_recv()
        if j == 1:
            for yl in range(2):
                m = parts.at[yl, me["x"]]
                m[...] = (f32(m) + f32(self.xs.at[0, yl]) + f32(self.xs.at[1, yl]) + f32(self.xs.at[2, yl])).astype(BF16)
            self.ys[me["y"]] = parts[ylo, me["x"]]
            self.c = [rc(parts.at[lax.rem(me["y"] + d, 2), me["x"]], self.ys.at[me["y"]], s.at[3 + d], r.at[3 + d],
                         neighbour("y", d)) for d in (1, 2, 3)]
        elif j == 2:
            y = self.ys
            m = self.zs.at[me["z"]]
            m[...] = ((f32(y.at[0]) + f32(y.at[1])) + (f32(y.at[2]) + f32(y.at[3]))).astype(BF16)
            self.c = [rc(m, m, s.at[6 + d], r.at[6 + d], neighbour("z", d)) for d in (1, 2, 3)]
        elif j == 3:
            z = self.zs
            return (f32(z.at[0]) + f32(z.at[1])) + (f32(z.at[2]) + f32(z.at[3]))


def part_of(ref, item, pos, lo, n):
    z = slice(None) if pos["z"] is None else pos["z"]
    x = slice(None) if pos["x"] is None else pos["x"]
    if pos["y"] is None:
        yh = yl = slice(None)
    else:
        yh, yl = pos["y"] // 2, lax.rem(pos["y"], 2)
    return ref.at[item, z, yh, yl, x, pl.ds(lo, n)]


class Chunk:
    def __init__(self, rc, own, out, bufs, sems, item, slot, wide, r):
        self.rc, self.own, self.out, self.item, self.slot, self.r = rc, own, out, item, slot, r
        full, half, second, third = bufs
        self.full, self.half = full[r].at[wide], half[r].at[wide]
        self.direct = {1: second[r].at[slot], 2: third.at[slot * 3 + r]}
        self.send, self.recv = sems
        self.number = slot * 3 + r
        self.base = self.number * 10
        self.me = my_place()
        self.flying = {}

    def slab(self, st, d, lo=0, n=SUB):
        p = {a: (self.me[a] if i < st else None) for i, a in enumerate(ORDERS[self.r])}
        a = ORDERS[self.r][st]
        p[a] = lax.rem(self.me[a] + (d + 4), 4)
        return part_of(self.own, self.slot, p, self.r * SUB + lo, n)

    def loop(self, st, body):
        sizes = []
        for a, n in (("z", (4,)), ("y", (2, 2)), ("x", (4,))):
            if ORDERS[self.r].index(a) > st:
                sizes += n
        if not sizes:
            body(())
        elif len(sizes) == 1 or sizes == [2, 2]:
            for i in range(4):
                body((i,) if len(sizes) == 1 else (i // 2, i % 2))
        else:
            @pl.loop(0, 4)
            def _(i):
                for k in range(4):
                    if sizes == [4, 4]:
                        body((i, k))
                    elif sizes == [4, 2, 2]:
                        body((i, k // 2, k % 2))
                    else:
                        body((i // 2, lax.rem(i, 2), k))

    def push(self, k, src, dst, st, d):
        s = k % 2 if k < 4 else (k - 4) % 3
        if s in self.flying:
            self.rc.sent(self.flying[s])
        c = self.rc(src, dst, self.send.at[3 * self.number + s], self.recv.at[self.base + k], neighbour(ORDERS[self.r][st], d))
        self.flying[s] = c
        return c

    def far(self):
        self.far_c = [self.push(i, self.slab(0, 2, 16 * i, 16), self.half.at[i], 0, d) for i, d in enumerate((1, -1))]

    def near(self):
        self.near_c = []
        for i, d in enumerate((1, -1)):
            self.far_c[i].wait_recv()
            mine = self.slab(0, d, 16 * i, 16)

            def add(index, mine=mine, i=i):
                m = mine.at[index]
                m[...] = m[...] + self.half[(i, *index)]

            self.loop(0, add)
            self.near_c.append(self.push(2 + i, self.slab(0, d), self.full.at[i], 0, d))

    def straight(self, st):
        self.straight_c = [self.push(1 + 3 * st + d - 1, self.slab(st, d), self.direct[st].at[d - 1], st, d) for d in (1, 2, 3)]

    def step(self, j):
        if j == 0:
            self.far()
        elif j == 1:
            self.near()
        elif j == 2:
            for c in self.near_c:
                c.wait_recv()
            mine = self.slab(0, 0)

            def add(index):
                m = mine.at[index]
                m[...] = (f32(m) + f32(self.full.at[(0, *index)]) + f32(self.full.at[(1, *index)])).astype(BF16)

            self.loop(0, add)
            self.straight(1)
        else:
            for c in self.straight_c:
                c.wait_recv()
            st = j - 2
            mine = self.slab(st, 0)
            got = self.direct[st]

            def total(index):
                m = mine.at[index] if index else mine
                return (f32(m) + f32(got.at[(0, *index)])) + (f32(got.at[(1, *index)]) + f32(got.at[(2, *index)]))

            if st == 1:
                def add(index):
                    mine[index] = total(index).astype(BF16)

                self.loop(1, add)
                self.straight(2)
            else:
                self.out(pl.ds(self.r * SUB, SUB))[...] = total(())


def backward_kernel(g_ref, x_conv_ref, d_x_ref, x_pre_ref, cols_ref, d_cols_ref, slope_ref, leaving_ref, cot_t_ref, cot_t2_ref, out_in_ref, out_in2_ref,
                    normed_t_ref, normed_t2_ref, d_z_ref, d_z2_ref, state_ref, d_state_ref, w_small_ref, hid_ref, cot_ref,
                    taps, d_bc_in, bc_pre, bc_conv, taps_bc, norm_gain, shifted, rates, gain_part, skip_part,
                    zx_out, wo_out, wbc_out, wdt_out, taps_out, taps_bc_out, log_out, shift_out, skip_out, gate_out, norm_out,
                    grad_hidden, *scr):
    (own, l_c, l_c2, l_n, l_n2, rhs_o, rhs_z, rhs_x, state, d_state, w_small, hid, cot, tails, halo_src, halo_dst, halo_x, halo_x_in, halo_bc, halo_bc_in, acc, wbuf,
     bxc, bdx, bxp, bcols, bdc, bslope, bleave, d_b, d_all, parts, small2, s_xs, s_ys, s_zs,
     v_all, v_in, v_sum, v_lines, n_all, n_lines, gain) = scr[:43]
    bufs = [scr[43:46], scr[46:49], scr[49:52], scr[52]]
    (t_s, t_r, e_s, e_r, x_s, x_r, h_s, h_r, m_s, m_r, ss, sr, vms, vmr, vs, vr, ns, nr, wsem, lsem, isem, freed) = scr[53:]
    rc = Sender()
    gain[0] = norm_gain[...]
    core = lax.axis_index("core")
    block = lax.axis_index("z") * 2 + lax.axis_index("yhi")
    arrived = greet()

    loads = {}

    def load_in(name, *pairs):
        loads[name] = []
        for src, dst in pairs:
            c = pltpu.make_async_copy(src, dst, isem.at[sum(len(v) for v in loads.values())])
            c.start()
            loads[name].append(c)

    def ready(name):
        for c in loads[name]:
            c.wait()

    load_in("o", (cot_t_ref.at[:, core], l_c), (cot_t2_ref, l_c2), (out_in_ref, rhs_o.at[0]), (out_in2_ref, rhs_o.at[1]))
    load_in("z", (normed_t_ref.at[:, core], l_n), (normed_t2_ref, l_n2), (d_z_ref, rhs_z.at[0]), (d_z2_ref, rhs_z.at[1]))
    load_in("s", (state_ref, state), (d_state_ref.at[block], d_state.at[block]))

    outs = (lambda at: zx_out.at[at, 1], lambda at: zx_out.at[at, 0], lambda at: wo_out.at[at])

    def chunks(item, slot, wide):
        return [Chunk(rc, own, outs[item], bufs, (t_s, t_r), item, slot, wide, r) for r in range(3)]

    def steps(cs, j):
        for c in cs:
            c.step(j)

    def both_tokens(own_t, other_t):
        return jnp.concatenate([own_t[...].reshape(768, ROWS), other_t[...].reshape(768, ROWS)], axis=1)

    def gradient(left, left2, rhs, slot, ready=None):
        def one(i):
            if ready is not None:
                ready(2 * i)
                ready(2 * i + 1)
            right = jnp.concatenate([jnp.concatenate([rhs[0, 2 * i + k], rhs[1, 2 * i + k]], axis=0) for k in range(2)], axis=1)
            v = dot(both_tokens(left, left2), right).astype(BF16)
            for k in range(2):
                own[slot, i, k] = v[:, COLS * k : COLS * k + COLS].reshape(2, 4, 96, COLS)

        pl.loop(0, GROUPS // 2)(one)

    oc, zc, xc_ = chunks(2, 0, 0), chunks(1, 1, 1), chunks(0, 2, 0)
    arrived()
    back = to_peers(rc, lambda p: d_state_ref.at[p], d_state, e_s, e_r, block)
    ready("o")
    gradient(l_c, l_c2, rhs_o, 0)
    steps(oc, 0)
    ready("z")

    streams = ((x_conv_ref, bxc), (d_x_ref, bdx), (x_pre_ref, bxp), (cols_ref, bcols), (d_cols_ref, bdc), (slope_ref, bslope), (leaving_ref, bleave))

    def load(m):
        k = lax.rem(m, 3)
        return [pltpu.make_async_copy(src.at[m], dst.at[k], lsem.at[k, i]) for i, (src, dst) in enumerate(streams)]

    for c in load(0) + load(1):
        c.start()
    gradient(l_n, l_n2, rhs_z, 1)
    steps(zc, 0)
    ready("s")
    for c in back:
        c.wait_recv()

    def fifth_group(m):
        k = lax.rem(m, 3)

        @pl.when(m < GROUPS - 2)
        def _():
            for c in load(m + 2):
                c.start()

        for c in load(m):
            c.wait()
        ds = d_state[m]
        xf = bxc[k].astype(F32)
        cum, step = bcols[k][:, :8], bcols[k][:, 8:]
        last = cum[ROWS - 1 : ROWS]
        tail = jnp.exp(last - cum)
        weights = step * tail
        wide = bleave[k].astype(F32)
        d_weighted = dot(bc_conv[:, :128], ds, (1, 1))
        d_b[...] += dot((xf * wide).astype(BF16), ds)
        dx = bdx[k] + wide * d_weighted
        d_weights = gathered_heads(d_weighted * xf)
        both = weights * d_weights
        lane = lax.broadcasted_iota(jnp.int32, (1, 8), 1)
        product = jnp.sum(state[m].astype(F32) * ds.astype(F32), axis=1, keepdims=True)
        d_last = jnp.sum(both, axis=0, keepdims=True)
        for h in range(HEADS):
            dots = jnp.sum(product[64 * h : 64 * h + 64], axis=0, keepdims=True)
            d_last = jnp.where(lane == h, d_last + jnp.exp(last) * dots, d_last)
        row = lax.broadcasted_iota(jnp.int32, (ROWS, 8), 0)
        d_cum = bdc[k][:, :8] - both
        d_cum = jnp.where(row == ROWS - 1, d_cum + d_last, d_cum)
        d_all[m] = jnp.concatenate([d_cum, bdc[k][:, 8:] + both], axis=1)
        ext = bxp[k]
        tap = taps[m]
        dp = dx * bslope[k].astype(F32)
        v_all[m, 0:8] = conv_grads(dp, ext, gain_part[m], skip_part[m])
        whole_dx = conv_transposed(jnp.concatenate([dp, jnp.zeros((8, COLS), F32)], axis=0), tap)
        rhs_x[0, m] = whole_dx.astype(BF16)
        tails[m] = whole_dx[ROWS - 16 :]
        halo_src[m] = dp[:8]

    d_b[...] = jnp.zeros_like(d_b)
    pl.loop(0, 3)(fifth_group)
    steps(oc, 1)
    pl.loop(3, GROUPS)(fifth_group)

    load_in("end", (w_small_ref, w_small), (hid_ref, hid), (cot_ref, cot))
    for m in range(GROUPS):
        halo_x[3 * m : 3 * m + 3] = halo_src[m, 0:3]
    before = block_device(lax.rem(block + 7, 8))
    halo = [rc(halo_x, halo_x_in, h_s.at[0], h_r.at[0], before)]

    d_bc = jnp.concatenate([d_bc_in[:, :128] + d_b[...], d_bc_in[:, 128:]], axis=1)
    ext = bc_pre[...]
    pre = conv_pre(ext, taps_bc[...])
    sig = jax.nn.sigmoid(pre)
    dp_bc = d_bc * (sig * (1.0 + pre * (1.0 - sig)))
    halo_bc[...] = dp_bc[:8]
    halo.append(rc(halo_bc, halo_bc_in, h_s.at[1], h_r.at[1], before))
    steps(zc, 1)
    zero8 = jnp.zeros((1, 256), F32)
    d_cum = jnp.concatenate([d_all[m][:, :HEADS] for m in range(GROUPS)] + [jnp.zeros((ROWS, 80), F32)], axis=1)
    d_step = jnp.concatenate([d_all[m][:, 8 : 8 + HEADS] for m in range(GROUPS)] + [jnp.zeros((ROWS, 80), F32)], axis=1)
    d_decay = dot(triangle(True).astype(F32), d_cum, precision=lax.Precision.HIGHEST)
    rate = -jnp.exp(rates[0:1])
    v = shifted[...]
    sig = jax.nn.sigmoid(v)
    far = v < -16.0
    ratio = jnp.where(far, 1.0, sig / jnp.where(far, 1.0, softplus(v)))
    d_dt = d_step * ratio + rate * d_decay * sig
    log_grad = jnp.sum(d_decay * (softplus(v) * rate), axis=0, keepdims=True)
    shift_grad = jnp.sum(d_dt, axis=0, keepdims=True)
    bc_rows = conv_grads(dp_bc, ext, jnp.concatenate([log_grad, shift_grad], axis=1), zero8)
    bc_rows = jnp.concatenate([bc_rows, jnp.zeros((8, 128), F32)], axis=1)
    for m in range(GROUPS):
        v_all[m, 8:16] = bc_rows
    vec_c = to_peers(rc, lambda p: v_all.at[p], v_in, vms, vmr, block)
    v_in[block] = v_all[block]

    for c in halo:
        c.wait_recv()
    inside = block < 7
    halo_dst[...] = jnp.zeros_like(halo_dst)
    for m in range(GROUPS):
        halo_dst[m, 0:3] = jnp.where(inside, halo_x_in[3 * m : 3 * m + 3], 0.0)

    def below(k):
        return halo_dst[k]

    def across(m):
        return pltpu.make_async_remote_copy(src_ref=rhs_x.at[0, m], dst_ref=rhs_x.at[1, m], send_sem=x_s.at[m],
                                            recv_sem=x_r.at[m], device_id=neighbour("core", 1), device_id_type=MESHID)

    def fix(m):
        ext = jnp.concatenate([jnp.zeros((16, COLS), F32), below(m)], axis=0)
        rhs_x[0, m, pl.ds(ROWS - 16, 16)] = (tails[m] + conv_transposed(ext, taps[m], 16)).astype(BF16)
        across(m).start()

    d_bc = conv_transposed(jnp.concatenate([dp_bc, jnp.where(inside, halo_bc_in[...], 0.0)], axis=0), taps_bc[...])
    small2[0] = jnp.concatenate([d_bc, d_dt], axis=1).astype(BF16)
    small_c = rc(small2.at[0], small2.at[1], m_s, m_r, neighbour("core", 1))
    pl.loop(0, GROUPS)(fix)

    def weights(m):
        k = lax.rem(m, 2)
        return [pltpu.make_async_copy(g_ref.at[i, m], wbuf.at[k, i], wsem.at[k, i]) for i in range(2)]

    for c in weights(0):
        c.start()
    steps(oc, 2)
    for a in "xyz":
        for s in (1, -1):
            pl.semaphore_signal(freed, inc=1, device_id=neighbour(a, s), device_id_type=MESHID)
    gradient(l_n, l_n2, rhs_x, 2, lambda m: across(m).wait())
    pl.semaphore_wait(freed, 6)
    steps(xc_, 0)
    small_c.wait_recv()
    parts[...] = dot(both_tokens(l_n, l_n2), small2[...].reshape(2 * ROWS, COLS)).astype(BF16).reshape(2, 4, 96, COLS)
    sums = SmallSum(rc, parts, s_xs, s_ys, s_zs, ss, sr)
    ready("end")
    acc[...] = dot(small2[0], w_small[...], (1, 1))
    def input_group(m):
        k = lax.rem(m, 2)

        @pl.when(m < GROUPS - 1)
        def _():
            for c in weights(m + 1):
                c.start()

        for c in weights(m):
            c.wait()
        lhs = jnp.concatenate([rhs_x[0, m], rhs_z[0, m]], axis=1)
        rhs = jnp.concatenate([wbuf[k, 0], wbuf[k, 1]], axis=1)
        acc[...] += dot(lhs, rhs, (1, 1))

    pl.loop(0, 2)(input_group)
    sums.step(0)
    pl.loop(2, 4)(input_group)
    steps(zc, 2)
    for c in vec_c:
        c.wait_recv()
    t = v_in[0]
    for i in range(1, BLOCKS):
        t = t + v_in[i]
    v_sum[...] = t
    vec = Total(rc, v_sum, v_lines, ("core", "x", "ylo"), vs, vr)
    vec.step(0)
    steps(xc_, 1)
    pl.loop(4, GROUPS)(input_group)
    steps(oc, 3)
    v = hid[...].astype(F32)
    r = lax.rsqrt(jnp.mean(v * v, axis=1, keepdims=True) + EPS)
    unit = v * r
    dn = acc[...]
    gain_grad = jnp.sum(dn * unit, axis=0, keepdims=True)
    for i in range(4):
        n_all[pl.ds(i, 1)] = gain_grad[:, COLS * i : COLS * i + COLS]
    n_all[pl.ds(4, 4)] = jnp.zeros((4, COLS), F32)
    nvec = Total(rc, n_all, n_lines, ("core", "x", "y", "z"), ns, nr)
    nvec.step(0)
    sums.step(1)
    vec.step(1)
    steps(zc, 3)
    d_in = dn * gain[...]
    grad_hidden[...] = r * (d_in - unit * jnp.mean(d_in * unit, axis=1, keepdims=True)) + cot[...].astype(F32)
    nvec.step(1)
    steps(xc_, 2)
    sums.step(2)
    vec.step(2)
    nvec.step(2)
    steps(oc, 4)
    steps(zc, 4)
    steps(xc_, 3)
    vec.step(3)
    nvec.step(3)

    pick = lax.broadcasted_iota(jnp.int32, (8, 128), 0) + block * HEADS
    pick = (pick == lax.broadcasted_iota(jnp.int32, (8, 128), 1)).astype(F32)

    def own_heads(row):
        return dot(row, pick, (1, 1), precision=lax.Precision.HIGHEST)

    mine = v_sum[...]
    taps_out[...] = mine[:5]
    gate_out[...] = mine[5]
    skip_out[...] = gathered_heads(mine[6:7])[0, :HEADS]
    taps_bc_out[...] = mine[8:13, :256]
    log_out[...] = own_heads(mine[13:14, :128])[0, :HEADS]
    shift_out[...] = own_heads(mine[13:14, 128:256])[0, :HEADS]
    steps(xc_, 4)
    little = sums.step(3)
    wbc_out[...] = little[:, :256]
    wdt_out[...] = dot(pick, little[:, 256:], (1, 1), precision=lax.Precision.HIGHEST)[:HEADS]
    nvec.step(4)
    for i in range(4):
        norm_out[pl.ds(COLS * i, COLS)] = n_all[i]
    rc.all_sent()


def backward(w_all, r, w_small, hid, cot, norm_gain, conv_bc):
    hbm = pl.BlockSpec(memory_space=pl.ANY)
    vmem = pl.BlockSpec(memory_space=pltpu.VMEM)
    sem = pltpu.SemaphoreType.DMA

    def buf(*shape, dtype=BF16):
        return pltpu.VMEM((*shape, COLS), dtype)

    def v(*shape, dtype=F32):
        return pltpu.VMEM(shape, dtype)

    def b(*shape):
        return v(*shape, dtype=BF16)

    scratch = [
        buf(3, 4, 2, 2, 4, 96), b(8, 96, ROWS), b(8, 96, ROWS), b(8, 96, ROWS), b(8, 96, ROWS),
        buf(2, GROUPS, ROWS), buf(2, GROUPS, ROWS), buf(2, GROUPS, ROWS), b(GROUPS, COLS, 128), b(GROUPS, COLS, 128),
        buf(WIDTH), b(ROWS, WIDTH), b(ROWS, WIDTH),
        buf(GROUPS, 16, dtype=F32), buf(GROUPS, 8, dtype=F32), buf(GROUPS, 8, dtype=F32),
        buf(24, dtype=F32), buf(24, dtype=F32), v(8, 256), v(8, 256),
        v(ROWS, WIDTH), buf(2, 2, WIDTH),
        buf(3, ROWS), buf(3, ROWS, dtype=F32), buf(3, HALO + ROWS, dtype=F32), v(3, ROWS, 16), v(3, ROWS, 16),
        buf(3, ROWS), buf(3, ROWS),
        v(ROWS, 128), v(GROUPS, ROWS, 16), buf(2, 4, 96), buf(2, ROWS), buf(3, 2, 96), buf(4, 96), buf(4, 96),
    ]
    scratch += [buf(GROUPS, 16, dtype=F32), buf(GROUPS, 16, dtype=F32), buf(16, dtype=F32), buf(3, 4, 16, dtype=F32)]
    scratch += [buf(8, dtype=F32), buf(4, 4, 8, dtype=F32), v(1, WIDTH)]
    scratch += [buf(2, 2, 4, 2, 2, SUB), buf(2, 2, 4, 4, SUB), buf(2, 2, 2, 2, 4, SUB)]
    scratch += [buf(2, 2, 4, 2, 2, 16), buf(2, 2, 4, 4, 16), buf(2, 2, 2, 2, 4, 16)]
    scratch += [buf(3, 3, 4, SUB), buf(3, 3, 4, SUB), buf(3, 3, 2, 2, SUB), buf(9, 3, SUB)]
    scratch += [sem((27,)), sem((90,)), sem((8,)), sem((8,)), sem((8,)), sem((8,)), sem((2,)), sem((2,)), sem, sem, sem((10,)), sem((10,)), sem((8,)), sem((8,)),
                sem((3,)), sem((9,)), sem((3,)), sem((12,)), sem((2, 2)), sem((3, 7)), sem((13,)), pltpu.SemaphoreType.REGULAR]
    names = ("x_conv", "d_x", "x_pre", "cols", "d_cols", "conv_slope", "leaving", "cot_t", "cot_t2", "out_in", "out_in2", "normed_t", "normed_t2", "d_z",
             "d_z2", "state", "d_state")
    return pl.pallas_call(
        backward_kernel,
        out_shape=(sds(96, 2, COLS), sds(96, COLS), sds(96, 256), sds(HEADS, 96), sds(5, COLS), sds(5, 256), sds(HEADS), sds(HEADS),
                   sds(HEADS), sds(COLS), sds(WIDTH), sds(ROWS, WIDTH)),
        in_specs=[hbm] * 21 + [vmem] * 10,
        out_specs=(vmem,) * 12,
        scratch_shapes=scratch,
        compiler_params=pltpu.CompilerParams(collective_id=1, has_side_effects=True, vmem_limit_bytes=63 * 2**20),
        name="backward_between_devices",
    )(w_all, *[r[name] for name in names], w_small, hid, cot, r["pk"], r["d_bc"], r["bc_pre"], r["bc_conv"], conv_bc, norm_gain,
      r["steps"], r["rates"], r["gain_part"], r["skip_part"])
def results_kernel(*refs):
    n = (len(refs) - 2) // 3
    sems = refs[-2:]
    into = [pltpu.make_async_copy(refs[i], refs[2 * n + i], sems[0].at[i]) for i in range(n)]
    back = [pltpu.make_async_copy(refs[2 * n + i], refs[n + i], sems[1].at[i]) for i in range(n)]
    for c in into:
        c.start()
    for c, d in zip(into, back):
        c.wait()
        d.start()
    for d in back:
        d.wait()


def as_results(*arrays):
    hbm = pl.BlockSpec(memory_space=pl.ANY)
    return pl.pallas_call(
        results_kernel,
        out_shape=tuple(jax.ShapeDtypeStruct(a.shape, a.dtype) for a in arrays),
        in_specs=[hbm] * len(arrays),
        out_specs=(hbm,) * len(arrays),
        scratch_shapes=[*[pltpu.VMEM(a.shape, a.dtype) for a in arrays], *[pltpu.SemaphoreType.DMA((len(arrays),))] * 2],
        name="results",
    )(*arrays)


def shards(hidden, grad_out, norm_gain, w_zx, w_bc, w_dt, conv_x, conv_bc, a_log, dt_bias, d_skip, gate_gain, w_out):
    w_all, w_small, r = forward(w_zx, w_out.T, w_bc, hidden, grad_out, norm_gain, w_dt.T, conv_x, conv_bc,
                                a_log, dt_bias, d_skip, gate_gain)
    w_all = w_all.reshape(2, GROUPS, WIDTH, COLS)
    w_small = w_small.reshape(WIDTH, COLS)
    zx, wo, wbc, wdt, grad_taps, grad_taps_bc, log_rate, shift, skip, gate, norm, grad_hidden = backward(
        w_all, r, w_small, hidden, grad_out, norm_gain, conv_bc)
    result, grad_hidden, norm, zx, wbc, wdt, grad_taps, grad_taps_bc, log_rate, shift, skip, gate, wo = as_results(
        r["result"], grad_hidden, norm, zx, wbc, wdt, grad_taps, grad_taps_bc, log_rate, shift, skip, gate, wo)
    return (result, grad_hidden, norm, zx, wbc, wdt.T, grad_taps, grad_taps_bc, log_rate, shift, skip, gate, wo.T)


def solution(mesh):
    finer = Mesh(mesh.devices.reshape(2, 4, 2, 4, 2), DP_MP)
    rows = P(DP_MP, None)
    placed = (rows, rows, P(), P(DP, None, MP), P(DP, None), P(DP, MP), P(None, MP), P(), P(MP), P(MP), P(MP), P(MP),
              P(MP, DP))
    return jax.shard_map(
        shards,
        mesh=finer,
        in_specs=placed,
        out_specs=(rows, rows, P(), P(DP, None, MP), P(DP, None), P(DP, MP), P(None, MP), P(), P(MP), P(MP), P(MP), P(MP),
                   P(MP, DP)),
        check_vma=False,
    )
```
